32 devices in a mesh: grp: 2 (over x), lon: 4 (over y, core), lat: 4 (over z).
Axes of the slice: x: 2, y: 2, z: 4, core: 2. Of those that a mesh axis runs over, the one named last changes fastest.
Arguments:
- fields: bfloat16 [256, 128, 512], P(('grp', 'lat'), 'lon'), parts along dimension 0, may hold values from -6 to 6
- land_mask: int32 [256, 128], P(('grp', 'lat'), 'lon'), parts along dimension 0, may hold values from 0 to 1
- cotangent: bfloat16 [256, 128, 512], P(('grp', 'lat'), 'lon'), parts along dimension 0, may hold values from -6 to 6
- kernel: float32 [7, 7, 512], replicated, may hold values from -0.875 to 0.875
- layer_norm_gain: float32 [512], replicated, may hold values from 0.5 to 1.5
- layer_norm_bias: float32 [512], replicated, may hold values from -3 to 3
- w_in: bfloat16 [512, 2048], replicated, may hold values from -0.25 to 0.25
- b_in: float32 [2048], replicated, may hold values from -3 to 3
- w_out: bfloat16 [2048, 512], replicated, may hold values from -0.125 to 0.125
- b_out: float32 [512], replicated, may hold values from -3 to 3
- layer_scale: float32 [512], replicated, may hold values from 0.3 to 1.5
Outputs:
- mixed: bfloat16 [256, 128, 512], P(('grp', 'lat'), 'lon'), parts along dimension 0
- grad_fields: bfloat16 [256, 128, 512], P(('grp', 'lat'), 'lon'), parts along dimension 0
- grad_kernel: float32 [14, 7, 512], P('grp'), parts along dimension 0
- grad_gain: float32 [1024], P('grp'), parts along dimension 0
- grad_shift: float32 [1024], P('grp'), parts along dimension 0
- grad_w_in: float32 [1024, 2048], P('grp', ('lon', 'lat')), parts along dimension 0
- grad_b_in: float32 [4096], P('grp'), parts along dimension 0
- grad_w_out: float32 [2048, 1024], P(('lon', 'lat'), 'grp'), parts along dimension 1
- grad_b_out: float32 [1024], P('grp'), parts along dimension 0
- grad_scale: float32 [1024], P('grp'), parts along dimension 0
The draws below stay inside these ranges and needn't reach their ends.
There are 2 independent parts, one for each index of `grp`. The reference program is written for one: setup_inputs(seed, part) draws one part's arguments, and reference() takes and returns one part's arrays. A program takes and returns all parts, laid end to end along the dimension named above; an argument that names none is the same for every part. Nothing has to cross between parts.
All inputs are finite; a program needn't handle non-finite values.
Results may differ from the reference program's by a relative error of at most 0.0067.
Values may be sent and summed in bfloat16 or wider, within the bound.
No kernel may reach another device: no remote copies, remote signals or barrier semaphores. Data moves between devices by JAX's collectives and lax.ppermute only.
A program may use at most 128 MiB of HBM per device.

```python
import math
import jax
import jax.numpy as jnp
from jax import lax

CHAN = 512
HIDN = 2048
CLAT = 32
NLAT = 128
NLON = 128
N_LAT = 4


def draw_land_mask(key, part):
    key = jax.random.fold_in(key, 11)
    lat_idx = lax.broadcasted_iota(jnp.int32, (NLAT, NLON), 0)
    lon_idx = lax.broadcasted_iota(jnp.int32, (NLAT, NLON), 1)
    land = lat_idx < max(NLAT // 16, 1)
    for count in range(8):
        sub = jax.random.fold_in(key, count + 1)
        keys = jax.random.split(sub, 4)
        lat_start = jax.random.randint(keys[0], (), 0, NLAT)
        height = jax.random.randint(keys[1], (), NLAT // 8 + 1, NLAT // 2 + 1)
        lon_start = jax.random.randint(keys[2], (), 0, NLON)
        breadth = jax.random.randint(keys[3], (), NLON // 8 + 1, NLON // 3 + 1)
        offset = lat_idx - lat_start
        inside = (offset >= 0) & (offset < height) & ((lon_idx - lon_start) % NLON < breadth)
        land = land | inside
    noise = jax.random.randint(jax.random.fold_in(key, 99), (NLAT, NLON), 0, 10) == 0
    land = land | noise
    return jnp.where(land, 0, 1).astype(jnp.int32)


def steps_of(key, extent, cuts, low, largest):
    factor_of = 1.0
    for position, parts in cuts:
        heights = jax.random.uniform(jax.random.fold_in(jax.random.fold_in(key, 6), position), (parts,), jnp.float32, low / len(cuts), largest / len(cuts))
        factor_of = factor_of * jnp.repeat(jnp.exp(heights), extent[position] // parts).reshape((-1,) + (1,) * (len(extent) - 1 - position))
    return factor_of


def bell_draw(own_key, shape, spread, bound, cuts=(), kind=jnp.bfloat16):
    values = spread * jax.random.normal(own_key, shape, jnp.float32)
    if cuts:
        values = values * steps_of(own_key, shape, cuts, -0.22, 0.18)
    return jnp.clip(values, -bound, bound).astype(kind)


def setup_inputs(seed: int = 0, part: int = 0) -> dict:
    streams_of = jax.random.split(jax.random.key(seed), 12)
    own_keys = jax.random.split(jax.random.fold_in(streams_of[11], part), 12)
    return {
        "fields": bell_draw(own_keys[0], (NLAT, NLON, CHAN), 1.0, 6.0, ((0, 4), (1, 4))),
        "land_mask": draw_land_mask(jax.random.fold_in(jax.random.fold_in(streams_of[11], part), 71), part),
        "cotangent": bell_draw(own_keys[2], (NLAT, NLON, CHAN), 1.0, 6.0, ((0, 4), (1, 4))),
        "kernel": bell_draw(streams_of[3], (7, 7, CHAN), 49 ** -0.5, 0.875, (), jnp.float32),
        "layer_norm_gain": jnp.clip(1.0 + 0.1 * jax.random.normal(streams_of[4], (CHAN,), jnp.float32), 0.5, 1.5),
        "layer_norm_bias": bell_draw(streams_of[5], (CHAN,), 0.5, 3.0, (), jnp.float32),
        "w_in": bell_draw(streams_of[6], (CHAN, HIDN), CHAN ** -0.5, 0.25),
        "b_in": bell_draw(streams_of[7], (HIDN,), 0.5, 3.0, (), jnp.float32),
        "w_out": bell_draw(streams_of[8], (HIDN, CHAN), HIDN ** -0.5, 0.125),
        "b_out": bell_draw(streams_of[9], (CHAN,), 0.5, 3.0, (), jnp.float32),
        "layer_scale": jnp.clip(jnp.exp(jax.random.uniform(streams_of[10], (CHAN,), jnp.float32, math.log(0.3), math.log(1.5))), 0.3, 1.5),
    }


def pad_field(field):
    wrapped = jnp.concatenate([field[:, -3:], field, field[:, :3]], axis=1)
    return jnp.pad(wrapped, ((3, 3), (0, 0), (0, 0)))

def depthwise(padded, kernel, tile_rows, tile_cols):
    result = jnp.zeros((tile_rows, tile_cols, padded.shape[2]), jnp.float32)
    for row_off in range(7):
        for col_off in range(7):
            window = padded[row_off:row_off + tile_rows, col_off:col_off + tile_cols].astype(jnp.float32)
            result = result + kernel[row_off, col_off] * window
    return result

def kernel_grad(padded, convolution_gradient, tile_rows, tile_cols):
    grad_f = convolution_gradient.astype(jnp.float32)
    entries = []
    for row_off in range(7):
        for col_off in range(7):
            window = padded[row_off:row_off + tile_rows, col_off:col_off + tile_cols].astype(jnp.float32)
            entries.append(lax.optimization_barrier(jnp.sum(grad_f * window, axis=(0, 1))))
    return jnp.stack(entries).reshape(7, 7, padded.shape[2])

def input_grad(d_padded, kernel, tile_rows, tile_cols):
    result = jnp.zeros((tile_rows, tile_cols, d_padded.shape[2]), jnp.float32)
    for row_off in range(7):
        for col_off in range(7):
            window = d_padded[6 - row_off:6 - row_off + tile_rows, 6 - col_off:6 - col_off + tile_cols].astype(jnp.float32)
            result = result + kernel[row_off, col_off] * window
    return result

def pointwise(conv_rows, field_rows, mask_rows, cot_rows, layer_norm_gain, layer_norm_bias, w_in, b_in, w_out, b_out, layer_scale):
    average = lax.optimization_barrier(jnp.mean(conv_rows, axis=-1, keepdims=True))
    mean_centered = conv_rows - average
    variance = lax.optimization_barrier(jnp.mean(mean_centered * mean_centered, axis=-1, keepdims=True))
    inverse_deviation = lax.rsqrt(variance + 1e-06)
    standardized_input = mean_centered * inverse_deviation
    normalized_input = (standardized_input * layer_norm_gain + layer_norm_bias).astype(jnp.bfloat16)
    pre_act = jnp.dot(normalized_input, w_in, preferred_element_type=jnp.float32) + b_in
    activ = jax.nn.gelu(pre_act).astype(jnp.bfloat16)
    residual_branch = jnp.dot(activ, w_out, preferred_element_type=jnp.float32) + b_out
    ocean_mask = mask_rows.astype(jnp.float32)[:, None]
    mixed = (field_rows.astype(jnp.float32) + ocean_mask * layer_scale * residual_branch).astype(jnp.bfloat16)
    cotangent_field = cot_rows.astype(jnp.float32)
    branch_field_gradient = ocean_mask * layer_scale * cotangent_field
    d_branch = branch_field_gradient.astype(jnp.bfloat16)
    d_act = jnp.dot(d_branch, w_out.T, preferred_element_type=jnp.float32)
    _, gelu_back = jax.vjp(jax.nn.gelu, pre_act)
    preactivation_gradient = gelu_back(d_act)[0]
    d_pre_b = preactivation_gradient.astype(jnp.bfloat16)
    normalized_gradient = jnp.dot(d_pre_b, w_in.T, preferred_element_type=jnp.float32)
    scaled_branch = normalized_gradient * layer_norm_gain
    convolution_gradient = inverse_deviation * (scaled_branch - lax.optimization_barrier(jnp.mean(scaled_branch, axis=-1, keepdims=True)) - standardized_input * lax.optimization_barrier(jnp.mean(scaled_branch * standardized_input, axis=-1, keepdims=True)))
    partial_totals = (lax.optimization_barrier(jnp.sum(ocean_mask * cotangent_field * residual_branch, axis=0)), lax.optimization_barrier(jnp.sum(branch_field_gradient, axis=0)), lax.optimization_barrier(jnp.sum(preactivation_gradient, axis=0)), lax.optimization_barrier(jnp.sum(normalized_gradient * standardized_input, axis=0)), lax.optimization_barrier(jnp.sum(normalized_gradient, axis=0)))
    return (mixed, convolution_gradient.astype(jnp.bfloat16), partial_totals, activ, d_branch, normalized_input, d_pre_b)

def reference(fields, land_mask, cotangent, kernel, layer_norm_gain, layer_norm_bias, w_in, b_in, w_out, b_out, layer_scale):
    masked = fields * land_mask.astype(jnp.bfloat16)[:, :, None]
    padded = pad_field(masked)
    conv = depthwise(padded, kernel, NLAT, NLON)
    block = CLAT * NLON

    def stepper(carry, inputs):
        conv_rows, field_rows, mask_rows, cot_rows = inputs
        mixed, convolution_gradient, partial_totals, activ, d_branch, normalized_input, d_pre_b = pointwise(conv_rows, field_rows, mask_rows, cot_rows, layer_norm_gain, layer_norm_bias, w_in, b_in, w_out, b_out, layer_scale)
        grad_wi = carry[0] + jnp.dot(normalized_input.T, d_pre_b, preferred_element_type=jnp.float32)
        grad_wo = carry[1] + jnp.dot(activ.T, d_branch, preferred_element_type=jnp.float32)
        others = tuple((old + new for old, new in zip(carry[2:], partial_totals)))
        return ((grad_wi, grad_wo) + others, (mixed, convolution_gradient))
    inputs = (conv.reshape(N_LAT, block, CHAN), fields.reshape(N_LAT, block, CHAN), land_mask.reshape(N_LAT, block), cotangent.reshape(N_LAT, block, CHAN))
    start = (jnp.zeros((CHAN, HIDN), jnp.float32), jnp.zeros((HIDN, CHAN), jnp.float32), jnp.zeros((CHAN,), jnp.float32), jnp.zeros((CHAN,), jnp.float32), jnp.zeros((HIDN,), jnp.float32), jnp.zeros((CHAN,), jnp.float32), jnp.zeros((CHAN,), jnp.float32))
    carry, outputs = lax.scan(stepper, start, inputs)
    grad_wi, grad_wo, grad_sc, grad_bo, grad_bi, grad_ga, grad_sh = carry
    mixed = outputs[0].reshape(NLAT, NLON, CHAN)
    convolution_gradient = outputs[1].reshape(NLAT, NLON, CHAN)
    grad_k = kernel_grad(padded, convolution_gradient, NLAT, NLON)
    d_masked = input_grad(pad_field(convolution_gradient), kernel, NLAT, NLON)
    ocean_mask = land_mask.astype(jnp.float32)[:, :, None]
    grad_fields = (cotangent.astype(jnp.float32) + ocean_mask * d_masked).astype(jnp.bfloat16)
    return (mixed, grad_fields, grad_k, grad_ga, grad_sh, grad_wi, grad_bi, grad_wo, grad_bo, grad_sc)
```

```python
import functools
import math

import jax
import jax.numpy as jnp
from jax import lax
from jax.experimental import pallas as pl
from jax.experimental.pallas import tpu as pltpu
from jax.sharding import PartitionSpec as P

F32 = jnp.float32
BF16 = jnp.bfloat16
LANES = 128
SUB = 8
VMEM_LIMIT = 56 * 1024 * 1024


def params():
    return pltpu.CompilerParams(vmem_limit_bytes=VMEM_LIMIT)


def whole_spec(shape):
    zeros = (0,) * len(shape)
    return pl.BlockSpec(shape, lambda *_: zeros)


def shifted(window, row, start, offset):
    return window[row, pl.ds(start + offset, SUB), :]


def band_conv(window, taps, start, rows, pad):
    sums = [None] * rows
    for col_off in range(7):
        weights = [taps(row_off, col_off) for row_off in range(7)]
        for src in range(window.shape[0]):
            hits = [(src - pad - row_off + 3, row_off) for row_off in range(7)]
            hits = [(out, row_off) for out, row_off in hits if 0 <= out < rows]
            if not hits:
                continue
            cells = shifted(window, src, start, 5 + col_off)
            for out, row_off in hits:
                term = weights[row_off] * cells
                sums[out] = term if sums[out] is None else sums[out] + term
    return sums


def conv_inner_kernel(f_ref, m_ref, k_ref, o_ref, window):
    rows, cols, _ = f_ref.shape
    window[:, 8 : 8 + cols, :] = f_ref[...].astype(F32) * m_ref[...]
    for start in range(8, cols - 8, 8):
        sums = band_conv(window, lambda p, q: k_ref[pl.ds(p * 7 + q, 1), :], start, rows, 0)
        for row in range(rows):
            o_ref[row, start - 8 : start, :] = sums[row]


def conv_side_kernel(f_ref, m_ref, k_ref, l_ref, r_ref, o_ref, window):
    rows, cols, _ = f_ref.shape
    window[:, 5:8, :] = l_ref[...].astype(F32)
    window[:, 8 : 8 + cols, :] = f_ref[...].astype(F32) * m_ref[...]
    window[:, 8 + cols : 11 + cols, :] = r_ref[...].astype(F32)
    for at, start in ((0, 0), (8, cols - 8)):
        sums = band_conv(window, lambda p, q: k_ref[pl.ds(p * 7 + q, 1), :], start, rows, 0)
        for row in range(rows):
            o_ref[row, at : at + 8, :] = sums[row]


def by_channels(shape):
    return pl.BlockSpec(shape[:-1] + (LANES,), lambda c: (0,) * (len(shape) - 1) + (c,))


def conv_cost(rows, cols, channels):
    return pl.CostEstimate(
        flops=98 * rows * cols * channels, bytes_accessed=6 * rows * cols * channels, transcendentals=0
    )


def conv_inner(fields, mask_b, taps):
    rows, cols, channels = fields.shape
    return pl.pallas_call(
        conv_inner_kernel,
        grid=(channels // LANES,),
        out_shape=jax.ShapeDtypeStruct((rows, cols - 16, channels), F32),
        in_specs=[by_channels(fields.shape), whole_spec(mask_b.shape), by_channels(taps.shape)],
        out_specs=by_channels((rows, cols - 16, channels)),
        scratch_shapes=[pltpu.VMEM((rows, cols + 16, LANES), F32)],
        compiler_params=params(),
        cost_estimate=conv_cost(rows, cols - 16, channels),
        name="conv_inner",
    )(fields, mask_b, taps)


def conv_side(fields, mask_b, taps, left, right):
    rows, cols, channels = fields.shape
    return pl.pallas_call(
        conv_side_kernel,
        grid=(channels // LANES,),
        out_shape=jax.ShapeDtypeStruct((rows, 16, channels), F32),
        in_specs=[
            by_channels(fields.shape),
            whole_spec(mask_b.shape),
            by_channels(taps.shape),
            by_channels(left.shape),
            by_channels(right.shape),
        ],
        out_specs=by_channels((rows, 16, channels)),
        scratch_shapes=[pltpu.VMEM((rows, cols + 16, LANES), F32)],
        compiler_params=params(),
        cost_estimate=conv_cost(rows, 16, channels),
        name="conv_side",
    )(fields, mask_b, taps, left, right)


def gelu_pair(x):
    root = math.sqrt(2.0 / math.pi)
    square = x * x
    half = 0.5 * jnp.tanh(x * (root + (root * 0.044715) * square)) + 0.5
    value = x * half
    slope = half + 2.0 * value * (1.0 - half) * (root + (3.0 * root * 0.044715) * square)
    return value, slope


def expand_kernel(
    inner_ref, side_ref, top_ref, bot_ref, k_ref, gain_ref, bias_ref, scale_ref, m_ref, cot_ref,
    wi_ref, bi_ref, wo_ref,
    xhat_ref, inv_ref, act_ref, dpre_ref, gwo_ref, gwi_ref, gbi_ref, gbo_ref,
    conv, halo, normed, normed_t, dbr, dbr_t,
):
    rows, cols, channels = conv.shape
    cells = rows * cols

    @pl.when(pl.program_id(0) == 0)
    def _():
        conv[:, 0:8, :] = side_ref[:, 0:8, :]
        conv[:, 8 : cols - 8, :] = inner_ref[...]
        conv[:, cols - 8 : cols, :] = side_ref[:, 8:16, :]
        halo[0:3, 5 : 11 + cols, :] = top_ref[...].astype(F32)
        halo[3:6, 5 : 11 + cols, :] = bot_ref[...].astype(F32)
        for block in range(channels // LANES):
            lanes = slice(block * LANES, (block + 1) * LANES)
            for start in range(0, cols, 8):
                outs = list(range(3)) + list(range(rows - 3, rows))
                sums = {out: conv[out, start : start + 8, lanes] for out in outs}
                for col_off in range(7):
                    for src in range(6):
                        lat = src - 3 if src < 3 else rows + src - 3
                        cell = halo[src, start + 5 + col_off : start + 13 + col_off, lanes]
                        for out in outs:
                            row_off = lat - out + 3
                            if 0 <= row_off < 7:
                                tap = k_ref[row_off * 7 + col_off : row_off * 7 + col_off + 1, lanes]
                                sums[out] = sums[out] + tap * cell
                for out in outs:
                    conv[out, start : start + 8, lanes] = sums[out]
        gbo_ref[...] = jnp.zeros_like(gbo_ref)

        chunk = 128
        chunk_rows = chunk // cols

        def standardize(step, _):
            at = pl.multiple_of(step * chunk, chunk)
            here = pl.ds(at, chunk)
            x = conv[pl.ds(step * chunk_rows, chunk_rows)].reshape(chunk, channels)
            mean = jnp.mean(x, axis=-1, keepdims=True)
            centered = x - mean
            var = jnp.mean(centered * centered, axis=-1, keepdims=True)
            inv = lax.rsqrt(var + 1e-06)
            xhat = centered * inv
            xhat_ref[here, :] = xhat
            inv_ref[here, :] = jnp.broadcast_to(inv, (chunk, LANES))
            scaled = xhat * gain_ref[...] + bias_ref[...]
            normed[here, :] = scaled.astype(BF16)
            normed_t[:, here] = scaled.T.astype(BF16)
            ocean = jnp.concatenate([m_ref[here, :]] * (channels // LANES), axis=1)
            grad = ocean * scale_ref[...] * cot_ref[here, :].astype(F32)
            gbo_ref[...] += jnp.sum(grad, axis=0, keepdims=True)
            dbr[here, :] = grad.astype(BF16)
            dbr_t[:, here] = grad.T.astype(BF16)
            return 0

        lax.fori_loop(0, cells // chunk, standardize, 0)

    part = 256
    total = None
    for at in range(0, cells, part):
        here = slice(at, at + part)
        pre = jnp.dot(normed[here, :], wi_ref[...], preferred_element_type=F32) + bi_ref[...]
        d_act = lax.dot_general(
            dbr[here, :], wo_ref[...], (((1,), (1,)), ((), ())), preferred_element_type=F32
        )
        value, slope = gelu_pair(pre)
        act_ref[here, :] = value.astype(BF16)
        d_pre = d_act * slope
        dpre_ref[here, :] = d_pre.astype(BF16)
        sums = jnp.sum(d_pre, axis=0, keepdims=True)
        total = sums if total is None else total + sums
    gbi_ref[...] = total
    gwo = jnp.dot(dbr_t[...], act_ref[...], preferred_element_type=F32).astype(BF16)
    gwi = jnp.dot(normed_t[...], dpre_ref[...], preferred_element_type=F32).astype(BF16)
    parts, _, width = gwo_ref.shape
    for index in range(parts):
        gwo_ref[index] = gwo[:, index * width : (index + 1) * width]
        gwi_ref[index] = gwi[:, index * width : (index + 1) * width]


def expand(inner, side, top, bot, taps, gain, bias, scale, mask_b, cot, w_in, b_in, w_out, n_lon, n_lat):
    rows, _, channels = inner.shape
    hidden = w_in.shape[1]
    cells, _ = cot.shape
    cols = cells // rows
    block = hidden // n_lon
    split = n_lat if (block // n_lat) % LANES == 0 else 1
    grads = (n_lon, split, channels, block // split)
    grad_spec = pl.BlockSpec((None,) + grads[1:], lambda h: (h, 0, 0, 0))
    out = pl.pallas_call(
        expand_kernel,
        grid=(n_lon,),
        out_shape=[
            jax.ShapeDtypeStruct((cells, channels), F32),
            jax.ShapeDtypeStruct((cells, LANES), F32),
            jax.ShapeDtypeStruct((cells, hidden), BF16),
            jax.ShapeDtypeStruct((cells, hidden), BF16),
            jax.ShapeDtypeStruct(grads, BF16),
            jax.ShapeDtypeStruct(grads, BF16),
            jax.ShapeDtypeStruct((1, hidden), F32),
            jax.ShapeDtypeStruct((1, channels), F32),
        ],
        in_specs=[
            whole_spec(inner.shape),
            whole_spec(side.shape),
            whole_spec(top.shape),
            whole_spec(bot.shape),
            whole_spec(taps.shape),
            whole_spec(gain.shape),
            whole_spec(bias.shape),
            whole_spec(scale.shape),
            whole_spec(mask_b.shape),
            whole_spec(cot.shape),
            pl.BlockSpec((channels, block), lambda h: (0, h)),
            pl.BlockSpec((1, block), lambda h: (0, h)),
            pl.BlockSpec((block, channels), lambda h: (h, 0)),
        ],
        out_specs=[
            whole_spec((cells, channels)),
            whole_spec((cells, LANES)),
            pl.BlockSpec((cells, block), lambda h: (0, h)),
            pl.BlockSpec((cells, block), lambda h: (0, h)),
            grad_spec,
            grad_spec,
            pl.BlockSpec((1, block), lambda h: (0, h)),
            whole_spec((1, channels)),
        ],
        scratch_shapes=[
            pltpu.VMEM((rows, cols, channels), F32),
            pltpu.VMEM((6, cols + 16, channels), F32),
            pltpu.VMEM((cells, channels), BF16),
            pltpu.VMEM((channels, cells), BF16),
            pltpu.VMEM((cells, channels), BF16),
            pltpu.VMEM((channels, cells), BF16),
        ],
        compiler_params=params(),
        cost_estimate=pl.CostEstimate(
            flops=8 * cells * channels * hidden,
            bytes_accessed=20 * cells * channels,
            transcendentals=cells * hidden,
        ),
        name="expand",
    )(inner, side, top, bot, taps, gain, bias, scale, mask_b, cot, w_in, b_in, w_out)
    return out


def project_kernel(
    act_ref, dpre_ref, wo_ref, wi_ref, xhat_ref, inv_ref, f_ref, cot_ref, m_ref, scale_ref, gain_ref, bo_ref,
    mixed_ref, dconv_ref, sums_ref,
):
    channels = xhat_ref.shape[1]

    def wide(ref):
        return jnp.concatenate([ref[...]] * (channels // LANES), axis=1)

    @pl.when(pl.program_id(0) == 0)
    def _():
        sums_ref[...] = jnp.zeros_like(sums_ref)

    branch = jnp.dot(act_ref[...], wo_ref[...], preferred_element_type=F32) + bo_ref[...]
    d_normed = lax.dot_general(
        dpre_ref[...], wi_ref[...], (((1,), (1,)), ((), ())), preferred_element_type=F32
    )
    ocean = wide(m_ref) * branch
    mixed_ref[...] = (f_ref[...].astype(F32) + ocean * scale_ref[...]).astype(BF16)
    xhat = xhat_ref[...]
    normed_term = d_normed * xhat
    sums_ref[0:1, :] += jnp.sum(ocean * cot_ref[...].astype(F32), axis=0, keepdims=True)
    sums_ref[1:2, :] += jnp.sum(normed_term, axis=0, keepdims=True)
    sums_ref[2:3, :] += jnp.sum(d_normed, axis=0, keepdims=True)
    e = d_normed * gain_ref[...]
    m1 = jnp.mean(e, axis=-1, keepdims=True)
    m2 = jnp.mean(normed_term * gain_ref[...], axis=-1, keepdims=True)
    dconv_ref[...] = (wide(inv_ref) * (e - m1 - xhat * m2)).astype(BF16)


def project(act, dpre, w_out, w_in, xhat, inv, fields, cot, mask_b, scale, gain, b_out):
    cells, hidden = act.shape
    channels = w_out.shape[1]
    part = 256

    def rows_of(width):
        return pl.BlockSpec((part, width), lambda i: (i, 0))

    return pl.pallas_call(
        project_kernel,
        grid=(cells // part,),
        out_shape=[
            jax.ShapeDtypeStruct((cells, channels), BF16),
            jax.ShapeDtypeStruct((cells, channels), BF16),
            jax.ShapeDtypeStruct((SUB, channels), F32),
        ],
        in_specs=[
            rows_of(hidden),
            rows_of(hidden),
            whole_spec(w_out.shape),
            whole_spec(w_in.shape),
            rows_of(channels),
            rows_of(LANES),
            rows_of(channels),
            rows_of(channels),
            rows_of(LANES),
            whole_spec(scale.shape),
            whole_spec(gain.shape),
            whole_spec(b_out.shape),
        ],
        out_specs=[rows_of(channels), rows_of(channels), whole_spec((SUB, channels))],
        compiler_params=params(),
        cost_estimate=pl.CostEstimate(
            flops=4 * cells * channels * hidden, bytes_accessed=16 * cells * channels, transcendentals=0
        ),
        name="project",
    )(act, dpre, w_out, w_in, xhat, inv, fields, cot, mask_b, scale, gain, b_out)


def fill_window(window, center, left, right, top, bot):
    rows, cols, _ = center.shape
    window[3 : 3 + rows, 5:8, :] = left[...].astype(F32)
    window[3 : 3 + rows, 8 : 8 + cols, :] = center
    window[3 : 3 + rows, 8 + cols : 11 + cols, :] = right[...].astype(F32)
    window[0:3, 5 : 11 + cols, :] = top[...].astype(F32)
    window[3 + rows : 6 + rows, 5 : 11 + cols, :] = bot[...].astype(F32)


def filter_grad_kernel(f_ref, m_ref, l_ref, r_ref, t_ref, b_ref, d_ref, o_ref, window, grad):
    rows, cols, _ = f_ref.shape
    fill_window(window, f_ref[...].astype(F32) * m_ref[...], l_ref, r_ref, t_ref, b_ref)
    grad[...] = d_ref[...].astype(F32)
    for col_off in range(7):

        def band(index, sums):
            start = pl.multiple_of(index * 8, 8)
            sums = list(sums)
            held = {}
            for src in range(rows + 6):
                if src < rows:
                    held[src] = grad[src, pl.ds(start, SUB), :]
                cells = shifted(window, src, start, 5 + col_off)
                for row_off in range(7):
                    out = src - row_off
                    if 0 <= out < rows:
                        sums[row_off] = sums[row_off] + held[out] * cells
            return tuple(sums)

        start = tuple(jnp.zeros((SUB, LANES), F32) for _ in range(7))
        sums = lax.fori_loop(0, cols // 8, band, start)
        for row_off in range(7):
            at = row_off * 7 + col_off
            o_ref[at : at + 1, :] = jnp.sum(sums[row_off], axis=0, keepdims=True)


def filter_grad(fields, mask_b, left, right, top, bot, d_conv):
    rows, cols, channels = fields.shape
    return pl.pallas_call(
        filter_grad_kernel,
        grid=(channels // LANES,),
        out_shape=jax.ShapeDtypeStruct((49, channels), F32),
        in_specs=[
            by_channels(fields.shape),
            whole_spec(mask_b.shape),
            by_channels(left.shape),
            by_channels(right.shape),
            by_channels(top.shape),
            by_channels(bot.shape),
            by_channels(d_conv.shape),
        ],
        out_specs=by_channels((49, channels)),
        scratch_shapes=[
            pltpu.VMEM((rows + 6, cols + 16, LANES), F32),
            pltpu.VMEM((rows, cols, LANES), F32),
        ],
        compiler_params=params(),
        cost_estimate=conv_cost(rows, cols, channels),
        name="filter_grad",
    )(fields, mask_b, left, right, top, bot, d_conv)


def input_grad_kernel(d_ref, l_ref, r_ref, t_ref, b_ref, k_ref, m_ref, cot_ref, o_ref, window, grad):
    rows, cols, _ = d_ref.shape
    fill_window(window, d_ref[...].astype(F32), l_ref, r_ref, t_ref, b_ref)
    for start in range(0, cols, 8):
        sums = band_conv(window, lambda p, q: k_ref[pl.ds(48 - p * 7 - q, 1), :], start, rows, 3)
        for row in range(rows):
            grad[row, start : start + 8, :] = sums[row]
    o_ref[...] = (cot_ref[...].astype(F32) + m_ref[...] * grad[...]).astype(BF16)


def input_grad(d_conv, left, right, top, bot, taps, mask_b, cot):
    rows, cols, channels = d_conv.shape
    return pl.pallas_call(
        input_grad_kernel,
        grid=(channels // LANES,),
        out_shape=jax.ShapeDtypeStruct((rows, cols, channels), BF16),
        in_specs=[
            by_channels(d_conv.shape),
            by_channels(left.shape),
            by_channels(right.shape),
            by_channels(top.shape),
            by_channels(bot.shape),
            by_channels(taps.shape),
            whole_spec(mask_b.shape),
            by_channels(cot.shape),
        ],
        out_specs=by_channels((rows, cols, channels)),
        scratch_shapes=[
            pltpu.VMEM((rows + 6, cols + 16, LANES), F32),
            pltpu.VMEM((rows, cols, LANES), F32),
        ],
        compiler_params=params(),
        cost_estimate=conv_cost(rows, cols, channels),
        name="input_grad",
    )(d_conv, left, right, top, bot, taps, mask_b, cot)


def swap(values, axis, bit):
    count = lax.axis_size(axis)
    return lax.ppermute(values, axis, [(i, i ^ bit) for i in range(count)])


def bits_of(axis):
    return [1 << k for k in range(int(math.log2(lax.axis_size(axis))))]


def scatter_sum(values):
    for dim, axis in ((0, "lon"), (1, "lat")):
        for bit in bits_of(axis):
            mine = (lax.axis_index(axis) // bit) % 2
            shape = values.shape
            paired = values.reshape(shape[:dim] + (shape[dim] // 2, 2) + shape[dim + 1 :])
            kept = lax.dynamic_index_in_dim(paired, mine, dim + 1, keepdims=False)
            sent = lax.dynamic_index_in_dim(paired, 1 - mine, dim + 1, keepdims=False)
            values = kept.astype(F32) + swap(sent.astype(BF16), axis, bit).astype(F32)
    return values[0, 0]


def total_sum(values):
    for axis in ("lon", "lat"):
        for bit in bits_of(axis):
            values = values + swap(values, axis, bit)
    return values


def side_halo(cells):
    count = lax.axis_size("lon")
    ahead = [(i, (i + 1) % count) for i in range(count)]
    back = [((i + 1) % count, i) for i in range(count)]
    cols = cells.shape[1]
    return (
        lax.ppermute(cells[:, cols - 3 :], "lon", ahead),
        lax.ppermute(cells[:, :3], "lon", back),
    )


def end_halo(cells, left, right):
    count = lax.axis_size("lat")
    ahead = [(i, i + 1) for i in range(count - 1)]
    back = [(i + 1, i) for i in range(count - 1)]
    rows = cells.shape[0]
    tail = jnp.concatenate([left[rows - 3 :], cells[rows - 3 :], right[rows - 3 :]], axis=1)
    head = jnp.concatenate([left[:3], cells[:3], right[:3]], axis=1)
    return lax.ppermute(tail, "lat", ahead), lax.ppermute(head, "lat", back)


def per_device(
    fields,
    land_mask,
    cotangent,
    kernel,
    layer_norm_gain,
    layer_norm_bias,
    w_in,
    b_in,
    w_out,
    b_out,
    layer_scale,
):
    rows, cols, channels = fields.shape
    cells = rows * cols
    hidden = w_in.shape[1]
    n_lon, n_lat = lax.axis_size("lon"), lax.axis_size("lat")
    taps = kernel.reshape(49, channels)
    gain, bias = layer_norm_gain.reshape(1, -1), layer_norm_bias.reshape(1, -1)
    scale = layer_scale.reshape(1, -1)
    mask_b = jnp.broadcast_to(land_mask.astype(F32)[:, :, None], (rows, cols, LANES))
    mask_rows = mask_b.reshape(cells, LANES)
    cot_rows = cotangent.reshape(cells, channels)

    masked = fields * land_mask.astype(BF16)[:, :, None]
    left, right = side_halo(masked)
    inner = conv_inner(fields, mask_b, taps)
    top, bot = end_halo(masked, left, right)
    side = conv_side(fields, mask_b, taps, left, right)
    xhat, inv, act, d_pre, g_wo, g_wi, g_bi, g_bo = expand(
        inner, side, top, bot, taps, gain, bias, scale, mask_rows, cot_rows,
        w_in, b_in.reshape(1, -1), w_out, n_lon, n_lat,
    )
    mixed, d_conv, sums = project(
        act, d_pre, w_out, w_in, xhat, inv, fields.reshape(cells, channels), cot_rows, mask_rows,
        scale, gain, b_out.reshape(1, -1),
    )
    d_conv = d_conv.reshape(rows, cols, channels)
    d_left, d_right = side_halo(d_conv)
    d_top, d_bot = end_halo(d_conv, d_left, d_right)
    g_k = filter_grad(fields, mask_b, left, right, top, bot, d_conv)
    grad_fields = input_grad(d_conv, d_left, d_right, d_top, d_bot, taps, mask_b, cotangent)

    width = hidden // (n_lon * n_lat)

    def owned(grads):
        if grads.shape[1] != n_lat:
            grads = grads.reshape(n_lon, channels, n_lat, width).transpose(0, 2, 1, 3)
        return scatter_sum(grads)

    grad_wo = owned(g_wo).T
    grad_wi = owned(g_wi)
    small = total_sum(
        jnp.concatenate([g_k, sums[:3], g_bo, g_bi.reshape(-1, channels)], axis=0)
    )
    return (
        mixed.reshape(rows, cols, channels),
        grad_fields,
        small[:49].reshape(7, 7, channels),
        small[50],
        small[51],
        grad_wi,
        small[53:].reshape(hidden),
        grad_wo,
        small[52],
        small[49],
    )


def solution(mesh):
    placed = (
        P(("grp", "lat"), "lon", None),
        P(("grp", "lat"), "lon"),
        P(("grp", "lat"), "lon", None),
        P(),
        P(),
        P(),
        P(),
        P(),
        P(),
        P(),
        P(),
    )
    return jax.shard_map(
        per_device,
        mesh=mesh,
        in_specs=placed,
        out_specs=(
            P(("grp", "lat"), "lon", None),
            P(("grp", "lat"), "lon", None),
            P("grp", None, None),
            P("grp"),
            P("grp"),
            P("grp", ("lon", "lat")),
            P("grp"),
            P(("lon", "lat"), "grp"),
            P("grp"),
            P("grp"),
        ),
        check_vma=False,
    )
```

```python
import functools
import math

import jax
import jax.numpy as jnp
from jax import lax
from jax.experimental import pallas as pl
from jax.experimental.pallas import tpu as pltpu
from jax.sharding import PartitionSpec as P

F32 = jnp.float32
BF16 = jnp.bfloat16
LANES = 128
SUB = 8


def params(mib):
    return pltpu.CompilerParams(vmem_limit_bytes=mib * 1024 * 1024)


def estimate(micros):
    return pl.CostEstimate(
        flops=int(micros * 1.15e9), bytes_accessed=int(micros * 3.6e6), transcendentals=0
    )


def once(shape):
    zeros = (0,) * len(shape)
    return pl.BlockSpec(shape, lambda *_: zeros, pipeline_mode=pl.Buffered(1))


UNUSED = pl.BlockSpec(memory_space=pl.ANY)


def whole_spec(shape):
    zeros = (0,) * len(shape)
    return pl.BlockSpec(shape, lambda *_: zeros)


def shifted(window, row, start, offset):
    if offset % SUB == 0:
        return window[row, pl.ds(start + offset, SUB), :]
    base = start + offset // SUB * SUB
    pair = window[row, pl.ds(base, 2 * SUB), :]
    return pltpu.roll(pair, 2 * SUB - offset % SUB, axis=0)[:SUB]


def tap_rows(k_ref, col_off, flip):
    at = 6 - col_off if flip else col_off
    rows = [k_ref[6 - p if flip else p, at : at + 1, :] for p in range(7)]
    return [jnp.broadcast_to(row, (SUB, LANES)) for row in rows]


def band_conv(window, k_ref, start, rows, pad, flip):
    sums = [None] * rows
    for col_off in range(7):
        weights = tap_rows(k_ref, col_off, flip)
        for src in range(window.shape[0]):
            hits = [(src - pad - row_off + 3, row_off) for row_off in range(7)]
            hits = [(out, row_off) for out, row_off in hits if 0 <= out < rows]
            if not hits:
                continue
            cells = shifted(window, src, start, 5 + col_off)
            for out, row_off in hits:
                term = weights[row_off] * cells
                sums[out] = term if sums[out] is None else sums[out] + term
    return sums


def conv_inner_kernel(f_ref, m_ref, k_ref, o_ref, head_ref, tail_ref, window):
    rows, cols, _ = f_ref.shape
    masked = f_ref[...].astype(F32) * m_ref[...]
    window[:, 8 : 8 + cols, :] = masked
    head_ref[...] = masked[:3].astype(BF16)
    tail_ref[...] = masked[rows - 3 :].astype(BF16)
    for start in range(8, cols - 8, 8):
        sums = band_conv(window, k_ref, start, rows, 0, False)
        for row in range(rows):
            o_ref[row, start - 8 : start, :] = sums[row]


def conv_side_kernel(f_ref, m_ref, k_ref, l_ref, r_ref, o_ref, window):
    rows, cols, _ = f_ref.shape
    window[:, 5:8, :] = l_ref[...].astype(F32)
    window[:, 8 : 8 + cols, :] = f_ref[...].astype(F32) * m_ref[...]
    window[:, 8 + cols : 11 + cols, :] = r_ref[...].astype(F32)
    for at, start in ((0, 0), (8, cols - 8)):
        sums = band_conv(window, k_ref, start, rows, 0, False)
        for row in range(rows):
            o_ref[row, at : at + 8, :] = sums[row]


def by_channels(shape, first=0):
    return pl.BlockSpec(shape[:-1] + (LANES,), lambda c: (0,) * (len(shape) - 1) + (c + first,))


def conv_inner(fields, mask_b, kernel):
    rows, cols, channels = fields.shape
    ends = (3, cols, channels)
    return pl.pallas_call(
        conv_inner_kernel,
        grid=(channels // LANES,),
        out_shape=[
            jax.ShapeDtypeStruct((rows, cols - 16, channels), F32),
            jax.ShapeDtypeStruct(ends, BF16),
            jax.ShapeDtypeStruct(ends, BF16),
        ],
        in_specs=[by_channels(fields.shape), whole_spec(mask_b.shape), by_channels(kernel.shape)],
        out_specs=[by_channels((rows, cols - 16, channels)), by_channels(ends), by_channels(ends)],
        scratch_shapes=[pltpu.VMEM((rows, cols + 16, LANES), F32)],
        compiler_params=params(16),
        cost_estimate=estimate(4),
        name="conv_inner",
    )(fields, mask_b, kernel)


def conv_side(fields, mask_b, kernel, left, right):
    rows, cols, channels = fields.shape
    return pl.pallas_call(
        conv_side_kernel,
        grid=(channels // LANES,),
        out_shape=jax.ShapeDtypeStruct((rows, 16, channels), F32),
        in_specs=[
            by_channels(fields.shape),
            whole_spec(mask_b.shape),
            by_channels(kernel.shape),
            by_channels(left.shape),
            by_channels(right.shape),
        ],
        out_specs=by_channels((rows, 16, channels)),
        scratch_shapes=[pltpu.VMEM((rows, cols + 16, LANES), F32)],
        compiler_params=params(16),
        cost_estimate=estimate(4),
        name="conv_side",
    )(fields, mask_b, kernel, left, right)


def gelu_pair(x):
    root = math.sqrt(2.0 / math.pi)
    square = x * x
    tanh = jnp.tanh(x * (root + (root * 0.044715) * square))
    half = 0.5 * tanh + 0.5
    value = x * half
    slope = half + value * ((1.0 - tanh) * (root + (3.0 * root * 0.044715) * square))
    return value, slope


def hidden_block(normed, normed_t, dbr, dbr_t, wi_ref, bi_ref, wo_ref, act_ref, dpre_ref, gbi_ref, grads_ref):
    cells = normed.shape[0]
    part = 256
    total = None
    for at in range(0, cells, part):
        here = slice(at, at + part)
        pre = jnp.dot(normed[here, :], wi_ref[...], preferred_element_type=F32) + bi_ref[...]
        d_act = lax.dot_general(
            dbr[here, :], wo_ref[...], (((1,), (1,)), ((), ())), preferred_element_type=F32
        )
        value, slope = gelu_pair(pre)
        act_ref[here, :] = value.astype(BF16)
        d_pre = d_act * slope
        dpre_ref[here, :] = d_pre.astype(BF16)
        sums = jnp.sum(d_pre, axis=0, keepdims=True)
        total = sums if total is None else total + sums
    gbi_ref[...] = total
    _, parts, _, width = grads_ref.shape
    for index, (left, right) in enumerate(((dbr_t, act_ref), (normed_t, dpre_ref))):
        grad = jnp.dot(left[...], right[...], preferred_element_type=F32).astype(BF16)
        for lat in range(parts):
            grads_ref[index, lat] = grad[:, lat * width : (lat + 1) * width]


def expand_first_kernel(
    order_ref,
    inner_ref, side_ref, top_ref, bot_ref, k_ref, gain_ref, bias_ref, scale_ref, m_ref, cot_ref,
    wi_ref, bi_ref, wo_ref,
    xhat_ref, inv_ref, gbo_ref, normed, normed_t, dbr, dbr_t, act_ref, dpre_ref, gbi_ref, grads_ref,
    conv, halo,
):
    rows, cols, channels = conv.shape
    cells = rows * cols

    @pl.when(pl.program_id(0) == 0)
    def _():
        conv[:, 0:8, :] = side_ref[:, 0:8, :]
        conv[:, 8 : cols - 8, :] = inner_ref[...]
        conv[:, cols - 8 : cols, :] = side_ref[:, 8:16, :]
        halo[0:3, 5 : 11 + cols, :] = top_ref[...].astype(F32)
        halo[3:6, 5 : 11 + cols, :] = bot_ref[...].astype(F32)
        for block in range(channels // LANES):
            lanes = slice(block * LANES, (block + 1) * LANES)
            for start in range(0, cols, 8):
                outs = list(range(3)) + list(range(rows - 3, rows))
                sums = {out: conv[out, start : start + 8, lanes] for out in outs}
                for col_off in range(7):
                    for src in range(6):
                        lat = src - 3 if src < 3 else rows + src - 3
                        offset = (5 + col_off) % SUB
                        base = start + (5 + col_off) // SUB * SUB
                        pair = halo[src, base : base + 2 * SUB, lanes]
                        cell = pltpu.roll(pair, 2 * SUB - offset, axis=0)[:SUB] if offset else pair[:SUB]
                        for out in outs:
                            row_off = lat - out + 3
                            if 0 <= row_off < 7:
                                tap = k_ref[row_off, col_off : col_off + 1, lanes]
                                sums[out] = sums[out] + tap * cell
                for out in outs:
                    conv[out, start : start + 8, lanes] = sums[out]
        gbo_ref[...] = jnp.zeros_like(gbo_ref)

        chunk = 128
        chunk_rows = chunk // cols

        def standardize(step, _):
            at = pl.multiple_of(step * chunk, chunk)
            here = pl.ds(at, chunk)
            there = pl.ds(step * chunk_rows, chunk_rows)
            x = conv[there].reshape(chunk, channels)
            mean = jnp.mean(x, axis=-1, keepdims=True)
            centered = x - mean
            var = jnp.mean(centered * centered, axis=-1, keepdims=True)
            inv = lax.rsqrt(var + 1e-06)
            xhat = centered * inv
            xhat_ref[here, :] = xhat
            inv_ref[here, :] = jnp.broadcast_to(inv, (chunk, LANES))
            scaled = xhat * gain_ref[...] + bias_ref[...]
            normed[here, :] = scaled.astype(BF16)
            normed_t[:, here] = scaled.T.astype(BF16)
            ocean = jnp.concatenate([m_ref[there].reshape(chunk, LANES)] * (channels // LANES), axis=1)
            grad = ocean * scale_ref[...] * cot_ref[here, :].astype(F32)
            gbo_ref[...] += jnp.sum(grad, axis=0, keepdims=True)
            dbr[here, :] = grad.astype(BF16)
            dbr_t[:, here] = grad.T.astype(BF16)
            return 0

        lax.fori_loop(0, cells // chunk, standardize, 0)

    hidden_block(
        normed, normed_t, dbr, dbr_t, wi_ref, bi_ref, wo_ref, act_ref, dpre_ref, gbi_ref, grads_ref
    )


def expand_second_kernel(
    order_ref, normed, normed_t, dbr, dbr_t, wi_ref, bi_ref, wo_ref, act_in, dpre_in, gbi_in,
    act_ref, dpre_ref, gbi_ref, grads_ref,
):
    hidden_block(
        normed, normed_t, dbr, dbr_t, wi_ref, bi_ref, wo_ref, act_ref, dpre_ref, gbi_ref, grads_ref
    )


def hidden_specs(cells, channels, hidden, n_lon, n_lat, first):
    block = hidden // n_lon
    split = n_lat if (block // n_lat) % LANES == 0 else 1
    weights = [
        pl.BlockSpec((channels, block), lambda h, order: (0, order[h + first])),
        pl.BlockSpec((1, block), lambda h, order: (0, order[h + first])),
        pl.BlockSpec((block, channels), lambda h, order: (order[h + first], 0)),
    ]
    results = [
        pl.BlockSpec((cells, block), lambda h, order: (0, order[h + first])),
        pl.BlockSpec((cells, block), lambda h, order: (0, order[h + first])),
        pl.BlockSpec((1, block), lambda h, order: (0, order[h + first])),
        pl.BlockSpec((2, None, split, channels, block // split), lambda h, order: (0, h, 0, 0, 0)),
    ]
    shapes = [
        jax.ShapeDtypeStruct((cells, hidden), BF16),
        jax.ShapeDtypeStruct((cells, hidden), BF16),
        jax.ShapeDtypeStruct((1, hidden), F32),
        jax.ShapeDtypeStruct((2, n_lon // 2, split, channels, block // split), BF16),
    ]
    return weights, results, shapes


def expand_first(order, inner, side, top, bot, kernel, gain, bias, scale, mask_b, cot, w_in, b_in, w_out, n_lon, n_lat):
    rows, _, channels = inner.shape
    hidden = w_in.shape[1]
    cells, _ = cot.shape
    cols = cells // rows
    weights, results, shapes = hidden_specs(cells, channels, hidden, n_lon, n_lat, 0)
    flat = (cells, channels)
    turned = (channels, cells)
    own = [
        jax.ShapeDtypeStruct(flat, F32),
        jax.ShapeDtypeStruct((cells, LANES), F32),
        jax.ShapeDtypeStruct((1, channels), F32),
        jax.ShapeDtypeStruct(flat, BF16),
        jax.ShapeDtypeStruct(turned, BF16),
        jax.ShapeDtypeStruct(flat, BF16),
        jax.ShapeDtypeStruct(turned, BF16),
    ]
    given = (inner, side, top, bot, kernel, gain, bias, scale, mask_b, cot)
    return pl.pallas_call(
        expand_first_kernel,
        grid_spec=pltpu.PrefetchScalarGridSpec(
            num_scalar_prefetch=1,
            grid=(n_lon // 2,),
            in_specs=[once(x.shape) for x in given] + weights,
            out_specs=[once(x.shape) for x in own] + results,
            scratch_shapes=[
                pltpu.VMEM((rows, cols, channels), F32),
                pltpu.VMEM((6, cols + 16, channels), F32),
            ],
        ),
        out_shape=own + shapes,
        compiler_params=params(32),
        cost_estimate=estimate(12),
        name="expand_first",
    )(order, *given, w_in, b_in, w_out)


def expand_second(order, rows, w_in, b_in, w_out, act, dpre, gbi, n_lon, n_lat):
    cells, channels = rows[0].shape
    hidden = w_in.shape[1]
    weights, results, shapes = hidden_specs(cells, channels, hidden, n_lon, n_lat, n_lon // 2)
    return pl.pallas_call(
        expand_second_kernel,
        grid_spec=pltpu.PrefetchScalarGridSpec(
            num_scalar_prefetch=1,
            grid=(n_lon // 2,),
            in_specs=[once(x.shape) for x in rows] + weights + [UNUSED] * 3,
            out_specs=results,
        ),
        out_shape=shapes,
        input_output_aliases={8: 0, 9: 1, 10: 2},
        compiler_params=params(24),
        cost_estimate=estimate(8),
        name="expand_second",
    )(order, *rows, w_in, b_in, w_out, act, dpre, gbi)


def project_kernel(
    act_ref, dpre_ref, wo_ref, wi_ref, xhat_ref, inv_ref, f_ref, cot_ref, m_ref, scale_ref, gain_ref, bo_ref,
    ahead_wo, ahead_wi,
    mixed_ref, dconv_ref, sums_ref,
):
    cells, channels = xhat_ref.shape

    def wide(ref):
        return jnp.concatenate([ref[...].reshape(cells, LANES)] * (channels // LANES), axis=1)

    @pl.when(pl.program_id(0) == 0)
    def _():
        sums_ref[...] = jnp.zeros_like(sums_ref)

    branch = jnp.dot(act_ref[...], wo_ref[...], preferred_element_type=F32) + bo_ref[...]
    d_normed = lax.dot_general(
        dpre_ref[...], wi_ref[...], (((1,), (1,)), ((), ())), preferred_element_type=F32
    )
    ocean = wide(m_ref) * branch
    mixed_ref[...] = (f_ref[...].astype(F32) + ocean * scale_ref[...]).astype(BF16)
    xhat = xhat_ref[...]
    normed_term = d_normed * xhat
    sums_ref[0:1, :] += jnp.sum(ocean * cot_ref[...].astype(F32), axis=0, keepdims=True)
    sums_ref[1:2, :] += jnp.sum(normed_term, axis=0, keepdims=True)
    sums_ref[2:3, :] += jnp.sum(d_normed, axis=0, keepdims=True)
    e = d_normed * gain_ref[...]
    m1 = jnp.mean(e, axis=-1, keepdims=True)
    m2 = jnp.mean(normed_term * gain_ref[...], axis=-1, keepdims=True)
    dconv_ref[...] = (wide(inv_ref) * (e - m1 - xhat * m2)).astype(BF16)


def project(act, dpre, w_out, w_in, xhat, inv, fields, cot, mask_b, scale, gain, b_out, ahead_wo, ahead_wi):
    cells, hidden = act.shape
    channels = w_out.shape[1]
    part = 256

    def rows_of(width):
        return pl.BlockSpec((part, width), lambda i: (i, 0))

    return pl.pallas_call(
        project_kernel,
        grid=(cells // part,),
        out_shape=[
            jax.ShapeDtypeStruct((cells, channels), BF16),
            jax.ShapeDtypeStruct((cells, channels), BF16),
            jax.ShapeDtypeStruct((SUB, channels), F32),
        ],
        in_specs=[
            rows_of(hidden),
            rows_of(hidden),
            once(w_out.shape),
            once(w_in.shape),
            rows_of(channels),
            rows_of(LANES),
            rows_of(channels),
            rows_of(channels),
            pl.BlockSpec((part // mask_b.shape[1],) + mask_b.shape[1:], lambda i: (i, 0, 0)),
            whole_spec(scale.shape),
            whole_spec(gain.shape),
            whole_spec(b_out.shape),
            UNUSED,
            UNUSED,
        ],
        out_specs=[rows_of(channels), rows_of(channels), whole_spec((SUB, channels))],
        compiler_params=params(24),
        cost_estimate=estimate(9),
        name="project",
    )(act, dpre, w_out, w_in, xhat, inv, fields, cot, mask_b, scale, gain, b_out, ahead_wo, ahead_wi)


def fill_window(window, center, left, right, top, bot):
    rows, cols, _ = center.shape
    window[3 : 3 + rows, 5:8, :] = left[...].astype(F32)
    window[3 : 3 + rows, 8 : 8 + cols, :] = center
    window[3 : 3 + rows, 8 + cols : 11 + cols, :] = right[...].astype(F32)
    window[0:3, 5 : 11 + cols, :] = top[...].astype(F32)
    window[3 + rows : 6 + rows, 5 : 11 + cols, :] = bot[...].astype(F32)


def filter_grad_kernel(
    f_ref, m_ref, l_ref, r_ref, t_ref, b_ref, d_ref, sums_ref, gbo_ref, gbi_ref, ahead_a, ahead_b,
    o_ref, window, grad,
):
    rows, cols, _ = f_ref.shape
    fill_window(window, f_ref[...].astype(F32) * m_ref[...], l_ref, r_ref, t_ref, b_ref)
    grad[...] = d_ref[...].astype(F32)
    for col_off in range(7):

        def band(index, sums):
            start = pl.multiple_of(index * 8, 8)
            sums = list(sums)
            held = {}
            for src in range(rows + 6):
                if src < rows:
                    held[src] = grad[src, pl.ds(start, SUB), :]
                cells = shifted(window, src, start, 5 + col_off)
                for row_off in range(7):
                    out = src - row_off
                    if 0 <= out < rows:
                        sums[row_off] = sums[row_off] + held[out] * cells
            return tuple(sums)

        start = tuple(jnp.zeros((SUB, LANES), F32) for _ in range(7))
        sums = lax.fori_loop(0, cols // 8, band, start)
        for row_off in range(7):
            o_ref[row_off, col_off : col_off + 1, :] = jnp.sum(sums[row_off], axis=0, keepdims=True)
    o_ref[7, 0:3, :] = sums_ref[0:3, :]
    o_ref[7, 3:4, :] = gbo_ref[...]
    o_ref[7, 4:8, :] = gbi_ref[...]
    for row_off in range(7):
        o_ref[row_off, 7:8, :] = jnp.zeros((1, LANES), F32)


def filter_grad(fields, mask_b, left, right, top, bot, d_conv, sums, gbo, gbi, ahead, blocks, first):
    rows, cols, channels = fields.shape

    def part(x):
        return by_channels(x.shape, first)

    return pl.pallas_call(
        filter_grad_kernel,
        grid=(blocks,),
        out_shape=jax.ShapeDtypeStruct((8, 8, blocks * LANES), F32),
        in_specs=[
            part(fields),
            whole_spec(mask_b.shape),
            part(left),
            part(right),
            part(top),
            part(bot),
            part(d_conv),
            part(sums),
            part(gbo),
            part(gbi),
            UNUSED,
            UNUSED,
        ],
        out_specs=by_channels((8, 8, blocks * LANES)),
        scratch_shapes=[
            pltpu.VMEM((rows + 6, cols + 16, LANES), F32),
            pltpu.VMEM((rows, cols, LANES), F32),
        ],
        compiler_params=params(16),
        cost_estimate=estimate(4),
        name="filter_grad",
    )(fields, mask_b, left, right, top, bot, d_conv, sums, gbo, gbi, *ahead)


def input_grad_kernel(d_ref, l_ref, r_ref, t_ref, b_ref, k_ref, m_ref, cot_ref, a_ref, b2_ref, o_ref, window, grad):
    rows, cols, _ = d_ref.shape
    fill_window(window, d_ref[...].astype(F32), l_ref, r_ref, t_ref, b_ref)
    for start in range(0, cols, 8):
        sums = band_conv(window, k_ref, start, rows, 3, True)
        for row in range(rows):
            grad[row, start : start + 8, :] = sums[row]
    o_ref[...] = (cot_ref[...].astype(F32) + m_ref[...] * grad[...]).astype(BF16)


def input_grad_more_kernel(d_ref, l_ref, r_ref, t_ref, b_ref, k_ref, m_ref, cot_ref, a_ref, b2_ref, old_ref, o_ref, window, grad):
    input_grad_kernel(d_ref, l_ref, r_ref, t_ref, b_ref, k_ref, m_ref, cot_ref, a_ref, b2_ref, o_ref, window, grad)


def input_grad(d_conv, left, right, top, bot, kernel, mask_b, cot, ahead, blocks, first, old=None):
    rows, cols, channels = d_conv.shape

    def part(x):
        return by_channels(x.shape, first)

    more = [] if old is None else [old]
    return pl.pallas_call(
        input_grad_kernel if old is None else input_grad_more_kernel,
        grid=(blocks,),
        out_shape=jax.ShapeDtypeStruct((rows, cols, channels), BF16),
        in_specs=[
            part(d_conv),
            part(left),
            part(right),
            part(top),
            part(bot),
            part(kernel),
            whole_spec(mask_b.shape),
            part(cot),
        ]
        + [UNUSED] * (2 + len(more)),
        out_specs=part(d_conv),
        scratch_shapes=[
            pltpu.VMEM((rows + 6, cols + 16, LANES), F32),
            pltpu.VMEM((rows, cols, LANES), F32),
        ],
        input_output_aliases={} if old is None else {10: 0},
        compiler_params=params(16),
        cost_estimate=estimate(4),
        name="input_grad",
    )(d_conv, left, right, top, bot, kernel, mask_b, cot, *ahead, *more)


def swap(values, axis, bit):
    count = lax.axis_size(axis)
    return lax.ppermute(values, axis, [(i, i ^ bit) for i in range(count)])


def bits_of(axis):
    return [1 << k for k in range(int(math.log2(lax.axis_size(axis))))]


def halves(values, axis, dim, bit):
    mine = (lax.axis_index(axis) // bit) % 2
    shape = values.shape
    paired = values.reshape(shape[:dim] + (shape[dim] // 2, 2) + shape[dim + 1 :])
    kept = lax.dynamic_index_in_dim(paired, mine, dim + 1, keepdims=False)
    sent = lax.dynamic_index_in_dim(paired, 1 - mine, dim + 1, keepdims=False)
    return kept, sent.astype(BF16)


def total_sum(values):
    for axis in ("lon", "lat"):
        for bit in bits_of(axis):
            values = values + swap(values, axis, bit)
    return values


def side_halo(cells):
    count = lax.axis_size("lon")
    ahead = [(i, (i + 1) % count) for i in range(count)]
    back = [((i + 1) % count, i) for i in range(count)]
    cols = cells.shape[1]
    return (
        lax.ppermute(cells[:, cols - 3 :], "lon", ahead),
        lax.ppermute(cells[:, :3], "lon", back),
    )


def end_halo(head, tail, left, right):
    count = lax.axis_size("lat")
    ahead = [(i, i + 1) for i in range(count - 1)]
    back = [(i + 1, i) for i in range(count - 1)]
    rows = left.shape[0]
    tail = jnp.concatenate([left[rows - 3 :], tail, right[rows - 3 :]], axis=1)
    head = jnp.concatenate([left[:3], head, right[:3]], axis=1)
    return lax.ppermute(tail, "lat", ahead), lax.ppermute(head, "lat", back)


def per_device(
    fields,
    land_mask,
    cotangent,
    kernel,
    layer_norm_gain,
    layer_norm_bias,
    w_in,
    b_in,
    w_out,
    b_out,
    layer_scale,
):
    rows, cols, channels = fields.shape
    cells = rows * cols
    hidden = w_in.shape[1]
    n_lon, n_lat = lax.axis_size("lon"), lax.axis_size("lat")
    gain, bias = layer_norm_gain.reshape(1, -1), layer_norm_bias.reshape(1, -1)
    scale = layer_scale.reshape(1, -1)
    mask_b = jnp.broadcast_to(land_mask.astype(F32)[:, :, None], (rows, cols, LANES))
    cot_rows = cotangent.reshape(cells, channels)
    ocean = land_mask.astype(BF16)[:, :, None]
    edges = jnp.concatenate([fields[:, :3] * ocean[:, :3], fields[:, cols - 3 :] * ocean[:, cols - 3 :]], axis=1)

    left, right = side_halo(edges)
    inner, head, tail = conv_inner(fields, mask_b, kernel)
    top, bot = end_halo(head, tail, left, right)
    side = conv_side(fields, mask_b, kernel, left, right)

    core = lax.axis_index("lon") % 2
    pairs = 2 * jnp.arange(n_lon // 2, dtype=jnp.int32)
    order = jnp.concatenate([pairs + 1 - core, pairs + core])
    xhat, inv, g_bo, *row_forms, act, d_pre, g_bi, sent = expand_first(
        order, inner, side, top, bot, kernel, gain, bias, scale, mask_b, cot_rows,
        w_in, b_in.reshape(1, -1), w_out, n_lon, n_lat,
    )
    got = swap(sent, "lon", 1)
    act, d_pre, g_bi, kept = expand_second(
        order, row_forms, w_in, b_in.reshape(1, -1), w_out, act, d_pre, g_bi, n_lon, n_lat
    )

    def width_split(grads):
        if grads.shape[1] != n_lat:
            grads = grads.reshape(n_lon // 2, channels, n_lat, -1).transpose(0, 2, 1, 3)
        return grads

    owned = [width_split(kept[i]).astype(F32) + width_split(got[i]).astype(F32) for i in range(2)]
    steps = [("lon", 0, bit) for bit in bits_of("lon")[1:]] + [("lat", 1, bit) for bit in bits_of("lat")]
    cut = [halves(x, *steps[0][:2], steps[0][2]) for x in owned]

    mixed, d_conv, sums = project(
        act, d_pre, w_out, w_in, xhat, inv, fields.reshape(cells, channels), cot_rows, mask_b,
        scale, gain, b_out.reshape(1, -1), cut[0][1], cut[1][1],
    )
    d_conv = d_conv.reshape(rows, cols, channels)
    d_left, d_right = side_halo(d_conv)
    half = channels // LANES // 2
    g_bi = g_bi.reshape(-1, channels)
    low = filter_grad(
        fields, mask_b, left, right, top, bot, d_conv, sums, g_bo, g_bi, (sums, sums), half, 0
    )
    d_top, d_bot = end_halo(d_conv[:3], d_conv[rows - 3 :], d_left, d_right)
    high = filter_grad(
        fields, mask_b, left, right, top, bot, d_conv, sums, g_bo, g_bi, (d_left, low), half, half
    )

    def advance(index, step):
        axis, dim, bit = steps[step]
        kept, sent = cut[index]
        owned[index] = kept + swap(sent, axis, bit).astype(F32)
        if step + 1 < len(steps):
            axis, dim, bit = steps[step + 1]
            cut[index] = halves(owned[index], axis, dim, bit)

    for step in range(len(steps) - 2):
        advance(0, step)
    small = jnp.concatenate([low, high], axis=2)
    small = total_sum(small)
    grad_fields = input_grad(
        d_conv, d_left, d_right, d_top, d_bot, kernel, mask_b, cotangent, (cut[0][1], high), half, 0
    )
    for step in range(len(steps) - 2):
        advance(1, step)
    advance(0, len(steps) - 2)
    grad_fields = input_grad(
        d_conv, d_left, d_right, d_top, d_bot, kernel, mask_b, cotangent, (cut[0][1], cut[1][1]), half, half,
        grad_fields,
    )
    advance(1, len(steps) - 2)
    advance(0, len(steps) - 1)
    advance(1, len(steps) - 1)
    return (
        mixed.reshape(rows, cols, channels),
        grad_fields,
        small[:7, :7],
        small[7, 1],
        small[7, 2],
        owned[1][0, 0],
        small[7, 4:].reshape(hidden),
        owned[0][0, 0].T,
        small[7, 3],
        small[7, 0],
    )


def solution(mesh):
    placed = (
        P(("grp", "lat"), "lon", None),
        P(("grp", "lat"), "lon"),
        P(("grp", "lat"), "lon", None),
        P(),
        P(),
        P(),
        P(),
        P(),
        P(),
        P(),
        P(),
    )
    return jax.shard_map(
        per_device,
        mesh=mesh,
        in_specs=placed,
        out_specs=(
            P(("grp", "lat"), "lon", None),
            P(("grp", "lat"), "lon", None),
            P("grp", None, None),
            P("grp"),
            P("grp"),
            P("grp", ("lon", "lat")),
            P("grp"),
            P(("lon", "lat"), "grp"),
            P("grp"),
            P("grp"),
        ),
        check_vma=False,
    )
```

```python
import functools
import math

import jax
import jax.numpy as jnp
from jax import lax
from jax.experimental import pallas as pl
from jax.experimental.pallas import tpu as pltpu
from jax.sharding import PartitionSpec as P

F32 = jnp.float32
BF16 = jnp.bfloat16
LANES = 128
SUB = 8


def params(mib):
    return pltpu.CompilerParams(vmem_limit_bytes=mib * 1024 * 1024)


def estimate(micros):
    return pl.CostEstimate(
        flops=int(micros * 1.15e9), bytes_accessed=int(micros * 3.6e6), transcendentals=0
    )


def once(shape):
    zeros = (0,) * len(shape)
    return pl.BlockSpec(shape, lambda *_: zeros, pipeline_mode=pl.Buffered(1))


UNUSED = pl.BlockSpec(memory_space=pl.ANY)


def whole_spec(shape):
    zeros = (0,) * len(shape)
    return pl.BlockSpec(shape, lambda *_: zeros)


def shifted(window, row, start, offset):
    if offset % SUB == 0:
        return window[row, pl.ds(start + offset, SUB), :]
    base = start + offset // SUB * SUB
    pair = window[row, pl.ds(base, 2 * SUB), :]
    return pltpu.roll(pair, 2 * SUB - offset % SUB, axis=0)[:SUB]


def tap_rows(k_ref, col_off, flip):
    at = 6 - col_off if flip else col_off
    rows = [k_ref[6 - p if flip else p, at : at + 1, :] for p in range(7)]
    return [jnp.broadcast_to(row, (SUB, LANES)) for row in rows]


def band_conv(window, k_ref, start, rows, pad, flip):
    sums = [None] * rows
    for col_off in range(7):
        weights = tap_rows(k_ref, col_off, flip)
        for src in range(window.shape[0]):
            hits = [(src - pad - row_off + 3, row_off) for row_off in range(7)]
            hits = [(out, row_off) for out, row_off in hits if 0 <= out < rows]
            if not hits:
                continue
            cells = shifted(window, src, start, 5 + col_off)
            for out, row_off in hits:
                term = weights[row_off] * cells
                sums[out] = term if sums[out] is None else sums[out] + term
    return sums


def conv_inner_kernel(f_ref, m_ref, k_ref, o_ref, head_ref, tail_ref, window):
    rows, cols, _ = f_ref.shape
    masked = f_ref[...].astype(F32) * m_ref[...]
    window[:, 8 : 8 + cols, :] = masked
    head_ref[...] = masked[:3].astype(BF16)
    tail_ref[...] = masked[rows - 3 :].astype(BF16)
    for start in range(8, cols - 8, 8):
        sums = band_conv(window, k_ref, start, rows, 0, False)
        for row in range(rows):
            o_ref[row, start - 8 : start, :] = sums[row]


def conv_side_kernel(f_ref, m_ref, k_ref, l_ref, r_ref, o_ref, window):
    rows, cols, _ = f_ref.shape
    window[:, 5:8, :] = l_ref[...].astype(F32)
    window[:, 8 : 8 + cols, :] = f_ref[...].astype(F32) * m_ref[...]
    window[:, 8 + cols : 11 + cols, :] = r_ref[...].astype(F32)
    for at, start in ((0, 0), (8, cols - 8)):
        sums = band_conv(window, k_ref, start, rows, 0, False)
        for row in range(rows):
            o_ref[row, at : at + 8, :] = sums[row]


def by_channels(shape, first=0):
    return pl.BlockSpec(shape[:-1] + (LANES,), lambda c: (0,) * (len(shape) - 1) + (c + first,))


def conv_inner(fields, mask_b, kernel):
    rows, cols, channels = fields.shape
    ends = (3, cols, channels)
    return pl.pallas_call(
        conv_inner_kernel,
        grid=(channels // LANES,),
        out_shape=[
            jax.ShapeDtypeStruct((rows, cols - 16, channels), F32),
            jax.ShapeDtypeStruct(ends, BF16),
            jax.ShapeDtypeStruct(ends, BF16),
        ],
        in_specs=[by_channels(fields.shape), whole_spec(mask_b.shape), by_channels(kernel.shape)],
        out_specs=[by_channels((rows, cols - 16, channels)), by_channels(ends), by_channels(ends)],
        scratch_shapes=[pltpu.VMEM((rows, cols + 16, LANES), F32)],
        compiler_params=params(56),
        cost_estimate=estimate(4),
        name="conv_inner",
    )(fields, mask_b, kernel)


def conv_side(fields, mask_b, kernel, left, right):
    rows, cols, channels = fields.shape
    return pl.pallas_call(
        conv_side_kernel,
        grid=(channels // LANES,),
        out_shape=jax.ShapeDtypeStruct((rows, 16, channels), F32),
        in_specs=[
            by_channels(fields.shape),
            whole_spec(mask_b.shape),
            by_channels(kernel.shape),
            by_channels(left.shape),
            by_channels(right.shape),
        ],
        out_specs=by_channels((rows, 16, channels)),
        scratch_shapes=[pltpu.VMEM((rows, cols + 16, LANES), F32)],
        compiler_params=params(56),
        cost_estimate=estimate(4),
        name="conv_side",
    )(fields, mask_b, kernel, left, right)


def gelu_pair(x):
    root = math.sqrt(2.0 / math.pi)
    square = x * x
    tanh = jnp.tanh(x * (root + (root * 0.044715) * square))
    half = 0.5 * tanh + 0.5
    value = x * half
    slope = half + value * ((1.0 - tanh) * (root + (3.0 * root * 0.044715) * square))
    return value, slope


def hidden_block(
    normed, normed_t, dbr, dbr_t, wi_ref, bi_ref, wo_ref, act_ref, dpre_ref, gbi_ref, sent_ref, kept_ref
):
    cells = normed.shape[0]
    part = 256
    total = None
    for at in range(0, cells, part):
        here = slice(at, at + part)
        pre = jnp.dot(normed[here, :], wi_ref[...], preferred_element_type=F32) + bi_ref[...]
        d_act = lax.dot_general(
            dbr[here, :], wo_ref[...], (((1,), (1,)), ((), ())), preferred_element_type=F32
        )
        value, slope = gelu_pair(pre)
        act_ref[here, :] = value.astype(BF16)
        d_pre = d_act * slope
        dpre_ref[here, :] = d_pre.astype(BF16)
        sums = jnp.sum(d_pre, axis=0, keepdims=True)
        total = sums if total is None else total + sums
    gbi_ref[...] = total
    _, parts, _, width = sent_ref.shape
    first = pl.program_id(0) < pl.num_programs(0) // 2
    for index, (left, right) in enumerate(((dbr_t, act_ref), (normed_t, dpre_ref))):
        grad = jnp.dot(left[...], right[...], preferred_element_type=F32).astype(BF16)

        def store(ref):
            for lat in range(parts):
                ref[index, lat] = grad[:, lat * width : (lat + 1) * width]

        pl.when(first)(functools.partial(store, sent_ref))
        pl.when(jnp.logical_not(first))(functools.partial(store, kept_ref))


def expand_first_kernel(
    order_ref,
    inner_ref, side_ref, top_ref, bot_ref, k_ref, gain_ref, bias_ref, scale_ref, m_ref, cot_ref,
    wi_ref, bi_ref, wo_ref,
    xhat_ref, inv_ref, gbo_ref, normed, normed_t, dbr, dbr_t, act_ref, dpre_ref, gbi_ref, sent_ref, kept_ref,
    conv, halo,
):
    rows, cols, channels = conv.shape
    cells = rows * cols

    @pl.when(pl.program_id(0) == 0)
    def _():
        conv[:, 0:8, :] = side_ref[:, 0:8, :]
        conv[:, 8 : cols - 8, :] = inner_ref[...]
        conv[:, cols - 8 : cols, :] = side_ref[:, 8:16, :]
        halo[0:3, 5 : 11 + cols, :] = top_ref[...].astype(F32)
        halo[3:6, 5 : 11 + cols, :] = bot_ref[...].astype(F32)
        for block in range(channels // LANES):
            lanes = slice(block * LANES, (block + 1) * LANES)
            for start in range(0, cols, 8):
                outs = list(range(3)) + list(range(rows - 3, rows))
                sums = {out: conv[out, start : start + 8, lanes] for out in outs}
                for col_off in range(7):
                    for src in range(6):
                        lat = src - 3 if src < 3 else rows + src - 3
                        offset = (5 + col_off) % SUB
                        base = start + (5 + col_off) // SUB * SUB
                        pair = halo[src, base : base + 2 * SUB, lanes]
                        cell = pltpu.roll(pair, 2 * SUB - offset, axis=0)[:SUB] if offset else pair[:SUB]
                        for out in outs:
                            row_off = lat - out + 3
                            if 0 <= row_off < 7:
                                tap = k_ref[row_off, col_off : col_off + 1, lanes]
                                sums[out] = sums[out] + tap * cell
                for out in outs:
                    conv[out, start : start + 8, lanes] = sums[out]
        gbo_ref[...] = jnp.zeros_like(gbo_ref)

        chunk = 128
        chunk_rows = chunk // cols

        def standardize(step, _):
            at = pl.multiple_of(step * chunk, chunk)
            here = pl.ds(at, chunk)
            there = pl.ds(step * chunk_rows, chunk_rows)
            x = conv[there].reshape(chunk, channels)
            mean = jnp.mean(x, axis=-1, keepdims=True)
            centered = x - mean
            var = jnp.mean(centered * centered, axis=-1, keepdims=True)
            inv = lax.rsqrt(var + 1e-06)
            xhat = centered * inv
            xhat_ref[here, :] = xhat
            inv_ref[here, :] = jnp.broadcast_to(inv, (chunk, LANES))
            scaled = xhat * gain_ref[...] + bias_ref[...]
            normed[here, :] = scaled.astype(BF16)
            normed_t[:, here] = scaled.T.astype(BF16)
            ocean = jnp.concatenate([m_ref[there].reshape(chunk, LANES)] * (channels // LANES), axis=1)
            grad = ocean * scale_ref[...] * cot_ref[here, :].astype(F32)
            gbo_ref[...] += jnp.sum(grad, axis=0, keepdims=True)
            dbr[here, :] = grad.astype(BF16)
            dbr_t[:, here] = grad.T.astype(BF16)
            return 0

        lax.fori_loop(0, cells // chunk, standardize, 0)

    hidden_block(
        normed, normed_t, dbr, dbr_t, wi_ref, bi_ref, wo_ref, act_ref, dpre_ref, gbi_ref, sent_ref, kept_ref
    )


def expand_second_kernel(
    order_ref, normed, normed_t, dbr, dbr_t, wi_ref, bi_ref, wo_ref, act_in, dpre_in, gbi_in,
    act_ref, dpre_ref, gbi_ref, sent_ref, kept_ref,
):
    hidden_block(
        normed, normed_t, dbr, dbr_t, wi_ref, bi_ref, wo_ref, act_ref, dpre_ref, gbi_ref, sent_ref, kept_ref
    )


def hidden_specs(cells, channels, hidden, n_lon, n_lat, first):
    block = hidden // n_lon
    split = n_lat if (block // n_lat) % LANES == 0 else 1
    turn = n_lon // 4
    grads = (2, None, split, channels, block // split)
    weights = [
        pl.BlockSpec((channels, block), lambda h, order: (0, order[h + first])),
        pl.BlockSpec((1, block), lambda h, order: (0, order[h + first])),
        pl.BlockSpec((block, channels), lambda h, order: (order[h + first], 0)),
    ]
    results = [
        pl.BlockSpec((cells, block), lambda h, order: (0, order[h + first])),
        pl.BlockSpec((cells, block), lambda h, order: (0, order[h + first])),
        pl.BlockSpec((1, block), lambda h, order: (0, order[h + first])),
        pl.BlockSpec(grads, lambda h, order: (0, jnp.minimum(h, turn - 1), 0, 0, 0)),
        pl.BlockSpec(grads, lambda h, order: (0, jnp.maximum(h - turn, 0), 0, 0, 0)),
    ]
    shapes = [
        jax.ShapeDtypeStruct((cells, hidden), BF16),
        jax.ShapeDtypeStruct((cells, hidden), BF16),
        jax.ShapeDtypeStruct((1, hidden), F32),
        jax.ShapeDtypeStruct((2, turn, split, channels, block // split), BF16),
        jax.ShapeDtypeStruct((2, turn, split, channels, block // split), BF16),
    ]
    return weights, results, shapes


def expand_first(order, inner, side, top, bot, kernel, gain, bias, scale, mask_b, cot, w_in, b_in, w_out, n_lon, n_lat):
    rows, _, channels = inner.shape
    hidden = w_in.shape[1]
    cells, _ = cot.shape
    cols = cells // rows
    weights, results, shapes = hidden_specs(cells, channels, hidden, n_lon, n_lat, 0)
    flat = (cells, channels)
    turned = (channels, cells)
    own = [
        jax.ShapeDtypeStruct(flat, F32),
        jax.ShapeDtypeStruct((cells, LANES), F32),
        jax.ShapeDtypeStruct((1, channels), F32),
        jax.ShapeDtypeStruct(flat, BF16),
        jax.ShapeDtypeStruct(turned, BF16),
        jax.ShapeDtypeStruct(flat, BF16),
        jax.ShapeDtypeStruct(turned, BF16),
    ]
    given = (inner, side, top, bot, kernel, gain, bias, scale, mask_b, cot)
    return pl.pallas_call(
        expand_first_kernel,
        grid_spec=pltpu.PrefetchScalarGridSpec(
            num_scalar_prefetch=1,
            grid=(n_lon // 2,),
            in_specs=[once(x.shape) for x in given] + weights,
            out_specs=[once(x.shape) for x in own] + results,
            scratch_shapes=[
                pltpu.VMEM((rows, cols, channels), F32),
                pltpu.VMEM((6, cols + 16, channels), F32),
            ],
        ),
        out_shape=own + shapes,
        compiler_params=params(56),
        cost_estimate=estimate(12),
        name="expand_first",
    )(order, *given, w_in, b_in, w_out)


def expand_second(order, rows, w_in, b_in, w_out, act, dpre, gbi, n_lon, n_lat):
    cells, channels = rows[0].shape
    hidden = w_in.shape[1]
    weights, results, shapes = hidden_specs(cells, channels, hidden, n_lon, n_lat, n_lon // 2)
    return pl.pallas_call(
        expand_second_kernel,
        grid_spec=pltpu.PrefetchScalarGridSpec(
            num_scalar_prefetch=1,
            grid=(n_lon // 2,),
            in_specs=[once(x.shape) for x in rows] + weights + [UNUSED] * 3,
            out_specs=results,
        ),
        out_shape=shapes,
        input_output_aliases={8: 0, 9: 1, 10: 2},
        compiler_params=params(56),
        cost_estimate=estimate(8),
        name="expand_second",
    )(order, *rows, w_in, b_in, w_out, act, dpre, gbi)


def norm_back_kernel(dpre_ref, wi_ref, xhat_ref, inv_ref, gain_ref, ahead_ref, dconv_ref, sums_ref):
    channels = xhat_ref.shape[1]

    @pl.when(pl.program_id(0) == 0)
    def _():
        sums_ref[...] = jnp.zeros_like(sums_ref)

    d_normed = lax.dot_general(
        dpre_ref[...], wi_ref[...], (((1,), (1,)), ((), ())), preferred_element_type=F32
    )
    xhat = xhat_ref[...]
    normed_term = d_normed * xhat
    sums_ref[0:1, :] += jnp.sum(normed_term, axis=0, keepdims=True)
    sums_ref[1:2, :] += jnp.sum(d_normed, axis=0, keepdims=True)
    e = d_normed * gain_ref[...]
    m1 = jnp.mean(e, axis=-1, keepdims=True)
    m2 = jnp.mean(normed_term * gain_ref[...], axis=-1, keepdims=True)
    inv = jnp.concatenate([inv_ref[...]] * (channels // LANES), axis=1)
    dconv_ref[...] = (inv * (e - m1 - xhat * m2)).astype(BF16)


def norm_back(dpre, w_in, xhat, inv, gain, ahead):
    cells, hidden = dpre.shape
    channels = w_in.shape[0]
    part = 256

    def rows_of(width):
        return pl.BlockSpec((part, width), lambda i: (i, 0))

    return pl.pallas_call(
        norm_back_kernel,
        grid=(cells // part,),
        out_shape=[
            jax.ShapeDtypeStruct((cells, channels), BF16),
            jax.ShapeDtypeStruct((SUB, channels), F32),
        ],
        in_specs=[
            rows_of(hidden),
            once(w_in.shape),
            rows_of(channels),
            rows_of(LANES),
            whole_spec(gain.shape),
            UNUSED,
        ],
        out_specs=[rows_of(channels), whole_spec((SUB, channels))],
        compiler_params=params(56),
        cost_estimate=estimate(4),
        name="norm_back",
    )(dpre, w_in, xhat, inv, gain, ahead)


def project_kernel(
    act_ref, wo_ref, f_ref, cot_ref, m_ref, scale_ref, bo_ref, kept_ref, got_ref,
    mixed_ref, sums_ref, sent_ref,
):
    cells, channels = f_ref.shape

    @pl.when(pl.program_id(0) == 0)
    def _():
        sums_ref[...] = jnp.zeros_like(sums_ref)

    branch = jnp.dot(act_ref[...], wo_ref[...], preferred_element_type=F32) + bo_ref[...]
    ocean = jnp.concatenate([m_ref[...].reshape(cells, LANES)] * (channels // LANES), axis=1) * branch
    mixed_ref[...] = (f_ref[...].astype(F32) + ocean * scale_ref[...]).astype(BF16)
    sums_ref[0:1, :] += jnp.sum(ocean * cot_ref[...].astype(F32), axis=0, keepdims=True)
    sent_ref[...] = (kept_ref[...].astype(F32) + got_ref[...].astype(F32)).astype(BF16)


def project(act, w_out, fields, cot, mask_b, scale, b_out, kept, got):
    cells, hidden = act.shape
    channels = w_out.shape[1]
    part = 256
    steps = cells // part

    def rows_of(width):
        return pl.BlockSpec((part, width), lambda i: (i, 0))

    grads = kept.shape[1:3] + (channels // steps, kept.shape[4])
    both = pl.BlockSpec((None,) + grads, lambda i: (1, 0, 0, i, 0))
    return pl.pallas_call(
        project_kernel,
        grid=(steps,),
        out_shape=[
            jax.ShapeDtypeStruct((cells, channels), BF16),
            jax.ShapeDtypeStruct((SUB, channels), F32),
            jax.ShapeDtypeStruct(kept.shape[1:], BF16),
        ],
        in_specs=[
            rows_of(hidden),
            once(w_out.shape),
            rows_of(channels),
            rows_of(channels),
            pl.BlockSpec((part // mask_b.shape[1],) + mask_b.shape[1:], lambda i: (i, 0, 0)),
            whole_spec(scale.shape),
            whole_spec(b_out.shape),
            both,
            both,
        ],
        out_specs=[
            rows_of(channels),
            whole_spec((SUB, channels)),
            pl.BlockSpec(grads, lambda i: (0, 0, i, 0)),
        ],
        compiler_params=params(56),
        cost_estimate=estimate(4),
        name="project",
    )(act, w_out, fields, cot, mask_b, scale, b_out, kept, got)


def fill_window(window, center, left, right, top, bot):
    rows, cols, _ = center.shape
    window[3 : 3 + rows, 5:8, :] = left[...].astype(F32)
    window[3 : 3 + rows, 8 : 8 + cols, :] = center
    window[3 : 3 + rows, 8 + cols : 11 + cols, :] = right[...].astype(F32)
    window[0:3, 5 : 11 + cols, :] = top[...].astype(F32)
    window[3 + rows : 6 + rows, 5 : 11 + cols, :] = bot[...].astype(F32)


def filter_grad_kernel(
    f_ref, m_ref, l_ref, r_ref, t_ref, b_ref, d_ref, gsc_ref, sums_ref, gbo_ref, gbi_ref,
    o_ref, window, grad,
):
    rows, cols, _ = f_ref.shape
    fill_window(window, f_ref[...].astype(F32) * m_ref[...], l_ref, r_ref, t_ref, b_ref)
    grad[...] = d_ref[...].astype(F32)
    for col_off in range(7):

        def band(index, sums):
            start = pl.multiple_of(index * 8, 8)
            sums = list(sums)
            held = {}
            for src in range(rows + 6):
                if src < rows:
                    held[src] = grad[src, pl.ds(start, SUB), :]
                cells = shifted(window, src, start, 5 + col_off)
                for row_off in range(7):
                    out = src - row_off
                    if 0 <= out < rows:
                        sums[row_off] = sums[row_off] + held[out] * cells
            return tuple(sums)

        start = tuple(jnp.zeros((SUB, LANES), F32) for _ in range(7))
        sums = lax.fori_loop(0, cols // 8, band, start)
        for row_off in range(7):
            o_ref[row_off, col_off : col_off + 1, :] = jnp.sum(sums[row_off], axis=0, keepdims=True)
    o_ref[7, 0:1, :] = gsc_ref[0:1, :]
    o_ref[7, 1:3, :] = sums_ref[0:2, :]
    o_ref[7, 3:4, :] = gbo_ref[...]
    o_ref[7, 4:8, :] = gbi_ref[...]
    for row_off in range(7):
        o_ref[row_off, 7:8, :] = jnp.zeros((1, LANES), F32)


def filter_grad(fields, mask_b, left, right, top, bot, d_conv, gsc, sums, gbo, gbi):
    rows, cols, channels = fields.shape

    def part(x):
        return by_channels(x.shape)

    return pl.pallas_call(
        filter_grad_kernel,
        grid=(channels // LANES,),
        out_shape=jax.ShapeDtypeStruct((8, 8, channels), F32),
        in_specs=[
            part(fields),
            whole_spec(mask_b.shape),
            part(left),
            part(right),
            part(top),
            part(bot),
            part(d_conv),
            part(gsc),
            part(sums),
            part(gbo),
            part(gbi),
        ],
        out_specs=by_channels((8, 8, channels)),
        scratch_shapes=[
            pltpu.VMEM((rows + 6, cols + 16, LANES), F32),
            pltpu.VMEM((rows, cols, LANES), F32),
        ],
        compiler_params=params(56),
        cost_estimate=estimate(4),
        name="filter_grad",
    )(fields, mask_b, left, right, top, bot, d_conv, gsc, sums, gbo, gbi)


def input_grad_kernel(d_ref, l_ref, r_ref, t_ref, b_ref, k_ref, m_ref, cot_ref, o_ref, window, grad):
    rows, cols, _ = d_ref.shape
    fill_window(window, d_ref[...].astype(F32), l_ref, r_ref, t_ref, b_ref)
    for start in range(0, cols, 8):
        sums = band_conv(window, k_ref, start, rows, 3, True)
        for row in range(rows):
            grad[row, start : start + 8, :] = sums[row]
    o_ref[...] = (cot_ref[...].astype(F32) + m_ref[...] * grad[...]).astype(BF16)


def input_grad_more_kernel(d_ref, l_ref, r_ref, t_ref, b_ref, k_ref, m_ref, cot_ref, old_ref, o_ref, window, grad):
    input_grad_kernel(d_ref, l_ref, r_ref, t_ref, b_ref, k_ref, m_ref, cot_ref, o_ref, window, grad)


def input_grad(d_conv, left, right, top, bot, kernel, mask_b, cot, blocks, first, old=None):
    rows, cols, channels = d_conv.shape

    def part(x):
        return by_channels(x.shape, first)

    more = [] if old is None else [old]
    return pl.pallas_call(
        input_grad_kernel if old is None else input_grad_more_kernel,
        grid=(blocks,),
        out_shape=jax.ShapeDtypeStruct((rows, cols, channels), BF16),
        in_specs=[
            part(d_conv),
            part(left),
            part(right),
            part(top),
            part(bot),
            part(kernel),
            whole_spec(mask_b.shape),
            part(cot),
        ]
        + [UNUSED] * len(more),
        out_specs=part(d_conv),
        scratch_shapes=[
            pltpu.VMEM((rows + 6, cols + 16, LANES), F32),
            pltpu.VMEM((rows, cols, LANES), F32),
        ],
        input_output_aliases={} if old is None else {8: 0},
        compiler_params=params(56),
        cost_estimate=estimate(4),
        name="input_grad",
    )(d_conv, left, right, top, bot, kernel, mask_b, cot, *more)


def swap(values, axis, bit):
    count = lax.axis_size(axis)
    return lax.ppermute(values, axis, [(i, i ^ bit) for i in range(count)])


def bits_of(axis):
    return [1 << k for k in range(int(math.log2(lax.axis_size(axis))))]


def after(value, *others):
    return lax.optimization_barrier((value,) + others)[0]


def halves(values, axis, dim, bit):
    mine = (lax.axis_index(axis) // bit) % 2
    shape = values.shape
    paired = values.reshape(shape[:dim] + (shape[dim] // 2, 2) + shape[dim + 1 :])
    kept = lax.dynamic_index_in_dim(paired, mine, dim + 1, keepdims=False)
    sent = lax.dynamic_index_in_dim(paired, 1 - mine, dim + 1, keepdims=False)
    return kept, sent.astype(BF16)


def side_halo(last, first):
    count = lax.axis_size("lon")
    ahead = [(i, (i + 1) % count) for i in range(count)]
    back = [((i + 1) % count, i) for i in range(count)]
    return lax.ppermute(last, "lon", ahead), lax.ppermute(first, "lon", back)


def end_rows(head, tail, left, right):
    rows = left.shape[0]
    return (
        jnp.concatenate([left[rows - 3 :], tail, right[rows - 3 :]], axis=1),
        jnp.concatenate([left[:3], head, right[:3]], axis=1),
    )


def end_halo(tail, head):
    count = lax.axis_size("lat")
    ahead = [(i, i + 1) for i in range(count - 1)]
    back = [(i + 1, i) for i in range(count - 1)]
    return lax.ppermute(tail, "lat", ahead), lax.ppermute(head, "lat", back)


def per_device(
    fields,
    land_mask,
    cotangent,
    kernel,
    layer_norm_gain,
    layer_norm_bias,
    w_in,
    b_in,
    w_out,
    b_out,
    layer_scale,
):
    rows, cols, channels = fields.shape
    cells = rows * cols
    hidden = w_in.shape[1]
    n_lon, n_lat = lax.axis_size("lon"), lax.axis_size("lat")
    gain, bias = layer_norm_gain.reshape(1, -1), layer_norm_bias.reshape(1, -1)
    scale = layer_scale.reshape(1, -1)
    mask_b = jnp.broadcast_to(land_mask.astype(F32)[:, :, None], (rows, cols, LANES))
    cot_rows = cotangent.reshape(cells, channels)
    ocean = land_mask.astype(BF16)[:, :, None]
    left, right = side_halo(fields[:, cols - 3 :] * ocean[:, cols - 3 :], fields[:, :3] * ocean[:, :3])
    inner, head, tail = conv_inner(fields, mask_b, kernel)
    top, bot = end_halo(*end_rows(head, tail, left, right))
    side = conv_side(fields, mask_b, kernel, left, right)

    lon = lax.axis_index("lon")
    core, side_y = lon % 2, (lon // 2) % 2
    quads = 4 * jnp.arange(n_lon // 4, dtype=jnp.int32)
    order = jnp.concatenate(
        [quads + 2 * y + c for y in (1 - side_y, side_y) for c in (1 - core, core)]
    )
    xhat, inv, g_bo, *row_forms, act, d_pre, g_bi, sent_far, kept_far = expand_first(
        order, inner, side, top, bot, kernel, gain, bias, scale, mask_b, cot_rows,
        w_in, b_in.reshape(1, -1), w_out, n_lon, n_lat,
    )
    got_far = swap(sent_far, "lon", 1)
    act, d_pre, g_bi, sent_near, kept_near = expand_second(
        order, row_forms, w_in, b_in.reshape(1, -1), w_out, act, d_pre, g_bi, n_lon, n_lat
    )
    got_near = swap(sent_near, "lon", 1)

    far_wo = (kept_far[0].astype(F32) + got_far[0].astype(F32)).astype(BF16)
    got_wo = swap(far_wo, "lon", 2)
    d_conv, sums = norm_back(d_pre, w_in, xhat, inv, gain, far_wo)
    d_conv = d_conv.reshape(rows, cols, channels)
    d_last, d_first = d_conv[:, cols - 3 :], d_conv[:, :3]
    d_left, d_right = side_halo(d_last, d_first)
    mixed, g_scale, far_wi = project(
        after(act, d_last, d_first), w_out, fields.reshape(cells, channels), cot_rows, mask_b, scale,
        b_out.reshape(1, -1), kept_far, got_far,
    )
    got_wi = swap(far_wi, "lon", 2)
    d_tail, d_head = end_rows(
        d_conv[:3], d_conv[rows - 3 :], after(d_left, mixed), after(d_right, mixed)
    )
    d_top, d_bot = end_halo(d_tail, d_head)

    steps = [("lon", 0, bit) for bit in bits_of("lon")[2:]] + [("lat", 1, bit) for bit in bits_of("lat")]
    owned, cut = [None, None], [None, None]

    def begin(index, got, last):
        both = after(kept_near[index], last).astype(F32) + after(got_near[index], last).astype(F32)
        x = both + after(got, last).astype(F32)
        if x.shape[1] != n_lat:
            x = x.reshape(n_lon // 4, channels, n_lat, -1).transpose(0, 2, 1, 3)
        cut[index] = halves(x, *steps[0])

    def advance(index, step, last):
        axis, dim, bit = steps[step]
        kept, sent = cut[index]
        owned[index] = after(kept, last) + after(swap(sent, axis, bit), last).astype(F32)
        if step + 1 < len(steps):
            cut[index] = halves(owned[index], *steps[step + 1])

    hops = [(axis, bit) for axis in ("lon", "lat") for bit in bits_of(axis)]

    def spread(hop, last):
        return after(small, last) + after(swap(small, *hops[hop]), last)

    begin(0, got_wo, mixed)
    small = filter_grad(
        after(fields, d_tail, d_head, far_wi, cut[0][1]), mask_b, left, right, top, bot, d_conv,
        g_scale, sums, g_bo, g_bi.reshape(-1, channels),
    )
    for step in range(len(steps) - 1):
        advance(0, step, small)
    begin(1, got_wi, small)
    for step in range(len(steps) - 2):
        advance(1, step, small)
    half = channels // LANES // 2
    back = (d_left, d_right, d_top, d_bot, kernel, mask_b, cotangent)
    grad_fields = input_grad(after(d_conv, small, cut[0][1], cut[1][1]), *back, half, 0)
    small = spread(0, grad_fields)
    advance(1, len(steps) - 2, grad_fields)
    advance(0, len(steps) - 1, grad_fields)
    grad_fields = input_grad(after(d_conv, small, cut[1][1]), *back, half // 2, half, grad_fields)
    small = spread(1, grad_fields)
    grad_fields = input_grad(
        after(d_conv, small), *back, half // 2, half + half // 2, grad_fields
    )
    for hop in range(2, len(hops)):
        small = spread(hop, grad_fields)
    advance(1, len(steps) - 1, grad_fields)
    return (
        mixed.reshape(rows, cols, channels),
        grad_fields,
        small[:7, :7],
        small[7, 1],
        small[7, 2],
        owned[1][0, 0],
        small[7, 4:].reshape(hidden),
        owned[0][0, 0].T,
        small[7, 3],
        small[7, 0],
    )


def solution(mesh):
    placed = (
        P(("grp", "lat"), "lon", None),
        P(("grp", "lat"), "lon"),
        P(("grp", "lat"), "lon", None),
        P(),
        P(),
        P(),
        P(),
        P(),
        P(),
        P(),
        P(),
    )
    return jax.shard_map(
        per_device,
        mesh=mesh,
        in_specs=placed,
        out_specs=(
            P(("grp", "lat"), "lon", None),
            P(("grp", "lat"), "lon", None),
            P("grp", None, None),
            P("grp"),
            P("grp"),
            P("grp", ("lon", "lat")),
            P("grp"),
            P(("lon", "lat"), "grp"),
            P("grp"),
            P("grp"),
        ),
        check_vma=False,
    )
```

```python
import functools
import math

import jax
import jax.numpy as jnp
from jax import lax
from jax.experimental import pallas as pl
from jax.experimental.pallas import tpu as pltpu
from jax.sharding import PartitionSpec as P

F32 = jnp.float32
BF16 = jnp.bfloat16
LANES = 128
SUB = 8


def params(mib):
    return pltpu.CompilerParams(vmem_limit_bytes=mib * 1024 * 1024)


def estimate(micros):
    return pl.CostEstimate(
        flops=int(micros * 1.15e9), bytes_accessed=int(micros * 3.6e6), transcendentals=0
    )


def once(shape):
    zeros = (0,) * len(shape)
    return pl.BlockSpec(shape, lambda *_: zeros, pipeline_mode=pl.Buffered(1))


UNUSED = pl.BlockSpec(memory_space=pl.ANY)


def whole_spec(shape):
    zeros = (0,) * len(shape)
    return pl.BlockSpec(shape, lambda *_: zeros)


def shifted(window, row, start, offset):
    if offset % SUB == 0:
        return window[row, pl.ds(start + offset, SUB), :]
    base = start + offset // SUB * SUB
    pair = window[row, pl.ds(base, 2 * SUB), :]
    return pltpu.roll(pair, 2 * SUB - offset % SUB, axis=0)[:SUB]


def tap_rows(k_ref, col_off, flip):
    at = 6 - col_off if flip else col_off
    rows = [k_ref[6 - p if flip else p, at : at + 1, :] for p in range(7)]
    return [jnp.broadcast_to(row, (SUB, LANES)) for row in rows]


def band_conv(window, k_ref, start, rows, pad, flip):
    sums = [None] * rows
    for col_off in range(7):
        weights = tap_rows(k_ref, col_off, flip)
        for src in range(window.shape[0]):
            hits = [(src - pad - row_off + 3, row_off) for row_off in range(7)]
            hits = [(out, row_off) for out, row_off in hits if 0 <= out < rows]
            if not hits:
                continue
            cells = shifted(window, src, start, 5 + col_off)
            for out, row_off in hits:
                term = weights[row_off] * cells
                sums[out] = term if sums[out] is None else sums[out] + term
    return sums


def conv_inner_kernel(f_ref, m_ref, k_ref, o_ref, head_ref, tail_ref, window):
    rows, cols, _ = f_ref.shape
    masked = f_ref[...].astype(F32) * m_ref[...]
    window[:, 8 : 8 + cols, :] = masked
    head_ref[...] = masked[:3].astype(BF16)
    tail_ref[...] = masked[rows - 3 :].astype(BF16)
    for start in range(8, cols - 8, 8):
        sums = band_conv(window, k_ref, start, rows, 0, False)
        for row in range(rows):
            o_ref[row, start - 8 : start, :] = sums[row]


def conv_side_kernel(f_ref, m_ref, k_ref, l_ref, r_ref, o_ref, window):
    rows, cols, _ = f_ref.shape
    window[:, 5:8, :] = l_ref[...].astype(F32)
    window[:, 8 : 8 + cols, :] = f_ref[...].astype(F32) * m_ref[...]
    window[:, 8 + cols : 11 + cols, :] = r_ref[...].astype(F32)
    for at, start in ((0, 0), (8, cols - 8)):
        sums = band_conv(window, k_ref, start, rows, 0, False)
        for row in range(rows):
            o_ref[row, at : at + 8, :] = sums[row]


def by_channels(shape, first=0):
    return pl.BlockSpec(shape[:-1] + (LANES,), lambda c: (0,) * (len(shape) - 1) + (c + first,))


def conv_inner(fields, mask_b, kernel):
    rows, cols, channels = fields.shape
    ends = (3, cols, channels)
    return pl.pallas_call(
        conv_inner_kernel,
        grid=(channels // LANES,),
        out_shape=[
            jax.ShapeDtypeStruct((rows, cols - 16, channels), F32),
            jax.ShapeDtypeStruct(ends, BF16),
            jax.ShapeDtypeStruct(ends, BF16),
        ],
        in_specs=[by_channels(fields.shape), whole_spec(mask_b.shape), by_channels(kernel.shape)],
        out_specs=[by_channels((rows, cols - 16, channels)), by_channels(ends), by_channels(ends)],
        scratch_shapes=[pltpu.VMEM((rows, cols + 16, LANES), F32)],
        compiler_params=params(56),
        cost_estimate=estimate(4),
        name="conv_inner",
    )(fields, mask_b, kernel)


def conv_side(fields, mask_b, kernel, left, right):
    rows, cols, channels = fields.shape
    return pl.pallas_call(
        conv_side_kernel,
        grid=(channels // LANES,),
        out_shape=jax.ShapeDtypeStruct((rows, 16, channels), F32),
        in_specs=[
            by_channels(fields.shape),
            whole_spec(mask_b.shape),
            by_channels(kernel.shape),
            by_channels(left.shape),
            by_channels(right.shape),
        ],
        out_specs=by_channels((rows, 16, channels)),
        scratch_shapes=[pltpu.VMEM((rows, cols + 16, LANES), F32)],
        compiler_params=params(56),
        cost_estimate=estimate(4),
        name="conv_side",
    )(fields, mask_b, kernel, left, right)


def gelu_pair(x):
    root = math.sqrt(2.0 / math.pi)
    square = x * x
    tanh = jnp.tanh(x * (root + (root * 0.044715) * square))
    half = 0.5 * tanh + 0.5
    value = x * half
    slope = half + value * ((1.0 - tanh) * (root + (3.0 * root * 0.044715) * square))
    return value, slope


def expand_kernel(
    order_ref,
    inner_ref, side_ref, top_ref, bot_ref, k_ref, gain_ref, bias_ref, scale_ref, m_ref, cot_ref,
    wi_ref, bi_ref, wo_ref,
    gbo_ref, dconv_ref, sums_ref, act_ref, gbi_ref, sent_ref, kept_wo_ref, kept_wi_ref,
    conv, halo, inv_s, normed, normed_t, dbr, dbr_t, dpre, d_normed,
):
    rows, cols, channels = conv.shape
    cells = rows * cols
    chunk = 128
    chunk_rows = chunk // cols
    step_now = pl.program_id(0)

    @pl.when(step_now == 0)
    def _():
        conv[:, 0:8, :] = side_ref[:, 0:8, :]
        conv[:, 8 : cols - 8, :] = inner_ref[...]
        conv[:, cols - 8 : cols, :] = side_ref[:, 8:16, :]
        halo[0:3, 5 : 11 + cols, :] = top_ref[...].astype(F32)
        halo[3:6, 5 : 11 + cols, :] = bot_ref[...].astype(F32)
        for block in range(channels // LANES):
            lanes = slice(block * LANES, (block + 1) * LANES)
            for start in range(0, cols, 8):
                outs = list(range(3)) + list(range(rows - 3, rows))
                sums = {out: conv[out, start : start + 8, lanes] for out in outs}
                for col_off in range(7):
                    for src in range(6):
                        lat = src - 3 if src < 3 else rows + src - 3
                        offset = (5 + col_off) % SUB
                        base = start + (5 + col_off) // SUB * SUB
                        pair = halo[src, base : base + 2 * SUB, lanes]
                        cell = pltpu.roll(pair, 2 * SUB - offset, axis=0)[:SUB] if offset else pair[:SUB]
                        for out in outs:
                            row_off = lat - out + 3
                            if 0 <= row_off < 7:
                                tap = k_ref[row_off, col_off : col_off + 1, lanes]
                                sums[out] = sums[out] + tap * cell
                for out in outs:
                    conv[out, start : start + 8, lanes] = sums[out]
        gbo_ref[...] = jnp.zeros_like(gbo_ref)

        def standardize(step, _):
            at = pl.multiple_of(step * chunk, chunk)
            here = pl.ds(at, chunk)
            there = pl.ds(step * chunk_rows, chunk_rows)
            x = conv[there].reshape(chunk, channels)
            mean = jnp.mean(x, axis=-1, keepdims=True)
            centered = x - mean
            var = jnp.mean(centered * centered, axis=-1, keepdims=True)
            inv = lax.rsqrt(var + 1e-06)
            xhat = centered * inv
            conv[there] = xhat.reshape(chunk_rows, cols, channels)
            inv_s[here, :] = jnp.broadcast_to(inv, (chunk, LANES))
            scaled = xhat * gain_ref[...] + bias_ref[...]
            normed[here, :] = scaled.astype(BF16)
            normed_t[:, here] = scaled.T.astype(BF16)
            ocean = jnp.concatenate([m_ref[there].reshape(chunk, LANES)] * (channels // LANES), axis=1)
            grad = ocean * scale_ref[...] * cot_ref[here, :].astype(F32)
            gbo_ref[...] += jnp.sum(grad, axis=0, keepdims=True)
            dbr[here, :] = grad.astype(BF16)
            dbr_t[:, here] = grad.T.astype(BF16)
            d_normed[here, :] = jnp.zeros((chunk, channels), F32)
            return 0

        lax.fori_loop(0, cells // chunk, standardize, 0)

    part = 256
    starts = list(range(0, cells, part))

    def products(at):
        here = slice(at, at + part)
        pre = jnp.dot(normed[here, :], wi_ref[...], preferred_element_type=F32)
        d_act = lax.dot_general(
            dbr[here, :], wo_ref[...], (((1,), (1,)), ((), ())), preferred_element_type=F32
        )
        return pre, d_act

    total = None
    ahead = products(0)
    for at in starts:
        here = slice(at, at + part)
        pre, d_act = ahead
        if at + part < cells:
            ahead = products(at + part)
        value, slope = gelu_pair(pre + bi_ref[...])
        act_ref[here, :] = value.astype(BF16)
        d_pre = d_act * slope
        dpre[here, :] = d_pre.astype(BF16)
        sums = jnp.sum(d_pre, axis=0, keepdims=True)
        total = sums if total is None else total + sums
        d_normed[here, :] += lax.dot_general(
            dpre[here, :], wi_ref[...], (((1,), (1,)), ((), ())), preferred_element_type=F32
        )
    gbi_ref[...] = total
    _, parts, _, width = sent_ref.shape
    first = step_now < pl.num_programs(0) // 2
    for index, (left, right, kept_ref) in enumerate(
        ((dbr_t, act_ref, kept_wo_ref), (normed_t, dpre, kept_wi_ref))
    ):
        grad = jnp.dot(left[...], right[...], preferred_element_type=F32).astype(BF16)

        def store(ref):
            for lat in range(parts):
                ref[lat] = grad[:, lat * width : (lat + 1) * width]

        pl.when(first)(functools.partial(store, sent_ref.at[index]))
        pl.when(jnp.logical_not(first))(functools.partial(store, kept_ref))

    @pl.when(step_now == pl.num_programs(0) - 1)
    def _():
        sums_ref[...] = jnp.zeros_like(sums_ref)

        def norm_back(step, _):
            here = pl.ds(pl.multiple_of(step * chunk, chunk), chunk)
            there = pl.ds(step * chunk_rows, chunk_rows)
            grad = d_normed[here, :]
            xhat = conv[there].reshape(chunk, channels)
            term = grad * xhat
            sums_ref[0:1, :] += jnp.sum(term, axis=0, keepdims=True)
            sums_ref[1:2, :] += jnp.sum(grad, axis=0, keepdims=True)
            e = grad * gain_ref[...]
            m1 = jnp.mean(e, axis=-1, keepdims=True)
            m2 = jnp.mean(term * gain_ref[...], axis=-1, keepdims=True)
            inv = jnp.concatenate([inv_s[here, :]] * (channels // LANES), axis=1)
            dconv_ref[here, :] = (inv * (e - m1 - xhat * m2)).astype(BF16)
            return 0

        lax.fori_loop(0, cells // chunk, norm_back, 0)


def expand(order, inner, side, top, bot, kernel, gain, bias, scale, mask_b, cot, w_in, b_in, w_out, n_lon, n_lat):
    rows, _, channels = inner.shape
    hidden = w_in.shape[1]
    cells, _ = cot.shape
    cols = cells // rows
    block = hidden // n_lon
    split = n_lat if (block // n_lat) % LANES == 0 else 1
    turn = n_lon // 2
    grads = (split, channels, block // split)
    given = (inner, side, top, bot, kernel, gain, bias, scale, mask_b, cot)

    def sent_at(h, order):
        return (0, jnp.minimum(h, turn - 1), 0, 0, 0)

    def kept_at(h, order):
        return (jnp.maximum(h - turn, 0), 0, 0, 0)

    return pl.pallas_call(
        expand_kernel,
        grid_spec=pltpu.PrefetchScalarGridSpec(
            num_scalar_prefetch=1,
            grid=(n_lon,),
            in_specs=[once(x.shape) for x in given]
            + [
                pl.BlockSpec((channels, block), lambda h, order: (0, order[h])),
                pl.BlockSpec((1, block), lambda h, order: (0, order[h])),
                pl.BlockSpec((block, channels), lambda h, order: (order[h], 0)),
            ],
            out_specs=[
                once((1, channels)),
                once((cells, channels)),
                once((SUB, channels)),
                pl.BlockSpec((cells, block), lambda h, order: (0, order[h])),
                pl.BlockSpec((1, block), lambda h, order: (0, order[h])),
                pl.BlockSpec((2, None) + grads, sent_at),
                pl.BlockSpec((None,) + grads, kept_at),
                pl.BlockSpec((None,) + grads, kept_at),
            ],
            scratch_shapes=[
                pltpu.VMEM((rows, cols, channels), F32),
                pltpu.VMEM((6, cols + 16, channels), F32),
                pltpu.VMEM((cells, LANES), F32),
                pltpu.VMEM((cells, channels), BF16),
                pltpu.VMEM((channels, cells), BF16),
                pltpu.VMEM((cells, channels), BF16),
                pltpu.VMEM((channels, cells), BF16),
                pltpu.VMEM((cells, block), BF16),
                pltpu.VMEM((cells, channels), F32),
            ],
        ),
        out_shape=[
            jax.ShapeDtypeStruct((1, channels), F32),
            jax.ShapeDtypeStruct((cells, channels), BF16),
            jax.ShapeDtypeStruct((SUB, channels), F32),
            jax.ShapeDtypeStruct((cells, hidden), BF16),
            jax.ShapeDtypeStruct((1, hidden), F32),
            jax.ShapeDtypeStruct((2, turn) + grads, BF16),
            jax.ShapeDtypeStruct((turn,) + grads, BF16),
            jax.ShapeDtypeStruct((turn,) + grads, BF16),
        ],
        compiler_params=params(56),
        cost_estimate=estimate(20),
        name="expand",
    )(order, *given, w_in, b_in, w_out)


def project_kernel(act_ref, wo_ref, f_ref, cot_ref, m_ref, scale_ref, bo_ref, mixed_ref, sums_ref):
    cells, channels = f_ref.shape

    @pl.when(pl.program_id(0) == 0)
    def _():
        sums_ref[...] = jnp.zeros_like(sums_ref)

    branch = jnp.dot(act_ref[...], wo_ref[...], preferred_element_type=F32) + bo_ref[...]
    ocean = jnp.concatenate([m_ref[...].reshape(cells, LANES)] * (channels // LANES), axis=1) * branch
    mixed_ref[...] = (f_ref[...].astype(F32) + ocean * scale_ref[...]).astype(BF16)
    sums_ref[0:1, :] += jnp.sum(ocean * cot_ref[...].astype(F32), axis=0, keepdims=True)


def project(act, w_out, fields, cot, mask_b, scale, b_out):
    cells, hidden = act.shape
    channels = w_out.shape[1]
    part = 256

    def rows_of(width):
        return pl.BlockSpec((part, width), lambda i: (i, 0))

    return pl.pallas_call(
        project_kernel,
        grid=(cells // part,),
        out_shape=[
            jax.ShapeDtypeStruct((cells, channels), BF16),
            jax.ShapeDtypeStruct((SUB, channels), F32),
        ],
        in_specs=[
            rows_of(hidden),
            once(w_out.shape),
            rows_of(channels),
            rows_of(channels),
            pl.BlockSpec((part // mask_b.shape[1],) + mask_b.shape[1:], lambda i: (i, 0, 0)),
            whole_spec(scale.shape),
            whole_spec(b_out.shape),
        ],
        out_specs=[rows_of(channels), whole_spec((SUB, channels))],
        compiler_params=params(56),
        cost_estimate=estimate(4),
        name="project",
    )(act, w_out, fields, cot, mask_b, scale, b_out)


def fill_window(window, center, left, right, top, bot):
    rows, cols, _ = center.shape
    window[3 : 3 + rows, 5:8, :] = left[...].astype(F32)
    window[3 : 3 + rows, 8 : 8 + cols, :] = center
    window[3 : 3 + rows, 8 + cols : 11 + cols, :] = right[...].astype(F32)
    window[0:3, 5 : 11 + cols, :] = top[...].astype(F32)
    window[3 + rows : 6 + rows, 5 : 11 + cols, :] = bot[...].astype(F32)


def filter_grad_kernel(
    f_ref, m_ref, l_ref, r_ref, t_ref, b_ref, d_ref, gsc_ref, sums_ref, gbo_ref, gbi_0, gbi_1, gbi_2, gbi_3,
    o_ref, window, grad,
):
    rows, cols, _ = f_ref.shape
    fill_window(window, f_ref[...].astype(F32) * m_ref[...], l_ref, r_ref, t_ref, b_ref)
    grad[...] = d_ref[...].astype(F32)
    for col_off in range(7):

        def band(index, sums):
            start = pl.multiple_of(index * 8, 8)
            sums = list(sums)
            held = {}
            for src in range(rows + 6):
                if src < rows:
                    held[src] = grad[src, pl.ds(start, SUB), :]
                cells = shifted(window, src, start, 5 + col_off)
                for row_off in range(7):
                    out = src - row_off
                    if 0 <= out < rows:
                        sums[row_off] = sums[row_off] + held[out] * cells
            return tuple(sums)

        start = tuple(jnp.zeros((SUB, LANES), F32) for _ in range(7))
        sums = lax.fori_loop(0, cols // 8, band, start)
        for row_off in range(7):
            o_ref[row_off, col_off : col_off + 1, :] = jnp.sum(sums[row_off], axis=0, keepdims=True)
    o_ref[7, 0:1, :] = gsc_ref[0:1, :]
    o_ref[7, 1:3, :] = sums_ref[0:2, :]
    o_ref[7, 3:4, :] = gbo_ref[...]
    for at, gbi_ref in enumerate((gbi_0, gbi_1, gbi_2, gbi_3)):
        o_ref[7, 4 + at : 5 + at, :] = gbi_ref[...]
    for row_off in range(7):
        o_ref[row_off, 7:8, :] = jnp.zeros((1, LANES), F32)


def filter_grad(fields, mask_b, left, right, top, bot, d_conv, gsc, sums, gbo, gbi):
    rows, cols, channels = fields.shape

    def part(x):
        return by_channels(x.shape)

    return pl.pallas_call(
        filter_grad_kernel,
        grid=(channels // LANES,),
        out_shape=jax.ShapeDtypeStruct((8, 8, channels), F32),
        in_specs=[
            part(fields),
            whole_spec(mask_b.shape),
            part(left),
            part(right),
            part(top),
            part(bot),
            part(d_conv),
            part(gsc),
            part(sums),
            part(gbo),
        ]
        + [by_channels(gbi.shape, at * (channels // LANES)) for at in range(4)],
        out_specs=by_channels((8, 8, channels)),
        scratch_shapes=[
            pltpu.VMEM((rows + 6, cols + 16, LANES), F32),
            pltpu.VMEM((rows, cols, LANES), F32),
        ],
        compiler_params=params(56),
        cost_estimate=estimate(4),
        name="filter_grad",
    )(fields, mask_b, left, right, top, bot, d_conv, gsc, sums, gbo, gbi, gbi, gbi, gbi)


def input_grad_kernel(d_ref, l_ref, r_ref, t_ref, b_ref, k_ref, m_ref, cot_ref, o_ref, window, grad):
    rows, cols, _ = d_ref.shape
    fill_window(window, d_ref[...].astype(F32), l_ref, r_ref, t_ref, b_ref)
    for start in range(0, cols, 8):
        sums = band_conv(window, k_ref, start, rows, 3, True)
        for row in range(rows):
            grad[row, start : start + 8, :] = sums[row]
    o_ref[...] = (cot_ref[...].astype(F32) + m_ref[...] * grad[...]).astype(BF16)


def input_grad_more_kernel(d_ref, l_ref, r_ref, t_ref, b_ref, k_ref, m_ref, cot_ref, old_ref, o_ref, window, grad):
    input_grad_kernel(d_ref, l_ref, r_ref, t_ref, b_ref, k_ref, m_ref, cot_ref, o_ref, window, grad)


def input_grad(d_conv, left, right, top, bot, kernel, mask_b, cot, blocks, first, old=None):
    rows, cols, channels = d_conv.shape

    def part(x):
        return by_channels(x.shape, first)

    more = [] if old is None else [old]
    return pl.pallas_call(
        input_grad_kernel if old is None else input_grad_more_kernel,
        grid=(blocks,),
        out_shape=jax.ShapeDtypeStruct((rows, cols, channels), BF16),
        in_specs=[
            part(d_conv),
            part(left),
            part(right),
            part(top),
            part(bot),
            part(kernel),
            whole_spec(mask_b.shape),
            part(cot),
        ]
        + [UNUSED] * len(more),
        out_specs=part(d_conv),
        scratch_shapes=[
            pltpu.VMEM((rows + 6, cols + 16, LANES), F32),
            pltpu.VMEM((rows, cols, LANES), F32),
        ],
        input_output_aliases={} if old is None else {8: 0},
        compiler_params=params(56),
        cost_estimate=estimate(4),
        name="input_grad",
    )(d_conv, left, right, top, bot, kernel, mask_b, cot, *more)


def swap(values, axis, bit):
    count = lax.axis_size(axis)
    return lax.ppermute(values, axis, [(i, i ^ bit) for i in range(count)])


def bits_of(axis):
    return [1 << k for k in range(int(math.log2(lax.axis_size(axis))))]


def after(value, *others):
    return lax.optimization_barrier((value,) + others)[0]


def halves(values, axis, dim, bit):
    mine = (lax.axis_index(axis) // bit) % 2
    shape = values.shape
    paired = values.reshape(shape[:dim] + (shape[dim] // 2, 2) + shape[dim + 1 :])
    kept = lax.dynamic_index_in_dim(paired, mine, dim + 1, keepdims=False)
    sent = lax.dynamic_index_in_dim(paired, 1 - mine, dim + 1, keepdims=False)
    return kept, sent.astype(BF16)


def side_halo(last, first):
    count = lax.axis_size("lon")
    ahead = [(i, (i + 1) % count) for i in range(count)]
    back = [((i + 1) % count, i) for i in range(count)]
    return lax.ppermute(last, "lon", ahead), lax.ppermute(first, "lon", back)


def end_rows(head, tail, left, right):
    rows = left.shape[0]
    return (
        jnp.concatenate([left[rows - 3 :], tail, right[rows - 3 :]], axis=1),
        jnp.concatenate([left[:3], head, right[:3]], axis=1),
    )


def end_halo(tail, head):
    count = lax.axis_size("lat")
    ahead = [(i, i + 1) for i in range(count - 1)]
    back = [(i + 1, i) for i in range(count - 1)]
    return lax.ppermute(tail, "lat", ahead), lax.ppermute(head, "lat", back)


def per_device(
    fields,
    land_mask,
    cotangent,
    kernel,
    layer_norm_gain,
    layer_norm_bias,
    w_in,
    b_in,
    w_out,
    b_out,
    layer_scale,
):
    rows, cols, channels = fields.shape
    cells = rows * cols
    hidden = w_in.shape[1]
    n_lon, n_lat = lax.axis_size("lon"), lax.axis_size("lat")
    gain, bias = layer_norm_gain.reshape(1, -1), layer_norm_bias.reshape(1, -1)
    scale = layer_scale.reshape(1, -1)
    mask_b = jnp.broadcast_to(land_mask.astype(F32)[:, :, None], (rows, cols, LANES))
    cot_rows = cotangent.reshape(cells, channels)
    ocean = land_mask.astype(BF16)[:, :, None]
    left, right = side_halo(fields[:, cols - 3 :] * ocean[:, cols - 3 :], fields[:, :3] * ocean[:, :3])
    inner, head, tail = conv_inner(fields, mask_b, kernel)
    top, bot = end_halo(*end_rows(head, tail, left, right))
    side = conv_side(fields, mask_b, kernel, left, right)

    lon = lax.axis_index("lon")
    core, side_y = lon % 2, (lon // 2) % 2
    quads = 4 * jnp.arange(n_lon // 4, dtype=jnp.int32)
    order = jnp.concatenate(
        [quads + 2 * y + c for c in (1 - core, core) for y in (1 - side_y, side_y)]
    )
    g_bo, d_conv, sums, act, g_bi, sent, kept_wo, kept_wi = expand(
        order, inner, side, top, bot, kernel, gain, bias, scale, mask_b, cot_rows,
        w_in, b_in.reshape(1, -1), w_out, n_lon, n_lat,
    )
    got = swap(sent, "lon", 1)
    d_conv = d_conv.reshape(rows, cols, channels)
    d_last, d_first = d_conv[:, cols - 3 :], d_conv[:, :3]
    d_left, d_right = side_halo(d_last, d_first)
    mixed, g_scale = project(
        after(act, d_last, d_first), w_out, fields.reshape(cells, channels), cot_rows, mask_b, scale,
        b_out.reshape(1, -1),
    )
    d_tail, d_head = end_rows(
        d_conv[:3], d_conv[rows - 3 :], after(d_left, mixed), after(d_right, mixed)
    )
    d_top, d_bot = end_halo(d_tail, d_head)
    got = after(got, mixed)
    far = n_lon // 4
    kept = (kept_wo, kept_wi)
    far_sums = [(kept[i][:far].astype(F32) + got[i, :far].astype(F32)).astype(BF16) for i in range(2)]
    got_far = [swap(x, "lon", 2) for x in far_sums]

    steps = [("lon", 0, bit) for bit in bits_of("lon")[2:]] + [("lat", 1, bit) for bit in bits_of("lat")]
    owned, cut = [None, None], [None, None]

    def begin(index, last):
        both = after(kept[index], last)[far:].astype(F32) + after(got, last)[index, far:].astype(F32)
        x = both + after(got_far[index], last).astype(F32)
        if x.shape[1] != n_lat:
            x = x.reshape(n_lon // 4, channels, n_lat, -1).transpose(0, 2, 1, 3)
        cut[index] = halves(x, *steps[0])

    def advance(index, step, last):
        axis, dim, bit = steps[step]
        kept, sent = cut[index]
        owned[index] = after(kept, last) + after(swap(sent, axis, bit), last).astype(F32)
        if step + 1 < len(steps):
            cut[index] = halves(owned[index], *steps[step + 1])

    hops = [(axis, bit) for axis in ("lon", "lat") for bit in bits_of(axis)]

    def spread(hop, last):
        return after(small, last) + after(swap(small, *hops[hop]), last)

    small = filter_grad(
        after(fields, d_tail, d_head, *far_sums), mask_b, left, right, top, bot, d_conv,
        g_scale, sums, g_bo, g_bi,
    )
    begin(0, small)
    for step in range(len(steps) - 2):
        advance(0, step, small)
    half = channels // LANES // 2
    back = (d_left, d_right, d_top, d_bot, kernel, mask_b, cotangent)
    grad_fields = input_grad(after(d_conv, small, cut[0][1]), *back, half, 0)
    small = spread(0, grad_fields)
    advance(0, len(steps) - 2, grad_fields)
    begin(1, grad_fields)
    for step in range(len(steps) - 2):
        advance(1, step, grad_fields)
    grad_fields = input_grad(
        after(d_conv, small, cut[0][1], cut[1][1]), *back, half // 2, half, grad_fields
    )
    small = spread(1, grad_fields)
    advance(0, len(steps) - 1, grad_fields)
    advance(1, len(steps) - 2, grad_fields)
    grad_fields = input_grad(
        after(d_conv, small, cut[1][1]), *back, half // 2, half + half // 2, grad_fields
    )
    for hop in range(2, len(hops)):
        small = spread(hop, grad_fields)
    advance(1, len(steps) - 1, grad_fields)
    return (
        mixed.reshape(rows, cols, channels),
        grad_fields,
        small[:7, :7],
        small[7, 1],
        small[7, 2],
        owned[1][0, 0],
        small[7, 4:].reshape(hidden),
        owned[0][0, 0].T,
        small[7, 3],
        small[7, 0],
    )


def solution(mesh):
    placed = (
        P(("grp", "lat"), "lon", None),
        P(("grp", "lat"), "lon"),
        P(("grp", "lat"), "lon", None),
        P(),
        P(),
        P(),
        P(),
        P(),
        P(),
        P(),
        P(),
    )
    return jax.shard_map(
        per_device,
        mesh=mesh,
        in_specs=placed,
        out_specs=(
            P(("grp", "lat"), "lon", None),
            P(("grp", "lat"), "lon", None),
            P("grp", None, None),
            P("grp"),
            P("grp"),
            P("grp", ("lon", "lat")),
            P("grp"),
            P(("lon", "lat"), "grp"),
            P("grp"),
            P("grp"),
        ),
        check_vma=False,
    )
```

```python
import functools
import math

import jax
import jax.numpy as jnp
from jax import lax
from jax.experimental import pallas as pl
from jax.experimental.pallas import tpu as pltpu
from jax.sharding import PartitionSpec as P

F32 = jnp.float32
BF16 = jnp.bfloat16
LANES = 128
SUB = 8


def params(mib):
    return pltpu.CompilerParams(vmem_limit_bytes=mib * 1024 * 1024)


def estimate(micros):
    return pl.CostEstimate(
        flops=int(micros * 1.15e9), bytes_accessed=int(micros * 3.6e6), transcendentals=0
    )


def once(shape):
    zeros = (0,) * len(shape)
    return pl.BlockSpec(shape, lambda *_: zeros, pipeline_mode=pl.Buffered(1))


UNUSED = pl.BlockSpec(memory_space=pl.ANY)


def whole_spec(shape):
    zeros = (0,) * len(shape)
    return pl.BlockSpec(shape, lambda *_: zeros)


def shifted(window, row, start, offset):
    if offset % SUB == 0:
        return window[row, pl.ds(start + offset, SUB), :]
    base = start + offset // SUB * SUB
    pair = window[row, pl.ds(base, 2 * SUB), :]
    return pltpu.roll(pair, 2 * SUB - offset % SUB, axis=0)[:SUB]


def tap_rows(k_ref, col_off, flip):
    at = 6 - col_off if flip else col_off
    rows = [k_ref[6 - p if flip else p, at : at + 1, :] for p in range(7)]
    return [jnp.broadcast_to(row, (SUB, LANES)) for row in rows]


def band_conv(window, k_ref, start, rows, pad, flip):
    sums = [None] * rows
    for col_off in range(7):
        weights = tap_rows(k_ref, col_off, flip)
        for src in range(window.shape[0]):
            hits = [(src - pad - row_off + 3, row_off) for row_off in range(7)]
            hits = [(out, row_off) for out, row_off in hits if 0 <= out < rows]
            if not hits:
                continue
            cells = shifted(window, src, start, 5 + col_off)
            for out, row_off in hits:
                term = weights[row_off] * cells
                sums[out] = term if sums[out] is None else sums[out] + term
    return sums


def mask_column(m_ref, row, start, count):
    line = m_ref[pl.ds(row, 1), :].astype(F32)
    spot = lax.broadcasted_iota(jnp.int32, (count, line.shape[1]), 1)
    want = lax.broadcasted_iota(jnp.int32, (count, line.shape[1]), 0) + start
    return jnp.sum(jnp.where(spot == want, line, 0.0), axis=1, keepdims=True)


def spread_mask(m_ref, wide):
    @pl.when(pl.program_id(0) == 0)
    def _():
        rows, cols, _ = wide.shape

        def one(row, _):
            column = mask_column(m_ref, row, 0, cols)
            wide[pl.ds(row, 1)] = jnp.broadcast_to(column, (cols, LANES))[None]
            return 0

        lax.fori_loop(0, rows, one, 0)


def conv_inner_kernel(f_ref, m_ref, k_ref, o_ref, head_ref, tail_ref, window, wide):
    rows, cols, _ = f_ref.shape
    spread_mask(m_ref, wide)
    masked = f_ref[...].astype(F32) * wide[...]
    window[:, 8 : 8 + cols, :] = masked
    head_ref[...] = masked[:3].astype(BF16)
    tail_ref[...] = masked[rows - 3 :].astype(BF16)
    for start in range(8, cols - 8, 8):
        sums = band_conv(window, k_ref, start, rows, 0, False)
        for row in range(rows):
            o_ref[row, start - 8 : start, :] = sums[row]


def conv_side_kernel(f_ref, m_ref, k_ref, l_ref, r_ref, o_ref, window, wide):
    rows, cols, _ = f_ref.shape
    spread_mask(m_ref, wide)
    window[:, 5:8, :] = l_ref[...].astype(F32)
    window[:, 8 : 8 + cols, :] = f_ref[...].astype(F32) * wide[...]
    window[:, 8 + cols : 11 + cols, :] = r_ref[...].astype(F32)
    for at, start in ((0, 0), (8, cols - 8)):
        sums = band_conv(window, k_ref, start, rows, 0, False)
        for row in range(rows):
            o_ref[row, at : at + 8, :] = sums[row]


def by_channels(shape, first=0):
    return pl.BlockSpec(shape[:-1] + (LANES,), lambda c: (0,) * (len(shape) - 1) + (c + first,))


def conv_inner(fields, mask, kernel):
    rows, cols, channels = fields.shape
    ends = (3, cols, channels)
    return pl.pallas_call(
        conv_inner_kernel,
        grid=(channels // LANES,),
        out_shape=[
            jax.ShapeDtypeStruct((rows, cols - 16, channels), F32),
            jax.ShapeDtypeStruct(ends, BF16),
            jax.ShapeDtypeStruct(ends, BF16),
        ],
        in_specs=[by_channels(fields.shape), whole_spec(mask.shape), by_channels(kernel.shape)],
        out_specs=[by_channels((rows, cols - 16, channels)), by_channels(ends), by_channels(ends)],
        scratch_shapes=[
            pltpu.VMEM((rows, cols + 16, LANES), F32),
            pltpu.VMEM((rows, cols, LANES), F32),
        ],
        compiler_params=params(56),
        cost_estimate=estimate(4),
        name="conv_inner",
    )(fields, mask, kernel)


def conv_side(fields, mask, kernel, left, right):
    rows, cols, channels = fields.shape
    return pl.pallas_call(
        conv_side_kernel,
        grid=(channels // LANES,),
        out_shape=jax.ShapeDtypeStruct((rows, 16, channels), F32),
        in_specs=[
            by_channels(fields.shape),
            whole_spec(mask.shape),
            by_channels(kernel.shape),
            by_channels(left.shape),
            by_channels(right.shape),
        ],
        out_specs=by_channels((rows, 16, channels)),
        scratch_shapes=[
            pltpu.VMEM((rows, cols + 16, LANES), F32),
            pltpu.VMEM((rows, cols, LANES), F32),
        ],
        compiler_params=params(56),
        cost_estimate=estimate(4),
        name="conv_side",
    )(fields, mask, kernel, left, right)


def gelu_twice(x):
    root = math.sqrt(2.0 / math.pi)
    inner = root + (root * 0.044715) * (x * x)
    tanh = jnp.tanh(x * inner)
    both = 1.0 + tanh
    value = x * both
    slope = both + value * ((1.0 - tanh) * (3.0 * inner - 2.0 * root))
    return value, slope


def expand_kernel(
    order_ref,
    inner_ref, side_ref, top_ref, bot_ref, k_ref, gain_ref, bias_ref, scale_ref, bo_ref, m_ref, cot_ref, f_ref,
    wi_ref, bi_ref, wo_ref,
    dconv_ref, mixed_ref, sums_ref, gbi_ref, sent_ref, kept_ref,
    conv, halo, inv_s, normed, normed_t, dbr, dbr_t, act, dpre, d_normed, branch, pre_s, dact_s,
):
    rows, cols, channels = conv.shape
    cells = rows * cols
    strip = 16
    chunk = 128
    step_now = pl.program_id(0)
    wide = channels // LANES

    def strips(body):
        def one(row, _):
            for at in range(0, cols, strip):
                body(row, at, pl.ds(pl.multiple_of(row * cols + at, strip), strip))
            return 0

        lax.fori_loop(0, rows, one, 0)

    @pl.when(step_now == 0)
    def _():
        conv[:, 0:8, :] = side_ref[:, 0:8, :]
        conv[:, 8 : cols - 8, :] = inner_ref[...]
        conv[:, cols - 8 : cols, :] = side_ref[:, 8:16, :]
        halo[0:3, 5 : 11 + cols, :] = top_ref[...].astype(F32)
        halo[3:6, 5 : 11 + cols, :] = bot_ref[...].astype(F32)
        for block in range(wide):
            lanes = slice(block * LANES, (block + 1) * LANES)
            for start in range(0, cols, 8):
                outs = list(range(3)) + list(range(rows - 3, rows))
                sums = {out: conv[out, start : start + 8, lanes] for out in outs}
                for col_off in range(7):
                    for src in range(6):
                        lat = src - 3 if src < 3 else rows + src - 3
                        offset = (5 + col_off) % SUB
                        base = start + (5 + col_off) // SUB * SUB
                        pair = halo[src, base : base + 2 * SUB, lanes]
                        cell = pltpu.roll(pair, 2 * SUB - offset, axis=0)[:SUB] if offset else pair[:SUB]
                        for out in outs:
                            row_off = lat - out + 3
                            if 0 <= row_off < 7:
                                tap = k_ref[row_off, col_off : col_off + 1, lanes]
                                sums[out] = sums[out] + tap * cell
                for out in outs:
                    conv[out, start : start + 8, lanes] = sums[out]
        sums_ref[...] = jnp.zeros_like(sums_ref)

        def standardize(row, at, here):
            x = conv[row, at : at + strip, :]
            mean = jnp.mean(x, axis=-1, keepdims=True)
            centered = x - mean
            var = jnp.mean(centered * centered, axis=-1, keepdims=True)
            inv = lax.rsqrt(var + 1e-06)
            xhat = centered * inv
            conv[row, at : at + strip, :] = xhat
            inv_s[here, :] = jnp.broadcast_to(inv, (strip, LANES))
            normed[here, :] = (xhat * gain_ref[...] + bias_ref[...]).astype(BF16)
            grad = mask_column(m_ref, row, at, strip) * (scale_ref[...] * cot_ref[here, :].astype(F32))
            sums_ref[0] += grad[:SUB] + grad[SUB:]
            dbr[here, :] = (0.5 * grad).astype(BF16)

        strips(standardize)
        for at in range(0, cells, chunk):
            here = slice(at, at + chunk)
            normed_t[:, here] = normed[here, :].T
            dbr_t[:, here] = dbr[here, :].T

    part = 256
    count = cells // part
    block = act.shape[1]
    cut = min(block, 256)

    def products(index):
        here = slice(index * part, (index + 1) * part)
        pre_s[index % 2] = jnp.dot(normed[here, :], wi_ref[...], preferred_element_type=F32)
        dact_s[index % 2] = lax.dot_general(
            dbr[here, :], wo_ref[...], (((1,), (1,)), ((), ())), preferred_element_type=F32
        )

    first_block = step_now == 0

    def project(index):
        here = slice(index * part, (index + 1) * part)
        branch[here, :] = jnp.where(first_block, 0.0, branch[here, :]) + jnp.dot(
            act[here, :], wo_ref[...], preferred_element_type=F32
        )
        d_normed[here, :] = jnp.where(first_block, 0.0, d_normed[here, :]) + lax.dot_general(
            dpre[here, :], wi_ref[...], (((1,), (1,)), ((), ())), preferred_element_type=F32
        )

    totals = [jnp.zeros((SUB, cut), F32) for _ in range(0, block, cut)]
    products(0)
    for index in range(count):
        if index + 1 < count:
            products(index + 1)
        for at in range(0, part, strip):
            here = slice(index * part + at, index * part + at + strip)
            for which, left in enumerate(range(0, block, cut)):
                lanes = slice(left, left + cut)
                x = pre_s[index % 2, at : at + strip, lanes] + bi_ref[:, lanes]
                value, slope = gelu_twice(x)
                act[here, lanes] = value.astype(BF16)
                d_pre = dact_s[index % 2, at : at + strip, lanes] * slope
                dpre[here, lanes] = d_pre.astype(BF16)
                totals[which] = totals[which] + (d_pre[:SUB] + d_pre[SUB:])
        if index > 0:
            project(index - 1)
    project(count - 1)
    for which, left in enumerate(range(0, block, cut)):
        gbi_ref[:, left : left + cut] = jnp.sum(totals[which], axis=0, keepdims=True)
    _, parts, _, width = sent_ref.shape
    is_sent = step_now < pl.num_programs(0) // 2
    for index, (rows_t, source) in enumerate(((dbr_t, act), (normed_t, dpre))):
        for left in range(0, block, cut):
            grad = jnp.dot(
                rows_t[...], source[:, left : left + cut], preferred_element_type=F32
            ).astype(BF16)

            def store(ref):
                for at in range(0, cut, min(width, cut)):
                    lat, into = divmod(left + at, width)
                    size = min(width, cut)
                    ref[index, lat, :, into : into + size] = grad[:, at : at + size]

            pl.when(is_sent)(functools.partial(store, sent_ref))
            pl.when(jnp.logical_not(is_sent))(functools.partial(store, kept_ref))

    @pl.when(step_now == pl.num_programs(0) - 1)
    def _():
        def norm_back(row, at, here):
            cot = cot_ref[here, :].astype(F32)
            ocean = mask_column(m_ref, row, at, strip) * (0.5 * branch[here, :] + bo_ref[...])
            mixed_ref[here, :] = (f_ref[here, :].astype(F32) + ocean * scale_ref[...]).astype(BF16)
            term = ocean * cot
            sums_ref[1] += term[:SUB] + term[SUB:]
            grad = d_normed[here, :]
            xhat = conv[row, at : at + strip, :]
            term = grad * xhat
            sums_ref[2] += term[:SUB] + term[SUB:]
            sums_ref[3] += grad[:SUB] + grad[SUB:]
            e = grad * gain_ref[...]
            m1 = jnp.mean(e, axis=-1, keepdims=True)
            m2 = jnp.mean(term * gain_ref[...], axis=-1, keepdims=True)
            inv = jnp.concatenate([inv_s[here, :]] * wide, axis=1)
            dconv_ref[here, :] = (inv * (e - m1 - xhat * m2)).astype(BF16)

        strips(norm_back)


def expand(
    order, inner, side, top, bot, kernel, gain, bias, scale, b_out, mask, cot, fields, w_in, b_in, w_out, n_lon, n_lat
):
    rows, _, channels = inner.shape
    hidden = w_in.shape[1]
    cells, _ = cot.shape
    cols = cells // rows
    block = hidden // n_lon
    split = n_lat if (block // n_lat) % LANES == 0 else 1
    turn = n_lon // 2
    grads = (split, channels, block // split)
    given = (inner, side, top, bot, kernel, gain, bias, scale, b_out, mask, cot, fields)

    def sent_at(h, order):
        return (0, jnp.minimum(h, turn - 1), 0, 0, 0)

    def kept_at(h, order):
        return (0, jnp.maximum(h - turn, 0), 0, 0, 0)

    return pl.pallas_call(
        expand_kernel,
        grid_spec=pltpu.PrefetchScalarGridSpec(
            num_scalar_prefetch=1,
            grid=(n_lon,),
            in_specs=[once(x.shape) for x in given]
            + [
                pl.BlockSpec((channels, block), lambda h, order: (0, order[h])),
                pl.BlockSpec((1, block), lambda h, order: (0, order[h])),
                pl.BlockSpec((block, channels), lambda h, order: (order[h], 0)),
            ],
            out_specs=[
                once((cells, channels)),
                once((cells, channels)),
                once((4, SUB, channels)),
                pl.BlockSpec((1, block), lambda h, order: (0, order[h])),
                pl.BlockSpec((2, None) + grads, sent_at),
                pl.BlockSpec((2, None) + grads, kept_at),
            ],
            scratch_shapes=[
                pltpu.VMEM((rows, cols, channels), F32),
                pltpu.VMEM((6, cols + 16, channels), F32),
                pltpu.VMEM((cells, LANES), F32),
                pltpu.VMEM((cells, channels), BF16),
                pltpu.VMEM((channels, cells), BF16),
                pltpu.VMEM((cells, channels), BF16),
                pltpu.VMEM((channels, cells), BF16),
                pltpu.VMEM((cells, block), BF16),
                pltpu.VMEM((cells, block), BF16),
                pltpu.VMEM((cells, channels), F32),
                pltpu.VMEM((cells, channels), F32),
                pltpu.VMEM((2, 256, block), F32),
                pltpu.VMEM((2, 256, block), F32),
            ],
        ),
        out_shape=[
            jax.ShapeDtypeStruct((cells, channels), BF16),
            jax.ShapeDtypeStruct((cells, channels), BF16),
            jax.ShapeDtypeStruct((4, SUB, channels), F32),
            jax.ShapeDtypeStruct((1, hidden), F32),
            jax.ShapeDtypeStruct((2, turn) + grads, BF16),
            jax.ShapeDtypeStruct((2, turn) + grads, BF16),
        ],
        compiler_params=params(56),
        cost_estimate=estimate(20),
        name="expand",
    )(order, *given, w_in, b_in, w_out)


def fill_window(window, center, left, right, top, bot):
    rows, cols, _ = center.shape
    window[3 : 3 + rows, 5:8, :] = left[...].astype(F32)
    window[3 : 3 + rows, 8 : 8 + cols, :] = center
    window[3 : 3 + rows, 8 + cols : 11 + cols, :] = right[...].astype(F32)
    window[0:3, 5 : 11 + cols, :] = top[...].astype(F32)
    window[3 + rows : 6 + rows, 5 : 11 + cols, :] = bot[...].astype(F32)


def filter_grad_kernel(
    f_ref, m_ref, l_ref, r_ref, t_ref, b_ref, d_ref, sums_ref, gbi_0, gbi_1, gbi_2, gbi_3,
    o_ref, window, grad, wide,
):
    rows, cols, _ = f_ref.shape
    spread_mask(m_ref, wide)
    fill_window(window, f_ref[...].astype(F32) * wide[...], l_ref, r_ref, t_ref, b_ref)
    grad[...] = d_ref[...].astype(F32)
    for col_off in range(7):

        def band(index, sums):
            start = pl.multiple_of(index * 8, 8)
            sums = list(sums)
            held = {}
            for src in range(rows + 6):
                if src < rows:
                    held[src] = grad[src, pl.ds(start, SUB), :]
                cells = shifted(window, src, start, 5 + col_off)
                for row_off in range(7):
                    out = src - row_off
                    if 0 <= out < rows:
                        sums[row_off] = sums[row_off] + held[out] * cells
            return tuple(sums)

        start = tuple(jnp.zeros((SUB, LANES), F32) for _ in range(7))
        sums = lax.fori_loop(0, cols // 8, band, start)
        for row_off in range(7):
            o_ref[row_off, col_off : col_off + 1, :] = jnp.sum(sums[row_off], axis=0, keepdims=True)
    for at, source in enumerate((1, 2, 3, 0)):
        o_ref[7, at : at + 1, :] = jnp.sum(sums_ref[source], axis=0, keepdims=True)
    for at, gbi_ref in enumerate((gbi_0, gbi_1, gbi_2, gbi_3)):
        o_ref[7, 4 + at : 5 + at, :] = gbi_ref[...]
    for row_off in range(7):
        o_ref[row_off, 7:8, :] = jnp.zeros((1, LANES), F32)


def filter_grad(fields, mask, left, right, top, bot, d_conv, sums, gbi):
    rows, cols, channels = fields.shape

    def part(x):
        return by_channels(x.shape)

    return pl.pallas_call(
        filter_grad_kernel,
        grid=(channels // LANES,),
        out_shape=jax.ShapeDtypeStruct((8, 8, channels), F32),
        in_specs=[
            part(fields),
            whole_spec(mask.shape),
            part(left),
            part(right),
            part(top),
            part(bot),
            part(d_conv),
            part(sums),
        ]
        + [by_channels(gbi.shape, at * (channels // LANES)) for at in range(4)],
        out_specs=by_channels((8, 8, channels)),
        scratch_shapes=[
            pltpu.VMEM((rows + 6, cols + 16, LANES), F32),
            pltpu.VMEM((rows, cols, LANES), F32),
            pltpu.VMEM((rows, cols, LANES), F32),
        ],
        compiler_params=params(56),
        cost_estimate=estimate(4),
        name="filter_grad",
    )(fields, mask, left, right, top, bot, d_conv, sums, gbi, gbi, gbi, gbi)


def input_grad_kernel(d_ref, l_ref, r_ref, t_ref, b_ref, k_ref, m_ref, cot_ref, o_ref, window, grad, wide):
    rows, cols, _ = d_ref.shape
    spread_mask(m_ref, wide)
    fill_window(window, d_ref[...].astype(F32), l_ref, r_ref, t_ref, b_ref)
    for start in range(0, cols, 8):
        sums = band_conv(window, k_ref, start, rows, 3, True)
        for row in range(rows):
            grad[row, start : start + 8, :] = sums[row]
    o_ref[...] = (cot_ref[...].astype(F32) + wide[...] * grad[...]).astype(BF16)


def input_grad_more_kernel(d_ref, l_ref, r_ref, t_ref, b_ref, k_ref, m_ref, cot_ref, old_ref, o_ref, window, grad, wide):
    input_grad_kernel(d_ref, l_ref, r_ref, t_ref, b_ref, k_ref, m_ref, cot_ref, o_ref, window, grad, wide)


def input_grad(d_conv, left, right, top, bot, kernel, mask, cot, blocks, first, old=None):
    rows, cols, channels = d_conv.shape

    def part(x):
        return by_channels(x.shape, first)

    more = [] if old is None else [old]
    return pl.pallas_call(
        input_grad_kernel if old is None else input_grad_more_kernel,
        grid=(blocks,),
        out_shape=jax.ShapeDtypeStruct((rows, cols, channels), BF16),
        in_specs=[
            part(d_conv),
            part(left),
            part(right),
            part(top),
            part(bot),
            part(kernel),
            whole_spec(mask.shape),
            part(cot),
        ]
        + [UNUSED] * len(more),
        out_specs=part(d_conv),
        scratch_shapes=[
            pltpu.VMEM((rows + 6, cols + 16, LANES), F32),
            pltpu.VMEM((rows, cols, LANES), F32),
            pltpu.VMEM((rows, cols, LANES), F32),
        ],
        input_output_aliases={} if old is None else {8: 0},
        compiler_params=params(56),
        cost_estimate=estimate(4),
        name="input_grad",
    )(d_conv, left, right, top, bot, kernel, mask, cot, *more)


def swap(values, axis, bit):
    count = lax.axis_size(axis)
    return lax.ppermute(values, axis, [(i, i ^ bit) for i in range(count)])


def bits_of(axis):
    return [1 << k for k in range(int(math.log2(lax.axis_size(axis))))]


def after(value, *others):
    return lax.optimization_barrier((value,) + others)[0]


def halves(values, axis, dim, bit):
    mine = (lax.axis_index(axis) // bit) % 2 == 1
    shape = values.shape
    paired = values.reshape(shape[:dim] + (shape[dim] // 2, 2) + shape[dim + 1 :])
    low = lax.index_in_dim(paired, 0, dim + 1, keepdims=False)
    high = lax.index_in_dim(paired, 1, dim + 1, keepdims=False)
    return jnp.where(mine, high, low), jnp.where(mine, low, high).astype(BF16)


def side_halo(last, first):
    count = lax.axis_size("lon")
    ahead = [(i, (i + 1) % count) for i in range(count)]
    back = [((i + 1) % count, i) for i in range(count)]
    return lax.ppermute(last, "lon", ahead), lax.ppermute(first, "lon", back)


def end_rows(head, tail, left, right):
    rows = left.shape[0]
    return (
        jnp.concatenate([left[rows - 3 :], tail, right[rows - 3 :]], axis=1),
        jnp.concatenate([left[:3], head, right[:3]], axis=1),
    )


def end_halo(tail, head):
    count = lax.axis_size("lat")
    ahead = [(i, i + 1) for i in range(count - 1)]
    back = [(i + 1, i) for i in range(count - 1)]
    return lax.ppermute(tail, "lat", ahead), lax.ppermute(head, "lat", back)


def per_device(
    fields,
    land_mask,
    cotangent,
    kernel,
    layer_norm_gain,
    layer_norm_bias,
    w_in,
    b_in,
    w_out,
    b_out,
    layer_scale,
):
    rows, cols, channels = fields.shape
    cells = rows * cols
    hidden = w_in.shape[1]
    n_lon, n_lat = lax.axis_size("lon"), lax.axis_size("lat")
    gain, bias = layer_norm_gain.reshape(1, -1), layer_norm_bias.reshape(1, -1)
    scale = layer_scale.reshape(1, -1)
    cot_rows = cotangent.reshape(cells, channels)
    ocean = land_mask.astype(BF16)[:, :, None]
    left, right = side_halo(fields[:, cols - 3 :] * ocean[:, cols - 3 :], fields[:, :3] * ocean[:, :3])
    inner, head, tail = conv_inner(fields, land_mask, kernel)
    top, bot = end_halo(*end_rows(head, tail, left, right))
    side = conv_side(fields, land_mask, kernel, left, right)

    lon = lax.axis_index("lon")
    core, side_y = lon % 2, (lon // 2) % 2
    quads = 4 * jnp.arange(n_lon // 4, dtype=jnp.int32)
    order = jnp.concatenate(
        [quads + 2 * y + c for c in (1 - core, core) for y in (1 - side_y, side_y)]
    )
    d_conv, mixed, sums, g_bi, sent, kept = expand(
        order, inner, side, top, bot, kernel, gain, bias, scale, b_out.reshape(1, -1), land_mask, cot_rows,
        fields.reshape(cells, channels), w_in, b_in.reshape(1, -1), w_out, n_lon, n_lat,
    )
    got = swap(sent, "lon", 1)
    d_conv = d_conv.reshape(rows, cols, channels)
    d_left, d_right = side_halo(d_conv[:, cols - 3 :], d_conv[:, :3])
    d_tail, d_head = end_rows(d_conv[:3], d_conv[rows - 3 :], d_left, d_right)
    d_top, d_bot = end_halo(d_tail, d_head)

    far = n_lon // 4
    border = channels * 5 // 8
    pieces = (slice(0, border), slice(border, channels))
    far_sums = [
        (kept[:, :far, :, piece].astype(F32) + got[:, :far, :, piece].astype(F32)).astype(BF16)
        for piece in pieces
    ]
    got_far = [swap(x, "lon", 2) for x in far_sums]
    steps = [("lon", 1, bit) for bit in bits_of("lon")[2:]] + [("lat", 2, bit) for bit in bits_of("lat")]
    owned, cut = [None, None], [None, None]

    def begin(index, last):
        here = pieces[index]
        x = after(kept, last)[:, far:, :, here].astype(F32) + after(got, last)[:, far:, :, here].astype(F32)
        x = x + after(got_far[index], last).astype(F32)
        if x.shape[2] != n_lat:
            x = x.reshape(2, far, x.shape[3], n_lat, -1).transpose(0, 1, 3, 2, 4)
        cut[index] = halves(x, *steps[0])

    def advance(index, step, last):
        axis, dim, bit = steps[step]
        mine, sent = cut[index]
        owned[index] = after(mine, last) + after(swap(sent, axis, bit), last).astype(F32)
        if step + 1 < len(steps):
            cut[index] = halves(owned[index], *steps[step + 1])

    hops = [(axis, bit) for axis in ("lon", "lat") for bit in bits_of(axis)]

    def spread(hop, last):
        return after(small, last) + after(swap(small, *hops[hop]), last)

    small = filter_grad(
        after(fields, d_tail, d_head, far_sums[0]), land_mask, left, right, top, bot, d_conv, sums, g_bi
    )
    begin(0, small)
    for step in range(len(steps) - 2):
        advance(0, step, small)
    half = channels // LANES // 2
    back = (d_left, d_right, d_top, d_bot, kernel, land_mask, cotangent)
    grad_fields = input_grad(after(d_conv, small, cut[0][1], far_sums[1]), *back, half, 0)
    small = spread(0, grad_fields)
    advance(0, len(steps) - 2, grad_fields)
    begin(1, grad_fields)
    for step in range(len(steps) - 2):
        advance(1, step, grad_fields)
    grad_fields = input_grad(
        after(d_conv, small, cut[0][1], cut[1][1]), *back, half // 2, half, grad_fields
    )
    small = spread(1, grad_fields)
    advance(0, len(steps) - 1, grad_fields)
    advance(1, len(steps) - 2, grad_fields)
    grad_fields = input_grad(
        after(d_conv, small, cut[1][1]), *back, half // 2, half + half // 2, grad_fields
    )
    for hop in range(2, len(hops)):
        small = spread(hop, grad_fields)
    advance(1, len(steps) - 1, grad_fields)
    grad_w = jnp.concatenate([x[:, 0, 0] for x in owned], axis=1)
    return (
        mixed.reshape(rows, cols, channels),
        grad_fields,
        small[:7, :7],
        small[7, 1],
        small[7, 2],
        grad_w[1],
        small[7, 4:].reshape(hidden),
        grad_w[0].T,
        small[7, 3],
        small[7, 0],
    )


def solution(mesh):
    placed = (
        P(("grp", "lat"), "lon", None),
        P(("grp", "lat"), "lon"),
        P(("grp", "lat"), "lon", None),
        P(),
        P(),
        P(),
        P(),
        P(),
        P(),
        P(),
        P(),
    )
    return jax.shard_map(
        per_device,
        mesh=mesh,
        in_specs=placed,
        out_specs=(
            P(("grp", "lat"), "lon", None),
            P(("grp", "lat"), "lon", None),
            P("grp", None, None),
            P("grp"),
            P("grp"),
            P("grp", ("lon", "lat")),
            P("grp"),
            P(("lon", "lat"), "grp"),
            P("grp"),
            P("grp"),
        ),
        check_vma=False,
    )
```

```python
import functools
import math

import jax
import jax.numpy as jnp
from jax import lax
from jax.experimental import pallas as pl
from jax.experimental.pallas import tpu as pltpu
from jax.sharding import PartitionSpec as P

F32 = jnp.float32
BF16 = jnp.bfloat16
LANES = 128
SUB = 8


def params(mib):
    return pltpu.CompilerParams(vmem_limit_bytes=mib * 1024 * 1024)


def estimate(micros):
    return pl.CostEstimate(
        flops=int(micros * 1.15e9), bytes_accessed=int(micros * 3.6e6), transcendentals=0
    )


def once(shape):
    zeros = (0,) * len(shape)
    return pl.BlockSpec(shape, lambda *_: zeros, pipeline_mode=pl.Buffered(1))


UNUSED = pl.BlockSpec(memory_space=pl.ANY)


def whole_spec(shape):
    zeros = (0,) * len(shape)
    return pl.BlockSpec(shape, lambda *_: zeros)


def shifted(window, row, start, offset):
    if offset % SUB == 0:
        return window[row, pl.ds(start + offset, SUB), :]
    base = start + offset // SUB * SUB
    pair = window[row, pl.ds(base, 2 * SUB), :]
    return pltpu.roll(pair, 2 * SUB - offset % SUB, axis=0)[:SUB]


def tap_rows(k_ref, col_off, flip):
    at = 6 - col_off if flip else col_off
    rows = [k_ref[6 - p if flip else p, at : at + 1, :] for p in range(7)]
    return [jnp.broadcast_to(row, (SUB, LANES)) for row in rows]


def band_conv(window, k_ref, o_ref, start, into, pad, flip):
    rows = o_ref.shape[0]
    bound = window.shape[0]
    part = 16
    for top in range(0, rows, part):
        sums = {}
        for col_off in range(7):
            weights = tap_rows(k_ref, col_off, flip)
            sources = range(max(0, top + pad - 3), min(bound, top + pad + part + 3))
            cells = {src: shifted(window, src, start, 5 + col_off) for src in sources}
            for row_off in range(7):
                for out in range(top, top + part):
                    src = out + pad + row_off - 3
                    if src in cells:
                        term = weights[row_off] * cells[src]
                        sums[out] = sums[out] + term if out in sums else term
        for out in range(top, top + part):
            o_ref[out, into : into + SUB, :] = sums[out]


def conv_inner_kernel(f_ref, m_ref, k_ref, o_ref, head_ref, tail_ref, window):
    rows, cols, _ = f_ref.shape
    masked = f_ref[...].astype(F32) * m_ref[...]
    window[:, 8 : 8 + cols, :] = masked
    head_ref[...] = masked[:3].astype(BF16)
    tail_ref[...] = masked[rows - 3 :].astype(BF16)
    for start in range(8, cols - 8, 8):
        band_conv(window, k_ref, o_ref, start, start - 8, 0, False)


def conv_side_kernel(f_ref, m_ref, k_ref, l_ref, r_ref, o_ref, window):
    rows, cols, _ = f_ref.shape
    window[:, 5:8, :] = l_ref[...].astype(F32)
    window[:, 8 : 8 + cols, :] = f_ref[...].astype(F32) * m_ref[...]
    window[:, 8 + cols : 11 + cols, :] = r_ref[...].astype(F32)
    for at, start in ((0, 0), (8, cols - 8)):
        band_conv(window, k_ref, o_ref, start, at, 0, False)


def by_channels(shape, first=0):
    return pl.BlockSpec(shape[:-1] + (LANES,), lambda c: (0,) * (len(shape) - 1) + (c + first,))


def conv_inner(fields, mask, kernel):
    rows, cols, channels = fields.shape
    ends = (3, cols, channels)
    return pl.pallas_call(
        conv_inner_kernel,
        grid=(channels // LANES,),
        out_shape=[
            jax.ShapeDtypeStruct((rows, cols - 16, channels), F32),
            jax.ShapeDtypeStruct(ends, BF16),
            jax.ShapeDtypeStruct(ends, BF16),
        ],
        in_specs=[by_channels(fields.shape), whole_spec(mask.shape), by_channels(kernel.shape)],
        out_specs=[by_channels((rows, cols - 16, channels)), by_channels(ends), by_channels(ends)],
        scratch_shapes=[pltpu.VMEM((rows, cols + 16, LANES), F32)],
        compiler_params=params(56),
        cost_estimate=estimate(4),
        name="conv_inner",
    )(fields, mask, kernel)


def conv_side(fields, mask, kernel, left, right):
    rows, cols, channels = fields.shape
    return pl.pallas_call(
        conv_side_kernel,
        grid=(channels // LANES,),
        out_shape=jax.ShapeDtypeStruct((rows, 16, channels), F32),
        in_specs=[
            by_channels(fields.shape),
            whole_spec(mask.shape),
            by_channels(kernel.shape),
            by_channels(left.shape),
            by_channels(right.shape),
        ],
        out_specs=by_channels((rows, 16, channels)),
        scratch_shapes=[pltpu.VMEM((rows, cols + 16, LANES), F32)],
        compiler_params=params(56),
        cost_estimate=estimate(4),
        name="conv_side",
    )(fields, mask, kernel, left, right)


def gelu_twice(x):
    root = math.sqrt(2.0 / math.pi)
    inner = root + (root * 0.044715) * (x * x)
    tanh = jnp.tanh(x * inner)
    both = 1.0 + tanh
    value = x * both
    slope = both + value * ((1.0 - tanh) * (3.0 * inner - 2.0 * root))
    return value, slope


def expand_kernel(
    order_ref,
    inner_ref, side_ref, top_ref, bot_ref, k_ref, gain_ref, bias_ref, scale_ref, bo_ref, m_ref, cot_ref, f_ref,
    wi_ref, bi_ref, wo_ref,
    dconv_ref, mixed_ref, sums_ref, gbi_ref, sent_ref, kept_ref,
    conv, halo, inv_s, normed, normed_t, dbr, dbr_t, act, dpre, d_normed, branch, pre_s, dact_s,
):
    rows, cols, channels = conv.shape
    cells = rows * cols
    strip = 16
    chunk = 128
    step_now = pl.program_id(0)
    wide = channels // LANES

    def strips(body):
        def some(index, _):
            for more in range(4):
                row = index * 4 + more
                for at in range(0, cols, strip):
                    body(row, at, pl.ds(pl.multiple_of(row * cols + at, strip), strip))
            return 0

        lax.fori_loop(0, rows // 4, some, 0)

    @pl.when(step_now == 0)
    def _():
        conv[:, 0:8, :] = side_ref[:, 0:8, :]
        conv[:, 8 : cols - 8, :] = inner_ref[...]
        conv[:, cols - 8 : cols, :] = side_ref[:, 8:16, :]
        halo[0:3, 5 : 11 + cols, :] = top_ref[...].astype(F32)
        halo[3:6, 5 : 11 + cols, :] = bot_ref[...].astype(F32)
        for block in range(wide):
            lanes = slice(block * LANES, (block + 1) * LANES)
            for start in range(0, cols, 8):
                outs = list(range(3)) + list(range(rows - 3, rows))
                sums = {out: conv[out, start : start + 8, lanes] for out in outs}
                for col_off in range(7):
                    for src in range(6):
                        lat = src - 3 if src < 3 else rows + src - 3
                        offset = (5 + col_off) % SUB
                        base = start + (5 + col_off) // SUB * SUB
                        pair = halo[src, base : base + 2 * SUB, lanes]
                        cell = pltpu.roll(pair, 2 * SUB - offset, axis=0)[:SUB] if offset else pair[:SUB]
                        for out in outs:
                            row_off = lat - out + 3
                            if 0 <= row_off < 7:
                                tap = k_ref[row_off, col_off : col_off + 1, lanes]
                                sums[out] = sums[out] + tap * cell
                for out in outs:
                    conv[out, start : start + 8, lanes] = sums[out]
        sums_ref[...] = jnp.zeros_like(sums_ref)

        def standardize(row, at, here):
            x = conv[row, at : at + strip, :]
            mean = jnp.mean(x, axis=-1, keepdims=True)
            centered = x - mean
            var = jnp.mean(centered * centered, axis=-1, keepdims=True)
            inv = lax.rsqrt(var + 1e-06)
            xhat = centered * inv
            conv[row, at : at + strip, :] = xhat
            inv_s[here, :] = jnp.broadcast_to(inv, (strip, LANES))
            normed[here, :] = (xhat * gain_ref[...] + bias_ref[...]).astype(BF16)
            ocean = jnp.concatenate([m_ref[row, at : at + strip, :]] * wide, axis=1)
            grad = ocean * (scale_ref[...] * cot_ref[here, :].astype(F32))
            sums_ref[0] += grad[:SUB] + grad[SUB:]
            dbr[here, :] = (0.5 * grad).astype(BF16)

        strips(standardize)
        for at in range(0, cells, chunk):
            here = slice(at, at + chunk)
            normed_t[:, here] = normed[here, :].T
            dbr_t[:, here] = dbr[here, :].T

    part = 256
    count = cells // part
    block = act.shape[1]
    cut = min(block, 256)

    def products(index):
        here = slice(index * part, (index + 1) * part)
        pre_s[index % 2] = jnp.dot(normed[here, :], wi_ref[...], preferred_element_type=F32)
        dact_s[index % 2] = lax.dot_general(
            dbr[here, :], wo_ref[...], (((1,), (1,)), ((), ())), preferred_element_type=F32
        )

    first_block = step_now == 0

    def project(index):
        here = slice(index * part, (index + 1) * part)
        branch[here, :] = jnp.where(first_block, 0.0, branch[here, :]) + jnp.dot(
            act[here, :], wo_ref[...], preferred_element_type=F32
        )
        d_normed[here, :] = jnp.where(first_block, 0.0, d_normed[here, :]) + lax.dot_general(
            dpre[here, :], wi_ref[...], (((1,), (1,)), ((), ())), preferred_element_type=F32
        )

    totals = [jnp.zeros((SUB, cut), F32) for _ in range(0, block, cut)]
    products(0)
    for index in range(count):
        if index + 1 < count:
            products(index + 1)
        for at in range(0, part, strip):
            here = slice(index * part + at, index * part + at + strip)
            for which, left in enumerate(range(0, block, cut)):
                lanes = slice(left, left + cut)
                x = pre_s[index % 2, at : at + strip, lanes] + bi_ref[:, lanes]
                value, slope = gelu_twice(x)
                act[here, lanes] = value.astype(BF16)
                d_pre = dact_s[index % 2, at : at + strip, lanes] * slope
                dpre[here, lanes] = d_pre.astype(BF16)
                totals[which] = totals[which] + (d_pre[:SUB] + d_pre[SUB:])
        if index > 0:
            project(index - 1)
    project(count - 1)
    for which, left in enumerate(range(0, block, cut)):
        gbi_ref[:, left : left + cut] = jnp.sum(totals[which], axis=0, keepdims=True)
    _, parts, _, width = sent_ref.shape
    is_sent = step_now < pl.num_programs(0) // 2
    for index, (rows_t, source) in enumerate(((dbr_t, act), (normed_t, dpre))):
        for left in range(0, block, cut):
            grad = jnp.dot(
                rows_t[...], source[:, left : left + cut], preferred_element_type=F32
            ).astype(BF16)

            def store(ref):
                for at in range(0, cut, min(width, cut)):
                    lat, into = divmod(left + at, width)
                    size = min(width, cut)
                    ref[index, lat, :, into : into + size] = grad[:, at : at + size]

            pl.when(is_sent)(functools.partial(store, sent_ref))
            pl.when(jnp.logical_not(is_sent))(functools.partial(store, kept_ref))

    @pl.when(step_now == pl.num_programs(0) - 1)
    def _():
        def norm_back(row, at, here):
            cot = cot_ref[here, :].astype(F32)
            ocean = jnp.concatenate([m_ref[row, at : at + strip, :]] * wide, axis=1)
            ocean = ocean * (0.5 * branch[here, :] + bo_ref[...])
            mixed_ref[here, :] = (f_ref[here, :].astype(F32) + ocean * scale_ref[...]).astype(BF16)
            term = ocean * cot
            sums_ref[1] += term[:SUB] + term[SUB:]
            grad = d_normed[here, :]
            xhat = conv[row, at : at + strip, :]
            term = grad * xhat
            sums_ref[2] += term[:SUB] + term[SUB:]
            sums_ref[3] += grad[:SUB] + grad[SUB:]
            e = grad * gain_ref[...]
            m1 = jnp.mean(e, axis=-1, keepdims=True)
            m2 = jnp.mean(term * gain_ref[...], axis=-1, keepdims=True)
            inv = jnp.concatenate([inv_s[here, :]] * wide, axis=1)
            dconv_ref[here, :] = (inv * (e - m1 - xhat * m2)).astype(BF16)

        strips(norm_back)


def expand(
    order, inner, side, top, bot, kernel, gain, bias, scale, b_out, mask, cot, fields, w_in, b_in, w_out, n_lon, n_lat
):
    rows, _, channels = inner.shape
    hidden = w_in.shape[1]
    cells, _ = cot.shape
    cols = cells // rows
    block = hidden // n_lon
    split = n_lat if (block // n_lat) % LANES == 0 else 1
    turn = n_lon // 2
    grads = (split, channels, block // split)
    given = (inner, side, top, bot, kernel, gain, bias, scale, b_out, mask, cot, fields)

    def sent_at(h, order):
        return (0, jnp.minimum(h, turn - 1), 0, 0, 0)

    def kept_at(h, order):
        return (0, jnp.maximum(h - turn, 0), 0, 0, 0)

    return pl.pallas_call(
        expand_kernel,
        grid_spec=pltpu.PrefetchScalarGridSpec(
            num_scalar_prefetch=1,
            grid=(n_lon,),
            in_specs=[once(x.shape) for x in given]
            + [
                pl.BlockSpec((channels, block), lambda h, order: (0, order[h])),
                pl.BlockSpec((1, block), lambda h, order: (0, order[h])),
                pl.BlockSpec((block, channels), lambda h, order: (order[h], 0)),
            ],
            out_specs=[
                once((cells, channels)),
                once((cells, channels)),
                once((4, SUB, channels)),
                pl.BlockSpec((1, block), lambda h, order: (0, order[h])),
                pl.BlockSpec((2, None) + grads, sent_at),
                pl.BlockSpec((2, None) + grads, kept_at),
            ],
            scratch_shapes=[
                pltpu.VMEM((rows, cols, channels), F32),
                pltpu.VMEM((6, cols + 16, channels), F32),
                pltpu.VMEM((cells, LANES), F32),
                pltpu.VMEM((cells, channels), BF16),
                pltpu.VMEM((channels, cells), BF16),
                pltpu.VMEM((cells, channels), BF16),
                pltpu.VMEM((channels, cells), BF16),
                pltpu.VMEM((cells, block), BF16),
                pltpu.VMEM((cells, block), BF16),
                pltpu.VMEM((cells, channels), F32),
                pltpu.VMEM((cells, channels), F32),
                pltpu.VMEM((2, 256, block), F32),
                pltpu.VMEM((2, 256, block), F32),
            ],
        ),
        out_shape=[
            jax.ShapeDtypeStruct((cells, channels), BF16),
            jax.ShapeDtypeStruct((cells, channels), BF16),
            jax.ShapeDtypeStruct((4, SUB, channels), F32),
            jax.ShapeDtypeStruct((1, hidden), F32),
            jax.ShapeDtypeStruct((2, turn) + grads, BF16),
            jax.ShapeDtypeStruct((2, turn) + grads, BF16),
        ],
        compiler_params=params(56),
        cost_estimate=estimate(20),
        name="expand",
    )(order, *given, w_in, b_in, w_out)


def fill_window(window, center, left, right, top, bot):
    rows, cols, _ = center.shape
    window[3 : 3 + rows, 5:8, :] = left[...].astype(F32)
    window[3 : 3 + rows, 8 : 8 + cols, :] = center
    window[3 : 3 + rows, 8 + cols : 11 + cols, :] = right[...].astype(F32)
    window[0:3, 5 : 11 + cols, :] = top[...].astype(F32)
    window[3 + rows : 6 + rows, 5 : 11 + cols, :] = bot[...].astype(F32)


def filter_grad_kernel(
    f_ref, m_ref, l_ref, r_ref, t_ref, b_ref, d_ref, sums_ref, gbi_0, gbi_1, gbi_2, gbi_3,
    o_ref, window, grad,
):
    rows, cols, _ = f_ref.shape
    fill_window(window, f_ref[...].astype(F32) * m_ref[...], l_ref, r_ref, t_ref, b_ref)
    grad[...] = d_ref[...].astype(F32)
    for col_off in range(7):

        def band(index, sums):
            start = pl.multiple_of(index * 8, 8)
            sums = list(sums)
            held = {}
            for src in range(rows + 6):
                if src < rows:
                    held[src] = grad[src, pl.ds(start, SUB), :]
                cells = shifted(window, src, start, 5 + col_off)
                for row_off in range(7):
                    out = src - row_off
                    if 0 <= out < rows:
                        at = row_off + 7 * (src % 3)
                        sums[at] = sums[at] + held[out] * cells
            return tuple(sums)

        start = tuple(jnp.zeros((SUB, LANES), F32) for _ in range(21))
        sums = lax.fori_loop(0, cols // 8, band, start)
        for row_off in range(7):
            total = sums[row_off] + sums[row_off + 7] + sums[row_off + 14]
            o_ref[row_off, col_off : col_off + 1, :] = jnp.sum(total, axis=0, keepdims=True)
    for at, source in enumerate((1, 2, 3, 0)):
        o_ref[7, at : at + 1, :] = jnp.sum(sums_ref[source], axis=0, keepdims=True)
    for at, gbi_ref in enumerate((gbi_0, gbi_1, gbi_2, gbi_3)):
        o_ref[7, 4 + at : 5 + at, :] = gbi_ref[...]
    for row_off in range(7):
        o_ref[row_off, 7:8, :] = jnp.zeros((1, LANES), F32)


def filter_grad(fields, mask, left, right, top, bot, d_conv, sums, gbi):
    rows, cols, channels = fields.shape

    def part(x):
        return by_channels(x.shape)

    return pl.pallas_call(
        filter_grad_kernel,
        grid=(channels // LANES,),
        out_shape=jax.ShapeDtypeStruct((8, 8, channels), F32),
        in_specs=[
            part(fields),
            whole_spec(mask.shape),
            part(left),
            part(right),
            part(top),
            part(bot),
            part(d_conv),
            part(sums),
        ]
        + [by_channels(gbi.shape, at * (channels // LANES)) for at in range(4)],
        out_specs=by_channels((8, 8, channels)),
        scratch_shapes=[
            pltpu.VMEM((rows + 6, cols + 16, LANES), F32),
            pltpu.VMEM((rows, cols, LANES), F32),
        ],
        compiler_params=params(56),
        cost_estimate=estimate(4),
        name="filter_grad",
    )(fields, mask, left, right, top, bot, d_conv, sums, gbi, gbi, gbi, gbi)


def input_grad_kernel(d_ref, l_ref, r_ref, t_ref, b_ref, k_ref, m_ref, cot_ref, o_ref, window, grad):
    rows, cols, _ = d_ref.shape
    fill_window(window, d_ref[...].astype(F32), l_ref, r_ref, t_ref, b_ref)
    for start in range(0, cols, 8):
        band_conv(window, k_ref, grad, start, start, 3, True)
    o_ref[...] = (cot_ref[...].astype(F32) + m_ref[...] * grad[...]).astype(BF16)


def input_grad_more_kernel(d_ref, l_ref, r_ref, t_ref, b_ref, k_ref, m_ref, cot_ref, old_ref, o_ref, window, grad):
    input_grad_kernel(d_ref, l_ref, r_ref, t_ref, b_ref, k_ref, m_ref, cot_ref, o_ref, window, grad)


def input_grad(d_conv, left, right, top, bot, kernel, mask, cot, blocks, first, old=None):
    rows, cols, channels = d_conv.shape

    def part(x):
        return by_channels(x.shape, first)

    more = [] if old is None else [old]
    return pl.pallas_call(
        input_grad_kernel if old is None else input_grad_more_kernel,
        grid=(blocks,),
        out_shape=jax.ShapeDtypeStruct((rows, cols, channels), BF16),
        in_specs=[
            part(d_conv),
            part(left),
            part(right),
            part(top),
            part(bot),
            part(kernel),
            whole_spec(mask.shape),
            part(cot),
        ]
        + [UNUSED] * len(more),
        out_specs=part(d_conv),
        scratch_shapes=[
            pltpu.VMEM((rows + 6, cols + 16, LANES), F32),
            pltpu.VMEM((rows, cols, LANES), F32),
        ],
        input_output_aliases={} if old is None else {8: 0},
        compiler_params=params(56),
        cost_estimate=estimate(4),
        name="input_grad",
    )(d_conv, left, right, top, bot, kernel, mask, cot, *more)


def swap(values, axis, bit):
    count = lax.axis_size(axis)
    return lax.ppermute(values, axis, [(i, i ^ bit) for i in range(count)])


def bits_of(axis):
    return [1 << k for k in range(int(math.log2(lax.axis_size(axis))))]


def after(value, *others):
    return lax.optimization_barrier((value,) + others)[0]


def halves(values, axis, dim, bit):
    mine = (lax.axis_index(axis) // bit) % 2 == 1
    shape = values.shape
    paired = values.reshape(shape[:dim] + (shape[dim] // 2, 2) + shape[dim + 1 :])
    low = lax.index_in_dim(paired, 0, dim + 1, keepdims=False)
    high = lax.index_in_dim(paired, 1, dim + 1, keepdims=False)
    return jnp.where(mine, high, low), jnp.where(mine, low, high).astype(BF16)


def side_halo(last, first):
    count = lax.axis_size("lon")
    ahead = [(i, (i + 1) % count) for i in range(count)]
    back = [((i + 1) % count, i) for i in range(count)]
    return lax.ppermute(last, "lon", ahead), lax.ppermute(first, "lon", back)


def end_rows(head, tail, left, right):
    rows = left.shape[0]
    return (
        jnp.concatenate([left[rows - 3 :], tail, right[rows - 3 :]], axis=1),
        jnp.concatenate([left[:3], head, right[:3]], axis=1),
    )


def end_halo(tail, head):
    count = lax.axis_size("lat")
    ahead = [(i, i + 1) for i in range(count - 1)]
    back = [(i + 1, i) for i in range(count - 1)]
    return lax.ppermute(tail, "lat", ahead), lax.ppermute(head, "lat", back)


def per_device(
    fields,
    land_mask,
    cotangent,
    kernel,
    layer_norm_gain,
    layer_norm_bias,
    w_in,
    b_in,
    w_out,
    b_out,
    layer_scale,
):
    rows, cols, channels = fields.shape
    cells = rows * cols
    hidden = w_in.shape[1]
    n_lon, n_lat = lax.axis_size("lon"), lax.axis_size("lat")
    gain, bias = layer_norm_gain.reshape(1, -1), layer_norm_bias.reshape(1, -1)
    scale = layer_scale.reshape(1, -1)
    cot_rows = cotangent.reshape(cells, channels)
    mask = jnp.broadcast_to(land_mask.astype(F32)[:, :, None], (rows, cols, LANES))
    ocean = land_mask.astype(BF16)[:, :, None]
    left, right = side_halo(fields[:, cols - 3 :] * ocean[:, cols - 3 :], fields[:, :3] * ocean[:, :3])
    inner, head, tail = conv_inner(fields, mask, kernel)
    top, bot = end_halo(*end_rows(head, tail, left, right))
    side = conv_side(fields, mask, kernel, left, right)

    lon = lax.axis_index("lon")
    core, side_y = lon % 2, (lon // 2) % 2
    quads = 4 * jnp.arange(n_lon // 4, dtype=jnp.int32)
    order = jnp.concatenate(
        [quads + 2 * y + c for c in (1 - core, core) for y in (1 - side_y, side_y)]
    )
    d_conv, mixed, sums, g_bi, sent, kept = expand(
        order, inner, side, top, bot, kernel, gain, bias, scale, b_out.reshape(1, -1), mask, cot_rows,
        fields.reshape(cells, channels), w_in, b_in.reshape(1, -1), w_out, n_lon, n_lat,
    )
    got = swap(sent, "lon", 1)
    d_conv = d_conv.reshape(rows, cols, channels)
    d_left, d_right = side_halo(d_conv[:, cols - 3 :], d_conv[:, :3])
    d_tail, d_head = end_rows(d_conv[:3], d_conv[rows - 3 :], d_left, d_right)
    d_top, d_bot = end_halo(d_tail, d_head)

    far = n_lon // 4
    border = channels * 5 // 8
    pieces = (slice(0, border), slice(border, channels))
    far_sums = [
        (kept[:, :far, :, piece].astype(F32) + got[:, :far, :, piece].astype(F32)).astype(BF16)
        for piece in pieces
    ]
    got_far = [swap(x, "lon", 2) for x in far_sums]
    steps = [("lon", 1, bit) for bit in bits_of("lon")[2:]] + [("lat", 2, bit) for bit in bits_of("lat")]
    owned, cut = [None, None], [None, None]

    def begin(index, last):
        here = pieces[index]
        x = after(kept, last)[:, far:, :, here].astype(F32) + after(got, last)[:, far:, :, here].astype(F32)
        x = x + after(got_far[index], last).astype(F32)
        if x.shape[2] != n_lat:
            x = x.reshape(2, far, x.shape[3], n_lat, -1).transpose(0, 1, 3, 2, 4)
        cut[index] = halves(x, *steps[0])

    def advance(index, step, last):
        axis, dim, bit = steps[step]
        mine, sent = cut[index]
        owned[index] = after(mine, last) + after(swap(sent, axis, bit), last).astype(F32)
        if step + 1 < len(steps):
            cut[index] = halves(owned[index], *steps[step + 1])

    hops = [(axis, bit) for axis in ("lon", "lat") for bit in bits_of(axis)]

    def spread(hop, last):
        return after(small, last) + after(swap(small, *hops[hop]), last)

    small = filter_grad(
        after(fields, d_tail, d_head, far_sums[0]), mask, left, right, top, bot, d_conv, sums, g_bi
    )
    begin(0, small)
    for step in range(len(steps) - 2):
        advance(0, step, small)
    quarter = channels // LANES // 4
    back = (d_left, d_right, d_top, d_bot, kernel, mask, cotangent)
    grad_fields = input_grad(after(d_conv, small, cut[0][1], far_sums[1]), *back, quarter, 0)
    small = spread(0, grad_fields)
    grad_fields = input_grad(after(d_conv, small), *back, quarter, quarter, grad_fields)
    small = spread(1, grad_fields)
    advance(0, len(steps) - 2, grad_fields)
    begin(1, grad_fields)
    for step in range(len(steps) - 2):
        advance(1, step, grad_fields)
    grad_fields = input_grad(
        after(d_conv, small, cut[0][1], cut[1][1]), *back, quarter, 2 * quarter, grad_fields
    )
    small = spread(2, grad_fields)
    advance(0, len(steps) - 1, grad_fields)
    advance(1, len(steps) - 2, grad_fields)
    grad_fields = input_grad(after(d_conv, small, cut[1][1]), *back, quarter, 3 * quarter, grad_fields)
    for hop in range(3, len(hops)):
        small = spread(hop, grad_fields)
    advance(1, len(steps) - 1, grad_fields)
    grad_w = jnp.concatenate([x[:, 0, 0] for x in owned], axis=1)
    return (
        mixed.reshape(rows, cols, channels),
        grad_fields,
        small[:7, :7],
        small[7, 1],
        small[7, 2],
        grad_w[1],
        small[7, 4:].reshape(hidden),
        grad_w[0].T,
        small[7, 3],
        small[7, 0],
    )


def solution(mesh):
    placed = (
        P(("grp", "lat"), "lon", None),
        P(("grp", "lat"), "lon"),
        P(("grp", "lat"), "lon", None),
        P(),
        P(),
        P(),
        P(),
        P(),
        P(),
        P(),
        P(),
    )
    return jax.shard_map(
        per_device,
        mesh=mesh,
        in_specs=placed,
        out_specs=(
            P(("grp", "lat"), "lon", None),
            P(("grp", "lat"), "lon", None),
            P("grp", None, None),
            P("grp"),
            P("grp"),
            P("grp", ("lon", "lat")),
            P("grp"),
            P(("lon", "lat"), "grp"),
            P("grp"),
            P("grp"),
        ),
        check_vma=False,
    )
```

```python
import functools
import math

import jax
import jax.numpy as jnp
from jax import lax
from jax.experimental import pallas as pl
from jax.experimental.pallas import tpu as pltpu
from jax.sharding import PartitionSpec as P

F32 = jnp.float32
BF16 = jnp.bfloat16
LANES = 128
SUB = 8


def params(mib):
    return pltpu.CompilerParams(vmem_limit_bytes=mib * 1024 * 1024)


def estimate(micros):
    return pl.CostEstimate(
        flops=int(micros * 1.15e9), bytes_accessed=int(micros * 3.6e6), transcendentals=0
    )


def once(shape):
    zeros = (0,) * len(shape)
    return pl.BlockSpec(shape, lambda *_: zeros, pipeline_mode=pl.Buffered(1))


UNUSED = pl.BlockSpec(memory_space=pl.ANY)


def whole_spec(shape):
    zeros = (0,) * len(shape)
    return pl.BlockSpec(shape, lambda *_: zeros)


def shifted(window, row, start, offset):
    return window[row, pl.ds(start + offset, SUB), :]


def lane_block(index):
    return pl.ds(pl.multiple_of(index * LANES, LANES), LANES)


def each_lane_block(channels, body):
    def one(index, _):
        body(lane_block(index))
        return 0

    lax.fori_loop(0, channels // LANES, one, 0)


def band_conv(window, k_ref, lanes, starts, rows, pad, flip):
    sums = {}
    for col_off in range(7):
        at = 6 - col_off if flip else col_off
        weights = [k_ref[6 - p if flip else p, at : at + 1, lanes] for p in range(7)]
        for start in starts:
            for src in range(window.shape[0]):
                hits = [(src - pad - row_off + 3, row_off) for row_off in range(7)]
                hits = [(out, row_off) for out, row_off in hits if 0 <= out < rows]
                if not hits:
                    continue
                cells = shifted(window, src, start, 5 + col_off)
                for out, row_off in hits:
                    term = weights[row_off] * cells
                    key = (out, start)
                    sums[key] = sums[key] + term if key in sums else term
    return sums


def conv_inner_kernel(f_ref, m_ref, k_ref, o_ref, head_ref, tail_ref, window):
    rows, cols, channels = f_ref.shape

    def block(lanes):
        masked = f_ref[:, :, lanes].astype(F32) * m_ref[...]
        window[:, 8 : 8 + cols, :] = masked
        head_ref[:, :, lanes] = masked[:3].astype(BF16)
        tail_ref[:, :, lanes] = masked[rows - 3 :].astype(BF16)
        for start in range(8, cols - 8, 8):
            sums = band_conv(window, k_ref, lanes, (start,), rows, 0, False)
            for row in range(rows):
                o_ref[row, start - 8 : start, lanes] = sums[row, start]

    each_lane_block(channels, block)


def conv_side_kernel(f_ref, m_ref, k_ref, l_ref, r_ref, o_ref, window):
    rows, cols, channels = f_ref.shape

    def block(lanes):
        window[:, 5:8, :] = l_ref[:, :, lanes].astype(F32)
        window[:, 8 : 8 + cols, :] = f_ref[:, :, lanes].astype(F32) * m_ref[...]
        window[:, 8 + cols : 11 + cols, :] = r_ref[:, :, lanes].astype(F32)
        for at, start in ((0, 0), (8, cols - 8)):
            sums = band_conv(window, k_ref, lanes, (start,), rows, 0, False)
            for row in range(rows):
                o_ref[row, at : at + 8, lanes] = sums[row, start]

    each_lane_block(channels, block)


def conv_inner(fields, mask, kernel):
    rows, cols, channels = fields.shape
    ends = (3, cols, channels)
    return pl.pallas_call(
        conv_inner_kernel,
        out_shape=[
            jax.ShapeDtypeStruct((rows, cols - 16, channels), F32),
            jax.ShapeDtypeStruct(ends, BF16),
            jax.ShapeDtypeStruct(ends, BF16),
        ],
        scratch_shapes=[pltpu.VMEM((rows, cols + 16, LANES), F32)],
        compiler_params=params(56),
        cost_estimate=estimate(4),
        name="conv_inner",
    )(fields, mask, kernel)


def conv_side(fields, mask, kernel, left, right):
    rows, cols, channels = fields.shape
    return pl.pallas_call(
        conv_side_kernel,
        out_shape=jax.ShapeDtypeStruct((rows, 16, channels), F32),
        scratch_shapes=[pltpu.VMEM((rows, cols + 16, LANES), F32)],
        compiler_params=params(56),
        cost_estimate=estimate(4),
        name="conv_side",
    )(fields, mask, kernel, left, right)


def gelu_twice(x):
    root = math.sqrt(2.0 / math.pi)
    inner = root + (root * 0.044715) * (x * x)
    tanh = jnp.tanh(x * inner)
    both = 1.0 + tanh
    value = x * both
    slope = both + value * ((1.0 - tanh) * (3.0 * inner - 2.0 * root))
    return value, slope


def expand_kernel(
    order_ref,
    inner_ref, side_ref, top_ref, bot_ref, k_ref, gain_ref, bias_ref, scale_ref, bo_ref, m_ref, cot_ref, f_ref,
    wi_ref, bi_ref, wo_ref,
    dconv_ref, mixed_ref, sums_ref, gbi_ref, sent_ref, kept_ref,
    conv, halo, inv_s, normed, normed_t, dbr, dbr_t, act, dpre, d_normed, branch, pre_s, dact_s,
):
    rows, cols, channels = conv.shape
    cells = rows * cols
    strip = 16
    chunk = 128
    step_now = pl.program_id(0)
    wide = channels // LANES

    def strips(body):
        def some(index, _):
            for more in range(4):
                row = index * 4 + more
                for at in range(0, cols, strip):
                    body(row, at, pl.ds(pl.multiple_of(row * cols + at, strip), strip))
            return 0

        lax.fori_loop(0, rows // 4, some, 0)

    @pl.when(step_now == 0)
    def _():
        conv[:, 0:8, :] = side_ref[:, 0:8, :]
        conv[:, 8 : cols - 8, :] = inner_ref[...]
        conv[:, cols - 8 : cols, :] = side_ref[:, 8:16, :]
        halo[0:3, 5 : 11 + cols, :] = top_ref[...].astype(F32)
        halo[3:6, 5 : 11 + cols, :] = bot_ref[...].astype(F32)
        for block in range(wide):
            lanes = slice(block * LANES, (block + 1) * LANES)
            for start in range(0, cols, 8):
                outs = list(range(3)) + list(range(rows - 3, rows))
                sums = {out: conv[out, start : start + 8, lanes] for out in outs}
                for col_off in range(7):
                    for src in range(6):
                        lat = src - 3 if src < 3 else rows + src - 3
                        offset = (5 + col_off) % SUB
                        base = start + (5 + col_off) // SUB * SUB
                        pair = halo[src, base : base + 2 * SUB, lanes]
                        cell = pltpu.roll(pair, 2 * SUB - offset, axis=0)[:SUB] if offset else pair[:SUB]
                        for out in outs:
                            row_off = lat - out + 3
                            if 0 <= row_off < 7:
                                tap = k_ref[row_off, col_off : col_off + 1, lanes]
                                sums[out] = sums[out] + tap * cell
                for out in outs:
                    conv[out, start : start + 8, lanes] = sums[out]
        sums_ref[...] = jnp.zeros_like(sums_ref)
        branch[...] = jnp.zeros_like(branch)
        d_normed[...] = jnp.zeros_like(d_normed)

        def standardize(row, at, here):
            x = conv[row, at : at + strip, :]
            mean = jnp.mean(x, axis=-1, keepdims=True)
            centered = x - mean
            var = jnp.mean(centered * centered, axis=-1, keepdims=True)
            inv = lax.rsqrt(var + 1e-06)
            xhat = centered * inv
            conv[row, at : at + strip, :] = xhat
            inv_s[here, :] = jnp.broadcast_to(inv, (strip, LANES))
            normed[here, :] = (xhat * gain_ref[...] + bias_ref[...]).astype(BF16)
            ocean = jnp.concatenate([m_ref[row, at : at + strip, :]] * wide, axis=1)
            grad = ocean * (scale_ref[...] * cot_ref[here, :].astype(F32))
            sums_ref[0] += grad[:SUB] + grad[SUB:]
            dbr[here, :] = (0.5 * grad).astype(BF16)

        strips(standardize)
        for at in range(0, cells, chunk):
            here = slice(at, at + chunk)
            normed_t[:, here] = normed[here, :].T
            dbr_t[:, here] = dbr[here, :].T

    part = 256
    count = cells // part
    block = act.shape[1]
    cut = min(block, 256)

    def products(index):
        here = slice(index * part, (index + 1) * part)
        pre_s[index % 2] = jnp.dot(normed[here, :], wi_ref[...], preferred_element_type=F32)
        dact_s[index % 2] = lax.dot_general(
            dbr[here, :], wo_ref[...], (((1,), (1,)), ((), ())), preferred_element_type=F32
        )

    def project(index):
        here = slice(index * part, (index + 1) * part)
        branch[here, :] += jnp.dot(act[here, :], wo_ref[...], preferred_element_type=F32)
        d_normed[here, :] += lax.dot_general(
            dpre[here, :], wi_ref[...], (((1,), (1,)), ((), ())), preferred_element_type=F32
        )

    totals = [jnp.zeros((SUB, cut), F32) for _ in range(0, block, cut)]
    products(0)
    for index in range(count):
        if index + 1 < count:
            products(index + 1)
        for at in range(0, part, strip):
            here = slice(index * part + at, index * part + at + strip)
            for which, left in enumerate(range(0, block, cut)):
                lanes = slice(left, left + cut)
                x = pre_s[index % 2, at : at + strip, lanes] + bi_ref[:, lanes]
                value, slope = gelu_twice(x)
                act[here, lanes] = value.astype(BF16)
                d_pre = dact_s[index % 2, at : at + strip, lanes] * slope
                dpre[here, lanes] = d_pre.astype(BF16)
                totals[which] = totals[which] + (d_pre[:SUB] + d_pre[SUB:])
        if index > 0:
            project(index - 1)
    project(count - 1)
    for which, left in enumerate(range(0, block, cut)):
        gbi_ref[:, left : left + cut] = jnp.sum(totals[which], axis=0, keepdims=True)
    _, parts, _, width = sent_ref.shape
    is_sent = step_now < pl.num_programs(0) // 2
    for index, (rows_t, source) in enumerate(((dbr_t, act), (normed_t, dpre))):
        for left in range(0, block, cut):
            grad = jnp.dot(
                rows_t[...], source[:, left : left + cut], preferred_element_type=F32
            ).astype(BF16)

            def store(ref):
                for at in range(0, cut, min(width, cut)):
                    lat, into = divmod(left + at, width)
                    size = min(width, cut)
                    ref[index, lat, :, into : into + size] = grad[:, at : at + size]

            pl.when(is_sent)(functools.partial(store, sent_ref))
            pl.when(jnp.logical_not(is_sent))(functools.partial(store, kept_ref))

    @pl.when(step_now == pl.num_programs(0) - 1)
    def _():
        def norm_back(row, at, here):
            cot = cot_ref[here, :].astype(F32)
            ocean = jnp.concatenate([m_ref[row, at : at + strip, :]] * wide, axis=1)
            ocean = ocean * (0.5 * branch[here, :] + bo_ref[...])
            mixed_ref[here, :] = (f_ref[here, :].astype(F32) + ocean * scale_ref[...]).astype(BF16)
            term = ocean * cot
            sums_ref[1] += term[:SUB] + term[SUB:]
            grad = d_normed[here, :]
            xhat = conv[row, at : at + strip, :]
            term = grad * xhat
            sums_ref[2] += term[:SUB] + term[SUB:]
            sums_ref[3] += grad[:SUB] + grad[SUB:]
            e = grad * gain_ref[...]
            m1 = jnp.mean(e, axis=-1, keepdims=True)
            m2 = jnp.mean(term * gain_ref[...], axis=-1, keepdims=True)
            inv = jnp.concatenate([inv_s[here, :]] * wide, axis=1)
            dconv_ref[here, :] = (inv * (e - m1 - xhat * m2)).astype(BF16)

        strips(norm_back)


def expand(
    order, inner, side, top, bot, kernel, gain, bias, scale, b_out, mask, cot, fields, w_in, b_in, w_out, n_lon, n_lat
):
    rows, _, channels = inner.shape
    hidden = w_in.shape[1]
    cells, _ = cot.shape
    cols = cells // rows
    block = hidden // n_lon
    split = n_lat if (block // n_lat) % LANES == 0 else 1
    turn = n_lon // 2
    grads = (split, channels, block // split)
    given = (inner, side, top, bot, kernel, gain, bias, scale, b_out, mask, cot, fields)

    def sent_at(h, order):
        return (0, jnp.minimum(h, turn - 1), 0, 0, 0)

    def kept_at(h, order):
        return (0, jnp.maximum(h - turn, 0), 0, 0, 0)

    return pl.pallas_call(
        expand_kernel,
        grid_spec=pltpu.PrefetchScalarGridSpec(
            num_scalar_prefetch=1,
            grid=(n_lon,),
            in_specs=[once(x.shape) for x in given]
            + [
                pl.BlockSpec((channels, block), lambda h, order: (0, order[h])),
                pl.BlockSpec((1, block), lambda h, order: (0, order[h])),
                pl.BlockSpec((block, channels), lambda h, order: (order[h], 0)),
            ],
            out_specs=[
                once((cells, channels)),
                once((cells, channels)),
                once((4, SUB, channels)),
                pl.BlockSpec((1, block), lambda h, order: (0, order[h])),
                pl.BlockSpec((2, None) + grads, sent_at),
                pl.BlockSpec((2, None) + grads, kept_at),
            ],
            scratch_shapes=[
                pltpu.VMEM((rows, cols, channels), F32),
                pltpu.VMEM((6, cols + 16, channels), F32),
                pltpu.VMEM((cells, LANES), F32),
                pltpu.VMEM((cells, channels), BF16),
                pltpu.VMEM((channels, cells), BF16),
                pltpu.VMEM((cells, channels), BF16),
                pltpu.VMEM((channels, cells), BF16),
                pltpu.VMEM((cells, block), BF16),
                pltpu.VMEM((cells, block), BF16),
                pltpu.VMEM((cells, channels), F32),
                pltpu.VMEM((cells, channels), F32),
                pltpu.VMEM((2, 256, block), F32),
                pltpu.VMEM((2, 256, block), F32),
            ],
        ),
        out_shape=[
            jax.ShapeDtypeStruct((cells, channels), BF16),
            jax.ShapeDtypeStruct((cells, channels), BF16),
            jax.ShapeDtypeStruct((4, SUB, channels), F32),
            jax.ShapeDtypeStruct((1, hidden), F32),
            jax.ShapeDtypeStruct((2, turn) + grads, BF16),
            jax.ShapeDtypeStruct((2, turn) + grads, BF16),
        ],
        compiler_params=params(56),
        cost_estimate=estimate(20),
        name="expand",
    )(order, *given, w_in, b_in, w_out)


def filter_grad_kernel(
    f_ref, m_ref, l_ref, r_ref, t_ref, b_ref, d_ref, sums_ref, gbi_ref, o_ref, window, grad
):
    rows, cols, channels = f_ref.shape
    blocks = channels // LANES

    def block(index, _):
        lanes = lane_block(index)
        window[0:3, 5 : 11 + cols, :] = t_ref[:, :, lanes].astype(F32)
        window[3 : 3 + rows, 5:8, :] = l_ref[:, :, lanes].astype(F32)
        window[3 : 3 + rows, 8 : 8 + cols, :] = f_ref[:, :, lanes].astype(F32) * m_ref[...]
        window[3 : 3 + rows, 8 + cols : 11 + cols, :] = r_ref[:, :, lanes].astype(F32)
        window[3 + rows : 6 + rows, 5 : 11 + cols, :] = b_ref[:, :, lanes].astype(F32)
        grad[...] = d_ref[:, :, lanes].astype(F32)
        for col_off in range(7):

            def band(step, sums):
                start = pl.multiple_of(step * SUB, SUB)
                sums = list(sums)
                held = {}
                for src in range(rows + 6):
                    if src < rows:
                        held[src] = grad[src, pl.ds(start, SUB), :]
                    cells = shifted(window, src, start, 5 + col_off)
                    for row_off in range(7):
                        out = src - row_off
                        if 0 <= out < rows:
                            sums[row_off] = sums[row_off] + held[out] * cells
                return tuple(sums)

            sums = tuple(jnp.zeros((SUB, LANES), F32) for _ in range(7))
            sums = lax.fori_loop(0, cols // SUB, band, sums)
            for row_off in range(7):
                at = row_off * 8 + col_off
                o_ref[index, at : at + 1, :] = jnp.sum(sums[row_off], axis=0, keepdims=True)
        for row_off in range(7):
            o_ref[index, row_off * 8 + 7 : row_off * 8 + 8, :] = jnp.zeros((1, LANES), F32)
        for at, source in enumerate((1, 2, 3, 0)):
            o_ref[index, 56 + at : 57 + at, :] = jnp.sum(sums_ref[source, :, lanes], axis=0, keepdims=True)
        for at in range(4):
            o_ref[index, 60 + at : 61 + at, :] = gbi_ref[:, lane_block(at * blocks + index)]
        return 0

    lax.fori_loop(0, blocks, block, 0)


def filter_grad(fields, mask, left, right, top, bot, d_conv, sums, gbi):
    rows, cols, channels = fields.shape
    return pl.pallas_call(
        filter_grad_kernel,
        out_shape=jax.ShapeDtypeStruct((channels // LANES, 64, LANES), F32),
        scratch_shapes=[
            pltpu.VMEM((rows + 6, cols + 16, LANES), F32),
            pltpu.VMEM((rows, cols, LANES), F32),
        ],
        compiler_params=params(56),
        cost_estimate=estimate(4),
        name="filter_grad",
    )(fields, mask, left, right, top, bot, d_conv, sums, gbi)


def input_grad_kernel(first, d_ref, l_ref, r_ref, t_ref, b_ref, k_ref, m_ref, cot_ref, *rest):
    o_ref, window, grad = rest[-3:]
    rows, cols, channels = d_ref.shape
    tall = o_ref.shape[0]
    low, high = max(0, first - 3), min(rows, first + tall + 3)
    inside = slice(low - first + 3, high - first + 3)

    def block(lanes):
        if first < 3:
            window[0 : 3 - first, 5 : 11 + cols, :] = t_ref[first:3, :, lanes].astype(F32)
        if first + tall > rows - 3:
            below = first + tall + 3 - rows
            window[tall + 6 - below : tall + 6, 5 : 11 + cols, :] = b_ref[:below, :, lanes].astype(F32)
        window[inside, 5:8, :] = l_ref[low:high, :, lanes].astype(F32)
        window[inside, 8 : 8 + cols, :] = d_ref[low:high, :, lanes].astype(F32)
        window[inside, 8 + cols : 11 + cols, :] = r_ref[low:high, :, lanes].astype(F32)
        for sums in [band_conv(window, k_ref, lanes, range(0, cols, SUB), tall, 3, True)]:
            for (row, start), value in sums.items():
                grad[row, start : start + SUB, :] = value
        o_ref[:, :, lanes] = (cot_ref[:, :, lanes].astype(F32) + m_ref[...] * grad[...]).astype(BF16)

    each_lane_block(channels, block)


def input_grad(d_conv, left, right, top, bot, kernel, mask, cot, part, parts, old=None):
    rows, cols, channels = d_conv.shape
    tall = rows // parts

    def rows_of(width):
        return pl.BlockSpec((tall, cols, width), lambda i: (part, 0, 0))

    whole = (d_conv, left, right, top, bot, kernel)
    more = [] if old is None else [old]
    return pl.pallas_call(
        functools.partial(input_grad_kernel, part * tall),
        grid=(1,),
        out_shape=jax.ShapeDtypeStruct((rows, cols, channels), BF16),
        in_specs=[once(x.shape) for x in whole]
        + [rows_of(LANES), rows_of(channels)]
        + [UNUSED] * len(more),
        out_specs=rows_of(channels),
        scratch_shapes=[
            pltpu.VMEM((tall + 6, cols + 16, LANES), F32),
            pltpu.VMEM((tall, cols, LANES), F32),
        ],
        input_output_aliases={8: 0} if more else {},
        compiler_params=params(56),
        cost_estimate=estimate(4),
        name="input_grad",
    )(*whole, mask, cot, *more)


def swap(values, axis, bit):
    count = lax.axis_size(axis)
    return lax.ppermute(values, axis, [(i, i ^ bit) for i in range(count)])


def bits_of(axis):
    return [1 << k for k in range(int(math.log2(lax.axis_size(axis))))]


def after(value, *others):
    return lax.optimization_barrier((value,) + others)[0]


def halves(values, axis, dim, bit):
    mine = (lax.axis_index(axis) // bit) % 2 == 1
    shape = values.shape
    paired = values.reshape(shape[:dim] + (shape[dim] // 2, 2) + shape[dim + 1 :])
    low = lax.index_in_dim(paired, 0, dim + 1, keepdims=False)
    high = lax.index_in_dim(paired, 1, dim + 1, keepdims=False)
    return jnp.where(mine, high, low), jnp.where(mine, low, high).astype(BF16)


def side_halo(last, first):
    count = lax.axis_size("lon")
    ahead = [(i, (i + 1) % count) for i in range(count)]
    back = [((i + 1) % count, i) for i in range(count)]
    return lax.ppermute(last, "lon", ahead), lax.ppermute(first, "lon", back)


def end_rows(head, tail, left, right):
    rows = left.shape[0]
    return (
        jnp.concatenate([left[rows - 3 :], tail, right[rows - 3 :]], axis=1),
        jnp.concatenate([left[:3], head, right[:3]], axis=1),
    )


def end_halo(tail, head):
    count = lax.axis_size("lat")
    ahead = [(i, i + 1) for i in range(count - 1)]
    back = [(i + 1, i) for i in range(count - 1)]
    return lax.ppermute(tail, "lat", ahead), lax.ppermute(head, "lat", back)


def per_device(
    fields,
    land_mask,
    cotangent,
    kernel,
    layer_norm_gain,
    layer_norm_bias,
    w_in,
    b_in,
    w_out,
    b_out,
    layer_scale,
):
    rows, cols, channels = fields.shape
    cells = rows * cols
    hidden = w_in.shape[1]
    n_lon, n_lat = lax.axis_size("lon"), lax.axis_size("lat")
    gain, bias = layer_norm_gain.reshape(1, -1), layer_norm_bias.reshape(1, -1)
    scale = layer_scale.reshape(1, -1)
    cot_rows = cotangent.reshape(cells, channels)
    mask = jnp.broadcast_to(land_mask.astype(F32)[:, :, None], (rows, cols, LANES))
    ocean = land_mask.astype(BF16)[:, :, None]
    left, right = side_halo(fields[:, cols - 3 :] * ocean[:, cols - 3 :], fields[:, :3] * ocean[:, :3])
    inner, head, tail = conv_inner(fields, mask, kernel)
    top, bot = end_halo(*end_rows(head, tail, left, right))
    side = conv_side(fields, mask, kernel, left, right)

    lon = lax.axis_index("lon")
    core, side_y = lon % 2, (lon // 2) % 2
    quads = 4 * jnp.arange(n_lon // 4, dtype=jnp.int32)
    order = jnp.concatenate(
        [quads + 2 * y + c for c in (1 - core, core) for y in (1 - side_y, side_y)]
    )
    d_conv, mixed, sums, g_bi, sent, kept = expand(
        order, inner, side, top, bot, kernel, gain, bias, scale, b_out.reshape(1, -1), mask, cot_rows,
        fields.reshape(cells, channels), w_in, b_in.reshape(1, -1), w_out, n_lon, n_lat,
    )
    got = swap(sent, "lon", 1)
    d_conv = d_conv.reshape(rows, cols, channels)
    d_left, d_right = side_halo(d_conv[:, cols - 3 :], d_conv[:, :3])

    far = n_lon // 4
    border = channels * 3 // 4
    pieces = (slice(0, border), slice(border, channels))
    far_sums = [
        (kept[:, :far, :, piece].astype(F32) + got[:, :far, :, piece].astype(F32)).astype(BF16)
        for piece in pieces
    ]
    d_tail, d_head = end_rows(
        d_conv[:3], d_conv[rows - 3 :], after(d_left, far_sums[0]), after(d_right, far_sums[0])
    )
    d_top, d_bot = end_halo(d_tail, d_head)
    steps = [("lon", 1, bit) for bit in bits_of("lon")[2:]] + [("lat", 2, bit) for bit in bits_of("lat")]
    got_far, owned, cut = [swap(far_sums[0], "lon", 2), None], [None, None], [None, None]

    def begin(index, last):
        here = pieces[index]
        x = after(kept, last)[:, far:, :, here].astype(F32) + after(got, last)[:, far:, :, here].astype(F32)
        x = x + after(got_far[index], last).astype(F32)
        if x.shape[2] != n_lat:
            x = x.reshape(2, far, x.shape[3], n_lat, -1).transpose(0, 1, 3, 2, 4)
        cut[index] = halves(x, *steps[0])

    def advance(index, step, last, came=None):
        axis, dim, bit = steps[step]
        mine, sent = cut[index]
        if came is None:
            came = after(swap(sent, axis, bit), last)
        owned[index] = after(mine, last) + came.astype(F32)
        if step + 1 < len(steps):
            cut[index] = halves(owned[index], *steps[step + 1])

    def pack(sent, small):
        high = lax.reduce_precision(small, 8, 7)
        low = lax.reduce_precision(small - high, 8, 7)
        flat = [x.astype(BF16).reshape(-1, LANES) for x in (sent, high, low)]
        return jnp.concatenate(flat), high + low

    def ride(load, small, shape, axis, bit, last):
        came = after(swap(load, axis, bit), last)
        size, more = math.prod(shape) // LANES, small.size // LANES
        both = came[size : size + more].astype(F32) + came[size + more :].astype(F32)
        return came[:size].reshape(shape), after(small, last) + both.reshape(small.shape)

    small = filter_grad(
        after(fields, d_tail, d_head, far_sums[0]), mask, left, right, top, bot, d_conv, sums, g_bi
    )
    begin(0, small)
    for step in range(len(steps) - 2):
        advance(0, step, small)
    back = (d_left, d_right, d_top, d_bot, kernel, mask, cotangent)
    grad_fields = input_grad(after(d_conv, small, cut[0][1]), *back, 0, 4)
    small = after(small, grad_fields) + after(swap(small, "lon", 1), grad_fields)
    advance(0, len(steps) - 2, grad_fields)
    load, small = pack(far_sums[1], small)
    grad_fields = input_grad(after(d_conv, load, cut[0][1]), *back, 1, 4, grad_fields)
    got_far[1], small = ride(load, small, far_sums[1].shape, "lon", 2, grad_fields)
    begin(1, grad_fields)
    advance(0, len(steps) - 1, grad_fields)
    for step, (axis, _, bit) in enumerate(steps):
        shape = cut[1][1].shape
        load, small = pack(cut[1][1], small)
        if step >= len(steps) - 2:
            part = step + 4 - len(steps)
            grad_fields = input_grad(after(d_conv, load), *back, part, 4, grad_fields)
        came, small = ride(load, small, shape, axis, bit, grad_fields)
        advance(1, step, grad_fields, came)
    grad_w = jnp.concatenate([x[:, 0, 0] for x in owned], axis=1)
    small = small.transpose(1, 0, 2).reshape(8, 8, channels)
    return (
        mixed.reshape(rows, cols, channels),
        grad_fields,
        small[:7, :7],
        small[7, 1],
        small[7, 2],
        grad_w[1],
        small[7, 4:].reshape(hidden),
        grad_w[0].T,
        small[7, 3],
        small[7, 0],
    )


def solution(mesh):
    placed = (
        P(("grp", "lat"), "lon", None),
        P(("grp", "lat"), "lon"),
        P(("grp", "lat"), "lon", None),
        P(),
        P(),
        P(),
        P(),
        P(),
        P(),
        P(),
        P(),
    )
    return jax.shard_map(
        per_device,
        mesh=mesh,
        in_specs=placed,
        out_specs=(
            P(("grp", "lat"), "lon", None),
            P(("grp", "lat"), "lon", None),
            P("grp", None, None),
            P("grp"),
            P("grp"),
            P("grp", ("lon", "lat")),
            P("grp"),
            P(("lon", "lat"), "grp"),
            P("grp"),
            P("grp"),
        ),
        check_vma=False,
    )
```

```python
import functools
import math

import jax
import jax.numpy as jnp
from jax import lax
from jax.experimental import pallas as pl
from jax.experimental.pallas import tpu as pltpu
from jax.sharding import PartitionSpec as P

F32 = jnp.float32
BF16 = jnp.bfloat16
LANES = 128
SUB = 8


def params(mib):
    return pltpu.CompilerParams(vmem_limit_bytes=mib * 1024 * 1024)


def estimate(micros):
    return pl.CostEstimate(
        flops=int(micros * 1.15e9), bytes_accessed=int(micros * 3.6e6), transcendentals=0
    )


def once(shape):
    zeros = (0,) * len(shape)
    return pl.BlockSpec(shape, lambda *_: zeros, pipeline_mode=pl.Buffered(1))


UNUSED = pl.BlockSpec(memory_space=pl.ANY)


def whole_spec(shape):
    zeros = (0,) * len(shape)
    return pl.BlockSpec(shape, lambda *_: zeros)


def shifted(window, row, start, offset):
    return window[row, pl.ds(start + offset, SUB), :]


def lane_block(index):
    return pl.ds(pl.multiple_of(index * LANES, LANES), LANES)


def each_lane_block(channels, body):
    def one(index, _):
        body(lane_block(index))
        return 0

    lax.fori_loop(0, channels // LANES, one, 0)


def band_conv(window, k_ref, lanes, starts, rows, pad, flip):
    sums = {}
    for col_off in range(7):
        at = 6 - col_off if flip else col_off
        weights = [k_ref[6 - p if flip else p, at : at + 1, lanes] for p in range(7)]
        for start in starts:
            for src in range(window.shape[0]):
                hits = [(src - pad - row_off + 3, row_off) for row_off in range(7)]
                hits = [(out, row_off) for out, row_off in hits if 0 <= out < rows]
                if not hits:
                    continue
                cells = shifted(window, src, start, 5 + col_off)
                for out, row_off in hits:
                    term = weights[row_off] * cells
                    key = (out, start)
                    sums[key] = sums[key] + term if key in sums else term
    return sums


def conv_inner_kernel(f_ref, m_ref, k_ref, o_ref, head_ref, tail_ref, window):
    rows, cols, channels = f_ref.shape

    def block(lanes):
        masked = f_ref[:, :, lanes].astype(F32) * m_ref[...]
        window[:, 8 : 8 + cols, :] = masked
        head_ref[:, :, lanes] = masked[:3].astype(BF16)
        tail_ref[:, :, lanes] = masked[rows - 3 :].astype(BF16)
        for start in range(8, cols - 8, 8):
            sums = band_conv(window, k_ref, lanes, (start,), rows, 0, False)
            for row in range(rows):
                o_ref[row, start - 8 : start, lanes] = sums[row, start]

    each_lane_block(channels, block)


def conv_side_kernel(f_ref, m_ref, k_ref, l_ref, r_ref, o_ref, window):
    rows, cols, channels = f_ref.shape

    def block(lanes):
        window[:, 5:8, :] = l_ref[:, :, lanes].astype(F32)
        window[:, 8 : 8 + cols, :] = f_ref[:, :, lanes].astype(F32) * m_ref[...]
        window[:, 8 + cols : 11 + cols, :] = r_ref[:, :, lanes].astype(F32)
        for at, start in ((0, 0), (8, cols - 8)):
            sums = band_conv(window, k_ref, lanes, (start,), rows, 0, False)
            for row in range(rows):
                o_ref[row, at : at + 8, lanes] = sums[row, start]

    each_lane_block(channels, block)


def conv_inner(fields, mask, kernel):
    rows, cols, channels = fields.shape
    ends = (3, cols, channels)
    return pl.pallas_call(
        conv_inner_kernel,
        out_shape=[
            jax.ShapeDtypeStruct((rows, cols - 16, channels), F32),
            jax.ShapeDtypeStruct(ends, BF16),
            jax.ShapeDtypeStruct(ends, BF16),
        ],
        scratch_shapes=[pltpu.VMEM((rows, cols + 16, LANES), F32)],
        compiler_params=params(56),
        cost_estimate=estimate(4),
        name="conv_inner",
    )(fields, mask, kernel)


def conv_side(fields, mask, kernel, left, right):
    rows, cols, channels = fields.shape
    return pl.pallas_call(
        conv_side_kernel,
        out_shape=jax.ShapeDtypeStruct((rows, 16, channels), F32),
        scratch_shapes=[pltpu.VMEM((rows, cols + 16, LANES), F32)],
        compiler_params=params(56),
        cost_estimate=estimate(4),
        name="conv_side",
    )(fields, mask, kernel, left, right)


def gelu_twice(x):
    root = math.sqrt(2.0 / math.pi)
    inner = root + (root * 0.044715) * (x * x)
    tanh = jnp.tanh(x * inner)
    both = 1.0 + tanh
    value = x * both
    slope = both + value * ((1.0 - tanh) * (3.0 * inner - 2.0 * root))
    return value, slope


def expand_kernel(
    order_ref,
    inner_ref, side_ref, top_ref, bot_ref, k_ref, gain_ref, bias_ref, scale_ref, bo_ref, m_ref, cot_ref, f_ref,
    wi_ref, bi_ref, wo_ref,
    dconv_ref, mixed_ref, sums_ref, gbi_ref, sent_ref, kept_ref,
    conv, halo, inv_s, normed, normed_t, dbr, dbr_t, act, dpre, d_normed, branch, pre_s, dact_s,
):
    rows, cols, channels = conv.shape
    cells = rows * cols
    strip = 16
    chunk = 128
    step_now = pl.program_id(0)
    wide = channels // LANES

    def strips(body):
        def some(index, _):
            for more in range(4):
                row = index * 4 + more
                for at in range(0, cols, strip):
                    body(row, at, pl.ds(pl.multiple_of(row * cols + at, strip), strip))
            return 0

        lax.fori_loop(0, rows // 4, some, 0)

    @pl.when(step_now == 0)
    def _():
        conv[:, 0:8, :] = side_ref[:, 0:8, :]
        conv[:, 8 : cols - 8, :] = inner_ref[...]
        conv[:, cols - 8 : cols, :] = side_ref[:, 8:16, :]
        halo[0:3, 5 : 11 + cols, :] = top_ref[...].astype(F32)
        halo[3:6, 5 : 11 + cols, :] = bot_ref[...].astype(F32)
        for block in range(wide):
            lanes = slice(block * LANES, (block + 1) * LANES)
            for start in range(0, cols, 8):
                outs = list(range(3)) + list(range(rows - 3, rows))
                sums = {out: conv[out, start : start + 8, lanes] for out in outs}
                for col_off in range(7):
                    for src in range(6):
                        lat = src - 3 if src < 3 else rows + src - 3
                        offset = (5 + col_off) % SUB
                        base = start + (5 + col_off) // SUB * SUB
                        pair = halo[src, base : base + 2 * SUB, lanes]
                        cell = pltpu.roll(pair, 2 * SUB - offset, axis=0)[:SUB] if offset else pair[:SUB]
                        for out in outs:
                            row_off = lat - out + 3
                            if 0 <= row_off < 7:
                                tap = k_ref[row_off, col_off : col_off + 1, lanes]
                                sums[out] = sums[out] + tap * cell
                for out in outs:
                    conv[out, start : start + 8, lanes] = sums[out]
        sums_ref[...] = jnp.zeros_like(sums_ref)
        branch[...] = jnp.zeros_like(branch)
        d_normed[...] = jnp.zeros_like(d_normed)

        def standardize(row, at, here):
            x = conv[row, at : at + strip, :]
            mean = jnp.mean(x, axis=-1, keepdims=True)
            centered = x - mean
            var = jnp.mean(centered * centered, axis=-1, keepdims=True)
            inv = lax.rsqrt(var + 1e-06)
            xhat = centered * inv
            conv[row, at : at + strip, :] = xhat
            inv_s[here, :] = jnp.broadcast_to(inv, (strip, LANES))
            normed[here, :] = (xhat * gain_ref[...] + bias_ref[...]).astype(BF16)
            ocean = jnp.concatenate([m_ref[row, at : at + strip, :]] * wide, axis=1)
            grad = ocean * (scale_ref[...] * cot_ref[here, :].astype(F32))
            sums_ref[0] += grad[:SUB] + grad[SUB:]
            dbr[here, :] = (0.5 * grad).astype(BF16)

        strips(standardize)
        for at in range(0, cells, chunk):
            here = slice(at, at + chunk)
            normed_t[:, here] = normed[here, :].T
            dbr_t[:, here] = dbr[here, :].T

    block = act.shape[1]
    cut = min(block, 256)
    count = block // cut
    _, parts, _, width = sent_ref.shape
    is_sent = step_now < pl.num_programs(0) // 2

    def products(index):
        lanes = slice(index * cut, (index + 1) * cut)
        pre_s[index % 2] = jnp.dot(normed[...], wi_ref[:, lanes], preferred_element_type=F32)
        dact_s[index % 2] = lax.dot_general(
            dbr[...], wo_ref[lanes, :], (((1,), (1,)), ((), ())), preferred_element_type=F32
        )

    def activate(index):
        lanes = slice(index * cut, (index + 1) * cut)
        bias = bi_ref[:, lanes]
        total = jnp.zeros((SUB, cut), F32)
        for at in range(0, cells, strip):
            here = slice(at, at + strip)
            value, slope = gelu_twice(pre_s[index % 2, here, :] + bias)
            act[here, lanes] = value.astype(BF16)
            d_pre = dact_s[index % 2, here, :] * slope
            dpre[here, lanes] = d_pre.astype(BF16)
            total = total + (d_pre[:SUB] + d_pre[SUB:])
        gbi_ref[:, lanes] = jnp.sum(total, axis=0, keepdims=True)

    def weight_grads(index):
        left = index * cut
        for which, (rows_t, source) in enumerate(((dbr_t, act), (normed_t, dpre))):
            grad = jnp.dot(
                rows_t[...], source[:, left : left + cut], preferred_element_type=F32
            ).astype(BF16)

            def store(ref):
                size = min(width, cut)
                for at in range(0, cut, size):
                    lat, into = divmod(left + at, width)
                    ref[which, lat, :, into : into + size] = grad[:, at : at + size]

            pl.when(is_sent)(functools.partial(store, sent_ref))
            pl.when(jnp.logical_not(is_sent))(functools.partial(store, kept_ref))

    products(0)
    for index in range(count):
        if index + 1 < count:
            products(index + 1)
        activate(index)
        if index > 0:
            weight_grads(index - 1)
    weight_grads(count - 1)
    branch[...] += jnp.dot(act[...], wo_ref[...], preferred_element_type=F32)
    d_normed[...] += lax.dot_general(
        dpre[...], wi_ref[...], (((1,), (1,)), ((), ())), preferred_element_type=F32
    )

    @pl.when(step_now == pl.num_programs(0) - 1)
    def _():
        def norm_back(row, at, here):
            cot = cot_ref[here, :].astype(F32)
            ocean = jnp.concatenate([m_ref[row, at : at + strip, :]] * wide, axis=1)
            ocean = ocean * (0.5 * branch[here, :] + bo_ref[...])
            mixed_ref[here, :] = (f_ref[here, :].astype(F32) + ocean * scale_ref[...]).astype(BF16)
            term = ocean * cot
            sums_ref[1] += term[:SUB] + term[SUB:]
            grad = d_normed[here, :]
            xhat = conv[row, at : at + strip, :]
            term = grad * xhat
            sums_ref[2] += term[:SUB] + term[SUB:]
            sums_ref[3] += grad[:SUB] + grad[SUB:]
            e = grad * gain_ref[...]
            m1 = jnp.mean(e, axis=-1, keepdims=True)
            m2 = jnp.mean(term * gain_ref[...], axis=-1, keepdims=True)
            inv = jnp.concatenate([inv_s[here, :]] * wide, axis=1)
            dconv_ref[here, :] = (inv * (e - m1 - xhat * m2)).astype(BF16)

        strips(norm_back)


def expand(
    order, inner, side, top, bot, kernel, gain, bias, scale, b_out, mask, cot, fields, w_in, b_in, w_out, n_lon, n_lat
):
    rows, _, channels = inner.shape
    hidden = w_in.shape[1]
    cells, _ = cot.shape
    cols = cells // rows
    block = hidden // n_lon
    split = n_lat if (block // n_lat) % LANES == 0 else 1
    turn = n_lon // 2
    grads = (split, channels, block // split)
    given = (inner, side, top, bot, kernel, gain, bias, scale, b_out, mask, cot, fields)

    def sent_at(h, order):
        return (0, jnp.minimum(h, turn - 1), 0, 0, 0)

    def kept_at(h, order):
        return (0, jnp.maximum(h - turn, 0), 0, 0, 0)

    return pl.pallas_call(
        expand_kernel,
        grid_spec=pltpu.PrefetchScalarGridSpec(
            num_scalar_prefetch=1,
            grid=(n_lon,),
            in_specs=[once(x.shape) for x in given]
            + [
                pl.BlockSpec((channels, block), lambda h, order: (0, order[h])),
                pl.BlockSpec((1, block), lambda h, order: (0, order[h])),
                pl.BlockSpec((block, channels), lambda h, order: (order[h], 0)),
            ],
            out_specs=[
                once((cells, channels)),
                once((cells, channels)),
                once((4, SUB, channels)),
                pl.BlockSpec((1, block), lambda h, order: (0, order[h])),
                pl.BlockSpec((2, None) + grads, sent_at),
                pl.BlockSpec((2, None) + grads, kept_at),
            ],
            scratch_shapes=[
                pltpu.VMEM((rows, cols, channels), F32),
                pltpu.VMEM((6, cols + 16, channels), F32),
                pltpu.VMEM((cells, LANES), F32),
                pltpu.VMEM((cells, channels), BF16),
                pltpu.VMEM((channels, cells), BF16),
                pltpu.VMEM((cells, channels), BF16),
                pltpu.VMEM((channels, cells), BF16),
                pltpu.VMEM((cells, block), BF16),
                pltpu.VMEM((cells, block), BF16),
                pltpu.VMEM((cells, channels), F32),
                pltpu.VMEM((cells, channels), F32),
                pltpu.VMEM((2, cells, min(block, 256)), F32),
                pltpu.VMEM((2, cells, min(block, 256)), F32),
            ],
        ),
        out_shape=[
            jax.ShapeDtypeStruct((cells, channels), BF16),
            jax.ShapeDtypeStruct((cells, channels), BF16),
            jax.ShapeDtypeStruct((4, SUB, channels), F32),
            jax.ShapeDtypeStruct((1, hidden), F32),
            jax.ShapeDtypeStruct((2, turn) + grads, BF16),
            jax.ShapeDtypeStruct((2, turn) + grads, BF16),
        ],
        compiler_params=params(56),
        cost_estimate=estimate(20),
        name="expand",
    )(order, *given, w_in, b_in, w_out)


def filter_grad_kernel(
    f_ref, m_ref, l_ref, r_ref, t_ref, b_ref, d_ref, sums_ref, gbi_ref, o_ref, window, grad
):
    rows, cols, channels = f_ref.shape
    blocks = channels // LANES

    def block(index, _):
        lanes = lane_block(index)
        window[0:3, 5 : 11 + cols, :] = t_ref[:, :, lanes].astype(F32)
        window[3 : 3 + rows, 5:8, :] = l_ref[:, :, lanes].astype(F32)
        window[3 : 3 + rows, 8 : 8 + cols, :] = f_ref[:, :, lanes].astype(F32) * m_ref[...]
        window[3 : 3 + rows, 8 + cols : 11 + cols, :] = r_ref[:, :, lanes].astype(F32)
        window[3 + rows : 6 + rows, 5 : 11 + cols, :] = b_ref[:, :, lanes].astype(F32)
        grad[...] = d_ref[:, :, lanes].astype(F32)
        for col_off in range(7):

            def band(step, sums):
                start = pl.multiple_of(step * SUB, SUB)
                sums = list(sums)
                held = {}
                for src in range(rows + 6):
                    if src < rows:
                        held[src] = grad[src, pl.ds(start, SUB), :]
                    cells = shifted(window, src, start, 5 + col_off)
                    for row_off in range(7):
                        out = src - row_off
                        if 0 <= out < rows:
                            sums[row_off] = sums[row_off] + held[out] * cells
                return tuple(sums)

            sums = tuple(jnp.zeros((SUB, LANES), F32) for _ in range(7))
            sums = lax.fori_loop(0, cols // SUB, band, sums)
            for row_off in range(7):
                at = row_off * 8 + col_off
                o_ref[index, at : at + 1, :] = jnp.sum(sums[row_off], axis=0, keepdims=True)
        for row_off in range(7):
            o_ref[index, row_off * 8 + 7 : row_off * 8 + 8, :] = jnp.zeros((1, LANES), F32)
        for at, source in enumerate((1, 2, 3, 0)):
            o_ref[index, 56 + at : 57 + at, :] = jnp.sum(sums_ref[source, :, lanes], axis=0, keepdims=True)
        for at in range(4):
            o_ref[index, 60 + at : 61 + at, :] = gbi_ref[:, lane_block(at * blocks + index)]
        return 0

    lax.fori_loop(0, blocks, block, 0)


def filter_grad(fields, mask, left, right, top, bot, d_conv, sums, gbi):
    rows, cols, channels = fields.shape
    return pl.pallas_call(
        filter_grad_kernel,
        out_shape=jax.ShapeDtypeStruct((channels // LANES, 64, LANES), F32),
        scratch_shapes=[
            pltpu.VMEM((rows + 6, cols + 16, LANES), F32),
            pltpu.VMEM((rows, cols, LANES), F32),
        ],
        compiler_params=params(56),
        cost_estimate=estimate(4),
        name="filter_grad",
    )(fields, mask, left, right, top, bot, d_conv, sums, gbi)


def input_grad_kernel(first_block, parts, d_ref, l_ref, r_ref, t_ref, b_ref, k_ref, m_ref, cot_ref, *rest):
    o_ref, window, grad = rest[-3:]
    rows, cols, channels = d_ref.shape
    tall = o_ref.shape[0]

    def fill(first, lanes):
        low, high = max(0, first - 3), min(rows, first + tall + 3)
        inside = slice(low - first + 3, high - first + 3)
        if first < 3:
            window[0 : 3 - first, 5 : 11 + cols, :] = t_ref[first:3, :, lanes].astype(F32)
        if first + tall > rows - 3:
            below = first + tall + 3 - rows
            window[tall + 6 - below : tall + 6, 5 : 11 + cols, :] = b_ref[:below, :, lanes].astype(F32)
        window[inside, 5:8, :] = l_ref[low:high, :, lanes].astype(F32)
        window[inside, 8 : 8 + cols, :] = d_ref[low:high, :, lanes].astype(F32)
        window[inside, 8 + cols : 11 + cols, :] = r_ref[low:high, :, lanes].astype(F32)

    def block(lanes):
        for at in range(parts):
            pl.when(pl.program_id(0) == at)(functools.partial(fill, (first_block + at) * tall, lanes))
        sums = band_conv(window, k_ref, lanes, range(0, cols, SUB), tall, 3, True)
        for (row, start), value in sums.items():
            grad[row, start : start + SUB, :] = value
        o_ref[:, :, lanes] = (cot_ref[:, :, lanes].astype(F32) + m_ref[...] * grad[...]).astype(BF16)

    each_lane_block(channels, block)


def input_grad(d_conv, left, right, top, bot, kernel, mask, cot, first, parts, old=None):
    rows, cols, channels = d_conv.shape
    tall = rows // 4

    def rows_of(width):
        return pl.BlockSpec((tall, cols, width), lambda i: (first + i, 0, 0))

    whole = (d_conv, left, right, top, bot, kernel)
    more = [] if old is None else [old]
    return pl.pallas_call(
        functools.partial(input_grad_kernel, first, parts),
        grid=(parts,),
        out_shape=jax.ShapeDtypeStruct((rows, cols, channels), BF16),
        in_specs=[once(x.shape) for x in whole]
        + [rows_of(LANES), rows_of(channels)]
        + [UNUSED] * len(more),
        out_specs=rows_of(channels),
        scratch_shapes=[
            pltpu.VMEM((tall + 6, cols + 16, LANES), F32),
            pltpu.VMEM((tall, cols, LANES), F32),
        ],
        input_output_aliases={8: 0} if more else {},
        compiler_params=params(56),
        cost_estimate=estimate(4),
        name="input_grad",
    )(*whole, mask, cot, *more)


def swap(values, axis, bit):
    count = lax.axis_size(axis)
    return lax.ppermute(values, axis, [(i, i ^ bit) for i in range(count)])


def bits_of(axis):
    return [1 << k for k in range(int(math.log2(lax.axis_size(axis))))]


def after(value, *others):
    return lax.optimization_barrier((value,) + others)[0]


def halves(values, axis, dim, bit):
    mine = (lax.axis_index(axis) // bit) % 2 == 1
    shape = values.shape
    paired = values.reshape(shape[:dim] + (shape[dim] // 2, 2) + shape[dim + 1 :])
    low = lax.index_in_dim(paired, 0, dim + 1, keepdims=False)
    high = lax.index_in_dim(paired, 1, dim + 1, keepdims=False)
    return jnp.where(mine, high, low), jnp.where(mine, low, high).astype(BF16)


def side_halo(last, first):
    count = lax.axis_size("lon")
    ahead = [(i, (i + 1) % count) for i in range(count)]
    back = [((i + 1) % count, i) for i in range(count)]
    return lax.ppermute(last, "lon", ahead), lax.ppermute(first, "lon", back)


def end_rows(head, tail, left, right):
    rows = left.shape[0]
    return (
        jnp.concatenate([left[rows - 3 :], tail, right[rows - 3 :]], axis=1),
        jnp.concatenate([left[:3], head, right[:3]], axis=1),
    )


def end_halo(tail, head):
    count = lax.axis_size("lat")
    ahead = [(i, i + 1) for i in range(count - 1)]
    back = [(i + 1, i) for i in range(count - 1)]
    return lax.ppermute(tail, "lat", ahead), lax.ppermute(head, "lat", back)


def per_device(
    fields,
    land_mask,
    cotangent,
    kernel,
    layer_norm_gain,
    layer_norm_bias,
    w_in,
    b_in,
    w_out,
    b_out,
    layer_scale,
):
    rows, cols, channels = fields.shape
    cells = rows * cols
    hidden = w_in.shape[1]
    n_lon, n_lat = lax.axis_size("lon"), lax.axis_size("lat")
    gain, bias = layer_norm_gain.reshape(1, -1), layer_norm_bias.reshape(1, -1)
    scale = layer_scale.reshape(1, -1)
    cot_rows = cotangent.reshape(cells, channels)
    mask = jnp.broadcast_to(land_mask.astype(F32)[:, :, None], (rows, cols, LANES))
    ocean = land_mask.astype(BF16)[:, :, None]
    left, right = side_halo(fields[:, cols - 3 :] * ocean[:, cols - 3 :], fields[:, :3] * ocean[:, :3])
    inner, head, tail = conv_inner(fields, mask, kernel)
    top, bot = end_halo(*end_rows(head, tail, left, right))
    side = conv_side(fields, mask, kernel, left, right)

    lon = lax.axis_index("lon")
    core, side_y = lon % 2, (lon // 2) % 2
    quads = 4 * jnp.arange(n_lon // 4, dtype=jnp.int32)
    order = jnp.concatenate(
        [quads + 2 * y + c for c in (1 - core, core) for y in (1 - side_y, side_y)]
    )
    d_conv, mixed, sums, g_bi, sent, kept = expand(
        order, inner, side, top, bot, kernel, gain, bias, scale, b_out.reshape(1, -1), mask, cot_rows,
        fields.reshape(cells, channels), w_in, b_in.reshape(1, -1), w_out, n_lon, n_lat,
    )
    got = swap(sent, "lon", 1)
    d_conv = d_conv.reshape(rows, cols, channels)
    d_left, d_right = side_halo(d_conv[:, cols - 3 :], d_conv[:, :3])

    far = n_lon // 4
    border = channels * 5 // 8
    lon_bits = [("lon", 1, bit) for bit in bits_of("lon")[2:]]
    lat_bits = [("lat", 2, bit) for bit in bits_of("lat")]

    def split_lat(x):
        if x.shape[2] != n_lat:
            x = x.reshape(x.shape[0], x.shape[1], x.shape[3], n_lat, -1).transpose(0, 1, 3, 2, 4)
        return x

    def pair(lons, piece, last=None):
        a, b = (kept, got) if last is None else (after(kept, last), after(got, last))
        return split_lat(a[:, lons, :, piece].astype(F32) + b[:, lons, :, piece].astype(F32))

    def fold(mine, sent, axis, bit, last):
        return after(mine, last) + after(swap(sent, axis, bit), last).astype(F32)

    first, second = slice(0, border), slice(border, channels)
    near_lons, far_lons = slice(far, 2 * far), slice(0, far)
    far_first = pair(far_lons, first).astype(BF16)
    got_first = swap(far_first, "lon", 2)
    cut_b = halves(pair(slice(0, 2 * far), second), *lat_bits[0])
    d_tail, d_head = end_rows(
        d_conv[:3], d_conv[rows - 3 :],
        after(d_left, far_first, cut_b[1]), after(d_right, far_first, cut_b[1]),
    )
    d_top, d_bot = end_halo(d_tail, d_head)
    for (axis, _, bit), follow in zip(lat_bits[:-1], lat_bits[1:]):
        cut_b = halves(fold(*cut_b, axis, bit, d_head), *follow)

    def pack(sent, small):
        return jnp.concatenate([sent.reshape(-1, LANES), small.astype(BF16).reshape(-1, LANES)])

    def ride(load, sent, small, axis, bit, last):
        came = after(swap(load, axis, bit), last)
        size = sent.size // LANES
        own = after(lax.reduce_precision(small, 8, 7), last)
        return came[:size].reshape(sent.shape).astype(F32), own + came[size:].astype(F32).reshape(small.shape)

    small = filter_grad(
        after(fields, d_tail, d_head, far_first, cut_b[1]),
        mask, left, right, top, bot, d_conv, sums, g_bi,
    )
    small = small + swap(small, "lon", 1)
    whole = pair(near_lons, first, small) + after(got_first, small).astype(F32)
    back = (d_left, d_right, d_top, d_bot, kernel, mask, cotangent)
    grad_fields, block = None, 0
    steps = lon_bits + lat_bits
    for index, (axis, dim, bit) in enumerate(steps):
        mine, sent = halves(whole, axis, dim, bit)
        load = pack(sent, small)
        last = load
        if index >= len(steps) - 2:
            count = 2 if grad_fields is None else 1
            last = grad_fields = input_grad(after(d_conv, load), *back, block, count, grad_fields)
            block += count
        came, small = ride(load, sent, small, axis, bit, last)
        whole = after(mine, last) + came
    whole_b = fold(*cut_b, lat_bits[-1][0], lat_bits[-1][2], load)
    far_second = whole_b[:, far_lons].astype(BF16)
    load = pack(far_second, small)
    last = grad_fields = input_grad(after(d_conv, load), *back, block, 1, grad_fields)
    came, small = ride(load, far_second, small, "lon", 2, last)
    whole_b = after(whole_b, last)[:, near_lons] + came
    for axis, dim, bit in lon_bits:
        whole_b = fold(*halves(whole_b, axis, dim, bit), axis, bit, last)
    owned = (whole, whole_b)
    grad_w = jnp.concatenate([x[:, 0, 0] for x in owned], axis=1)
    small = small.transpose(1, 0, 2).reshape(8, 8, channels)
    return (
        mixed.reshape(rows, cols, channels),
        grad_fields,
        small[:7, :7],
        small[7, 1],
        small[7, 2],
        grad_w[1],
        small[7, 4:].reshape(hidden),
        grad_w[0].T,
        small[7, 3],
        small[7, 0],
    )


def solution(mesh):
    placed = (
        P(("grp", "lat"), "lon", None),
        P(("grp", "lat"), "lon"),
        P(("grp", "lat"), "lon", None),
        P(),
        P(),
        P(),
        P(),
        P(),
        P(),
        P(),
        P(),
    )
    return jax.shard_map(
        per_device,
        mesh=mesh,
        in_specs=placed,
        out_specs=(
            P(("grp", "lat"), "lon", None),
            P(("grp", "lat"), "lon", None),
            P("grp", None, None),
            P("grp"),
            P("grp"),
            P("grp", ("lon", "lat")),
            P("grp"),
            P(("lon", "lat"), "grp"),
            P("grp"),
            P("grp"),
        ),
        check_vma=False,
    )
```

```python
import functools
import math

import jax
import jax.numpy as jnp
from jax import lax
from jax.experimental import pallas as pl
from jax.experimental.pallas import tpu as pltpu
from jax.sharding import PartitionSpec as P

F32 = jnp.float32
BF16 = jnp.bfloat16
LANES = 128
SUB = 8


def params(mib):
    return pltpu.CompilerParams(vmem_limit_bytes=mib * 1024 * 1024)


def estimate(micros):
    return pl.CostEstimate(
        flops=int(micros * 1.15e9), bytes_accessed=int(micros * 3.6e6), transcendentals=0
    )


def once(shape):
    zeros = (0,) * len(shape)
    return pl.BlockSpec(shape, lambda *_: zeros, pipeline_mode=pl.Buffered(1))


UNUSED = pl.BlockSpec(memory_space=pl.ANY)


def whole_spec(shape):
    zeros = (0,) * len(shape)
    return pl.BlockSpec(shape, lambda *_: zeros)


def shifted(window, row, start, offset):
    return window[row, pl.ds(start + offset, SUB), :]


def lane_block(index):
    return pl.ds(pl.multiple_of(index * LANES, LANES), LANES)


def each_lane_block(channels, body):
    def one(index, _):
        body(lane_block(index))
        return 0

    lax.fori_loop(0, channels // LANES, one, 0)


def band_conv(window, k_ref, lanes, starts, rows, pad, flip):
    sums = {}
    for col_off in range(7):
        at = 6 - col_off if flip else col_off
        weights = [k_ref[6 - p if flip else p, at : at + 1, lanes] for p in range(7)]
        for start in starts:
            for src in range(window.shape[0]):
                hits = [(src - pad - row_off + 3, row_off) for row_off in range(7)]
                hits = [(out, row_off) for out, row_off in hits if 0 <= out < rows]
                if not hits:
                    continue
                cells = shifted(window, src, start, 5 + col_off)
                for out, row_off in hits:
                    term = weights[row_off] * cells
                    key = (out, start)
                    sums[key] = sums[key] + term if key in sums else term
    return sums


def gelu_twice(x):
    root = math.sqrt(2.0 / math.pi)
    inner = root + (root * 0.044715) * (x * x)
    tanh = jnp.tanh(x * inner)
    both = 1.0 + tanh
    value = x * both
    slope = both + value * ((1.0 - tanh) * (3.0 * inner - 2.0 * root))
    return value, slope


def expand_kernel(
    order_ref,
    l_ref, r_ref, t_ref, b_ref, k_ref, gain_ref, bias_ref, scale_ref, bo_ref, m_ref, cot_ref, f_ref,
    wi_ref, bi_ref, wo_ref,
    dconv_ref, mixed_ref, sums_ref, gbi_ref, sent_ref, kept_ref,
    window, conv, xhat_s, inv_s, normed, normed_t, dbr, dbr_t, act, dpre, d_normed, branch, pre_s, dact_s,
):
    rows, cols, channels = f_ref.shape
    cells = rows * cols
    strip = 16
    chunk = 128
    step_now = pl.program_id(0)
    wide = channels // LANES

    def strips(body, sums):
        def some(index, sums):
            places = [
                (2 * index + more, at, pl.ds(pl.multiple_of((2 * index + more) * cols + at, strip), strip))
                for more in range(2)
                for at in range(0, cols, strip)
            ]
            return body(places, sums)

        return lax.fori_loop(0, rows // 2, some, sums)

    def folded(values):
        return sum(value[:SUB] + value[SUB:] for value in values)

    def mean(values):
        return [jnp.mean(value, axis=-1, keepdims=True) for value in values]

    def ocean(places):
        return [jnp.concatenate([m_ref[row, at : at + strip, :]] * wide, axis=1) for row, at, _ in places]

    zero = jnp.zeros((SUB, channels), F32)

    @pl.when(step_now == 0)
    def _():
        branch[...] = jnp.zeros_like(branch)
        d_normed[...] = jnp.zeros_like(d_normed)

        def convolve(lanes):
            fill_window(window, f_ref[:, :, lanes].astype(F32) * m_ref[...], l_ref, r_ref, t_ref, b_ref, lanes)
            for start in range(0, cols, SUB):
                sums = band_conv(window, k_ref, lanes, (start,), rows, 3, False)
                for row in range(rows):
                    conv[row, start : start + SUB, lanes] = sums[row, start]

        each_lane_block(channels, convolve)

        def standardize(places, total):
            xs = [conv[row, at : at + strip, :] for row, at, _ in places]
            centered = [x - average for x, average in zip(xs, mean(xs))]
            invs = [lax.rsqrt(var + 1e-06) for var in mean([x * x for x in centered])]
            xhats = [x * inv for x, inv in zip(centered, invs)]
            grads = [
                mask * (scale_ref[...] * cot_ref[here, :].astype(F32))
                for mask, (_, _, here) in zip(ocean(places), places)
            ]
            for (_, _, here), xhat, inv, grad in zip(places, xhats, invs, grads):
                xhat_s[here, :] = xhat
                inv_s[here, :] = jnp.broadcast_to(inv, (strip, LANES))
                normed[here, :] = (xhat * gain_ref[...] + bias_ref[...]).astype(BF16)
                dbr[here, :] = (0.5 * grad).astype(BF16)
            return total + folded(grads)

        sums_ref[0] = strips(standardize, zero)
        for at in range(0, cells, chunk):
            here = slice(at, at + chunk)
            normed_t[:, here] = normed[here, :].T
            dbr_t[:, here] = dbr[here, :].T

    block = act.shape[1]
    cut = min(block, 256)
    count = block // cut
    _, parts, _, width = sent_ref.shape
    is_sent = step_now < pl.num_programs(0) // 2

    def products(index):
        lanes = slice(index * cut, (index + 1) * cut)
        pre_s[index % 2] = jnp.dot(normed[...], wi_ref[:, lanes], preferred_element_type=F32)
        dact_s[index % 2] = lax.dot_general(
            dbr[...], wo_ref[lanes, :], (((1,), (1,)), ((), ())), preferred_element_type=F32
        )

    def activate(index):
        lanes = slice(index * cut, (index + 1) * cut)
        bias = bi_ref[:, lanes]
        total = jnp.zeros((SUB, cut), F32)
        for at in range(0, cells, strip):
            here = slice(at, at + strip)
            value, slope = gelu_twice(pre_s[index % 2, here, :] + bias)
            act[here, lanes] = value.astype(BF16)
            d_pre = dact_s[index % 2, here, :] * slope
            dpre[here, lanes] = d_pre.astype(BF16)
            total = total + (d_pre[:SUB] + d_pre[SUB:])
        gbi_ref[:, lanes] = jnp.sum(total, axis=0, keepdims=True)

    def weight_grads(index):
        left = index * cut
        for which, (rows_t, source) in enumerate(((dbr_t, act), (normed_t, dpre))):
            grad = jnp.dot(
                rows_t[...], source[:, left : left + cut], preferred_element_type=F32
            ).astype(BF16)

            def store(ref):
                size = min(width, cut)
                for at in range(0, cut, size):
                    lat, into = divmod(left + at, width)
                    ref[which, lat, :, into : into + size] = grad[:, at : at + size]

            pl.when(is_sent)(functools.partial(store, sent_ref))
            pl.when(jnp.logical_not(is_sent))(functools.partial(store, kept_ref))

    products(0)
    for index in range(count):
        if index + 1 < count:
            products(index + 1)
        activate(index)
        if index > 0:
            weight_grads(index - 1)
    weight_grads(count - 1)
    branch[...] += jnp.dot(act[...], wo_ref[...], preferred_element_type=F32)
    d_normed[...] += lax.dot_general(
        dpre[...], wi_ref[...], (((1,), (1,)), ((), ())), preferred_element_type=F32
    )

    @pl.when(step_now == pl.num_programs(0) - 1)
    def _():
        def norm_back(places, sums):
            heres = [here for _, _, here in places]
            branches = [
                mask * (0.5 * branch[here, :] + bo_ref[...]) for mask, here in zip(ocean(places), heres)
            ]
            xhats = [xhat_s[here, :] for here in heres]
            grads = [d_normed[here, :] for here in heres]
            terms = [grad * xhat for grad, xhat in zip(grads, xhats)]
            es = [grad * gain_ref[...] for grad in grads]
            m1s = mean(es)
            m2s = mean([e * xhat for e, xhat in zip(es, xhats)])
            for (row, at, here), e, xhat, m1, m2, value in zip(places, es, xhats, m1s, m2s, branches):
                inv = jnp.concatenate([inv_s[here, :]] * wide, axis=1)
                dconv_ref[here, :] = (inv * (e - m1 - xhat * m2)).astype(BF16)
                field = f_ref[row, at : at + strip, :].astype(F32)
                mixed_ref[here, :] = (field + value * scale_ref[...]).astype(BF16)
            products = [value * cot_ref[here, :].astype(F32) for value, here in zip(branches, heres)]
            return tuple(total + folded(x) for total, x in zip(sums, (products, terms, grads)))

        sums_ref[1], sums_ref[2], sums_ref[3] = strips(norm_back, (zero, zero, zero))


def expand(
    order, left, right, top, bot, kernel, gain, bias, scale, b_out, mask, cot, fields, w_in, b_in, w_out, n_lon, n_lat
):
    rows, cols, channels = fields.shape
    hidden = w_in.shape[1]
    cells = rows * cols
    block = hidden // n_lon
    split = n_lat if (block // n_lat) % LANES == 0 else 1
    turn = n_lon // 2
    grads = (split, channels, block // split)
    given = (left, right, top, bot, kernel, gain, bias, scale, b_out, mask, cot, fields)

    def sent_at(h, order):
        return (0, jnp.minimum(h, turn - 1), 0, 0, 0)

    def kept_at(h, order):
        return (0, jnp.maximum(h - turn, 0), 0, 0, 0)

    return pl.pallas_call(
        expand_kernel,
        grid_spec=pltpu.PrefetchScalarGridSpec(
            num_scalar_prefetch=1,
            grid=(n_lon,),
            in_specs=[once(x.shape) for x in given]
            + [
                pl.BlockSpec((channels, block), lambda h, order: (0, order[h])),
                pl.BlockSpec((1, block), lambda h, order: (0, order[h])),
                pl.BlockSpec((block, channels), lambda h, order: (order[h], 0)),
            ],
            out_specs=[
                once((cells, channels)),
                once((cells, channels)),
                once((4, SUB, channels)),
                pl.BlockSpec((1, block), lambda h, order: (0, order[h])),
                pl.BlockSpec((2, None) + grads, sent_at),
                pl.BlockSpec((2, None) + grads, kept_at),
            ],
            scratch_shapes=[
                pltpu.VMEM((rows + 6, cols + 16, LANES), F32),
                pltpu.VMEM((rows, cols, channels), F32),
                pltpu.VMEM((cells, channels), F32),
                pltpu.VMEM((cells, LANES), F32),
                pltpu.VMEM((cells, channels), BF16),
                pltpu.VMEM((channels, cells), BF16),
                pltpu.VMEM((cells, channels), BF16),
                pltpu.VMEM((channels, cells), BF16),
                pltpu.VMEM((cells, block), BF16),
                pltpu.VMEM((cells, block), BF16),
                pltpu.VMEM((cells, channels), F32),
                pltpu.VMEM((cells, channels), F32),
                pltpu.VMEM((2, cells, min(block, 256)), F32),
                pltpu.VMEM((2, cells, min(block, 256)), F32),
            ],
        ),
        out_shape=[
            jax.ShapeDtypeStruct((cells, channels), BF16),
            jax.ShapeDtypeStruct((cells, channels), BF16),
            jax.ShapeDtypeStruct((4, SUB, channels), F32),
            jax.ShapeDtypeStruct((1, hidden), F32),
            jax.ShapeDtypeStruct((2, turn) + grads, BF16),
            jax.ShapeDtypeStruct((2, turn) + grads, BF16),
        ],
        compiler_params=params(56),
        cost_estimate=estimate(20),
        name="expand",
    )(order, *given, w_in, b_in, w_out)


def fill_window(window, center, l_ref, r_ref, t_ref, b_ref, lanes):
    rows, cols, _ = center.shape
    window[0:3, 5 : 11 + cols, :] = t_ref[:, :, lanes].astype(F32)
    window[3 : 3 + rows, 5:8, :] = l_ref[:, :, lanes].astype(F32)
    window[3 : 3 + rows, 8 : 8 + cols, :] = center
    window[3 : 3 + rows, 8 + cols : 11 + cols, :] = r_ref[:, :, lanes].astype(F32)
    window[3 + rows : 6 + rows, 5 : 11 + cols, :] = b_ref[:, :, lanes].astype(F32)


def filter_grad_kernel(
    f_ref, m_ref, l_ref, r_ref, t_ref, b_ref, d_ref, sums_ref, gbi_ref, o_ref, window, grad
):
    rows, cols, channels = f_ref.shape
    blocks = channels // LANES

    def block(index, _):
        lanes = lane_block(index)
        fill_window(window, f_ref[:, :, lanes].astype(F32) * m_ref[...], l_ref, r_ref, t_ref, b_ref, lanes)
        grad[...] = d_ref[:, :, lanes].astype(F32)
        for col_off in range(7):

            def band(step, sums):
                start = pl.multiple_of(step * SUB, SUB)
                sums = list(sums)
                held = {}
                for src in range(rows + 6):
                    if src < rows:
                        held[src] = grad[src, pl.ds(start, SUB), :]
                    cells = shifted(window, src, start, 5 + col_off)
                    for row_off in range(7):
                        out = src - row_off
                        if 0 <= out < rows:
                            sums[row_off] = sums[row_off] + held[out] * cells
                return tuple(sums)

            sums = tuple(jnp.zeros((SUB, LANES), F32) for _ in range(7))
            sums = lax.fori_loop(0, cols // SUB, band, sums)
            for row_off in range(7):
                at = row_off * 8 + col_off
                o_ref[index, at : at + 1, :] = jnp.sum(sums[row_off], axis=0, keepdims=True)
        for row_off in range(7):
            o_ref[index, row_off * 8 + 7 : row_off * 8 + 8, :] = jnp.zeros((1, LANES), F32)
        for at, source in enumerate((1, 2, 3, 0)):
            o_ref[index, 56 + at : 57 + at, :] = jnp.sum(sums_ref[source, :, lanes], axis=0, keepdims=True)
        for at in range(4):
            o_ref[index, 60 + at : 61 + at, :] = gbi_ref[:, lane_block(at * blocks + index)]
        return 0

    lax.fori_loop(0, blocks, block, 0)


def filter_grad(fields, mask, left, right, top, bot, d_conv, sums, gbi):
    rows, cols, channels = fields.shape
    return pl.pallas_call(
        filter_grad_kernel,
        out_shape=jax.ShapeDtypeStruct((channels // LANES, 64, LANES), F32),
        scratch_shapes=[
            pltpu.VMEM((rows + 6, cols + 16, LANES), F32),
            pltpu.VMEM((rows, cols, LANES), F32),
        ],
        compiler_params=params(56),
        cost_estimate=estimate(4),
        name="filter_grad",
    )(fields, mask, left, right, top, bot, d_conv, sums, gbi)


def input_grad_kernel(first, d_ref, l_ref, r_ref, t_ref, b_ref, k_ref, m_ref, cot_ref, *rest):
    o_ref, window, grad = rest[-3:]
    rows, cols, channels = d_ref.shape
    tall = o_ref.shape[0]
    low, high = max(0, first - 3), min(rows, first + tall + 3)
    inside = slice(low - first + 3, high - first + 3)
    group = 32 // tall * SUB

    def block(lanes):
        if first < 3:
            window[0 : 3 - first, 5 : 11 + cols, :] = t_ref[first:3, :, lanes].astype(F32)
        if first + tall > rows - 3:
            below = first + tall + 3 - rows
            window[tall + 6 - below : tall + 6, 5 : 11 + cols, :] = b_ref[:below, :, lanes].astype(F32)
        window[inside, 5:8, :] = l_ref[low:high, :, lanes].astype(F32)
        window[inside, 8 : 8 + cols, :] = d_ref[low:high, :, lanes].astype(F32)
        window[inside, 8 + cols : 11 + cols, :] = r_ref[low:high, :, lanes].astype(F32)
        for left in range(0, cols, group):
            starts = range(left, min(left + group, cols), SUB)
            sums = band_conv(window, k_ref, lanes, starts, tall, 3, True)
            for (row, start), value in sums.items():
                grad[row, start : start + SUB, :] = value
        o_ref[:, :, lanes] = (cot_ref[:, :, lanes].astype(F32) + m_ref[...] * grad[...]).astype(BF16)

    each_lane_block(channels, block)


def input_grad(d_conv, left, right, top, bot, kernel, mask, cot, first, quarters, old=None):
    rows, cols, channels = d_conv.shape
    tall = rows // 4 * quarters

    def rows_of(width):
        return pl.BlockSpec((tall, cols, width), lambda i: (first // quarters, 0, 0))

    whole = (d_conv, left, right, top, bot, kernel)
    more = [] if old is None else [old]
    return pl.pallas_call(
        functools.partial(input_grad_kernel, rows // 4 * first),
        grid=(1,),
        out_shape=jax.ShapeDtypeStruct((rows, cols, channels), BF16),
        in_specs=[once(x.shape) for x in whole]
        + [rows_of(LANES), rows_of(channels)]
        + [UNUSED] * len(more),
        out_specs=rows_of(channels),
        scratch_shapes=[
            pltpu.VMEM((tall + 6, cols + 16, LANES), F32),
            pltpu.VMEM((tall, cols, LANES), F32),
        ],
        input_output_aliases={8: 0} if more else {},
        compiler_params=params(56),
        cost_estimate=estimate(4),
        name="input_grad",
    )(*whole, mask, cot, *more)


def swap(values, axis, bit):
    count = lax.axis_size(axis)
    return lax.ppermute(values, axis, [(i, i ^ bit) for i in range(count)])


def bits_of(axis):
    return [1 << k for k in range(int(math.log2(lax.axis_size(axis))))]


def after(value, *others):
    return lax.optimization_barrier((value,) + others)[0]


def halves(values, axis, dim, bit):
    mine = (lax.axis_index(axis) // bit) % 2 == 1
    shape = values.shape
    paired = values.reshape(shape[:dim] + (shape[dim] // 2, 2) + shape[dim + 1 :])
    low = lax.index_in_dim(paired, 0, dim + 1, keepdims=False)
    high = lax.index_in_dim(paired, 1, dim + 1, keepdims=False)
    return jnp.where(mine, high, low), jnp.where(mine, low, high).astype(BF16)


def side_halo(last, first):
    count = lax.axis_size("lon")
    ahead = [(i, (i + 1) % count) for i in range(count)]
    back = [((i + 1) % count, i) for i in range(count)]
    return lax.ppermute(last, "lon", ahead), lax.ppermute(first, "lon", back)


def end_rows(head, tail, left, right):
    rows = left.shape[0]
    return (
        jnp.concatenate([left[rows - 3 :], tail, right[rows - 3 :]], axis=1),
        jnp.concatenate([left[:3], head, right[:3]], axis=1),
    )


def end_halo(tail, head):
    count = lax.axis_size("lat")
    ahead = [(i, i + 1) for i in range(count - 1)]
    back = [(i + 1, i) for i in range(count - 1)]
    return lax.ppermute(tail, "lat", ahead), lax.ppermute(head, "lat", back)


def per_device(
    fields,
    land_mask,
    cotangent,
    kernel,
    layer_norm_gain,
    layer_norm_bias,
    w_in,
    b_in,
    w_out,
    b_out,
    layer_scale,
):
    rows, cols, channels = fields.shape
    cells = rows * cols
    hidden = w_in.shape[1]
    n_lon, n_lat = lax.axis_size("lon"), lax.axis_size("lat")
    gain, bias = layer_norm_gain.reshape(1, -1), layer_norm_bias.reshape(1, -1)
    scale = layer_scale.reshape(1, -1)
    cot_rows = cotangent.reshape(cells, channels)
    mask = jnp.broadcast_to(land_mask.astype(F32)[:, :, None], (rows, cols, LANES))
    ocean = land_mask.astype(BF16)[:, :, None]
    left, right = side_halo(fields[:, cols - 3 :] * ocean[:, cols - 3 :], fields[:, :3] * ocean[:, :3])
    lon = lax.axis_index("lon")
    core, side_y = lon % 2, (lon // 2) % 2
    quads = 4 * jnp.arange(n_lon // 4, dtype=jnp.int32)
    order = jnp.concatenate(
        [quads + 2 * y + c for c in (1 - core, core) for y in (1 - side_y, side_y)]
    )
    top, bot = end_halo(
        *end_rows(
            fields[:3] * ocean[:3], fields[rows - 3 :] * ocean[rows - 3 :],
            after(left, mask, order), after(right, mask, order),
        )
    )

    d_conv, mixed, sums, g_bi, sent, kept = expand(
        order, left, right, top, bot, kernel, gain, bias, scale, b_out.reshape(1, -1), mask, cot_rows,
        fields, w_in, b_in.reshape(1, -1), w_out, n_lon, n_lat,
    )
    got = swap(sent, "lon", 1)
    d_conv = d_conv.reshape(rows, cols, channels)
    d_left, d_right = side_halo(d_conv[:, cols - 3 :], d_conv[:, :3])

    far = n_lon // 4
    border = channels * 5 // 8
    lon_bits = [("lon", 1, bit) for bit in bits_of("lon")[2:]]
    lat_bits = [("lat", 2, bit) for bit in bits_of("lat")]

    def split_lat(x):
        if x.shape[2] != n_lat:
            x = x.reshape(x.shape[0], x.shape[1], x.shape[3], n_lat, -1).transpose(0, 1, 3, 2, 4)
        return x

    def pair(lons, piece, last=None):
        a, b = (kept, got) if last is None else (after(kept, last), after(got, last))
        return split_lat(a[:, lons, :, piece].astype(F32) + b[:, lons, :, piece].astype(F32))

    def fold(mine, sent, axis, bit, last):
        return after(mine, last) + after(swap(sent, axis, bit), last).astype(F32)

    first, second = slice(0, border), slice(border, channels)
    near_lons, far_lons = slice(far, 2 * far), slice(0, far)
    far_first = pair(far_lons, first).astype(BF16)
    got_first = swap(far_first, "lon", 2)
    cut_b = halves(pair(slice(0, 2 * far), second), *lat_bits[0])
    d_tail, d_head = end_rows(
        d_conv[:3], d_conv[rows - 3 :],
        after(d_left, far_first, cut_b[1]), after(d_right, far_first, cut_b[1]),
    )
    d_top, d_bot = end_halo(d_tail, d_head)
    for (axis, _, bit), follow in zip(lat_bits[:-1], lat_bits[1:]):
        cut_b = halves(fold(*cut_b, axis, bit, d_head), *follow)

    def pack(sent, small):
        return jnp.concatenate([sent.reshape(-1, LANES), small.astype(BF16).reshape(-1, LANES)])

    def ride(load, sent, small, axis, bit, last):
        came = after(swap(load, axis, bit), last)
        size = sent.size // LANES
        own = after(lax.reduce_precision(small, 8, 7), last)
        return came[:size].reshape(sent.shape).astype(F32), own + came[size:].astype(F32).reshape(small.shape)

    small = filter_grad(
        after(fields, d_tail, d_head, far_first, cut_b[1]),
        mask, left, right, top, bot, d_conv, sums, g_bi,
    )
    small = small + swap(small, "lon", 1)
    whole = pair(near_lons, first, small) + after(got_first, small).astype(F32)
    back = (d_left, d_right, d_top, d_bot, kernel, mask, cotangent)
    grad_fields, block = None, 0
    steps = lon_bits + lat_bits
    for index, (axis, dim, bit) in enumerate(steps):
        mine, sent = halves(whole, axis, dim, bit)
        load = pack(sent, small)
        last = load
        if index >= len(steps) - 2:
            count = 2 if grad_fields is None else 1
            last = grad_fields = input_grad(after(d_conv, load), *back, block, count, grad_fields)
            block += count
        came, small = ride(load, sent, small, axis, bit, last)
        whole = after(mine, last) + came
    whole_b = fold(*cut_b, lat_bits[-1][0], lat_bits[-1][2], load)
    far_second = whole_b[:, far_lons].astype(BF16)
    load = pack(far_second, small)
    last = grad_fields = input_grad(after(d_conv, load), *back, block, 1, grad_fields)
    came, small = ride(load, far_second, small, "lon", 2, last)
    whole_b = after(whole_b, last)[:, near_lons] + came
    for axis, dim, bit in lon_bits:
        whole_b = fold(*halves(whole_b, axis, dim, bit), axis, bit, last)
    owned = (whole, whole_b)
    grad_w = jnp.concatenate([x[:, 0, 0] for x in owned], axis=1)
    small = small.transpose(1, 0, 2).reshape(8, 8, channels)
    return (
        mixed.reshape(rows, cols, channels),
        grad_fields,
        small[:7, :7],
        small[7, 1],
        small[7, 2],
        grad_w[1],
        small[7, 4:].reshape(hidden),
        grad_w[0].T,
        small[7, 3],
        small[7, 0],
    )


def solution(mesh):
    placed = (
        P(("grp", "lat"), "lon", None),
        P(("grp", "lat"), "lon"),
        P(("grp", "lat"), "lon", None),
        P(),
        P(),
        P(),
        P(),
        P(),
        P(),
        P(),
        P(),
    )
    return jax.shard_map(
        per_device,
        mesh=mesh,
        in_specs=placed,
        out_specs=(
            P(("grp", "lat"), "lon", None),
            P(("grp", "lat"), "lon", None),
            P("grp", None, None),
            P("grp"),
            P("grp"),
            P("grp", ("lon", "lat")),
            P("grp"),
            P(("lon", "lat"), "grp"),
            P("grp"),
            P("grp"),
        ),
        check_vma=False,
    )
```

```python
import functools
import math

import jax
import jax.numpy as jnp
from jax import lax
from jax.experimental import pallas as pl
from jax.experimental.pallas import tpu as pltpu
from jax.sharding import PartitionSpec as P

F32 = jnp.float32
BF16 = jnp.bfloat16
LANES = 128
SUB = 8


def params(mib):
    return pltpu.CompilerParams(vmem_limit_bytes=mib * 1024 * 1024)


def estimate(micros):
    return pl.CostEstimate(
        flops=int(micros * 1.15e9), bytes_accessed=int(micros * 3.6e6), transcendentals=0
    )


def once(shape):
    zeros = (0,) * len(shape)
    return pl.BlockSpec(shape, lambda *_: zeros, pipeline_mode=pl.Buffered(1))


UNUSED = pl.BlockSpec(memory_space=pl.ANY)


def whole_spec(shape):
    zeros = (0,) * len(shape)
    return pl.BlockSpec(shape, lambda *_: zeros)


def shifted(window, row, start, offset):
    return window[row, pl.ds(start + offset, SUB), :]


def lane_block(index):
    return pl.ds(pl.multiple_of(index * LANES, LANES), LANES)


def each_lane_block(channels, body):
    def one(index, _):
        body(lane_block(index))
        return 0

    lax.fori_loop(0, channels // LANES, one, 0)


def band_conv(window, k_ref, lanes, starts, rows, pad, flip):
    sums = {}
    for col_off in range(7):
        at = 6 - col_off if flip else col_off
        weights = [k_ref[6 - p if flip else p, at : at + 1, lanes] for p in range(7)]
        for start in starts:
            for src in range(window.shape[0]):
                hits = [(src - pad - row_off + 3, row_off) for row_off in range(7)]
                hits = [(out, row_off) for out, row_off in hits if 0 <= out < rows]
                if not hits:
                    continue
                cells = shifted(window, src, start, 5 + col_off)
                for out, row_off in hits:
                    term = weights[row_off] * cells
                    key = (out, start)
                    sums[key] = sums[key] + term if key in sums else term
    return sums


def gelu_twice(x):
    root = math.sqrt(2.0 / math.pi)
    inner = root + (root * 0.044715) * (x * x)
    tanh = jnp.tanh(x * inner)
    both = 1.0 + tanh
    value = x * both
    slope = both + value * ((1.0 - tanh) * (3.0 * inner - 2.0 * root))
    return value, slope


def expand_kernel(
    order_ref,
    l_ref, r_ref, t_ref, b_ref, k_ref, gain_ref, bias_ref, scale_ref, bo_ref, m_ref, cot_ref, f_ref,
    wi_ref, bi_ref, wo_ref,
    dconv_ref, mixed_ref, sums_ref, gbi_ref, sent_ref, kept_ref,
    window, conv, xhat_s, inv_s, normed, normed_t, dbr, dbr_t, act, dpre, d_normed, branch, pre_s, dact_s,
):
    rows, cols, channels = f_ref.shape
    cells = rows * cols
    strip = 16
    chunk = 128
    step_now = pl.program_id(0)
    wide = channels // LANES

    def strips(body, sums):
        def some(index, sums):
            places = [
                (2 * index + more, at, pl.ds(pl.multiple_of((2 * index + more) * cols + at, strip), strip))
                for more in range(2)
                for at in range(0, cols, strip)
            ]
            return body(places, sums)

        return lax.fori_loop(0, rows // 2, some, sums)

    def folded(values):
        return sum(value[:SUB] + value[SUB:] for value in values)

    def mean(values):
        return [jnp.mean(value, axis=-1, keepdims=True) for value in values]

    def ocean(places):
        return [jnp.concatenate([m_ref[row, at : at + strip, :]] * wide, axis=1) for row, at, _ in places]

    zero = jnp.zeros((SUB, channels), F32)

    @pl.when(step_now == 0)
    def _():
        branch[...] = jnp.zeros_like(branch)
        d_normed[...] = jnp.zeros_like(d_normed)

        def convolve(lanes):
            fill_window(window, f_ref[:, :, lanes].astype(F32) * m_ref[...], l_ref, r_ref, t_ref, b_ref, lanes)
            for start in range(0, cols, SUB):
                sums = band_conv(window, k_ref, lanes, (start,), rows, 3, False)
                for row in range(rows):
                    conv[row, start : start + SUB, lanes] = sums[row, start]

        each_lane_block(channels, convolve)

        def standardize(places, total):
            xs = [conv[row, at : at + strip, :] for row, at, _ in places]
            centered = [x - average for x, average in zip(xs, mean(xs))]
            invs = [lax.rsqrt(var + 1e-06) for var in mean([x * x for x in centered])]
            xhats = [x * inv for x, inv in zip(centered, invs)]
            grads = [
                mask * (scale_ref[...] * cot_ref[here, :].astype(F32))
                for mask, (_, _, here) in zip(ocean(places), places)
            ]
            for (_, _, here), xhat, inv, grad in zip(places, xhats, invs, grads):
                xhat_s[here, :] = xhat
                inv_s[here, :] = jnp.broadcast_to(inv, (strip, LANES))
                normed[here, :] = (xhat * gain_ref[...] + bias_ref[...]).astype(BF16)
                dbr[here, :] = (0.5 * grad).astype(BF16)
            return total + folded(grads)

        sums_ref[0] = strips(standardize, zero)
        for at in range(0, cells, chunk):
            here = slice(at, at + chunk)
            normed_t[:, here] = normed[here, :].T
            dbr_t[:, here] = dbr[here, :].T

    block = act.shape[1]
    cut = min(block, 256)
    count = block // cut
    _, parts, _, width = sent_ref.shape
    is_sent = step_now < pl.num_programs(0) // 2

    def products(index):
        lanes = slice(index * cut, (index + 1) * cut)
        pre_s[index % 2] = jnp.dot(normed[...], wi_ref[:, lanes], preferred_element_type=F32)
        dact_s[index % 2] = lax.dot_general(
            dbr[...], wo_ref[lanes, :], (((1,), (1,)), ((), ())), preferred_element_type=F32
        )

    def activate(index):
        lanes = slice(index * cut, (index + 1) * cut)
        bias = bi_ref[:, lanes]
        total = jnp.zeros((SUB, cut), F32)
        for at in range(0, cells, strip):
            here = slice(at, at + strip)
            value, slope = gelu_twice(pre_s[index % 2, here, :] + bias)
            act[here, lanes] = value.astype(BF16)
            d_pre = dact_s[index % 2, here, :] * slope
            dpre[here, lanes] = d_pre.astype(BF16)
            total = total + (d_pre[:SUB] + d_pre[SUB:])
        gbi_ref[:, lanes] = jnp.sum(total, axis=0, keepdims=True)

    def weight_grads(index):
        left = index * cut
        for which, (rows_t, source) in enumerate(((dbr_t, act), (normed_t, dpre))):
            grad = jnp.dot(
                rows_t[...], source[:, left : left + cut], preferred_element_type=F32
            ).astype(BF16)

            size = min(width, cut)
            for at in range(0, cut, size):
                lat, into = divmod(left + at, width)
                spot = (which, lat, slice(None), slice(into, into + size))
                value = grad[:, at : at + size]
                kept_ref[spot] = value
                sent_ref[spot] = jnp.where(is_sent, value, sent_ref[spot])

    products(0)
    for index in range(count):
        if index + 1 < count:
            products(index + 1)
        activate(index)
        if index > 0:
            weight_grads(index - 1)
    weight_grads(count - 1)
    branch[...] += jnp.dot(act[...], wo_ref[...], preferred_element_type=F32)
    d_normed[...] += lax.dot_general(
        dpre[...], wi_ref[...], (((1,), (1,)), ((), ())), preferred_element_type=F32
    )

    @pl.when(step_now == pl.num_programs(0) - 1)
    def _():
        def norm_back(places, sums):
            heres = [here for _, _, here in places]
            branches = [
                mask * (0.5 * branch[here, :] + bo_ref[...]) for mask, here in zip(ocean(places), heres)
            ]
            xhats = [xhat_s[here, :] for here in heres]
            grads = [d_normed[here, :] for here in heres]
            terms = [grad * xhat for grad, xhat in zip(grads, xhats)]
            es = [grad * gain_ref[...] for grad in grads]
            m1s = mean(es)
            m2s = mean([e * xhat for e, xhat in zip(es, xhats)])
            for (row, at, here), e, xhat, m1, m2, value in zip(places, es, xhats, m1s, m2s, branches):
                inv = jnp.concatenate([inv_s[here, :]] * wide, axis=1)
                dconv_ref[here, :] = (inv * (e - m1 - xhat * m2)).astype(BF16)
                field = f_ref[row, at : at + strip, :].astype(F32)
                mixed_ref[here, :] = (field + value * scale_ref[...]).astype(BF16)
            products = [value * cot_ref[here, :].astype(F32) for value, here in zip(branches, heres)]
            return tuple(total + folded(x) for total, x in zip(sums, (products, terms, grads)))

        sums_ref[1], sums_ref[2], sums_ref[3] = strips(norm_back, (zero, zero, zero))


def expand(
    order, left, right, top, bot, kernel, gain, bias, scale, b_out, mask, cot, fields, w_in, b_in, w_out, n_lon, n_lat
):
    rows, cols, channels = fields.shape
    hidden = w_in.shape[1]
    cells = rows * cols
    block = hidden // n_lon
    split = n_lat if (block // n_lat) % LANES == 0 else 1
    turn = n_lon // 2
    grads = (split, channels, block // split)
    given = (left, right, top, bot, kernel, gain, bias, scale, b_out, mask, cot, fields)

    def sent_at(h, order):
        return (0, jnp.minimum(h, turn - 1), 0, 0, 0)

    def kept_at(h, order):
        return (0, jnp.maximum(h - turn, 0), 0, 0, 0)

    return pl.pallas_call(
        expand_kernel,
        grid_spec=pltpu.PrefetchScalarGridSpec(
            num_scalar_prefetch=1,
            grid=(n_lon,),
            in_specs=[once(x.shape) for x in given]
            + [
                pl.BlockSpec((channels, block), lambda h, order: (0, order[h])),
                pl.BlockSpec((1, block), lambda h, order: (0, order[h])),
                pl.BlockSpec((block, channels), lambda h, order: (order[h], 0)),
            ],
            out_specs=[
                once((cells, channels)),
                once((cells, channels)),
                once((4, SUB, channels)),
                pl.BlockSpec((1, block), lambda h, order: (0, order[h])),
                pl.BlockSpec((2, None) + grads, sent_at),
                pl.BlockSpec((2, None) + grads, kept_at),
            ],
            scratch_shapes=[
                pltpu.VMEM((rows + 6, cols + 16, LANES), F32),
                pltpu.VMEM((rows, cols, channels), F32),
                pltpu.VMEM((cells, channels), F32),
                pltpu.VMEM((cells, LANES), F32),
                pltpu.VMEM((cells, channels), BF16),
                pltpu.VMEM((channels, cells), BF16),
                pltpu.VMEM((cells, channels), BF16),
                pltpu.VMEM((channels, cells), BF16),
                pltpu.VMEM((cells, block), BF16),
                pltpu.VMEM((cells, block), BF16),
                pltpu.VMEM((cells, channels), F32),
                pltpu.VMEM((cells, channels), F32),
                pltpu.VMEM((2, cells, min(block, 256)), F32),
                pltpu.VMEM((2, cells, min(block, 256)), F32),
            ],
        ),
        out_shape=[
            jax.ShapeDtypeStruct((cells, channels), BF16),
            jax.ShapeDtypeStruct((cells, channels), BF16),
            jax.ShapeDtypeStruct((4, SUB, channels), F32),
            jax.ShapeDtypeStruct((1, hidden), F32),
            jax.ShapeDtypeStruct((2, turn) + grads, BF16),
            jax.ShapeDtypeStruct((2, turn) + grads, BF16),
        ],
        compiler_params=params(56),
        cost_estimate=estimate(20),
        name="expand",
    )(order, *given, w_in, b_in, w_out)


def fill_window(window, center, l_ref, r_ref, t_ref, b_ref, lanes):
    rows, cols, _ = center.shape
    window[0:3, 5 : 11 + cols, :] = t_ref[:, :, lanes].astype(F32)
    window[3 : 3 + rows, 5:8, :] = l_ref[:, :, lanes].astype(F32)
    window[3 : 3 + rows, 8 : 8 + cols, :] = center
    window[3 : 3 + rows, 8 + cols : 11 + cols, :] = r_ref[:, :, lanes].astype(F32)
    window[3 + rows : 6 + rows, 5 : 11 + cols, :] = b_ref[:, :, lanes].astype(F32)


def filter_grad_kernel(
    f_ref, m_ref, l_ref, r_ref, t_ref, b_ref, d_ref, sums_ref, gbi_ref, o_ref, window, grad
):
    rows, cols, channels = f_ref.shape
    blocks = channels // LANES

    def block(index, _):
        lanes = lane_block(index)
        fill_window(window, f_ref[:, :, lanes].astype(F32) * m_ref[...], l_ref, r_ref, t_ref, b_ref, lanes)
        grad[...] = d_ref[:, :, lanes].astype(F32)
        for col_off in range(7):

            def band(step, sums):
                start = pl.multiple_of(step * SUB, SUB)
                sums = list(sums)
                held = {}
                for src in range(rows + 6):
                    if src < rows:
                        held[src] = grad[src, pl.ds(start, SUB), :]
                    cells = shifted(window, src, start, 5 + col_off)
                    for row_off in range(7):
                        out = src - row_off
                        if 0 <= out < rows:
                            sums[row_off] = sums[row_off] + held[out] * cells
                return tuple(sums)

            sums = tuple(jnp.zeros((SUB, LANES), F32) for _ in range(7))
            sums = lax.fori_loop(0, cols // SUB, band, sums)
            for row_off in range(7):
                at = row_off * 8 + col_off
                o_ref[index, at : at + 1, :] = jnp.sum(sums[row_off], axis=0, keepdims=True)
        for row_off in range(7):
            o_ref[index, row_off * 8 + 7 : row_off * 8 + 8, :] = jnp.zeros((1, LANES), F32)
        for at, source in enumerate((1, 2, 3, 0)):
            o_ref[index, 56 + at : 57 + at, :] = jnp.sum(sums_ref[source, :, lanes], axis=0, keepdims=True)
        for at in range(4):
            o_ref[index, 60 + at : 61 + at, :] = gbi_ref[:, lane_block(at * blocks + index)]
        return 0

    lax.fori_loop(0, blocks, block, 0)


def filter_grad(fields, mask, left, right, top, bot, d_conv, sums, gbi):
    rows, cols, channels = fields.shape
    return pl.pallas_call(
        filter_grad_kernel,
        out_shape=jax.ShapeDtypeStruct((channels // LANES, 64, LANES), F32),
        scratch_shapes=[
            pltpu.VMEM((rows + 6, cols + 16, LANES), F32),
            pltpu.VMEM((rows, cols, LANES), F32),
        ],
        compiler_params=params(56),
        cost_estimate=estimate(4),
        name="filter_grad",
    )(fields, mask, left, right, top, bot, d_conv, sums, gbi)


def input_grad_kernel(first, d_ref, l_ref, r_ref, t_ref, b_ref, k_ref, m_ref, cot_ref, *rest):
    o_ref, window, grad = rest[-3:]
    rows, cols, channels = d_ref.shape
    tall = o_ref.shape[0]
    low, high = max(0, first - 3), min(rows, first + tall + 3)
    inside = slice(low - first + 3, high - first + 3)
    group = 32 // tall * SUB

    def block(lanes):
        if first < 3:
            window[0 : 3 - first, 5 : 11 + cols, :] = t_ref[first:3, :, lanes].astype(F32)
        if first + tall > rows - 3:
            below = first + tall + 3 - rows
            window[tall + 6 - below : tall + 6, 5 : 11 + cols, :] = b_ref[:below, :, lanes].astype(F32)
        window[inside, 5:8, :] = l_ref[low:high, :, lanes].astype(F32)
        window[inside, 8 : 8 + cols, :] = d_ref[low:high, :, lanes].astype(F32)
        window[inside, 8 + cols : 11 + cols, :] = r_ref[low:high, :, lanes].astype(F32)
        for left in range(0, cols, group):
            starts = range(left, min(left + group, cols), SUB)
            sums = band_conv(window, k_ref, lanes, starts, tall, 3, True)
            for (row, start), value in sums.items():
                grad[row, start : start + SUB, :] = value
        o_ref[:, :, lanes] = (cot_ref[:, :, lanes].astype(F32) + m_ref[...] * grad[...]).astype(BF16)

    each_lane_block(channels, block)


def input_grad(d_conv, left, right, top, bot, kernel, mask, cot, first, quarters, old=None):
    rows, cols, channels = d_conv.shape
    tall = rows // 4 * quarters

    def rows_of(width):
        return pl.BlockSpec((tall, cols, width), lambda i: (first // quarters, 0, 0))

    whole = (d_conv, left, right, top, bot, kernel)
    more = [] if old is None else [old]
    return pl.pallas_call(
        functools.partial(input_grad_kernel, rows // 4 * first),
        grid=(1,),
        out_shape=jax.ShapeDtypeStruct((rows, cols, channels), BF16),
        in_specs=[once(x.shape) for x in whole]
        + [rows_of(LANES), rows_of(channels)]
        + [UNUSED] * len(more),
        out_specs=rows_of(channels),
        scratch_shapes=[
            pltpu.VMEM((tall + 6, cols + 16, LANES), F32),
            pltpu.VMEM((tall, cols, LANES), F32),
        ],
        input_output_aliases={8: 0} if more else {},
        compiler_params=params(56),
        cost_estimate=estimate(4),
        name="input_grad",
    )(*whole, mask, cot, *more)


def finish_kernel(a_ref, b_ref, load_ref, small_ref, wo_ref, wi_ref, gk_ref, vec_ref, gbi_ref):
    channels = wi_ref.shape[0]
    border = a_ref.shape[1]
    rest = channels - border
    blocks = channels // LANES
    for index, ref in ((0, wo_ref), (1, wi_ref)):
        came = load_ref[index * rest : (index + 1) * rest, :].astype(F32)
        grad = jnp.concatenate([a_ref[index], b_ref[index] + came], axis=0)
        ref[...] = grad.T if index == 0 else grad
    for block in range(blocks):
        at = 2 * rest + block * 64
        total = small_ref[block] + load_ref[at : at + 64, :].astype(F32)
        lanes = slice(block * LANES, (block + 1) * LANES)
        for row in range(7):
            gk_ref[row, :, lanes] = total[row * 8 : row * 8 + 7]
        for row in range(4):
            vec_ref[row, :, lanes] = total[56 + row : 57 + row]
            gbi_ref[:, slice(row * channels + block * LANES, row * channels + (block + 1) * LANES)] = total[
                60 + row : 61 + row
            ]


def finish(first, second, load, small, hidden):
    channels = first.shape[1] + second.shape[1]
    width = first.shape[2]
    return pl.pallas_call(
        finish_kernel,
        out_shape=[
            jax.ShapeDtypeStruct((width, channels), F32),
            jax.ShapeDtypeStruct((channels, width), F32),
            jax.ShapeDtypeStruct((7, 7, channels), F32),
            jax.ShapeDtypeStruct((4, 1, channels), F32),
            jax.ShapeDtypeStruct((1, hidden), F32),
        ],
        compiler_params=params(56),
        cost_estimate=estimate(2),
        name="finish",
    )(first, second, load, small)


def swap(values, axis, bit):
    count = lax.axis_size(axis)
    return lax.ppermute(values, axis, [(i, i ^ bit) for i in range(count)])


def bits_of(axis):
    return [1 << k for k in range(int(math.log2(lax.axis_size(axis))))]


def after(value, *others):
    return lax.optimization_barrier((value,) + others)[0]


def halves(values, axis, dim, bit):
    mine = (lax.axis_index(axis) // bit) % 2 == 1
    shape = values.shape
    paired = values.reshape(shape[:dim] + (shape[dim] // 2, 2) + shape[dim + 1 :])
    low = lax.index_in_dim(paired, 0, dim + 1, keepdims=False)
    high = lax.index_in_dim(paired, 1, dim + 1, keepdims=False)
    return jnp.where(mine, high, low), jnp.where(mine, low, high).astype(BF16)


def side_halo(last, first):
    count = lax.axis_size("lon")
    ahead = [(i, (i + 1) % count) for i in range(count)]
    back = [((i + 1) % count, i) for i in range(count)]
    return lax.ppermute(last, "lon", ahead), lax.ppermute(first, "lon", back)


def end_rows(head, tail, left, right):
    rows = left.shape[0]
    return (
        jnp.concatenate([left[rows - 3 :], tail, right[rows - 3 :]], axis=1),
        jnp.concatenate([left[:3], head, right[:3]], axis=1),
    )


def end_halo(tail, head):
    count = lax.axis_size("lat")
    ahead = [(i, i + 1) for i in range(count - 1)]
    back = [(i + 1, i) for i in range(count - 1)]
    return lax.ppermute(tail, "lat", ahead), lax.ppermute(head, "lat", back)


def per_device(
    fields,
    land_mask,
    cotangent,
    kernel,
    layer_norm_gain,
    layer_norm_bias,
    w_in,
    b_in,
    w_out,
    b_out,
    layer_scale,
):
    rows, cols, channels = fields.shape
    cells = rows * cols
    hidden = w_in.shape[1]
    n_lon, n_lat = lax.axis_size("lon"), lax.axis_size("lat")
    gain, bias = layer_norm_gain.reshape(1, -1), layer_norm_bias.reshape(1, -1)
    scale = layer_scale.reshape(1, -1)
    cot_rows = cotangent.reshape(cells, channels)
    mask = jnp.broadcast_to(land_mask.astype(F32)[:, :, None], (rows, cols, LANES))
    ocean = land_mask.astype(BF16)[:, :, None]
    left, right = side_halo(fields[:, cols - 3 :] * ocean[:, cols - 3 :], fields[:, :3] * ocean[:, :3])
    lon = lax.axis_index("lon")
    core, side_y = lon % 2, (lon // 2) % 2
    quads = 4 * jnp.arange(n_lon // 4, dtype=jnp.int32)
    order = jnp.concatenate(
        [quads + 2 * y + c for c in (1 - core, core) for y in (1 - side_y, side_y)]
    )
    top, bot = end_halo(
        *end_rows(
            fields[:3] * ocean[:3], fields[rows - 3 :] * ocean[rows - 3 :],
            after(left, mask, order), after(right, mask, order),
        )
    )

    d_conv, mixed, sums, g_bi, sent, kept = expand(
        order, left, right, top, bot, kernel, gain, bias, scale, b_out.reshape(1, -1), mask, cot_rows,
        fields, w_in, b_in.reshape(1, -1), w_out, n_lon, n_lat,
    )
    got = swap(sent, "lon", 1)
    d_conv = d_conv.reshape(rows, cols, channels)
    d_left, d_right = side_halo(d_conv[:, cols - 3 :], d_conv[:, :3])

    far = n_lon // 4
    border = channels * 5 // 8
    lon_bits = [("lon", 1, bit) for bit in bits_of("lon")[2:]]
    lat_bits = [("lat", 2, bit) for bit in bits_of("lat")]

    def split_lat(x):
        if x.shape[2] != n_lat:
            x = x.reshape(x.shape[0], x.shape[1], x.shape[3], n_lat, -1).transpose(0, 1, 3, 2, 4)
        return x

    def pair(lons, piece, last=None):
        a, b = (kept, got) if last is None else (after(kept, last), after(got, last))
        return split_lat(a[:, lons, :, piece].astype(F32) + b[:, lons, :, piece].astype(F32))

    def fold(mine, sent, axis, bit, last):
        return after(mine, last) + after(swap(sent, axis, bit), last).astype(F32)

    first, second = slice(0, border), slice(border, channels)
    near_lons, far_lons = slice(far, 2 * far), slice(0, far)
    far_first = pair(far_lons, first).astype(BF16)
    got_first = swap(far_first, "lon", 2)
    cut_b = halves(pair(slice(0, 2 * far), second), *lat_bits[0])
    d_tail, d_head = end_rows(
        d_conv[:3], d_conv[rows - 3 :],
        after(d_left, far_first, cut_b[1]), after(d_right, far_first, cut_b[1]),
    )
    d_top, d_bot = end_halo(d_tail, d_head)
    for (axis, _, bit), follow in zip(lat_bits[:-1], lat_bits[1:]):
        cut_b = halves(fold(*cut_b, axis, bit, d_head), *follow)

    def pack(sent, small):
        return jnp.concatenate([sent.reshape(-1, LANES), small.astype(BF16).reshape(-1, LANES)])

    def ride(load, sent, small, axis, bit, last):
        came = after(swap(load, axis, bit), last)
        size = sent.size // LANES
        own = after(lax.reduce_precision(small, 8, 7), last)
        return came[:size].reshape(sent.shape).astype(F32), own + came[size:].astype(F32).reshape(small.shape)

    small = filter_grad(
        after(fields, d_tail, d_head, far_first, cut_b[1]),
        mask, left, right, top, bot, d_conv, sums, g_bi,
    )
    alone = small
    whole = pair(near_lons, first, alone) + after(got_first, alone).astype(F32)
    whole_b = fold(*cut_b, lat_bits[-1][0], lat_bits[-1][2], alone)
    far_second = whole_b[:, far_lons].astype(BF16)
    back = (d_left, d_right, d_top, d_bot, kernel, mask, cotangent)
    grad_fields, block = None, 0
    steps = lon_bits + lat_bits
    early = halves(whole, *steps[0])[1]
    small = after(alone, early, far_second) + after(swap(alone, "lon", 1), early, far_second)
    for index, (axis, dim, bit) in enumerate(steps):
        mine, sent = halves(whole, axis, dim, bit)
        load = pack(sent, small)
        last = load
        if index >= len(steps) - 2:
            count = 2 if grad_fields is None else 1
            last = grad_fields = input_grad(
                after(d_conv, load, far_second), *back, block, count, grad_fields
            )
            block += count
        came, small = ride(load, sent, small, axis, bit, last)
        whole = after(mine, last) + came
    load = pack(far_second, small)
    last = grad_fields = input_grad(after(d_conv, load), *back, block, 1, grad_fields)
    if not lon_bits and whole.shape[-1] == LANES:
        load = after(swap(load, "lon", 2), last)
        near = after(whole_b, last)[:, near_lons]
        grad_wo, grad_wi, grad_k, vectors, g_bi = finish(
            whole[:, 0, 0], near[:, 0, 0], load, after(lax.reduce_precision(small, 8, 7), last), hidden
        )
        g_scale, g_gain, g_shift, g_bo = (vectors[i, 0] for i in range(4))
    else:
        came, small = ride(load, far_second, small, "lon", 2, last)
        whole_b = after(whole_b, last)[:, near_lons] + came
        for axis, dim, bit in lon_bits:
            whole_b = fold(*halves(whole_b, axis, dim, bit), axis, bit, last)
        grad_w = jnp.concatenate([x[:, 0, 0] for x in (whole, whole_b)], axis=1)
        grad_wo, grad_wi = grad_w[0].T, grad_w[1]
        small = small.transpose(1, 0, 2).reshape(8, 8, channels)
        grad_k, g_bi = small[:7, :7], small[7, 4:]
        g_scale, g_gain, g_shift, g_bo = (small[7, i] for i in range(4))
    return (
        mixed.reshape(rows, cols, channels),
        grad_fields,
        grad_k,
        g_gain,
        g_shift,
        grad_wi,
        g_bi.reshape(hidden),
        grad_wo,
        g_bo,
        g_scale,
    )


def solution(mesh):
    placed = (
        P(("grp", "lat"), "lon", None),
        P(("grp", "lat"), "lon"),
        P(("grp", "lat"), "lon", None),
        P(),
        P(),
        P(),
        P(),
        P(),
        P(),
        P(),
        P(),
    )
    return jax.shard_map(
        per_device,
        mesh=mesh,
        in_specs=placed,
        out_specs=(
            P(("grp", "lat"), "lon", None),
            P(("grp", "lat"), "lon", None),
            P("grp", None, None),
            P("grp"),
            P("grp"),
            P("grp", ("lon", "lat")),
            P("grp"),
            P(("lon", "lat"), "grp"),
            P("grp"),
            P("grp"),
        ),
        check_vma=False,
    )
```

```python
import functools
import math

import jax
import jax.numpy as jnp
from jax import lax
from jax.experimental import pallas as pl
from jax.experimental.pallas import tpu as pltpu
from jax.sharding import PartitionSpec as P

F32 = jnp.float32
BF16 = jnp.bfloat16
LANES = 128
SUB = 8


def params(mib):
    return pltpu.CompilerParams(vmem_limit_bytes=mib * 1024 * 1024)


def estimate(micros):
    return pl.CostEstimate(
        flops=int(micros * 1.15e9), bytes_accessed=int(micros * 3.6e6), transcendentals=0
    )


def once(shape):
    zeros = (0,) * len(shape)
    return pl.BlockSpec(shape, lambda *_: zeros, pipeline_mode=pl.Buffered(1))


UNUSED = pl.BlockSpec(memory_space=pl.ANY)


def whole_spec(shape):
    zeros = (0,) * len(shape)
    return pl.BlockSpec(shape, lambda *_: zeros)


def shifted(window, row, start, offset):
    return window[row, pl.ds(start + offset, SUB), :]


def lane_block(index):
    return pl.ds(pl.multiple_of(index * LANES, LANES), LANES)


def each_lane_block(channels, body):
    def one(index, _):
        body(lane_block(index))
        return 0

    lax.fori_loop(0, channels // LANES, one, 0)


def band_conv(window, k_ref, lanes, starts, rows, pad, flip):
    sums = {}
    for col_off in range(7):
        at = 6 - col_off if flip else col_off
        weights = [k_ref[6 - p if flip else p, at : at + 1, lanes] for p in range(7)]
        for start in starts:
            for src in range(window.shape[0]):
                hits = [(src - pad - row_off + 3, row_off) for row_off in range(7)]
                hits = [(out, row_off) for out, row_off in hits if 0 <= out < rows]
                if not hits:
                    continue
                cells = shifted(window, src, start, 5 + col_off)
                for out, row_off in hits:
                    term = weights[row_off] * cells
                    key = (out, start)
                    sums[key] = sums[key] + term if key in sums else term
    return sums


def gelu_twice(x):
    root = math.sqrt(2.0 / math.pi)
    inner = root + (root * 0.044715) * (x * x)
    tanh = jnp.tanh(x * inner)
    both = 1.0 + tanh
    value = x * both
    slope = both + value * ((1.0 - tanh) * (3.0 * inner - 2.0 * root))
    return value, slope


def expand_kernel(
    order_ref,
    l_ref, r_ref, t_ref, b_ref, k_ref, gain_ref, bias_ref, scale_ref, bo_ref, m_ref, cot_ref, f_ref,
    wi_ref, bi_ref, wo_ref,
    dconv_ref, mixed_ref, sums_ref, gbi_ref, sent_ref, kept_ref,
    window, conv, xhat_s, inv_s, normed, normed_t, dbr, dbr_t, act, dpre, d_normed, branch, pre_s, d_act,
):
    rows, cols, channels = f_ref.shape
    cells = rows * cols
    strip = 16
    chunk = 128
    step_now = pl.program_id(0)
    wide = channels // LANES

    def strips(body, sums):
        def some(index, sums):
            places = [
                (2 * index + more, at, pl.ds(pl.multiple_of((2 * index + more) * cols + at, strip), strip))
                for more in range(2)
                for at in range(0, cols, strip)
            ]
            return body(places, sums)

        return lax.fori_loop(0, rows // 2, some, sums)

    def folded(values):
        return sum(value[:SUB] + value[SUB:] for value in values)

    def mean(values):
        return [jnp.mean(value, axis=-1, keepdims=True) for value in values]

    def ocean(places):
        return [jnp.concatenate([m_ref[row, at : at + strip, :]] * wide, axis=1) for row, at, _ in places]

    zero = jnp.zeros((SUB, channels), F32)

    @pl.when(step_now == 0)
    def _():
        branch[...] = jnp.zeros_like(branch)
        d_normed[...] = jnp.zeros_like(d_normed)

        def cotangents(places, total):
            grads = [
                mask * (scale_ref[...] * cot_ref[here, :].astype(F32))
                for mask, (_, _, here) in zip(ocean(places), places)
            ]
            for (_, _, here), grad in zip(places, grads):
                dbr[here, :] = (0.5 * grad).astype(BF16)
            return total + folded(grads)

        sums_ref[0] = strips(cotangents, zero)
        for at in range(0, cells, chunk):
            here = slice(at, at + chunk)
            dbr_t[:, here] = dbr[here, :].T
        share = wo_ref.shape[0] // wide

        def convolve(index, _):
            lanes = lane_block(index)
            units = pl.ds(pl.multiple_of(index * share, LANES), share)
            fill_window(window, f_ref[:, :, lanes].astype(F32) * m_ref[...], l_ref, r_ref, t_ref, b_ref, lanes)
            for start in range(0, cols, SUB):
                here = slice(start * rows, (start + SUB) * rows)
                d_act[here, units] = lax.dot_general(
                    dbr[here, :], wo_ref[units, :], (((1,), (1,)), ((), ())), preferred_element_type=F32
                )
                sums = band_conv(window, k_ref, lanes, (start,), rows, 3, False)
                for row in range(rows):
                    conv[row, start : start + SUB, lanes] = sums[row, start]
            return 0

        lax.fori_loop(0, wide, convolve, 0)

        def standardize(places, _):
            xs = [conv[row, at : at + strip, :] for row, at, _ in places]
            centered = [x - average for x, average in zip(xs, mean(xs))]
            invs = [lax.rsqrt(var + 1e-06) for var in mean([x * x for x in centered])]
            for (_, _, here), x, inv in zip(places, centered, invs):
                xhat = x * inv
                xhat_s[here, :] = xhat
                inv_s[here, :] = jnp.broadcast_to(inv, (strip, LANES))
                normed[here, :] = (xhat * gain_ref[...] + bias_ref[...]).astype(BF16)
            return 0

        strips(standardize, 0)
        for at in range(0, cells, chunk):
            here = slice(at, at + chunk)
            normed_t[:, here] = normed[here, :].T

    block = act.shape[1]
    cut = min(block, 256)
    count = block // cut
    _, parts, _, width = sent_ref.shape
    is_sent = step_now < pl.num_programs(0) // 2
    base = pl.multiple_of(order_ref[step_now] * block, LANES)

    def products(index):
        lanes = slice(index * cut, (index + 1) * cut)
        pre_s[index % 2] = jnp.dot(normed[...], wi_ref[:, lanes], preferred_element_type=F32)

    def activate(index):
        lanes = slice(index * cut, (index + 1) * cut)
        units = pl.ds(pl.multiple_of(base + index * cut, LANES), cut)
        bias = bi_ref[:, lanes]
        total = jnp.zeros((SUB, cut), F32)
        for at in range(0, cells, strip):
            here = slice(at, at + strip)
            value, slope = gelu_twice(pre_s[index % 2, here, :] + bias)
            act[here, lanes] = value.astype(BF16)
            d_pre = d_act[here, units] * slope
            dpre[here, lanes] = d_pre.astype(BF16)
            total = total + (d_pre[:SUB] + d_pre[SUB:])
        gbi_ref[:, lanes] = jnp.sum(total, axis=0, keepdims=True)

    def weight_grads(index):
        left = index * cut
        for which, (rows_t, source) in enumerate(((dbr_t, act), (normed_t, dpre))):
            grad = jnp.dot(
                rows_t[...], source[:, left : left + cut], preferred_element_type=F32
            ).astype(BF16)

            size = min(width, cut)
            for at in range(0, cut, size):
                lat, into = divmod(left + at, width)
                spot = (which, lat, slice(None), slice(into, into + size))
                value = grad[:, at : at + size]
                kept_ref[spot] = value
                sent_ref[spot] = jnp.where(is_sent, value, sent_ref[spot])

    products(0)
    for index in range(count):
        if index + 1 < count:
            products(index + 1)
        activate(index)
        if index > 0:
            weight_grads(index - 1)
    weight_grads(count - 1)
    branch[...] += jnp.dot(act[...], wo_ref[pl.ds(base, block), :], preferred_element_type=F32)
    d_normed[...] += lax.dot_general(
        dpre[...], wi_ref[...], (((1,), (1,)), ((), ())), preferred_element_type=F32
    )

    @pl.when(step_now == pl.num_programs(0) - 1)
    def _():
        def norm_back(places, sums):
            heres = [here for _, _, here in places]
            branches = [
                mask * (0.5 * branch[here, :] + bo_ref[...]) for mask, here in zip(ocean(places), heres)
            ]
            xhats = [xhat_s[here, :] for here in heres]
            grads = [d_normed[here, :] for here in heres]
            terms = [grad * xhat for grad, xhat in zip(grads, xhats)]
            es = [grad * gain_ref[...] for grad in grads]
            m1s = mean(es)
            m2s = mean([e * xhat for e, xhat in zip(es, xhats)])
            for (row, at, here), e, xhat, m1, m2, value in zip(places, es, xhats, m1s, m2s, branches):
                inv = jnp.concatenate([inv_s[here, :]] * wide, axis=1)
                dconv_ref[here, :] = (inv * (e - m1 - xhat * m2)).astype(BF16)
                field = f_ref[row, at : at + strip, :].astype(F32)
                mixed_ref[here, :] = (field + value * scale_ref[...]).astype(BF16)
            products = [value * cot_ref[here, :].astype(F32) for value, here in zip(branches, heres)]
            return tuple(total + folded(x) for total, x in zip(sums, (products, terms, grads)))

        sums_ref[1], sums_ref[2], sums_ref[3] = strips(norm_back, (zero, zero, zero))


def expand(
    order, left, right, top, bot, kernel, gain, bias, scale, b_out, mask, cot, fields, w_in, b_in, w_out, n_lon, n_lat
):
    rows, cols, channels = fields.shape
    hidden = w_in.shape[1]
    cells = rows * cols
    block = hidden // n_lon
    split = n_lat if (block // n_lat) % LANES == 0 else 1
    turn = n_lon // 2
    grads = (split, channels, block // split)
    given = (left, right, top, bot, kernel, gain, bias, scale, b_out, mask, cot, fields)

    def sent_at(h, order):
        return (0, jnp.minimum(h, turn - 1), 0, 0, 0)

    def kept_at(h, order):
        return (0, jnp.maximum(h - turn, 0), 0, 0, 0)

    return pl.pallas_call(
        expand_kernel,
        grid_spec=pltpu.PrefetchScalarGridSpec(
            num_scalar_prefetch=1,
            grid=(n_lon,),
            in_specs=[once(x.shape) for x in given]
            + [
                pl.BlockSpec((channels, block), lambda h, order: (0, order[h])),
                pl.BlockSpec((1, block), lambda h, order: (0, order[h])),
                once(w_out.shape),
            ],
            out_specs=[
                once((cells, channels)),
                once((cells, channels)),
                once((4, SUB, channels)),
                pl.BlockSpec((1, block), lambda h, order: (0, order[h])),
                pl.BlockSpec((2, None) + grads, sent_at),
                pl.BlockSpec((2, None) + grads, kept_at),
            ],
            scratch_shapes=[
                pltpu.VMEM((rows + 6, cols + 16, LANES), F32),
                pltpu.VMEM((rows, cols, channels), F32),
                pltpu.VMEM((cells, channels), F32),
                pltpu.VMEM((cells, LANES), F32),
                pltpu.VMEM((cells, channels), BF16),
                pltpu.VMEM((channels, cells), BF16),
                pltpu.VMEM((cells, channels), BF16),
                pltpu.VMEM((channels, cells), BF16),
                pltpu.VMEM((cells, block), BF16),
                pltpu.VMEM((cells, block), BF16),
                pltpu.VMEM((cells, channels), F32),
                pltpu.VMEM((cells, channels), F32),
                pltpu.VMEM((2, cells, min(block, 256)), F32),
                pltpu.VMEM((cells, hidden), F32),
            ],
        ),
        out_shape=[
            jax.ShapeDtypeStruct((cells, channels), BF16),
            jax.ShapeDtypeStruct((cells, channels), BF16),
            jax.ShapeDtypeStruct((4, SUB, channels), F32),
            jax.ShapeDtypeStruct((1, hidden), F32),
            jax.ShapeDtypeStruct((2, turn) + grads, BF16),
            jax.ShapeDtypeStruct((2, turn) + grads, BF16),
        ],
        compiler_params=params(56),
        cost_estimate=estimate(20),
        name="expand",
    )(order, *given, w_in, b_in, w_out)


def fill_window(window, center, l_ref, r_ref, t_ref, b_ref, lanes):
    rows, cols, _ = center.shape
    window[0:3, 5 : 11 + cols, :] = t_ref[:, :, lanes].astype(F32)
    window[3 : 3 + rows, 5:8, :] = l_ref[:, :, lanes].astype(F32)
    window[3 : 3 + rows, 8 : 8 + cols, :] = center
    window[3 : 3 + rows, 8 + cols : 11 + cols, :] = r_ref[:, :, lanes].astype(F32)
    window[3 + rows : 6 + rows, 5 : 11 + cols, :] = b_ref[:, :, lanes].astype(F32)


def filter_grad_kernel(first, f_ref, m_ref, l_ref, r_ref, t_ref, b_ref, d_ref, sums_ref, gbi_ref, *rest):
    o_ref, window, grad = rest[-3:]
    rows, cols, channels = f_ref.shape
    blocks = channels // LANES

    def block(index, _):
        lanes = lane_block(first + index)
        fill_window(window, f_ref[:, :, lanes].astype(F32) * m_ref[...], l_ref, r_ref, t_ref, b_ref, lanes)
        grad[...] = d_ref[:, :, lanes].astype(F32)
        for col_off in range(7):

            def band(step, sums):
                start = pl.multiple_of(step * SUB, SUB)
                sums = list(sums)
                held = {}
                for src in range(rows + 6):
                    if src < rows:
                        held[src] = grad[src, pl.ds(start, SUB), :]
                    cells = shifted(window, src, start, 5 + col_off)
                    for row_off in range(7):
                        out = src - row_off
                        if 0 <= out < rows:
                            sums[row_off] = sums[row_off] + held[out] * cells
                return tuple(sums)

            sums = tuple(jnp.zeros((SUB, LANES), F32) for _ in range(7))
            sums = lax.fori_loop(0, cols // SUB, band, sums)
            for row_off in range(7):
                at = row_off * 8 + col_off
                o_ref[index, at : at + 1, :] = jnp.sum(sums[row_off], axis=0, keepdims=True)
        for row_off in range(7):
            o_ref[index, row_off * 8 + 7 : row_off * 8 + 8, :] = jnp.zeros((1, LANES), F32)
        for at, source in enumerate((1, 2, 3, 0)):
            o_ref[index, 56 + at : 57 + at, :] = jnp.sum(sums_ref[source, :, lanes], axis=0, keepdims=True)
        for at in range(4):
            o_ref[index, 60 + at : 61 + at, :] = gbi_ref[:, lane_block(at * blocks + first + index)]
        return 0

    lax.fori_loop(0, o_ref.shape[0], block, 0)


def filter_grad(fields, mask, left, right, top, bot, d_conv, sums, gbi, half, old=None):
    rows, cols, channels = fields.shape
    blocks = channels // LANES
    whole = (fields, mask, left, right, top, bot, d_conv, sums, gbi)
    more = [] if old is None else [old]
    return pl.pallas_call(
        functools.partial(filter_grad_kernel, half * (blocks // 2)),
        grid=(1,),
        out_shape=jax.ShapeDtypeStruct((blocks, 64, LANES), F32),
        in_specs=[once(x.shape) for x in whole] + [UNUSED] * len(more),
        out_specs=pl.BlockSpec((blocks // 2, 64, LANES), lambda i: (half, 0, 0)),
        scratch_shapes=[
            pltpu.VMEM((rows + 6, cols + 16, LANES), F32),
            pltpu.VMEM((rows, cols, LANES), F32),
        ],
        input_output_aliases={9: 0} if more else {},
        compiler_params=params(56),
        cost_estimate=estimate(4),
        name="filter_grad",
    )(*whole, *more)


def input_grad_kernel(first, d_ref, l_ref, r_ref, t_ref, b_ref, k_ref, m_ref, cot_ref, *rest):
    o_ref, window, grad = rest[-3:]
    rows, cols, channels = d_ref.shape
    tall = o_ref.shape[0]
    low, high = max(0, first - 3), min(rows, first + tall + 3)
    inside = slice(low - first + 3, high - first + 3)
    group = 32 // tall * SUB

    def block(lanes):
        if first < 3:
            window[0 : 3 - first, 5 : 11 + cols, :] = t_ref[first:3, :, lanes].astype(F32)
        if first + tall > rows - 3:
            below = first + tall + 3 - rows
            window[tall + 6 - below : tall + 6, 5 : 11 + cols, :] = b_ref[:below, :, lanes].astype(F32)
        window[inside, 5:8, :] = l_ref[low:high, :, lanes].astype(F32)
        window[inside, 8 : 8 + cols, :] = d_ref[low:high, :, lanes].astype(F32)
        window[inside, 8 + cols : 11 + cols, :] = r_ref[low:high, :, lanes].astype(F32)
        for left in range(0, cols, group):
            starts = range(left, min(left + group, cols), SUB)
            sums = band_conv(window, k_ref, lanes, starts, tall, 3, True)
            for (row, start), value in sums.items():
                grad[row, start : start + SUB, :] = value
        o_ref[:, :, lanes] = (cot_ref[:, :, lanes].astype(F32) + m_ref[...] * grad[...]).astype(BF16)

    each_lane_block(channels, block)


def input_grad(d_conv, left, right, top, bot, kernel, mask, cot, first, quarters, old=None):
    rows, cols, channels = d_conv.shape
    tall = rows // 4 * quarters

    def rows_of(width):
        return pl.BlockSpec((tall, cols, width), lambda i: (first // quarters, 0, 0))

    whole = (d_conv, left, right, top, bot, kernel)
    more = [] if old is None else [old]
    return pl.pallas_call(
        functools.partial(input_grad_kernel, rows // 4 * first),
        grid=(1,),
        out_shape=jax.ShapeDtypeStruct((rows, cols, channels), BF16),
        in_specs=[once(x.shape) for x in whole]
        + [rows_of(LANES), rows_of(channels)]
        + [UNUSED] * len(more),
        out_specs=rows_of(channels),
        scratch_shapes=[
            pltpu.VMEM((tall + 6, cols + 16, LANES), F32),
            pltpu.VMEM((tall, cols, LANES), F32),
        ],
        input_output_aliases={8: 0} if more else {},
        compiler_params=params(56),
        cost_estimate=estimate(4),
        name="input_grad",
    )(*whole, mask, cot, *more)


def finish_kernel(
    a_ref, load_a_ref, b_ref, load_ref, small_ref, wo_ref, wi_ref, gk_ref, gsc_ref, gga_ref, gsh_ref, gbo_ref, gbi_ref
):
    channels = wi_ref.shape[0]
    border = a_ref.shape[3]
    rest = channels - border
    blocks = channels // LANES
    for index, ref in ((0, wo_ref), (1, wi_ref)):
        came_a = load_a_ref[index * border : (index + 1) * border, :].astype(F32)
        came_b = load_ref[index * rest : (index + 1) * rest, :].astype(F32)
        grad = jnp.concatenate([a_ref[index, 0, 0] + came_a, b_ref[index, 1, 0] + came_b], axis=0)
        ref[...] = grad.T if index == 0 else grad
    for block in range(blocks):
        at = 2 * rest + block * 64
        total = small_ref[block] + load_ref[at : at + 64, :].astype(F32)
        lanes = slice(block * LANES, (block + 1) * LANES)
        for row in range(7):
            gk_ref[row, :, lanes] = total[row * 8 : row * 8 + 7]
        for row, ref in enumerate((gsc_ref, gga_ref, gsh_ref, gbo_ref)):
            ref[:, lanes] = total[56 + row : 57 + row]
        for row in range(4):
            to = slice(row * channels + block * LANES, row * channels + (block + 1) * LANES)
            gbi_ref[:, to] = total[60 + row : 61 + row]


def finish(first, load_first, second, load, small, hidden):
    channels = first.shape[3] + second.shape[3]
    width = first.shape[4]
    line = jax.ShapeDtypeStruct((1, channels), F32)
    return pl.pallas_call(
        finish_kernel,
        out_shape=[
            jax.ShapeDtypeStruct((width, channels), F32),
            jax.ShapeDtypeStruct((channels, width), F32),
            jax.ShapeDtypeStruct((7, 7, channels), F32),
            line,
            line,
            line,
            line,
            jax.ShapeDtypeStruct((1, hidden), F32),
        ],
        compiler_params=params(56),
        cost_estimate=estimate(2),
        name="finish",
    )(first, load_first, second, load, small)


def swap(values, axis, bit):
    count = lax.axis_size(axis)
    return lax.ppermute(values, axis, [(i, i ^ bit) for i in range(count)])


def bits_of(axis):
    return [1 << k for k in range(int(math.log2(lax.axis_size(axis))))]


def after(value, *others):
    return lax.optimization_barrier((value,) + others)[0]


def halves(values, axis, dim, bit):
    mine = (lax.axis_index(axis) // bit) % 2 == 1
    shape = values.shape
    paired = values.reshape(shape[:dim] + (shape[dim] // 2, 2) + shape[dim + 1 :])
    low = lax.index_in_dim(paired, 0, dim + 1, keepdims=False)
    high = lax.index_in_dim(paired, 1, dim + 1, keepdims=False)
    return jnp.where(mine, high, low), jnp.where(mine, low, high).astype(BF16)


def side_halo(last, first):
    count = lax.axis_size("lon")
    ahead = [(i, (i + 1) % count) for i in range(count)]
    back = [((i + 1) % count, i) for i in range(count)]
    return lax.ppermute(last, "lon", ahead), lax.ppermute(first, "lon", back)


def end_rows(head, tail, left, right):
    rows = left.shape[0]
    return (
        jnp.concatenate([left[rows - 3 :], tail, right[rows - 3 :]], axis=1),
        jnp.concatenate([left[:3], head, right[:3]], axis=1),
    )


def end_halo(tail, head):
    count = lax.axis_size("lat")
    ahead = [(i, i + 1) for i in range(count - 1)]
    back = [(i + 1, i) for i in range(count - 1)]
    return lax.ppermute(tail, "lat", ahead), lax.ppermute(head, "lat", back)


def per_device(
    fields,
    land_mask,
    cotangent,
    kernel,
    layer_norm_gain,
    layer_norm_bias,
    w_in,
    b_in,
    w_out,
    b_out,
    layer_scale,
):
    rows, cols, channels = fields.shape
    cells = rows * cols
    hidden = w_in.shape[1]
    n_lon, n_lat = lax.axis_size("lon"), lax.axis_size("lat")
    gain, bias = layer_norm_gain.reshape(1, -1), layer_norm_bias.reshape(1, -1)
    scale = layer_scale.reshape(1, -1)
    cot_rows = cotangent.reshape(cells, channels)
    mask = jnp.broadcast_to(land_mask.astype(F32)[:, :, None], (rows, cols, LANES))
    ocean = land_mask.astype(BF16)[:, :, None]
    left, right = side_halo(fields[:, cols - 3 :] * ocean[:, cols - 3 :], fields[:, :3] * ocean[:, :3])
    lon = lax.axis_index("lon")
    core, side_y = lon % 2, (lon // 2) % 2
    quads = 4 * jnp.arange(n_lon // 4, dtype=jnp.int32)
    order = jnp.concatenate(
        [quads + 2 * y + c for c in (1 - core, core) for y in (1 - side_y, side_y)]
    )
    top, bot = end_halo(
        *end_rows(
            fields[:3] * ocean[:3], fields[rows - 3 :] * ocean[rows - 3 :],
            after(left, mask, order), after(right, mask, order),
        )
    )

    d_conv, mixed, sums, g_bi, sent, kept = expand(
        order, left, right, top, bot, kernel, gain, bias, scale, b_out.reshape(1, -1), mask, cot_rows,
        fields, w_in, b_in.reshape(1, -1), w_out, n_lon, n_lat,
    )
    got = swap(sent, "lon", 1)
    d_conv = d_conv.reshape(rows, cols, channels)
    d_left, d_right = side_halo(d_conv[:, cols - 3 :], d_conv[:, :3])

    far = n_lon // 4
    border = channels // 2
    lon_bits = [("lon", 1, bit) for bit in bits_of("lon")[2:]]
    lat_bits = [("lat", 2, bit) for bit in bits_of("lat")]

    def split_lat(x):
        if x.shape[2] != n_lat:
            x = x.reshape(x.shape[0], x.shape[1], x.shape[3], n_lat, -1).transpose(0, 1, 3, 2, 4)
        return x

    def pair(lons, piece, last=None):
        a, b = (kept, got) if last is None else (after(kept, last), after(got, last))
        return split_lat(a[:, lons, :, piece].astype(F32) + b[:, lons, :, piece].astype(F32))

    def fold(mine, sent, axis, bit, last):
        return after(mine, last) + after(swap(sent, axis, bit), last).astype(F32)

    first, second = slice(0, border), slice(border, channels)
    near_lons, far_lons = slice(far, 2 * far), slice(0, far)
    far_first = pair(far_lons, first).astype(BF16)
    got_first = swap(far_first, "lon", 2)
    cut_b = halves(pair(slice(0, 2 * far), second), *lat_bits[0])
    rest = (mask, left, right, top, bot, d_conv, sums, g_bi)
    small = filter_grad(after(fields, far_first, cut_b[1]), *rest, 0)
    d_tail, d_head = end_rows(
        d_conv[:3], d_conv[rows - 3 :], after(d_left, small), after(d_right, small)
    )
    d_top, d_bot = end_halo(d_tail, d_head)
    for (axis, _, bit), follow in zip(lat_bits[:-1], lat_bits[1:]):
        cut_b = halves(fold(*cut_b, axis, bit, small), *follow)

    def pack(sent, small):
        return jnp.concatenate([sent.reshape(-1, LANES), small.astype(BF16).reshape(-1, LANES)])

    def ride(came, sent, small, last):
        size = sent.size // LANES
        own = after(lax.reduce_precision(small, 8, 7), last)
        return came[:size].reshape(sent.shape).astype(F32), own + came[size:].astype(F32).reshape(small.shape)

    small = filter_grad(after(fields, d_tail, d_head, cut_b[1]), *rest, 1, small)
    alone = small
    whole = pair(near_lons, first, alone) + after(got_first, alone).astype(F32)
    whole_b = fold(*cut_b, lat_bits[-1][0], lat_bits[-1][2], alone)
    far_second = whole_b[:, far_lons].astype(BF16)
    back = (d_left, d_right, d_top, d_bot, kernel, mask, cotangent)
    grad_fields, block = None, 0
    steps = lon_bits + lat_bits
    early = halves(whole, *steps[0])[1]
    small = after(alone, early, far_second) + after(swap(alone, "lon", 1), early, far_second)
    for index, (axis, dim, bit) in enumerate(steps):
        mine, sent = halves(whole, axis, dim, bit)
        load = pack(sent, small)
        last = load
        if index >= len(steps) - 2:
            count = 2 if grad_fields is None else 1
            last = grad_fields = input_grad(
                after(d_conv, load, far_second), *back, block, count, grad_fields
            )
            block += count
        load_a, mine_a = after(swap(load, axis, bit), last), after(mine, last)
        came, small = ride(load_a, sent, small, last)
        whole = mine_a + came
    load = pack(far_second, small)
    last = grad_fields = input_grad(after(d_conv, load), *back, block, 1, grad_fields)
    if not lon_bits and whole.shape[-1] == LANES:
        load = after(swap(load, "lon", 2), last)
        grad_wo, grad_wi, grad_k, *lines, g_bi = finish(
            mine_a, load_a, after(whole_b, last), load, after(lax.reduce_precision(small, 8, 7), last), hidden
        )
        g_scale, g_gain, g_shift, g_bo = (line.reshape(channels) for line in lines)
    else:
        came, small = ride(after(swap(load, "lon", 2), last), far_second, small, last)
        whole_b = after(whole_b, last)[:, near_lons] + came
        for axis, dim, bit in lon_bits:
            whole_b = fold(*halves(whole_b, axis, dim, bit), axis, bit, last)
        grad_w = jnp.concatenate([x[:, 0, 0] for x in (whole, whole_b)], axis=1)
        grad_wo, grad_wi = grad_w[0].T, grad_w[1]
        small = small.transpose(1, 0, 2).reshape(8, 8, channels)
        grad_k, g_bi = small[:7, :7], small[7, 4:]
        g_scale, g_gain, g_shift, g_bo = (small[7, i] for i in range(4))
    return (
        mixed.reshape(rows, cols, channels),
        grad_fields,
        grad_k,
        g_gain,
        g_shift,
        grad_wi,
        g_bi.reshape(hidden),
        grad_wo,
        g_bo,
        g_scale,
    )


def solution(mesh):
    placed = (
        P(("grp", "lat"), "lon", None),
        P(("grp", "lat"), "lon"),
        P(("grp", "lat"), "lon", None),
        P(),
        P(),
        P(),
        P(),
        P(),
        P(),
        P(),
        P(),
    )
    return jax.shard_map(
        per_device,
        mesh=mesh,
        in_specs=placed,
        out_specs=(
            P(("grp", "lat"), "lon", None),
            P(("grp", "lat"), "lon", None),
            P("grp", None, None),
            P("grp"),
            P("grp"),
            P("grp", ("lon", "lat")),
            P("grp"),
            P(("lon", "lat"), "grp"),
            P("grp"),
            P("grp"),
        ),
        check_vma=False,
    )
```

```python
import functools
import math

import jax
import jax.numpy as jnp
from jax import lax
from jax.experimental import pallas as pl
from jax.experimental.pallas import tpu as pltpu
from jax.sharding import PartitionSpec as P

F32 = jnp.float32
BF16 = jnp.bfloat16
LANES = 128
SUB = 8


def params(mib):
    return pltpu.CompilerParams(vmem_limit_bytes=mib * 1024 * 1024)


def estimate(micros):
    return pl.CostEstimate(
        flops=int(micros * 1.15e9), bytes_accessed=int(micros * 3.6e6), transcendentals=0
    )


def once(shape):
    zeros = (0,) * len(shape)
    return pl.BlockSpec(shape, lambda *_: zeros, pipeline_mode=pl.Buffered(1))


UNUSED = pl.BlockSpec(memory_space=pl.ANY)


def whole_spec(shape):
    zeros = (0,) * len(shape)
    return pl.BlockSpec(shape, lambda *_: zeros)


def shifted(window, row, start, offset):
    return window[row, pl.ds(start + offset, SUB), :]


def lane_block(index):
    return pl.ds(pl.multiple_of(index * LANES, LANES), LANES)


def each_lane_block(channels, body):
    def one(index, _):
        body(lane_block(index))
        return 0

    lax.fori_loop(0, channels // LANES, one, 0)


def band_conv(window, k_ref, lanes, starts, rows, pad, flip):
    sums = {}
    for col_off in range(7):
        at = 6 - col_off if flip else col_off
        weights = [k_ref[6 - p if flip else p, at : at + 1, lanes] for p in range(7)]
        for start in starts:
            for src in range(window.shape[0]):
                hits = [(src - pad - row_off + 3, row_off) for row_off in range(7)]
                hits = [(out, row_off) for out, row_off in hits if 0 <= out < rows]
                if not hits:
                    continue
                cells = shifted(window, src, start, 5 + col_off)
                for out, row_off in hits:
                    term = weights[row_off] * cells
                    key = (out, start)
                    sums[key] = sums[key] + term if key in sums else term
    return sums


def gelu_twice(x):
    root = math.sqrt(2.0 / math.pi)
    inner = root + (root * 0.044715) * (x * x)
    tanh = jnp.tanh(x * inner)
    both = 1.0 + tanh
    value = x * both
    slope = both + value * ((1.0 - tanh) * (3.0 * inner - 2.0 * root))
    return value, slope


def expand_kernel(
    order_ref,
    l_ref, r_ref, t_ref, b_ref, k_ref, gain_ref, bias_ref, scale_ref, bo_ref, m_ref, cot_ref, f_ref,
    wi_ref, bi_ref, wo_ref,
    dconv_ref, first_ref, last_ref, mixed_ref, sums_ref, gbi_ref, sent_ref, kept_ref,
    window, conv, xhat_s, inv_s, normed, normed_t, dbr, dbr_t, act, dpre, d_normed, branch, pre_s, d_act,
):
    rows, cols, channels = f_ref.shape
    cells = rows * cols
    strip = 16
    chunk = 128
    step_now = pl.program_id(0)
    wide = channels // LANES

    def strips(body, sums):
        def some(index, sums):
            places = [
                (2 * index + more, at, pl.ds(pl.multiple_of((2 * index + more) * cols + at, strip), strip))
                for more in range(2)
                for at in range(0, cols, strip)
            ]
            return body(places, sums)

        return lax.fori_loop(0, rows // 2, some, sums)

    def folded(values):
        return sum(value[:SUB] + value[SUB:] for value in values)

    def mean(values):
        return [jnp.mean(value, axis=-1, keepdims=True) for value in values]

    def ocean(places):
        return [jnp.concatenate([m_ref[row, at : at + strip, :]] * wide, axis=1) for row, at, _ in places]

    zero = jnp.zeros((SUB, channels), F32)

    @pl.when(step_now == 0)
    def _():
        branch[...] = jnp.zeros_like(branch)
        d_normed[...] = jnp.zeros_like(d_normed)

        def cotangents(places, total):
            grads = [
                mask * (scale_ref[...] * cot_ref[here, :].astype(F32))
                for mask, (_, _, here) in zip(ocean(places), places)
            ]
            for (_, _, here), grad in zip(places, grads):
                dbr[here, :] = (0.5 * grad).astype(BF16)
            return total + folded(grads)

        sums_ref[0] = strips(cotangents, zero)
        for at in range(0, cells, chunk):
            here = slice(at, at + chunk)
            dbr_t[:, here] = dbr[here, :].T
        share = wo_ref.shape[0] // wide

        def convolve(index, _):
            lanes = lane_block(index)
            units = pl.ds(pl.multiple_of(index * share, LANES), share)
            fill_window(window, f_ref[:, :, lanes].astype(F32) * m_ref[...], l_ref, r_ref, t_ref, b_ref, lanes)
            for start in range(0, cols, SUB):
                here = slice(start * rows, (start + SUB) * rows)
                d_act[here, units] = lax.dot_general(
                    dbr[here, :], wo_ref[units, :], (((1,), (1,)), ((), ())), preferred_element_type=F32
                )
                sums = band_conv(window, k_ref, lanes, (start,), rows, 3, False)
                for row in range(rows):
                    conv[row, start : start + SUB, lanes] = sums[row, start]
            return 0

        lax.fori_loop(0, wide, convolve, 0)

        def standardize(places, _):
            xs = [conv[row, at : at + strip, :] for row, at, _ in places]
            centered = [x - average for x, average in zip(xs, mean(xs))]
            invs = [lax.rsqrt(var + 1e-06) for var in mean([x * x for x in centered])]
            for (_, _, here), x, inv in zip(places, centered, invs):
                xhat = x * inv
                xhat_s[here, :] = xhat
                inv_s[here, :] = jnp.broadcast_to(inv, (strip, LANES))
                normed[here, :] = (xhat * gain_ref[...] + bias_ref[...]).astype(BF16)
            return 0

        strips(standardize, 0)
        for at in range(0, cells, chunk):
            here = slice(at, at + chunk)
            normed_t[:, here] = normed[here, :].T

    block = act.shape[1]
    cut = min(block, 256)
    count = block // cut
    _, parts, _, width = sent_ref.shape
    is_sent = step_now < pl.num_programs(0) // 2
    base = pl.multiple_of(order_ref[step_now] * block, LANES)

    def products(index):
        lanes = slice(index * cut, (index + 1) * cut)
        pre_s[index % 2] = jnp.dot(normed[...], wi_ref[:, lanes], preferred_element_type=F32)

    def activate(index):
        lanes = slice(index * cut, (index + 1) * cut)
        units = pl.ds(pl.multiple_of(base + index * cut, LANES), cut)
        bias = bi_ref[:, lanes]
        total = jnp.zeros((SUB, cut), F32)
        for at in range(0, cells, strip):
            here = slice(at, at + strip)
            value, slope = gelu_twice(pre_s[index % 2, here, :] + bias)
            act[here, lanes] = value.astype(BF16)
            d_pre = d_act[here, units] * slope
            dpre[here, lanes] = d_pre.astype(BF16)
            total = total + (d_pre[:SUB] + d_pre[SUB:])
        gbi_ref[:, lanes] = jnp.sum(total, axis=0, keepdims=True)

    def weight_grads(index):
        left = index * cut
        for which, (rows_t, source) in enumerate(((dbr_t, act), (normed_t, dpre))):
            grad = jnp.dot(
                rows_t[...], source[:, left : left + cut], preferred_element_type=F32
            ).astype(BF16)

            size = min(width, cut)
            for at in range(0, cut, size):
                lat, into = divmod(left + at, width)
                spot = (which, lat, slice(None), slice(into, into + size))
                value = grad[:, at : at + size]
                kept_ref[spot] = value
                sent_ref[spot] = jnp.where(is_sent, value, sent_ref[spot])

    products(0)
    for index in range(count):
        if index + 1 < count:
            products(index + 1)
        activate(index)
        if index > 0:
            weight_grads(index - 1)
    weight_grads(count - 1)
    branch[...] += jnp.dot(act[...], wo_ref[pl.ds(base, block), :], preferred_element_type=F32)
    d_normed[...] += lax.dot_general(
        dpre[...], wi_ref[...], (((1,), (1,)), ((), ())), preferred_element_type=F32
    )

    @pl.when(step_now == pl.num_programs(0) - 1)
    def _():
        def norm_back(places, sums):
            heres = [here for _, _, here in places]
            branches = [
                mask * (0.5 * branch[here, :] + bo_ref[...]) for mask, here in zip(ocean(places), heres)
            ]
            xhats = [xhat_s[here, :] for here in heres]
            grads = [d_normed[here, :] for here in heres]
            terms = [grad * xhat for grad, xhat in zip(grads, xhats)]
            es = [grad * gain_ref[...] for grad in grads]
            m1s = mean(es)
            m2s = mean([e * xhat for e, xhat in zip(es, xhats)])
            for (row, at, here), e, xhat, m1, m2, value in zip(places, es, xhats, m1s, m2s, branches):
                inv = jnp.concatenate([inv_s[here, :]] * wide, axis=1)
                d_conv = inv * (e - m1 - xhat * m2)
                dconv_ref[here, :] = d_conv.astype(BF16)
                if at == 0:
                    first_ref[row] = d_conv[:3].astype(BF16)
                if at == cols - strip:
                    last_ref[row] = d_conv[strip - 3 :].astype(BF16)
                field = f_ref[row, at : at + strip, :].astype(F32)
                mixed_ref[here, :] = (field + value * scale_ref[...]).astype(BF16)
            products = [value * cot_ref[here, :].astype(F32) for value, here in zip(branches, heres)]
            return tuple(total + folded(x) for total, x in zip(sums, (products, terms, grads)))

        sums_ref[1], sums_ref[2], sums_ref[3] = strips(norm_back, (zero, zero, zero))


def expand(
    order, left, right, top, bot, kernel, gain, bias, scale, b_out, mask, cot, fields, w_in, b_in, w_out, n_lon, n_lat
):
    rows, cols, channels = fields.shape
    hidden = w_in.shape[1]
    cells = rows * cols
    block = hidden // n_lon
    split = n_lat if (block // n_lat) % LANES == 0 else 1
    turn = n_lon // 2
    grads = (split, channels, block // split)
    given = (left, right, top, bot, kernel, gain, bias, scale, b_out, mask, cot, fields)

    def sent_at(h, order):
        return (0, jnp.minimum(h, turn - 1), 0, 0, 0)

    def kept_at(h, order):
        return (0, jnp.maximum(h - turn, 0), 0, 0, 0)

    return pl.pallas_call(
        expand_kernel,
        grid_spec=pltpu.PrefetchScalarGridSpec(
            num_scalar_prefetch=1,
            grid=(n_lon,),
            in_specs=[once(x.shape) for x in given]
            + [
                pl.BlockSpec((channels, block), lambda h, order: (0, order[h])),
                pl.BlockSpec((1, block), lambda h, order: (0, order[h])),
                once(w_out.shape),
            ],
            out_specs=[
                once((cells, channels)),
                once((rows, 3, channels)),
                once((rows, 3, channels)),
                once((cells, channels)),
                once((4, SUB, channels)),
                pl.BlockSpec((1, block), lambda h, order: (0, order[h])),
                pl.BlockSpec((2, None) + grads, sent_at),
                pl.BlockSpec((2, None) + grads, kept_at),
            ],
            scratch_shapes=[
                pltpu.VMEM((rows + 6, cols + 16, LANES), F32),
                pltpu.VMEM((rows, cols, channels), F32),
                pltpu.VMEM((cells, channels), F32),
                pltpu.VMEM((cells, LANES), F32),
                pltpu.VMEM((cells, channels), BF16),
                pltpu.VMEM((channels, cells), BF16),
                pltpu.VMEM((cells, channels), BF16),
                pltpu.VMEM((channels, cells), BF16),
                pltpu.VMEM((cells, block), BF16),
                pltpu.VMEM((cells, block), BF16),
                pltpu.VMEM((cells, channels), F32),
                pltpu.VMEM((cells, channels), F32),
                pltpu.VMEM((2, cells, min(block, 256)), F32),
                pltpu.VMEM((cells, hidden), F32),
            ],
        ),
        out_shape=[
            jax.ShapeDtypeStruct((cells, channels), BF16),
            jax.ShapeDtypeStruct((rows, 3, channels), BF16),
            jax.ShapeDtypeStruct((rows, 3, channels), BF16),
            jax.ShapeDtypeStruct((cells, channels), BF16),
            jax.ShapeDtypeStruct((4, SUB, channels), F32),
            jax.ShapeDtypeStruct((1, hidden), F32),
            jax.ShapeDtypeStruct((2, turn) + grads, BF16),
            jax.ShapeDtypeStruct((2, turn) + grads, BF16),
        ],
        compiler_params=params(56),
        cost_estimate=estimate(20),
        name="expand",
    )(order, *given, w_in, b_in, w_out)


def fill_window(window, center, l_ref, r_ref, t_ref, b_ref, lanes):
    rows, cols, _ = center.shape
    window[0:3, 5 : 11 + cols, :] = t_ref[:, :, lanes].astype(F32)
    window[3 : 3 + rows, 5:8, :] = l_ref[:, :, lanes].astype(F32)
    window[3 : 3 + rows, 8 : 8 + cols, :] = center
    window[3 : 3 + rows, 8 + cols : 11 + cols, :] = r_ref[:, :, lanes].astype(F32)
    window[3 + rows : 6 + rows, 5 : 11 + cols, :] = b_ref[:, :, lanes].astype(F32)


def filter_grad_kernel(first, f_ref, m_ref, l_ref, r_ref, t_ref, b_ref, d_ref, sums_ref, gbi_ref, *rest):
    o_ref, window, grad = rest[-3:]
    rows, cols, channels = f_ref.shape
    blocks = channels // LANES

    def block(index, _):
        lanes = lane_block(first + index)
        fill_window(window, f_ref[:, :, lanes].astype(F32) * m_ref[...], l_ref, r_ref, t_ref, b_ref, lanes)
        grad[...] = d_ref[:, :, lanes].astype(F32)
        for col_off in range(7):

            def band(step, sums):
                start = pl.multiple_of(step * SUB, SUB)
                sums = list(sums)
                held = {}
                for src in range(rows + 6):
                    if src < rows:
                        held[src] = grad[src, pl.ds(start, SUB), :]
                    cells = shifted(window, src, start, 5 + col_off)
                    for row_off in range(7):
                        out = src - row_off
                        if 0 <= out < rows:
                            sums[row_off] = sums[row_off] + held[out] * cells
                return tuple(sums)

            sums = tuple(jnp.zeros((SUB, LANES), F32) for _ in range(7))
            sums = lax.fori_loop(0, cols // SUB, band, sums)
            for row_off in range(7):
                at = row_off * 8 + col_off
                o_ref[index, at : at + 1, :] = jnp.sum(sums[row_off], axis=0, keepdims=True)
        for row_off in range(7):
            o_ref[index, row_off * 8 + 7 : row_off * 8 + 8, :] = jnp.zeros((1, LANES), F32)
        for at, source in enumerate((1, 2, 3, 0)):
            o_ref[index, 56 + at : 57 + at, :] = jnp.sum(sums_ref[source, :, lanes], axis=0, keepdims=True)
        for at in range(4):
            o_ref[index, 60 + at : 61 + at, :] = gbi_ref[:, lane_block(at * blocks + first + index)]
        return 0

    lax.fori_loop(0, o_ref.shape[0], block, 0)


def filter_grad(fields, mask, left, right, top, bot, d_conv, sums, gbi, half, old=None):
    rows, cols, channels = fields.shape
    blocks = channels // LANES
    whole = (fields, mask, left, right, top, bot, d_conv, sums, gbi)
    more = [] if old is None else [old]
    return pl.pallas_call(
        functools.partial(filter_grad_kernel, half * (blocks // 2)),
        grid=(1,),
        out_shape=jax.ShapeDtypeStruct((blocks, 64, LANES), F32),
        in_specs=[once(x.shape) for x in whole] + [UNUSED] * len(more),
        out_specs=pl.BlockSpec((blocks // 2, 64, LANES), lambda i: (half, 0, 0)),
        scratch_shapes=[
            pltpu.VMEM((rows + 6, cols + 16, LANES), F32),
            pltpu.VMEM((rows, cols, LANES), F32),
        ],
        input_output_aliases={9: 0} if more else {},
        compiler_params=params(16),
        cost_estimate=estimate(4),
        name="filter_grad",
    )(*whole, *more)


def input_grad_kernel(first, d_ref, l_ref, r_ref, t_ref, b_ref, k_ref, m_ref, cot_ref, *rest):
    o_ref, window, grad = rest[-3:]
    rows, cols, channels = d_ref.shape
    tall = o_ref.shape[0]
    low, high = max(0, first - 3), min(rows, first + tall + 3)
    inside = slice(low - first + 3, high - first + 3)
    group = 32 // tall * SUB

    def block(lanes):
        if first < 3:
            window[0 : 3 - first, 5 : 11 + cols, :] = t_ref[first:3, :, lanes].astype(F32)
        if first + tall > rows - 3:
            below = first + tall + 3 - rows
            window[tall + 6 - below : tall + 6, 5 : 11 + cols, :] = b_ref[:below, :, lanes].astype(F32)
        window[inside, 5:8, :] = l_ref[low:high, :, lanes].astype(F32)
        window[inside, 8 : 8 + cols, :] = d_ref[low:high, :, lanes].astype(F32)
        window[inside, 8 + cols : 11 + cols, :] = r_ref[low:high, :, lanes].astype(F32)
        for left in range(0, cols, group):
            starts = range(left, min(left + group, cols), SUB)
            sums = band_conv(window, k_ref, lanes, starts, tall, 3, True)
            for (row, start), value in sums.items():
                grad[row, start : start + SUB, :] = value
        o_ref[:, :, lanes] = (cot_ref[:, :, lanes].astype(F32) + m_ref[...] * grad[...]).astype(BF16)

    each_lane_block(channels, block)


def input_grad(d_conv, left, right, top, bot, kernel, mask, cot, first, quarters, old=None):
    rows, cols, channels = d_conv.shape
    tall = rows // 4 * quarters

    def rows_of(width):
        return pl.BlockSpec((tall, cols, width), lambda i: (first // quarters, 0, 0))

    whole = (d_conv, left, right, top, bot, kernel)
    more = [] if old is None else [old]
    return pl.pallas_call(
        functools.partial(input_grad_kernel, rows // 4 * first),
        grid=(1,),
        out_shape=jax.ShapeDtypeStruct((rows, cols, channels), BF16),
        in_specs=[once(x.shape) for x in whole]
        + [rows_of(LANES), rows_of(channels)]
        + [UNUSED] * len(more),
        out_specs=rows_of(channels),
        scratch_shapes=[
            pltpu.VMEM((tall + 6, cols + 16, LANES), F32),
            pltpu.VMEM((tall, cols, LANES), F32),
        ],
        input_output_aliases={8: 0} if more else {},
        compiler_params=params(16),
        cost_estimate=estimate(4),
        name="input_grad",
    )(*whole, mask, cot, *more)


def finish_kernel(
    a_ref, load_a_ref, b_ref, load_ref, small_ref, wo_ref, wi_ref, gk_ref, gsc_ref, gga_ref, gsh_ref, gbo_ref, gbi_ref
):
    channels = wi_ref.shape[0]
    border = a_ref.shape[3]
    rest = channels - border
    blocks = channels // LANES
    for index, ref in ((0, wo_ref), (1, wi_ref)):
        came_a = load_a_ref[index * border : (index + 1) * border, :].astype(F32)
        came_b = load_ref[index * rest : (index + 1) * rest, :].astype(F32)
        grad = jnp.concatenate([a_ref[index, 0, 0] + came_a, b_ref[index, 1, 0] + came_b], axis=0)
        ref[...] = grad.T if index == 0 else grad
    for block in range(blocks):
        at = 2 * rest + block * 64
        total = small_ref[block] + load_ref[at : at + 64, :].astype(F32)
        lanes = slice(block * LANES, (block + 1) * LANES)
        for row in range(7):
            gk_ref[row, :, lanes] = total[row * 8 : row * 8 + 7]
        for row, ref in enumerate((gsc_ref, gga_ref, gsh_ref, gbo_ref)):
            ref[:, lanes] = total[56 + row : 57 + row]
        for row in range(4):
            to = slice(row * channels + block * LANES, row * channels + (block + 1) * LANES)
            gbi_ref[:, to] = total[60 + row : 61 + row]


def finish(first, load_first, second, load, small, hidden):
    channels = first.shape[3] + second.shape[3]
    width = first.shape[4]
    line = jax.ShapeDtypeStruct((1, channels), F32)
    return pl.pallas_call(
        finish_kernel,
        out_shape=[
            jax.ShapeDtypeStruct((width, channels), F32),
            jax.ShapeDtypeStruct((channels, width), F32),
            jax.ShapeDtypeStruct((7, 7, channels), F32),
            line,
            line,
            line,
            line,
            jax.ShapeDtypeStruct((1, hidden), F32),
        ],
        compiler_params=params(16),
        cost_estimate=estimate(2),
        name="finish",
    )(first, load_first, second, load, small)


def swap(values, axis, bit):
    count = lax.axis_size(axis)
    return lax.ppermute(values, axis, [(i, i ^ bit) for i in range(count)])


def bits_of(axis):
    return [1 << k for k in range(int(math.log2(lax.axis_size(axis))))]


def after(value, *others):
    return lax.optimization_barrier((value,) + others)[0]


def halves(values, axis, dim, bit):
    mine = (lax.axis_index(axis) // bit) % 2 == 1
    shape = values.shape
    paired = values.reshape(shape[:dim] + (shape[dim] // 2, 2) + shape[dim + 1 :])
    low = lax.index_in_dim(paired, 0, dim + 1, keepdims=False)
    high = lax.index_in_dim(paired, 1, dim + 1, keepdims=False)
    return jnp.where(mine, high, low), jnp.where(mine, low, high).astype(BF16)


def side_halo(last, first):
    count = lax.axis_size("lon")
    ahead = [(i, (i + 1) % count) for i in range(count)]
    back = [((i + 1) % count, i) for i in range(count)]
    return lax.ppermute(last, "lon", ahead), lax.ppermute(first, "lon", back)


def end_rows(head, tail, left, right):
    rows = left.shape[0]
    return (
        jnp.concatenate([left[rows - 3 :], tail, right[rows - 3 :]], axis=1),
        jnp.concatenate([left[:3], head, right[:3]], axis=1),
    )


def end_halo(tail, head):
    count = lax.axis_size("lat")
    ahead = [(i, i + 1) for i in range(count - 1)]
    back = [(i + 1, i) for i in range(count - 1)]
    return lax.ppermute(tail, "lat", ahead), lax.ppermute(head, "lat", back)


def per_device(
    fields,
    land_mask,
    cotangent,
    kernel,
    layer_norm_gain,
    layer_norm_bias,
    w_in,
    b_in,
    w_out,
    b_out,
    layer_scale,
):
    rows, cols, channels = fields.shape
    cells = rows * cols
    hidden = w_in.shape[1]
    n_lon, n_lat = lax.axis_size("lon"), lax.axis_size("lat")
    gain, bias = layer_norm_gain.reshape(1, -1), layer_norm_bias.reshape(1, -1)
    scale = layer_scale.reshape(1, -1)
    cot_rows = cotangent.reshape(cells, channels)
    mask = jnp.broadcast_to(land_mask.astype(F32)[:, :, None], (rows, cols, LANES))
    ocean = land_mask.astype(BF16)[:, :, None]
    left, right = side_halo(fields[:, cols - 3 :] * ocean[:, cols - 3 :], fields[:, :3] * ocean[:, :3])
    lon = lax.axis_index("lon")
    core, side_y = lon % 2, (lon // 2) % 2
    quads = 4 * jnp.arange(n_lon // 4, dtype=jnp.int32)
    order = jnp.concatenate(
        [quads + 2 * y + c for c in (1 - core, core) for y in (1 - side_y, side_y)]
    )
    top, bot = end_halo(
        *end_rows(
            fields[:3] * ocean[:3], fields[rows - 3 :] * ocean[rows - 3 :],
            after(left, mask, order), after(right, mask, order),
        )
    )

    d_conv, d_first, d_last, mixed, sums, g_bi, sent, kept = expand(
        order, left, right, top, bot, kernel, gain, bias, scale, b_out.reshape(1, -1), mask, cot_rows,
        fields, w_in, b_in.reshape(1, -1), w_out, n_lon, n_lat,
    )
    got = swap(sent, "lon", 1)
    d_conv = d_conv.reshape(rows, cols, channels)
    d_left, d_right = side_halo(d_last, d_first)

    far = n_lon // 4
    border = channels // 2
    lon_bits = [("lon", 1, bit) for bit in bits_of("lon")[2:]]
    lat_bits = [("lat", 2, bit) for bit in bits_of("lat")]

    def split_lat(x):
        if x.shape[2] != n_lat:
            x = x.reshape(x.shape[0], x.shape[1], x.shape[3], n_lat, -1).transpose(0, 1, 3, 2, 4)
        return x

    def pair(lons, piece, last=None):
        a, b = (kept, got) if last is None else (after(kept, last), after(got, last))
        return split_lat(a[:, lons, :, piece].astype(F32) + b[:, lons, :, piece].astype(F32))

    def fold(mine, sent, axis, bit, last):
        return after(mine, last) + after(swap(sent, axis, bit), last).astype(F32)

    first, second = slice(0, border), slice(border, channels)
    near_lons, far_lons = slice(far, 2 * far), slice(0, far)
    far_first = pair(far_lons, first).astype(BF16)
    got_first = swap(far_first, "lon", 2)
    cut_b = halves(pair(slice(0, 2 * far), second), *lat_bits[0])
    rest = (mask, left, right, top, bot, d_conv, sums, g_bi)
    small = filter_grad(after(fields, far_first, cut_b[1]), *rest, 0)
    d_tail, d_head = end_rows(
        d_conv[:3], d_conv[rows - 3 :], after(d_left, small), after(d_right, small)
    )
    d_top, d_bot = end_halo(d_tail, d_head)
    for (axis, _, bit), follow in zip(lat_bits[:-1], lat_bits[1:]):
        cut_b = halves(fold(*cut_b, axis, bit, small), *follow)

    def pack(sent, small):
        return jnp.concatenate([sent.reshape(-1, LANES), small.astype(BF16).reshape(-1, LANES)])

    def ride(came, sent, small, last):
        size = sent.size // LANES
        own = after(lax.reduce_precision(small, 8, 7), last)
        return came[:size].reshape(sent.shape).astype(F32), own + came[size:].astype(F32).reshape(small.shape)

    small = filter_grad(after(fields, d_tail, d_head, cut_b[1]), *rest, 1, small)
    alone = small
    whole = pair(near_lons, first, alone) + after(got_first, alone).astype(F32)
    whole_b = fold(*cut_b, lat_bits[-1][0], lat_bits[-1][2], alone)
    far_second = whole_b[:, far_lons].astype(BF16)
    back = (d_left, d_right, d_top, d_bot, kernel, mask, cotangent)
    grad_fields, block = None, 0
    steps = lon_bits + lat_bits
    early = halves(whole, *steps[0])[1]
    small = after(alone, early, far_second) + after(swap(alone, "lon", 1), early, far_second)
    for index, (axis, dim, bit) in enumerate(steps):
        mine, sent = halves(whole, axis, dim, bit)
        load = pack(sent, small)
        last = load
        if index >= len(steps) - 2:
            count = 2 if grad_fields is None else 1
            last = grad_fields = input_grad(
                after(d_conv, load, far_second), *back, block, count, grad_fields
            )
            block += count
        load_a, mine_a = after(swap(load, axis, bit), last), after(mine, last)
        came, small = ride(load_a, sent, small, last)
        whole = mine_a + came
    load = pack(far_second, small)
    last = grad_fields = input_grad(after(d_conv, load), *back, block, 1, grad_fields)
    if not lon_bits and whole.shape[-1] == LANES:
        load = after(swap(load, "lon", 2), last)
        grad_wo, grad_wi, grad_k, *lines, g_bi = finish(
            mine_a, load_a, after(whole_b, last), load, after(lax.reduce_precision(small, 8, 7), last), hidden
        )
        g_scale, g_gain, g_shift, g_bo = (line.reshape(channels) for line in lines)
    else:
        came, small = ride(after(swap(load, "lon", 2), last), far_second, small, last)
        whole_b = after(whole_b, last)[:, near_lons] + came
        for axis, dim, bit in lon_bits:
            whole_b = fold(*halves(whole_b, axis, dim, bit), axis, bit, last)
        grad_w = jnp.concatenate([x[:, 0, 0] for x in (whole, whole_b)], axis=1)
        grad_wo, grad_wi = grad_w[0].T, grad_w[1]
        small = small.transpose(1, 0, 2).reshape(8, 8, channels)
        grad_k, g_bi = small[:7, :7], small[7, 4:]
        g_scale, g_gain, g_shift, g_bo = (small[7, i] for i in range(4))
    return (
        mixed.reshape(rows, cols, channels),
        grad_fields,
        grad_k,
        g_gain,
        g_shift,
        grad_wi,
        g_bi.reshape(hidden),
        grad_wo,
        g_bo,
        g_scale,
    )


def solution(mesh):
    placed = (
        P(("grp", "lat"), "lon", None),
        P(("grp", "lat"), "lon"),
        P(("grp", "lat"), "lon", None),
        P(),
        P(),
        P(),
        P(),
        P(),
        P(),
        P(),
        P(),
    )
    return jax.shard_map(
        per_device,
        mesh=mesh,
        in_specs=placed,
        out_specs=(
            P(("grp", "lat"), "lon", None),
            P(("grp", "lat"), "lon", None),
            P("grp", None, None),
            P("grp"),
            P("grp"),
            P("grp", ("lon", "lat")),
            P("grp"),
            P(("lon", "lat"), "grp"),
            P("grp"),
            P("grp"),
        ),
        check_vma=False,
    )
```

```python
import functools
import math

import jax
import jax.numpy as jnp
from jax import lax
from jax.experimental import pallas as pl
from jax.experimental.pallas import tpu as pltpu
from jax.sharding import PartitionSpec as P

F32 = jnp.float32
BF16 = jnp.bfloat16
LANES = 128
SUB = 8


def params(mib):
    return pltpu.CompilerParams(vmem_limit_bytes=mib * 1024 * 1024)


def estimate(micros):
    return pl.CostEstimate(
        flops=int(micros * 1.15e9), bytes_accessed=int(micros * 3.6e6), transcendentals=0
    )


def once(shape):
    zeros = (0,) * len(shape)
    return pl.BlockSpec(shape, lambda *_: zeros, pipeline_mode=pl.Buffered(1))


UNUSED = pl.BlockSpec(memory_space=pl.ANY)


def whole_spec(shape):
    zeros = (0,) * len(shape)
    return pl.BlockSpec(shape, lambda *_: zeros)


def shifted(window, row, start, offset):
    return window[row, pl.ds(start + offset, SUB), :]


def lane_block(index):
    return pl.ds(pl.multiple_of(index * LANES, LANES), LANES)


def each_lane_block(channels, body):
    def one(index, _):
        body(lane_block(index))
        return 0

    lax.fori_loop(0, channels // LANES, one, 0)


def band_conv(window, k_ref, lanes, starts, rows, pad, flip):
    sums = {}
    for col_off in range(7):
        at = 6 - col_off if flip else col_off
        weights = [k_ref[6 - p if flip else p, at : at + 1, lanes] for p in range(7)]
        for start in starts:
            for src in range(window.shape[0]):
                hits = [(src - pad - row_off + 3, row_off) for row_off in range(7)]
                hits = [(out, row_off) for out, row_off in hits if 0 <= out < rows]
                if not hits:
                    continue
                cells = shifted(window, src, start, 5 + col_off)
                for out, row_off in hits:
                    term = weights[row_off] * cells
                    key = (out, start)
                    sums[key] = sums[key] + term if key in sums else term
    return sums


def gelu_twice(x):
    root = math.sqrt(2.0 / math.pi)
    inner = root + (root * 0.044715) * (x * x)
    tanh = jnp.tanh(x * inner)
    both = 1.0 + tanh
    value = x * both
    slope = both + value * ((1.0 - tanh) * (3.0 * inner - 2.0 * root))
    return value, slope


def expand_kernel(
    order_ref,
    l_ref, r_ref, t_ref, b_ref, k_ref, gain_ref, bias_ref, scale_ref, bo_ref, m_ref, cot_ref, f_ref,
    wi_ref, bi_ref, wo_ref,
    dconv_ref, first_ref, last_ref, mixed_ref, sums_ref, gbi_ref, sent_ref, kept_ref,
    window, conv, xhat_s, inv_s, normed, normed_t, dbr, dbr_t, act, dpre, d_normed, branch, pre_s, d_act,
):
    rows, cols, channels = f_ref.shape
    cells = rows * cols
    strip = 16
    chunk = 128
    step_now = pl.program_id(0)
    wide = channels // LANES

    def strips(body, sums):
        def some(index, sums):
            places = [
                (2 * index + more, at, pl.ds(pl.multiple_of((2 * index + more) * cols + at, strip), strip))
                for more in range(2)
                for at in range(0, cols, strip)
            ]
            return body(places, sums)

        return lax.fori_loop(0, rows // 2, some, sums)

    def folded(values):
        return sum(value[:SUB] + value[SUB:] for value in values)

    def mean(values):
        return [jnp.mean(value, axis=-1, keepdims=True) for value in values]

    def ocean(places):
        return [jnp.concatenate([m_ref[row, at : at + strip, :]] * wide, axis=1) for row, at, _ in places]

    zero = jnp.zeros((SUB, channels), F32)

    @pl.when(step_now == 0)
    def _():
        branch[...] = jnp.zeros_like(branch)
        d_normed[...] = jnp.zeros_like(d_normed)

        def cotangents(places, total):
            grads = [
                mask * (scale_ref[...] * cot_ref[here, :].astype(F32))
                for mask, (_, _, here) in zip(ocean(places), places)
            ]
            for (_, _, here), grad in zip(places, grads):
                dbr[here, :] = (0.5 * grad).astype(BF16)
            return total + folded(grads)

        sums_ref[0] = strips(cotangents, zero)
        for at in range(0, cells, chunk):
            here = slice(at, at + chunk)
            dbr_t[:, here] = dbr[here, :].T
        share = wo_ref.shape[0] // wide

        def convolve(index, _):
            lanes = lane_block(index)
            units = pl.ds(pl.multiple_of(index * share, LANES), share)
            fill_window(window, f_ref[:, :, lanes].astype(F32) * m_ref[...], l_ref, r_ref, t_ref, b_ref, lanes)
            for start in range(0, cols, SUB):
                here = slice(start * rows, (start + SUB) * rows)
                d_act[here, units] = lax.dot_general(
                    dbr[here, :], wo_ref[units, :], (((1,), (1,)), ((), ())), preferred_element_type=F32
                )
                sums = band_conv(window, k_ref, lanes, (start,), rows, 3, False)
                for row in range(rows):
                    conv[row, start : start + SUB, lanes] = sums[row, start]
            return 0

        lax.fori_loop(0, wide, convolve, 0)

        def standardize(places, _):
            xs = [conv[row, at : at + strip, :] for row, at, _ in places]
            centered = [x - average for x, average in zip(xs, mean(xs))]
            invs = [lax.rsqrt(var + 1e-06) for var in mean([x * x for x in centered])]
            for (_, _, here), x, inv in zip(places, centered, invs):
                xhat = x * inv
                xhat_s[here, :] = xhat
                inv_s[here, :] = jnp.broadcast_to(inv, (strip, LANES))
                normed[here, :] = (xhat * gain_ref[...] + bias_ref[...]).astype(BF16)
            return 0

        strips(standardize, 0)
        for at in range(0, cells, chunk):
            here = slice(at, at + chunk)
            normed_t[:, here] = normed[here, :].T

    block = act.shape[1]
    cut = min(block, 256)
    count = block // cut
    _, parts, _, width = sent_ref.shape
    is_sent = step_now < pl.num_programs(0) // 2
    base = pl.multiple_of(order_ref[step_now] * block, LANES)

    def products(index):
        lanes = slice(index * cut, (index + 1) * cut)
        pre_s[index % 2] = jnp.dot(normed[...], wi_ref[:, lanes], preferred_element_type=F32)

    def activate(index):
        lanes = slice(index * cut, (index + 1) * cut)
        units = pl.ds(pl.multiple_of(base + index * cut, LANES), cut)
        bias = bi_ref[:, lanes]
        total = jnp.zeros((SUB, cut), F32)
        for at in range(0, cells, strip):
            here = slice(at, at + strip)
            value, slope = gelu_twice(pre_s[index % 2, here, :] + bias)
            act[here, lanes] = value.astype(BF16)
            d_pre = d_act[here, units] * slope
            dpre[here, lanes] = d_pre.astype(BF16)
            total = total + (d_pre[:SUB] + d_pre[SUB:])
        gbi_ref[:, lanes] = jnp.sum(total, axis=0, keepdims=True)

    def weight_grads(index):
        left = index * cut
        for which, (rows_t, source) in enumerate(((dbr_t, act), (normed_t, dpre))):
            grad = jnp.dot(
                rows_t[...], source[:, left : left + cut], preferred_element_type=F32
            ).astype(BF16)

            size = min(width, cut)
            for at in range(0, cut, size):
                lat, into = divmod(left + at, width)
                spot = (which, lat, slice(None), slice(into, into + size))
                value = grad[:, at : at + size]
                kept_ref[spot] = value
                sent_ref[spot] = jnp.where(is_sent, value, sent_ref[spot])

    products(0)
    for index in range(count):
        if index + 1 < count:
            products(index + 1)
        activate(index)
        if index > 0:
            weight_grads(index - 1)
    weight_grads(count - 1)
    branch[...] += jnp.dot(act[...], wo_ref[pl.ds(base, block), :], preferred_element_type=F32)
    d_normed[...] += lax.dot_general(
        dpre[...], wi_ref[...], (((1,), (1,)), ((), ())), preferred_element_type=F32
    )

    @pl.when(step_now == pl.num_programs(0) - 1)
    def _():
        def norm_back(places, sums):
            heres = [here for _, _, here in places]
            branches = [
                mask * (0.5 * branch[here, :] + bo_ref[...]) for mask, here in zip(ocean(places), heres)
            ]
            xhats = [xhat_s[here, :] for here in heres]
            grads = [d_normed[here, :] for here in heres]
            terms = [grad * xhat for grad, xhat in zip(grads, xhats)]
            es = [grad * gain_ref[...] for grad in grads]
            m1s = mean(es)
            m2s = mean([e * xhat for e, xhat in zip(es, xhats)])
            for (row, at, here), e, xhat, m1, m2, value in zip(places, es, xhats, m1s, m2s, branches):
                inv = jnp.concatenate([inv_s[here, :]] * wide, axis=1)
                d_conv = inv * (e - m1 - xhat * m2)
                dconv_ref[here, :] = d_conv.astype(BF16)
                if at == 0:
                    first_ref[row] = d_conv[:3].astype(BF16)
                if at == cols - strip:
                    last_ref[row] = d_conv[strip - 3 :].astype(BF16)
                field = f_ref[row, at : at + strip, :].astype(F32)
                mixed_ref[here, :] = (field + value * scale_ref[...]).astype(BF16)
            products = [value * cot_ref[here, :].astype(F32) for value, here in zip(branches, heres)]
            return tuple(total + folded(x) for total, x in zip(sums, (products, terms, grads)))

        sums_ref[1], sums_ref[2], sums_ref[3] = strips(norm_back, (zero, zero, zero))


def expand(
    order, left, right, top, bot, kernel, gain, bias, scale, b_out, mask, cot, fields, w_in, b_in, w_out, n_lon, n_lat
):
    rows, cols, channels = fields.shape
    hidden = w_in.shape[1]
    cells = rows * cols
    block = hidden // n_lon
    split = n_lat if (block // n_lat) % LANES == 0 else 1
    turn = n_lon // 2
    grads = (split, channels, block // split)
    given = (left, right, top, bot, kernel, gain, bias, scale, b_out, mask, cot, fields)

    def sent_at(h, order):
        return (0, jnp.minimum(h, turn - 1), 0, 0, 0)

    def kept_at(h, order):
        return (0, jnp.maximum(h - turn, 0), 0, 0, 0)

    return pl.pallas_call(
        expand_kernel,
        grid_spec=pltpu.PrefetchScalarGridSpec(
            num_scalar_prefetch=1,
            grid=(n_lon,),
            in_specs=[once(x.shape) for x in given]
            + [
                pl.BlockSpec((channels, block), lambda h, order: (0, order[h])),
                pl.BlockSpec((1, block), lambda h, order: (0, order[h])),
                once(w_out.shape),
            ],
            out_specs=[
                once((cells, channels)),
                once((rows, 3, channels)),
                once((rows, 3, channels)),
                once((cells, channels)),
                once((4, SUB, channels)),
                pl.BlockSpec((1, block), lambda h, order: (0, order[h])),
                pl.BlockSpec((2, None) + grads, sent_at),
                pl.BlockSpec((2, None) + grads, kept_at),
            ],
            scratch_shapes=[
                pltpu.VMEM((rows + 6, cols + 16, LANES), F32),
                pltpu.VMEM((rows, cols, channels), F32),
                pltpu.VMEM((cells, channels), F32),
                pltpu.VMEM((cells, LANES), F32),
                pltpu.VMEM((cells, channels), BF16),
                pltpu.VMEM((channels, cells), BF16),
                pltpu.VMEM((cells, channels), BF16),
                pltpu.VMEM((channels, cells), BF16),
                pltpu.VMEM((cells, block), BF16),
                pltpu.VMEM((cells, block), BF16),
                pltpu.VMEM((cells, channels), F32),
                pltpu.VMEM((cells, channels), F32),
                pltpu.VMEM((2, cells, min(block, 256)), F32),
                pltpu.VMEM((cells, hidden), F32),
            ],
        ),
        out_shape=[
            jax.ShapeDtypeStruct((cells, channels), BF16),
            jax.ShapeDtypeStruct((rows, 3, channels), BF16),
            jax.ShapeDtypeStruct((rows, 3, channels), BF16),
            jax.ShapeDtypeStruct((cells, channels), BF16),
            jax.ShapeDtypeStruct((4, SUB, channels), F32),
            jax.ShapeDtypeStruct((1, hidden), F32),
            jax.ShapeDtypeStruct((2, turn) + grads, BF16),
            jax.ShapeDtypeStruct((2, turn) + grads, BF16),
        ],
        compiler_params=params(56),
        cost_estimate=estimate(20),
        name="expand",
    )(order, *given, w_in, b_in, w_out)


def fill_window(window, center, l_ref, r_ref, t_ref, b_ref, lanes):
    rows, cols, _ = center.shape
    window[0:3, 5 : 11 + cols, :] = t_ref[:, :, lanes].astype(F32)
    window[3 : 3 + rows, 5:8, :] = l_ref[:, :, lanes].astype(F32)
    window[3 : 3 + rows, 8 : 8 + cols, :] = center
    window[3 : 3 + rows, 8 + cols : 11 + cols, :] = r_ref[:, :, lanes].astype(F32)
    window[3 + rows : 6 + rows, 5 : 11 + cols, :] = b_ref[:, :, lanes].astype(F32)


def filter_grad_kernel(first, f_ref, m_ref, l_ref, r_ref, t_ref, b_ref, d_ref, sums_ref, gbi_ref, *rest):
    o_ref, window, grad = rest[-3:]
    rows, cols, channels = f_ref.shape
    blocks = channels // LANES

    def block(index, _):
        lanes = lane_block(first + index)
        fill_window(window, f_ref[:, :, lanes].astype(F32) * m_ref[...], l_ref, r_ref, t_ref, b_ref, lanes)
        grad[...] = d_ref[:, :, lanes].astype(F32)
        for col_off in range(7):

            def band(step, sums):
                start = pl.multiple_of(step * SUB, SUB)
                sums = list(sums)
                held = {}
                for src in range(rows + 6):
                    if src < rows:
                        held[src] = grad[src, pl.ds(start, SUB), :]
                    cells = shifted(window, src, start, 5 + col_off)
                    for row_off in range(7):
                        out = src - row_off
                        if 0 <= out < rows:
                            sums[row_off] = sums[row_off] + held[out] * cells
                return tuple(sums)

            sums = tuple(jnp.zeros((SUB, LANES), F32) for _ in range(7))
            sums = lax.fori_loop(0, cols // SUB, band, sums)
            for row_off in range(7):
                at = row_off * 8 + col_off
                o_ref[index, at : at + 1, :] = jnp.sum(sums[row_off], axis=0, keepdims=True)
        for row_off in range(7):
            o_ref[index, row_off * 8 + 7 : row_off * 8 + 8, :] = jnp.zeros((1, LANES), F32)
        for at, source in enumerate((1, 2, 3, 0)):
            o_ref[index, 56 + at : 57 + at, :] = jnp.sum(sums_ref[source, :, lanes], axis=0, keepdims=True)
        for at in range(4):
            o_ref[index, 60 + at : 61 + at, :] = gbi_ref[:, lane_block(at * blocks + first + index)]
        return 0

    lax.fori_loop(0, o_ref.shape[0], block, 0)


def filter_grad(fields, mask, left, right, top, bot, d_conv, sums, gbi, half, old=None):
    rows, cols, channels = fields.shape
    blocks = channels // LANES
    whole = (fields, mask, left, right, top, bot, d_conv, sums, gbi)
    more = [] if old is None else [old]
    return pl.pallas_call(
        functools.partial(filter_grad_kernel, half * (blocks // 2)),
        grid=(1,),
        out_shape=jax.ShapeDtypeStruct((blocks, 64, LANES), F32),
        in_specs=[once(x.shape) for x in whole] + [UNUSED] * len(more),
        out_specs=pl.BlockSpec((blocks // 2, 64, LANES), lambda i: (half, 0, 0)),
        scratch_shapes=[
            pltpu.VMEM((rows + 6, cols + 16, LANES), F32),
            pltpu.VMEM((rows, cols, LANES), F32),
        ],
        input_output_aliases={9: 0} if more else {},
        compiler_params=params(16),
        cost_estimate=estimate(4),
        name="filter_grad",
    )(*whole, *more)


def input_grad_kernel(first, d_ref, l_ref, r_ref, t_ref, b_ref, k_ref, m_ref, cot_ref, *rest):
    o_ref, window, grad = rest[-3:]
    rows, cols, channels = d_ref.shape
    tall = o_ref.shape[0]
    low, high = max(0, first - 3), min(rows, first + tall + 3)
    inside = slice(low - first + 3, high - first + 3)
    group = 32 // tall * SUB

    def block(lanes):
        if first < 3:
            window[0 : 3 - first, 5 : 11 + cols, :] = t_ref[first:3, :, lanes].astype(F32)
        if first + tall > rows - 3:
            below = first + tall + 3 - rows
            window[tall + 6 - below : tall + 6, 5 : 11 + cols, :] = b_ref[:below, :, lanes].astype(F32)
        window[inside, 5:8, :] = l_ref[low:high, :, lanes].astype(F32)
        window[inside, 8 : 8 + cols, :] = d_ref[low:high, :, lanes].astype(F32)
        window[inside, 8 + cols : 11 + cols, :] = r_ref[low:high, :, lanes].astype(F32)
        for left in range(0, cols, group):
            starts = range(left, min(left + group, cols), SUB)
            sums = band_conv(window, k_ref, lanes, starts, tall, 3, True)
            for (row, start), value in sums.items():
                grad[row, start : start + SUB, :] = value
        o_ref[:, :, lanes] = (cot_ref[:, :, lanes].astype(F32) + m_ref[...] * grad[...]).astype(BF16)

    each_lane_block(channels, block)


def input_grad(d_conv, left, right, top, bot, kernel, mask, cot, first, quarters, old=None):
    rows, cols, channels = d_conv.shape
    tall = rows // 4 * quarters

    def rows_of(width):
        return pl.BlockSpec((tall, cols, width), lambda i: (first // quarters, 0, 0))

    whole = (d_conv, left, right, top, bot, kernel)
    more = [] if old is None else [old]
    return pl.pallas_call(
        functools.partial(input_grad_kernel, rows // 4 * first),
        grid=(1,),
        out_shape=jax.ShapeDtypeStruct((rows, cols, channels), BF16),
        in_specs=[once(x.shape) for x in whole]
        + [rows_of(LANES), rows_of(channels)]
        + [UNUSED] * len(more),
        out_specs=rows_of(channels),
        scratch_shapes=[
            pltpu.VMEM((tall + 6, cols + 16, LANES), F32),
            pltpu.VMEM((tall, cols, LANES), F32),
        ],
        input_output_aliases={8: 0} if more else {},
        compiler_params=params(16),
        cost_estimate=estimate(4),
        name="input_grad",
    )(*whole, mask, cot, *more)


def finish_kernel(
    a_ref, load_a_ref, b_ref, load_ref, small_ref, wo_ref, wi_ref, gk_ref, gsc_ref, gga_ref, gsh_ref, gbo_ref, gbi_ref
):
    channels = wi_ref.shape[0]
    border = a_ref.shape[3]
    rest = channels - border
    blocks = channels // LANES
    for index, ref in ((0, wo_ref), (1, wi_ref)):
        came_a = load_a_ref[index * border : (index + 1) * border, :].astype(F32)
        came_b = load_ref[index * rest : (index + 1) * rest, :].astype(F32)
        grad = jnp.concatenate([a_ref[index, 0, 0] + came_a, b_ref[index, 1, 0] + came_b], axis=0)
        ref[...] = grad.T if index == 0 else grad
    for block in range(blocks):
        at = 2 * rest + block * 64
        total = small_ref[block] + load_ref[at : at + 64, :].astype(F32)
        lanes = slice(block * LANES, (block + 1) * LANES)
        for row in range(7):
            gk_ref[row, :, lanes] = total[row * 8 : row * 8 + 7]
        for row, ref in enumerate((gsc_ref, gga_ref, gsh_ref, gbo_ref)):
            ref[:, lanes] = total[56 + row : 57 + row]
        for row in range(4):
            to = slice(row * channels + block * LANES, row * channels + (block + 1) * LANES)
            gbi_ref[:, to] = total[60 + row : 61 + row]


def finish(first, load_first, second, load, small, hidden):
    channels = first.shape[3] + second.shape[3]
    width = first.shape[4]
    line = jax.ShapeDtypeStruct((1, channels), F32)
    return pl.pallas_call(
        finish_kernel,
        out_shape=[
            jax.ShapeDtypeStruct((width, channels), F32),
            jax.ShapeDtypeStruct((channels, width), F32),
            jax.ShapeDtypeStruct((7, 7, channels), F32),
            line,
            line,
            line,
            line,
            jax.ShapeDtypeStruct((1, hidden), F32),
        ],
        compiler_params=params(16),
        cost_estimate=estimate(2),
        name="finish",
    )(first, load_first, second, load, small)


def swap(values, axis, bit):
    count = lax.axis_size(axis)
    return lax.ppermute(values, axis, [(i, i ^ bit) for i in range(count)])


def bits_of(axis):
    return [1 << k for k in range(int(math.log2(lax.axis_size(axis))))]


def after(value, *others):
    return lax.optimization_barrier((value,) + others)[0]


def halves(values, axis, dim, bit):
    mine = (lax.axis_index(axis) // bit) % 2 == 1
    shape = values.shape
    paired = values.reshape(shape[:dim] + (shape[dim] // 2, 2) + shape[dim + 1 :])
    low = lax.index_in_dim(paired, 0, dim + 1, keepdims=False)
    high = lax.index_in_dim(paired, 1, dim + 1, keepdims=False)
    return jnp.where(mine, high, low), jnp.where(mine, low, high).astype(BF16)


def side_halo(last, first):
    count = lax.axis_size("lon")
    ahead = [(i, (i + 1) % count) for i in range(count)]
    back = [((i + 1) % count, i) for i in range(count)]
    return lax.ppermute(last, "lon", ahead), lax.ppermute(first, "lon", back)


def end_rows(head, tail, left, right):
    rows = left.shape[0]
    return (
        jnp.concatenate([left[rows - 3 :], tail, right[rows - 3 :]], axis=1),
        jnp.concatenate([left[:3], head, right[:3]], axis=1),
    )


def end_halo(tail, head):
    count = lax.axis_size("lat")
    ahead = [(i, i + 1) for i in range(count - 1)]
    back = [(i + 1, i) for i in range(count - 1)]
    return lax.ppermute(tail, "lat", ahead), lax.ppermute(head, "lat", back)


def per_device(
    fields,
    land_mask,
    cotangent,
    kernel,
    layer_norm_gain,
    layer_norm_bias,
    w_in,
    b_in,
    w_out,
    b_out,
    layer_scale,
):
    rows, cols, channels = fields.shape
    cells = rows * cols
    hidden = w_in.shape[1]
    n_lon, n_lat = lax.axis_size("lon"), lax.axis_size("lat")
    gain, bias = layer_norm_gain.reshape(1, -1), layer_norm_bias.reshape(1, -1)
    scale = layer_scale.reshape(1, -1)
    cot_rows = cotangent.reshape(cells, channels)
    mask = jnp.broadcast_to(land_mask.astype(F32)[:, :, None], (rows, cols, LANES))
    ocean = land_mask.astype(BF16)[:, :, None]
    left, right = side_halo(fields[:, cols - 3 :] * ocean[:, cols - 3 :], fields[:, :3] * ocean[:, :3])
    lon = lax.axis_index("lon")
    core, side_y = lon % 2, (lon // 2) % 2
    quads = 4 * jnp.arange(n_lon // 4, dtype=jnp.int32)
    order = jnp.concatenate(
        [quads + 2 * y + c for c in (1 - core, core) for y in (1 - side_y, side_y)]
    )
    top, bot = end_halo(
        *end_rows(
            fields[:3] * ocean[:3], fields[rows - 3 :] * ocean[rows - 3 :],
            after(left, mask, order), after(right, mask, order),
        )
    )

    d_conv, d_first, d_last, mixed, sums, g_bi, sent, kept = expand(
        order, left, right, top, bot, kernel, gain, bias, scale, b_out.reshape(1, -1), mask, cot_rows,
        fields, w_in, b_in.reshape(1, -1), w_out, n_lon, n_lat,
    )
    got = swap(sent, "lon", 1)
    d_conv = d_conv.reshape(rows, cols, channels)
    d_left, d_right = side_halo(d_last, d_first)

    far = n_lon // 4
    border = channels * 3 // 4
    lon_bits = [("lon", 1, bit) for bit in bits_of("lon")[2:]]
    lat_bits = [("lat", 2, bit) for bit in bits_of("lat")]

    def split_lat(x):
        if x.shape[2] != n_lat:
            x = x.reshape(x.shape[0], x.shape[1], x.shape[3], n_lat, -1).transpose(0, 1, 3, 2, 4)
        return x

    def pair(lons, piece, last=None):
        a, b = (kept, got) if last is None else (after(kept, last), after(got, last))
        return split_lat(a[:, lons, :, piece].astype(F32) + b[:, lons, :, piece].astype(F32))

    def fold(mine, sent, axis, bit, last):
        return after(mine, last) + after(swap(sent, axis, bit), last).astype(F32)

    first, second = slice(0, border), slice(border, channels)
    near_lons, far_lons = slice(far, 2 * far), slice(0, far)
    far_first = pair(far_lons, first).astype(BF16)
    got_first = swap(far_first, "lon", 2)
    cut_b = halves(pair(slice(0, 2 * far), second, far_first), *lat_bits[0])
    rest = (mask, left, right, top, bot, d_conv, sums, g_bi)
    small = filter_grad(after(fields, far_first, cut_b[1]), *rest, 0)
    d_tail, d_head = end_rows(
        d_conv[:3], d_conv[rows - 3 :], after(d_left, small), after(d_right, small)
    )
    d_top, d_bot = end_halo(d_tail, d_head)
    for (axis, _, bit), follow in zip(lat_bits[:-1], lat_bits[1:]):
        cut_b = halves(fold(*cut_b, axis, bit, small), *follow)

    def pack(sent, small):
        return jnp.concatenate([sent.reshape(-1, LANES), small.astype(BF16).reshape(-1, LANES)])

    def ride(came, sent, small, last):
        size = sent.size // LANES
        own = after(lax.reduce_precision(small, 8, 7), last)
        return came[:size].reshape(sent.shape).astype(F32), own + came[size:].astype(F32).reshape(small.shape)

    small = filter_grad(after(fields, d_tail, d_head, cut_b[1]), *rest, 1, small)
    alone = small
    whole = pair(near_lons, first, alone) + after(got_first, alone).astype(F32)
    whole_b = fold(*cut_b, lat_bits[-1][0], lat_bits[-1][2], alone)
    far_second = whole_b[:, far_lons].astype(BF16)
    back = (d_left, d_right, d_top, d_bot, kernel, mask, cotangent)
    grad_fields, block = None, 0
    steps = lon_bits + lat_bits
    early = halves(whole, *steps[0])[1]
    small = after(alone, early, far_second) + after(swap(alone, "lon", 1), early, far_second)
    for index, (axis, dim, bit) in enumerate(steps):
        mine, sent = halves(whole, axis, dim, bit)
        load = pack(sent, small)
        last = load
        if index >= len(steps) - 2:
            count = 2 if grad_fields is None else 1
            last = grad_fields = input_grad(
                after(d_conv, load, far_second), *back, block, count, grad_fields
            )
            block += count
        load_a, mine_a = after(swap(load, axis, bit), last), after(mine, last)
        came, small = ride(load_a, sent, small, last)
        whole = mine_a + came
    load = pack(far_second, small)
    last = grad_fields = input_grad(after(d_conv, load), *back, block, 1, grad_fields)
    if not lon_bits and whole.shape[-1] == LANES:
        load = after(swap(load, "lon", 2), last)
        grad_wo, grad_wi, grad_k, *lines, g_bi = finish(
            mine_a, load_a, after(whole_b, last), load, after(lax.reduce_precision(small, 8, 7), last), hidden
        )
        g_scale, g_gain, g_shift, g_bo = (line.reshape(channels) for line in lines)
    else:
        came, small = ride(after(swap(load, "lon", 2), last), far_second, small, last)
        whole_b = after(whole_b, last)[:, near_lons] + came
        for axis, dim, bit in lon_bits:
            whole_b = fold(*halves(whole_b, axis, dim, bit), axis, bit, last)
        grad_w = jnp.concatenate([x[:, 0, 0] for x in (whole, whole_b)], axis=1)
        grad_wo, grad_wi = grad_w[0].T, grad_w[1]
        small = small.transpose(1, 0, 2).reshape(8, 8, channels)
        grad_k, g_bi = small[:7, :7], small[7, 4:]
        g_scale, g_gain, g_shift, g_bo = (small[7, i] for i in range(4))
    return (
        mixed.reshape(rows, cols, channels),
        grad_fields,
        grad_k,
        g_gain,
        g_shift,
        grad_wi,
        g_bi.reshape(hidden),
        grad_wo,
        g_bo,
        g_scale,
    )


def solution(mesh):
    placed = (
        P(("grp", "lat"), "lon", None),
        P(("grp", "lat"), "lon"),
        P(("grp", "lat"), "lon", None),
        P(),
        P(),
        P(),
        P(),
        P(),
        P(),
        P(),
        P(),
    )
    return jax.shard_map(
        per_device,
        mesh=mesh,
        in_specs=placed,
        out_specs=(
            P(("grp", "lat"), "lon", None),
            P(("grp", "lat"), "lon", None),
            P("grp", None, None),
            P("grp"),
            P("grp"),
            P("grp", ("lon", "lat")),
            P("grp"),
            P(("lon", "lat"), "grp"),
            P("grp"),
            P("grp"),
        ),
        check_vma=False,
    )
```

```python
import functools
import math

import jax
import jax.numpy as jnp
from jax import lax
from jax.experimental import pallas as pl
from jax.experimental.pallas import tpu as pltpu
from jax.sharding import PartitionSpec as P

F32 = jnp.float32
BF16 = jnp.bfloat16
LANES = 128
SUB = 8


def params(mib):
    return pltpu.CompilerParams(vmem_limit_bytes=mib * 1024 * 1024)


def estimate(micros):
    return pl.CostEstimate(
        flops=int(micros * 1.15e9), bytes_accessed=int(micros * 3.6e6), transcendentals=0
    )


def once(shape):
    zeros = (0,) * len(shape)
    return pl.BlockSpec(shape, lambda *_: zeros, pipeline_mode=pl.Buffered(1))


UNUSED = pl.BlockSpec(memory_space=pl.ANY)


def whole_spec(shape):
    zeros = (0,) * len(shape)
    return pl.BlockSpec(shape, lambda *_: zeros)


def shifted(window, row, start, offset):
    return window[row, pl.ds(start + offset, SUB), :]


def lane_block(index):
    return pl.ds(pl.multiple_of(index * LANES, LANES), LANES)


def each_lane_block(channels, body):
    def one(index, _):
        body(lane_block(index))
        return 0

    lax.fori_loop(0, channels // LANES, one, 0)


def band_conv(window, k_ref, lanes, starts, rows, pad, flip):
    sums = {}
    for col_off in range(7):
        at = 6 - col_off if flip else col_off
        weights = [k_ref[6 - p if flip else p, at : at + 1, lanes] for p in range(7)]
        for start in starts:
            for src in range(window.shape[0]):
                hits = [(src - pad - row_off + 3, row_off) for row_off in range(7)]
                hits = [(out, row_off) for out, row_off in hits if 0 <= out < rows]
                if not hits:
                    continue
                cells = shifted(window, src, start, 5 + col_off)
                for out, row_off in hits:
                    term = weights[row_off] * cells
                    key = (out, start)
                    sums[key] = sums[key] + term if key in sums else term
    return sums


def gelu_twice(x):
    root = math.sqrt(2.0 / math.pi)
    inner = root + (root * 0.044715) * (x * x)
    tanh = jnp.tanh(x * inner)
    both = 1.0 + tanh
    value = x * both
    slope = both + value * ((1.0 - tanh) * (3.0 * inner - 2.0 * root))
    return value, slope


def expand_kernel(
    order_ref,
    l_ref, r_ref, t_ref, b_ref, k_ref, gain_ref, bias_ref, scale_ref, bo_ref, m_ref, cot_ref, f_ref,
    wi_ref, bi_ref, wo_ref,
    dconv_ref, first_ref, last_ref, mixed_ref, sums_ref, gbi_ref, sent_ref, kept_ref,
    window, conv, xhat_s, inv_s, normed, normed_t, dbr, dbr_t, act, dpre, d_normed, branch, pre_s, d_act,
):
    rows, cols, channels = f_ref.shape
    cells = rows * cols
    strip = 16
    chunk = 128
    step_now = pl.program_id(0)
    wide = channels // LANES

    def strips(body, sums):
        def some(index, sums):
            places = [
                (2 * index + more, at, pl.ds(pl.multiple_of((2 * index + more) * cols + at, strip), strip))
                for more in range(2)
                for at in range(0, cols, strip)
            ]
            return body(places, sums)

        return lax.fori_loop(0, rows // 2, some, sums)

    def folded(values):
        return sum(value[:SUB] + value[SUB:] for value in values)

    def mean(values):
        return [jnp.mean(value, axis=-1, keepdims=True) for value in values]

    def ocean(places):
        return [jnp.concatenate([m_ref[row, at : at + strip, :]] * wide, axis=1) for row, at, _ in places]

    zero = jnp.zeros((SUB, channels), F32)

    @pl.when(step_now == 0)
    def _():
        branch[...] = jnp.zeros_like(branch)
        d_normed[...] = jnp.zeros_like(d_normed)

        def cotangents(places, total):
            grads = [
                mask * (scale_ref[...] * cot_ref[here, :].astype(F32))
                for mask, (_, _, here) in zip(ocean(places), places)
            ]
            for (_, _, here), grad in zip(places, grads):
                dbr[here, :] = (0.5 * grad).astype(BF16)
            return total + folded(grads)

        sums_ref[0] = strips(cotangents, zero)
        for at in range(0, cells, chunk):
            here = slice(at, at + chunk)
            dbr_t[:, here] = dbr[here, :].T
        share = wo_ref.shape[0] // wide

        def convolve(index, _):
            lanes = lane_block(index)
            units = pl.ds(pl.multiple_of(index * share, LANES), share)
            fill_window(window, f_ref[:, :, lanes].astype(F32) * m_ref[...], l_ref, r_ref, t_ref, b_ref, lanes)
            for start in range(0, cols, SUB):
                here = slice(start * rows, (start + SUB) * rows)
                d_act[here, units] = lax.dot_general(
                    dbr[here, :], wo_ref[units, :], (((1,), (1,)), ((), ())), preferred_element_type=F32
                )
                sums = band_conv(window, k_ref, lanes, (start,), rows, 3, False)
                for row in range(rows):
                    conv[row, start : start + SUB, lanes] = sums[row, start]
            return 0

        lax.fori_loop(0, wide, convolve, 0)

        def standardize(places, _):
            xs = [conv[row, at : at + strip, :] for row, at, _ in places]
            centered = [x - average for x, average in zip(xs, mean(xs))]
            invs = [lax.rsqrt(var + 1e-06) for var in mean([x * x for x in centered])]
            for (_, _, here), x, inv in zip(places, centered, invs):
                xhat = x * inv
                xhat_s[here, :] = xhat
                inv_s[here, :] = jnp.broadcast_to(inv, (strip, LANES))
                normed[here, :] = (xhat * gain_ref[...] + bias_ref[...]).astype(BF16)
            return 0

        strips(standardize, 0)
        for at in range(0, cells, chunk):
            here = slice(at, at + chunk)
            normed_t[:, here] = normed[here, :].T

    block = act.shape[1]
    cut = min(block, 256)
    count = block // cut
    _, parts, _, width = sent_ref.shape
    is_sent = step_now < pl.num_programs(0) // 2
    base = pl.multiple_of(order_ref[step_now] * block, LANES)

    def products(index):
        lanes = slice(index * cut, (index + 1) * cut)
        pre_s[index % 2] = jnp.dot(normed[...], wi_ref[:, lanes], preferred_element_type=F32)

    def activate(index):
        lanes = slice(index * cut, (index + 1) * cut)
        units = pl.ds(pl.multiple_of(base + index * cut, LANES), cut)
        bias = bi_ref[:, lanes]
        total = jnp.zeros((SUB, cut), F32)
        for at in range(0, cells, strip):
            here = slice(at, at + strip)
            value, slope = gelu_twice(pre_s[index % 2, here, :] + bias)
            act[here, lanes] = value.astype(BF16)
            d_pre = d_act[here, units] * slope
            dpre[here, lanes] = d_pre.astype(BF16)
            total = total + (d_pre[:SUB] + d_pre[SUB:])
        gbi_ref[:, lanes] = jnp.sum(total, axis=0, keepdims=True)

    def weight_grads(index):
        left = index * cut
        for which, (rows_t, source) in enumerate(((dbr_t, act), (normed_t, dpre))):
            grad = jnp.dot(
                rows_t[...], source[:, left : left + cut], preferred_element_type=F32
            ).astype(BF16)

            size = min(width, cut)
            for at in range(0, cut, size):
                lat, into = divmod(left + at, width)
                spot = (which, lat, slice(None), slice(into, into + size))
                value = grad[:, at : at + size]
                kept_ref[spot] = value
                sent_ref[spot] = jnp.where(is_sent, value, sent_ref[spot])

    products(0)
    for index in range(count):
        if index + 1 < count:
            products(index + 1)
        activate(index)
        if index > 0:
            weight_grads(index - 1)
    weight_grads(count - 1)
    branch[...] += jnp.dot(act[...], wo_ref[pl.ds(base, block), :], preferred_element_type=F32)
    d_normed[...] += lax.dot_general(
        dpre[...], wi_ref[...], (((1,), (1,)), ((), ())), preferred_element_type=F32
    )

    @pl.when(step_now == pl.num_programs(0) - 1)
    def _():
        def norm_back(places, sums):
            heres = [here for _, _, here in places]
            branches = [
                mask * (0.5 * branch[here, :] + bo_ref[...]) for mask, here in zip(ocean(places), heres)
            ]
            xhats = [xhat_s[here, :] for here in heres]
            grads = [d_normed[here, :] for here in heres]
            terms = [grad * xhat for grad, xhat in zip(grads, xhats)]
            es = [grad * gain_ref[...] for grad in grads]
            m1s = mean(es)
            m2s = mean([e * xhat for e, xhat in zip(es, xhats)])
            for (row, at, here), e, xhat, m1, m2, value in zip(places, es, xhats, m1s, m2s, branches):
                inv = jnp.concatenate([inv_s[here, :]] * wide, axis=1)
                d_conv = inv * (e - m1 - xhat * m2)
                dconv_ref[here, :] = d_conv.astype(BF16)
                if at == 0:
                    first_ref[row] = d_conv[:3].astype(BF16)
                if at == cols - strip:
                    last_ref[row] = d_conv[strip - 3 :].astype(BF16)
                field = f_ref[row, at : at + strip, :].astype(F32)
                mixed_ref[here, :] = (field + value * scale_ref[...]).astype(BF16)
            products = [value * cot_ref[here, :].astype(F32) for value, here in zip(branches, heres)]
            return tuple(total + folded(x) for total, x in zip(sums, (products, terms, grads)))

        sums_ref[1], sums_ref[2], sums_ref[3] = strips(norm_back, (zero, zero, zero))


def expand(
    order, left, right, top, bot, kernel, gain, bias, scale, b_out, mask, cot, fields, w_in, b_in, w_out, n_lon, n_lat
):
    rows, cols, channels = fields.shape
    hidden = w_in.shape[1]
    cells = rows * cols
    block = hidden // n_lon
    split = n_lat if (block // n_lat) % LANES == 0 else 1
    turn = n_lon // 2
    grads = (split, channels, block // split)
    given = (left, right, top, bot, kernel, gain, bias, scale, b_out, mask, cot, fields)

    def sent_at(h, order):
        return (0, jnp.minimum(h, turn - 1), 0, 0, 0)

    def kept_at(h, order):
        return (0, jnp.maximum(h - turn, 0), 0, 0, 0)

    return pl.pallas_call(
        expand_kernel,
        grid_spec=pltpu.PrefetchScalarGridSpec(
            num_scalar_prefetch=1,
            grid=(n_lon,),
            in_specs=[once(x.shape) for x in given]
            + [
                pl.BlockSpec((channels, block), lambda h, order: (0, order[h])),
                pl.BlockSpec((1, block), lambda h, order: (0, order[h])),
                once(w_out.shape),
            ],
            out_specs=[
                once((cells, channels)),
                once((rows, 3, channels)),
                once((rows, 3, channels)),
                once((cells, channels)),
                once((4, SUB, channels)),
                pl.BlockSpec((1, block), lambda h, order: (0, order[h])),
                pl.BlockSpec((2, None) + grads, sent_at),
                pl.BlockSpec((2, None) + grads, kept_at),
            ],
            scratch_shapes=[
                pltpu.VMEM((rows + 6, cols + 16, LANES), F32),
                pltpu.VMEM((rows, cols, channels), F32),
                pltpu.VMEM((cells, channels), F32),
                pltpu.VMEM((cells, LANES), F32),
                pltpu.VMEM((cells, channels), BF16),
                pltpu.VMEM((channels, cells), BF16),
                pltpu.VMEM((cells, channels), BF16),
                pltpu.VMEM((channels, cells), BF16),
                pltpu.VMEM((cells, block), BF16),
                pltpu.VMEM((cells, block), BF16),
                pltpu.VMEM((cells, channels), F32),
                pltpu.VMEM((cells, channels), F32),
                pltpu.VMEM((2, cells, min(block, 256)), F32),
                pltpu.VMEM((cells, hidden), F32),
            ],
        ),
        out_shape=[
            jax.ShapeDtypeStruct((cells, channels), BF16),
            jax.ShapeDtypeStruct((rows, 3, channels), BF16),
            jax.ShapeDtypeStruct((rows, 3, channels), BF16),
            jax.ShapeDtypeStruct((cells, channels), BF16),
            jax.ShapeDtypeStruct((4, SUB, channels), F32),
            jax.ShapeDtypeStruct((1, hidden), F32),
            jax.ShapeDtypeStruct((2, turn) + grads, BF16),
            jax.ShapeDtypeStruct((2, turn) + grads, BF16),
        ],
        compiler_params=params(42),
        cost_estimate=estimate(20),
        name="expand",
    )(order, *given, w_in, b_in, w_out)


def fill_window(window, center, l_ref, r_ref, t_ref, b_ref, lanes):
    rows, cols, _ = center.shape
    window[0:3, 5 : 11 + cols, :] = t_ref[:, :, lanes].astype(F32)
    window[3 : 3 + rows, 5:8, :] = l_ref[:, :, lanes].astype(F32)
    window[3 : 3 + rows, 8 : 8 + cols, :] = center
    window[3 : 3 + rows, 8 + cols : 11 + cols, :] = r_ref[:, :, lanes].astype(F32)
    window[3 + rows : 6 + rows, 5 : 11 + cols, :] = b_ref[:, :, lanes].astype(F32)


def filter_grad_kernel(first, f_ref, m_ref, l_ref, r_ref, t_ref, b_ref, d_ref, sums_ref, gbi_ref, *rest):
    o_ref, window, grad = rest[-3:]
    rows, cols, channels = f_ref.shape
    blocks = channels // LANES

    def block(index, _):
        lanes = lane_block(first + index)
        fill_window(window, f_ref[:, :, lanes].astype(F32) * m_ref[...], l_ref, r_ref, t_ref, b_ref, lanes)
        grad[...] = d_ref[:, :, lanes].astype(F32)
        for col_off in range(7):

            def band(step, sums):
                start = pl.multiple_of(step * SUB, SUB)
                sums = list(sums)
                held = {}
                for src in range(rows + 6):
                    if src < rows:
                        held[src] = grad[src, pl.ds(start, SUB), :]
                    cells = shifted(window, src, start, 5 + col_off)
                    for row_off in range(7):
                        out = src - row_off
                        if 0 <= out < rows:
                            sums[row_off] = sums[row_off] + held[out] * cells
                return tuple(sums)

            sums = tuple(jnp.zeros((SUB, LANES), F32) for _ in range(7))
            sums = lax.fori_loop(0, cols // SUB, band, sums)
            for row_off in range(7):
                at = row_off * 8 + col_off
                o_ref[index, at : at + 1, :] = jnp.sum(sums[row_off], axis=0, keepdims=True)
        for row_off in range(7):
            o_ref[index, row_off * 8 + 7 : row_off * 8 + 8, :] = jnp.zeros((1, LANES), F32)
        for at, source in enumerate((1, 2, 3, 0)):
            o_ref[index, 56 + at : 57 + at, :] = jnp.sum(sums_ref[source, :, lanes], axis=0, keepdims=True)
        for at in range(4):
            o_ref[index, 60 + at : 61 + at, :] = gbi_ref[:, lane_block(at * blocks + first + index)]
        return 0

    lax.fori_loop(0, o_ref.shape[0], block, 0)


def filter_grad(fields, mask, left, right, top, bot, d_conv, sums, gbi, half, old=None):
    rows, cols, channels = fields.shape
    blocks = channels // LANES
    whole = (fields, mask, left, right, top, bot, d_conv, sums, gbi)
    more = [] if old is None else [old]
    return pl.pallas_call(
        functools.partial(filter_grad_kernel, half * (blocks // 2)),
        grid=(1,),
        out_shape=jax.ShapeDtypeStruct((blocks, 64, LANES), F32),
        in_specs=[once(x.shape) for x in whole] + [UNUSED] * len(more),
        out_specs=pl.BlockSpec((blocks // 2, 64, LANES), lambda i: (half, 0, 0)),
        scratch_shapes=[
            pltpu.VMEM((rows + 6, cols + 16, LANES), F32),
            pltpu.VMEM((rows, cols, LANES), F32),
        ],
        input_output_aliases={9: 0} if more else {},
        compiler_params=params(16),
        cost_estimate=estimate(4),
        name="filter_grad",
    )(*whole, *more)


def input_grad_kernel(first, d_ref, l_ref, r_ref, t_ref, b_ref, k_ref, m_ref, cot_ref, *rest):
    o_ref, window, grad = rest[-3:]
    rows, cols, channels = d_ref.shape
    tall = o_ref.shape[0]
    low, high = max(0, first - 3), min(rows, first + tall + 3)
    inside = slice(low - first + 3, high - first + 3)
    group = 32 // tall * SUB

    def block(lanes):
        if first < 3:
            window[0 : 3 - first, 5 : 11 + cols, :] = t_ref[first:3, :, lanes].astype(F32)
        if first + tall > rows - 3:
            below = first + tall + 3 - rows
            window[tall + 6 - below : tall + 6, 5 : 11 + cols, :] = b_ref[:below, :, lanes].astype(F32)
        window[inside, 5:8, :] = l_ref[low:high, :, lanes].astype(F32)
        window[inside, 8 : 8 + cols, :] = d_ref[low:high, :, lanes].astype(F32)
        window[inside, 8 + cols : 11 + cols, :] = r_ref[low:high, :, lanes].astype(F32)
        for left in range(0, cols, group):
            starts = range(left, min(left + group, cols), SUB)
            sums = band_conv(window, k_ref, lanes, starts, tall, 3, True)
            for (row, start), value in sums.items():
                grad[row, start : start + SUB, :] = value
        o_ref[:, :, lanes] = (cot_ref[:, :, lanes].astype(F32) + m_ref[...] * grad[...]).astype(BF16)

    each_lane_block(channels, block)


def input_grad(d_conv, left, right, top, bot, kernel, mask, cot, first, quarters, old=None):
    rows, cols, channels = d_conv.shape
    tall = rows // 4 * quarters

    def rows_of(width):
        return pl.BlockSpec((tall, cols, width), lambda i: (first // quarters, 0, 0))

    whole = (d_conv, left, right, top, bot, kernel)
    more = [] if old is None else [old]
    return pl.pallas_call(
        functools.partial(input_grad_kernel, rows // 4 * first),
        grid=(1,),
        out_shape=jax.ShapeDtypeStruct((rows, cols, channels), BF16),
        in_specs=[once(x.shape) for x in whole]
        + [rows_of(LANES), rows_of(channels)]
        + [UNUSED] * len(more),
        out_specs=rows_of(channels),
        scratch_shapes=[
            pltpu.VMEM((tall + 6, cols + 16, LANES), F32),
            pltpu.VMEM((tall, cols, LANES), F32),
        ],
        input_output_aliases={8: 0} if more else {},
        compiler_params=params(16),
        cost_estimate=estimate(4),
        name="input_grad",
    )(*whole, mask, cot, *more)


def finish_kernel(
    a_ref, load_a_ref, b_ref, load_ref, small_ref, wo_ref, wi_ref, gk_ref, gsc_ref, gga_ref, gsh_ref, gbo_ref, gbi_ref
):
    channels = wi_ref.shape[0]
    border = a_ref.shape[3]
    rest = channels - border
    blocks = channels // LANES
    for index, ref in ((0, wo_ref), (1, wi_ref)):
        came_a = load_a_ref[index * border : (index + 1) * border, :].astype(F32)
        came_b = load_ref[index * rest : (index + 1) * rest, :].astype(F32)
        grad = jnp.concatenate([a_ref[index, 0, 0] + came_a, b_ref[index, 1, 0] + came_b], axis=0)
        ref[...] = grad.T if index == 0 else grad
    for block in range(blocks):
        at = 2 * rest + block * 64
        total = small_ref[block] + load_ref[at : at + 64, :].astype(F32)
        lanes = slice(block * LANES, (block + 1) * LANES)
        for row in range(7):
            gk_ref[row, :, lanes] = total[row * 8 : row * 8 + 7]
        for row, ref in enumerate((gsc_ref, gga_ref, gsh_ref, gbo_ref)):
            ref[:, lanes] = total[56 + row : 57 + row]
        for row in range(4):
            to = slice(row * channels + block * LANES, row * channels + (block + 1) * LANES)
            gbi_ref[:, to] = total[60 + row : 61 + row]


def finish(first, load_first, second, load, small, hidden):
    channels = first.shape[3] + second.shape[3]
    width = first.shape[4]
    line = jax.ShapeDtypeStruct((1, channels), F32)
    return pl.pallas_call(
        finish_kernel,
        out_shape=[
            jax.ShapeDtypeStruct((width, channels), F32),
            jax.ShapeDtypeStruct((channels, width), F32),
            jax.ShapeDtypeStruct((7, 7, channels), F32),
            line,
            line,
            line,
            line,
            jax.ShapeDtypeStruct((1, hidden), F32),
        ],
        compiler_params=params(16),
        cost_estimate=estimate(2),
        name="finish",
    )(first, load_first, second, load, small)


def swap(values, axis, bit):
    count = lax.axis_size(axis)
    return lax.ppermute(values, axis, [(i, i ^ bit) for i in range(count)])


def bits_of(axis):
    return [1 << k for k in range(int(math.log2(lax.axis_size(axis))))]


def after(value, *others):
    return lax.optimization_barrier((value,) + others)[0]


def halves(values, axis, dim, bit):
    mine = (lax.axis_index(axis) // bit) % 2 == 1
    shape = values.shape
    paired = values.reshape(shape[:dim] + (shape[dim] // 2, 2) + shape[dim + 1 :])
    low = lax.index_in_dim(paired, 0, dim + 1, keepdims=False)
    high = lax.index_in_dim(paired, 1, dim + 1, keepdims=False)
    return jnp.where(mine, high, low), jnp.where(mine, low, high).astype(BF16)


def side_halo(last, first):
    count = lax.axis_size("lon")
    ahead = [(i, (i + 1) % count) for i in range(count)]
    back = [((i + 1) % count, i) for i in range(count)]
    return lax.ppermute(last, "lon", ahead), lax.ppermute(first, "lon", back)


def end_rows(head, tail, left, right):
    rows = left.shape[0]
    return (
        jnp.concatenate([left[rows - 3 :], tail, right[rows - 3 :]], axis=1),
        jnp.concatenate([left[:3], head, right[:3]], axis=1),
    )


def end_halo(tail, head):
    count = lax.axis_size("lat")
    ahead = [(i, i + 1) for i in range(count - 1)]
    back = [(i + 1, i) for i in range(count - 1)]
    return lax.ppermute(tail, "lat", ahead), lax.ppermute(head, "lat", back)


def per_device(
    fields,
    land_mask,
    cotangent,
    kernel,
    layer_norm_gain,
    layer_norm_bias,
    w_in,
    b_in,
    w_out,
    b_out,
    layer_scale,
):
    rows, cols, channels = fields.shape
    cells = rows * cols
    hidden = w_in.shape[1]
    n_lon, n_lat = lax.axis_size("lon"), lax.axis_size("lat")
    gain, bias = layer_norm_gain.reshape(1, -1), layer_norm_bias.reshape(1, -1)
    scale = layer_scale.reshape(1, -1)
    cot_rows = cotangent.reshape(cells, channels)
    mask = jnp.broadcast_to(land_mask.astype(F32)[:, :, None], (rows, cols, LANES))
    ocean = land_mask.astype(BF16)[:, :, None]
    left, right = side_halo(fields[:, cols - 3 :] * ocean[:, cols - 3 :], fields[:, :3] * ocean[:, :3])
    lon = lax.axis_index("lon")
    core, side_y = lon % 2, (lon // 2) % 2
    quads = 4 * jnp.arange(n_lon // 4, dtype=jnp.int32)
    order = jnp.concatenate(
        [quads + 2 * y + c for c in (1 - core, core) for y in (1 - side_y, side_y)]
    )
    top, bot = end_halo(
        *end_rows(
            fields[:3] * ocean[:3], fields[rows - 3 :] * ocean[rows - 3 :],
            after(left, mask, order), after(right, mask, order),
        )
    )

    d_conv, d_first, d_last, mixed, sums, g_bi, sent, kept = expand(
        order, left, right, top, bot, kernel, gain, bias, scale, b_out.reshape(1, -1), mask, cot_rows,
        fields, w_in, b_in.reshape(1, -1), w_out, n_lon, n_lat,
    )
    got = swap(sent, "lon", 1)
    d_conv = d_conv.reshape(rows, cols, channels)
    d_left, d_right = side_halo(d_last, d_first)

    far = n_lon // 4
    border = channels // 2
    lon_bits = [("lon", 1, bit) for bit in bits_of("lon")[2:]]
    lat_bits = [("lat", 2, bit) for bit in bits_of("lat")]

    def split_lat(x):
        if x.shape[2] != n_lat:
            x = x.reshape(x.shape[0], x.shape[1], x.shape[3], n_lat, -1).transpose(0, 1, 3, 2, 4)
        return x

    def pair(lons, piece, last=None):
        a, b = (kept, got) if last is None else (after(kept, last), after(got, last))
        return split_lat(a[:, lons, :, piece].astype(F32) + b[:, lons, :, piece].astype(F32))

    def fold(mine, sent, axis, bit, last):
        return after(mine, last) + after(swap(sent, axis, bit), last).astype(F32)

    first, second = slice(0, border), slice(border, channels)
    near_lons, far_lons = slice(far, 2 * far), slice(0, far)
    far_first = pair(far_lons, first).astype(BF16)
    got_first = swap(far_first, "lon", 2)
    cut_b = halves(pair(slice(0, 2 * far), second), *lat_bits[0])
    rest = (mask, left, right, top, bot, d_conv, sums, g_bi)
    small = filter_grad(after(fields, far_first, cut_b[1]), *rest, 0)
    d_tail, d_head = end_rows(
        d_conv[:3], d_conv[rows - 3 :], after(d_left, small), after(d_right, small)
    )
    d_top, d_bot = end_halo(d_tail, d_head)
    for (axis, _, bit), follow in zip(lat_bits[:-1], lat_bits[1:]):
        cut_b = halves(fold(*cut_b, axis, bit, small), *follow)

    def pack(sent, small):
        return jnp.concatenate([sent.reshape(-1, LANES), small.astype(BF16).reshape(-1, LANES)])

    def ride(came, sent, small, last):
        size = sent.size // LANES
        own = after(lax.reduce_precision(small, 8, 7), last)
        return came[:size].reshape(sent.shape).astype(F32), own + came[size:].astype(F32).reshape(small.shape)

    small = filter_grad(after(fields, d_tail, d_head, cut_b[1]), *rest, 1, small)
    alone = small
    whole = pair(near_lons, first, alone) + after(got_first, alone).astype(F32)
    whole_b = fold(*cut_b, lat_bits[-1][0], lat_bits[-1][2], alone)
    far_second = whole_b[:, far_lons].astype(BF16)
    back = (d_left, d_right, d_top, d_bot, kernel, mask, cotangent)
    grad_fields, block = None, 0
    steps = lon_bits + lat_bits
    early = halves(whole, *steps[0])[1]
    small = after(alone, early, far_second) + after(swap(alone, "lon", 1), early, far_second)
    for index, (axis, dim, bit) in enumerate(steps):
        mine, sent = halves(whole, axis, dim, bit)
        load = pack(sent, small)
        last = load
        if index >= len(steps) - 2:
            count = 2 if grad_fields is None else 1
            last = grad_fields = input_grad(
                after(d_conv, load, far_second), *back, block, count, grad_fields
            )
            block += count
        load_a, mine_a = after(swap(load, axis, bit), last), after(mine, last)
        came, small = ride(load_a, sent, small, last)
        whole = mine_a + came
    load = pack(far_second, small)
    last = grad_fields = input_grad(after(d_conv, load), *back, block, 1, grad_fields)
    if not lon_bits and whole.shape[-1] == LANES:
        load = after(swap(load, "lon", 2), last)
        grad_wo, grad_wi, grad_k, *lines, g_bi = finish(
            mine_a, load_a, after(whole_b, last), load, after(lax.reduce_precision(small, 8, 7), last), hidden
        )
        g_scale, g_gain, g_shift, g_bo = (line.reshape(channels) for line in lines)
    else:
        came, small = ride(after(swap(load, "lon", 2), last), far_second, small, last)
        whole_b = after(whole_b, last)[:, near_lons] + came
        for axis, dim, bit in lon_bits:
            whole_b = fold(*halves(whole_b, axis, dim, bit), axis, bit, last)
        grad_w = jnp.concatenate([x[:, 0, 0] for x in (whole, whole_b)], axis=1)
        grad_wo, grad_wi = grad_w[0].T, grad_w[1]
        small = small.transpose(1, 0, 2).reshape(8, 8, channels)
        grad_k, g_bi = small[:7, :7], small[7, 4:]
        g_scale, g_gain, g_shift, g_bo = (small[7, i] for i in range(4))
    return (
        mixed.reshape(rows, cols, channels),
        grad_fields,
        grad_k,
        g_gain,
        g_shift,
        grad_wi,
        g_bi.reshape(hidden),
        grad_wo,
        g_bo,
        g_scale,
    )


def solution(mesh):
    placed = (
        P(("grp", "lat"), "lon", None),
        P(("grp", "lat"), "lon"),
        P(("grp", "lat"), "lon", None),
        P(),
        P(),
        P(),
        P(),
        P(),
        P(),
        P(),
        P(),
    )
    return jax.shard_map(
        per_device,
        mesh=mesh,
        in_specs=placed,
        out_specs=(
            P(("grp", "lat"), "lon", None),
            P(("grp", "lat"), "lon", None),
            P("grp", None, None),
            P("grp"),
            P("grp"),
            P("grp", ("lon", "lat")),
            P("grp"),
            P(("lon", "lat"), "grp"),
            P("grp"),
            P("grp"),
        ),
        check_vma=False,
    )
```

```python
import functools
import math

import jax
import jax.numpy as jnp
from jax import lax
from jax.experimental import pallas as pl
from jax.experimental.pallas import tpu as pltpu
from jax.sharding import PartitionSpec as P

F32 = jnp.float32
BF16 = jnp.bfloat16
LANES = 128
SUB = 8


def params(mib):
    return pltpu.CompilerParams(vmem_limit_bytes=mib * 1024 * 1024)


def estimate(micros):
    return pl.CostEstimate(
        flops=int(micros * 1.15e9), bytes_accessed=int(micros * 3.6e6), transcendentals=0
    )


def once(shape):
    zeros = (0,) * len(shape)
    return pl.BlockSpec(shape, lambda *_: zeros, pipeline_mode=pl.Buffered(1))


UNUSED = pl.BlockSpec(memory_space=pl.ANY)


def whole_spec(shape):
    zeros = (0,) * len(shape)
    return pl.BlockSpec(shape, lambda *_: zeros)


def shifted(window, row, start, offset):
    return window[row, pl.ds(start + offset, SUB), :]


def lane_block(index):
    return pl.ds(pl.multiple_of(index * LANES, LANES), LANES)


def each_lane_block(channels, body):
    def one(index, _):
        body(lane_block(index))
        return 0

    lax.fori_loop(0, channels // LANES, one, 0)


def band_conv(window, k_ref, lanes, starts, rows, pad, flip):
    sums = {}
    for col_off in range(7):
        at = 6 - col_off if flip else col_off
        weights = [k_ref[6 - p if flip else p, at : at + 1, lanes] for p in range(7)]
        for start in starts:
            for src in range(window.shape[0]):
                hits = [(src - pad - row_off + 3, row_off) for row_off in range(7)]
                hits = [(out, row_off) for out, row_off in hits if 0 <= out < rows]
                if not hits:
                    continue
                cells = shifted(window, src, start, 5 + col_off)
                for out, row_off in hits:
                    term = weights[row_off] * cells
                    key = (out, start)
                    sums[key] = sums[key] + term if key in sums else term
    return sums


def gelu_twice(x):
    root = math.sqrt(2.0 / math.pi)
    inner = root + (root * 0.044715) * (x * x)
    tanh = jnp.tanh(x * inner)
    both = 1.0 + tanh
    value = x * both
    slope = both + value * ((1.0 - tanh) * (3.0 * inner - 2.0 * root))
    return value, slope


def expand_kernel(
    order_ref,
    l_ref, r_ref, t_ref, b_ref, k_ref, gain_ref, bias_ref, scale_ref, bo_ref, m_ref, cot_ref, f_ref,
    wi_ref, bi_ref, wo_ref,
    dconv_ref, first_ref, last_ref, mixed_ref, sums_ref, gbi_ref, sent_ref, kept_ref,
    window, conv, xhat_s, inv_s, normed, normed_t, dbr, dbr_t, act, dpre, d_normed, branch, pre_s, d_act,
):
    rows, cols, channels = f_ref.shape
    cells = rows * cols
    strip = 16
    chunk = 128
    step_now = pl.program_id(0)
    wide = channels // LANES

    def strips(body, sums):
        def some(index, sums):
            places = [
                (2 * index + more, at, pl.ds(pl.multiple_of((2 * index + more) * cols + at, strip), strip))
                for more in range(2)
                for at in range(0, cols, strip)
            ]
            return body(places, sums)

        return lax.fori_loop(0, rows // 2, some, sums)

    def folded(values):
        return sum(value[:SUB] + value[SUB:] for value in values)

    def mean(values):
        return [jnp.mean(value, axis=-1, keepdims=True) for value in values]

    def ocean(places):
        return [jnp.concatenate([m_ref[row, at : at + strip, :]] * wide, axis=1) for row, at, _ in places]

    zero = jnp.zeros((SUB, channels), F32)

    @pl.when(step_now == 0)
    def _():
        branch[...] = jnp.zeros_like(branch)
        d_normed[...] = jnp.zeros_like(d_normed)

        def cotangents(places, total):
            grads = [
                mask * (scale_ref[...] * cot_ref[here, :].astype(F32))
                for mask, (_, _, here) in zip(ocean(places), places)
            ]
            for (_, _, here), grad in zip(places, grads):
                dbr[here, :] = (0.5 * grad).astype(BF16)
            return total + folded(grads)

        sums_ref[0] = strips(cotangents, zero)
        for at in range(0, cells, chunk):
            here = slice(at, at + chunk)
            dbr_t[:, here] = dbr[here, :].T
        share = wo_ref.shape[0] // wide

        def convolve(index, _):
            lanes = lane_block(index)
            units = pl.ds(pl.multiple_of(index * share, LANES), share)
            fill_window(window, f_ref[:, :, lanes].astype(F32) * m_ref[...], l_ref, r_ref, t_ref, b_ref, lanes)
            for start in range(0, cols, SUB):
                here = slice(start * rows, (start + SUB) * rows)
                d_act[here, units] = lax.dot_general(
                    dbr[here, :], wo_ref[units, :], (((1,), (1,)), ((), ())), preferred_element_type=F32
                )
                sums = band_conv(window, k_ref, lanes, (start,), rows, 3, False)
                for row in range(rows):
                    conv[row, start : start + SUB, lanes] = sums[row, start]
            return 0

        lax.fori_loop(0, wide, convolve, 0)

        def standardize(places, _):
            xs = [conv[row, at : at + strip, :] for row, at, _ in places]
            centered = [x - average for x, average in zip(xs, mean(xs))]
            invs = [lax.rsqrt(var + 1e-06) for var in mean([x * x for x in centered])]
            for (_, _, here), x, inv in zip(places, centered, invs):
                xhat = x * inv
                xhat_s[here, :] = xhat
                inv_s[here, :] = jnp.broadcast_to(inv, (strip, LANES))
                normed[here, :] = (xhat * gain_ref[...] + bias_ref[...]).astype(BF16)
            return 0

        strips(standardize, 0)
        for at in range(0, cells, chunk):
            here = slice(at, at + chunk)
            normed_t[:, here] = normed[here, :].T

    block = act.shape[1]
    cut = min(block, 256)
    count = block // cut
    _, parts, _, width = sent_ref.shape
    is_sent = step_now < pl.num_programs(0) // 2
    base = pl.multiple_of(order_ref[step_now] * block, LANES)

    def products(index):
        lanes = slice(index * cut, (index + 1) * cut)
        pre_s[index % 2] = jnp.dot(normed[...], wi_ref[:, lanes], preferred_element_type=F32)

    def activate(index):
        lanes = slice(index * cut, (index + 1) * cut)
        units = pl.ds(pl.multiple_of(base + index * cut, LANES), cut)
        bias = bi_ref[:, lanes]
        total = jnp.zeros((SUB, cut), F32)
        for at in range(0, cells, strip):
            here = slice(at, at + strip)
            value, slope = gelu_twice(pre_s[index % 2, here, :] + bias)
            act[here, lanes] = value.astype(BF16)
            d_pre = d_act[here, units] * slope
            dpre[here, lanes] = d_pre.astype(BF16)
            total = total + (d_pre[:SUB] + d_pre[SUB:])
        gbi_ref[:, lanes] = jnp.sum(total, axis=0, keepdims=True)

    def weight_grads(index):
        left = index * cut
        for which, (rows_t, source) in enumerate(((dbr_t, act), (normed_t, dpre))):
            grad = jnp.dot(
                rows_t[...], source[:, left : left + cut], preferred_element_type=F32
            ).astype(BF16)

            size = min(width, cut)
            for at in range(0, cut, size):
                lat, into = divmod(left + at, width)
                spot = (which, lat, slice(None), slice(into, into + size))
                value = grad[:, at : at + size]
                kept_ref[spot] = value
                sent_ref[spot] = jnp.where(is_sent, value, sent_ref[spot])

    products(0)
    for index in range(count):
        if index + 1 < count:
            products(index + 1)
        activate(index)
        if index > 0:
            weight_grads(index - 1)
    weight_grads(count - 1)
    branch[...] += jnp.dot(act[...], wo_ref[pl.ds(base, block), :], preferred_element_type=F32)
    d_normed[...] += lax.dot_general(
        dpre[...], wi_ref[...], (((1,), (1,)), ((), ())), preferred_element_type=F32
    )

    @pl.when(step_now == pl.num_programs(0) - 1)
    def _():
        def norm_back(places, sums):
            heres = [here for _, _, here in places]
            branches = [
                mask * (0.5 * branch[here, :] + bo_ref[...]) for mask, here in zip(ocean(places), heres)
            ]
            xhats = [xhat_s[here, :] for here in heres]
            grads = [d_normed[here, :] for here in heres]
            terms = [grad * xhat for grad, xhat in zip(grads, xhats)]
            es = [grad * gain_ref[...] for grad in grads]
            m1s = mean(es)
            m2s = mean([e * xhat for e, xhat in zip(es, xhats)])
            for (row, at, here), e, xhat, m1, m2, value in zip(places, es, xhats, m1s, m2s, branches):
                inv = jnp.concatenate([inv_s[here, :]] * wide, axis=1)
                d_conv = inv * (e - m1 - xhat * m2)
                dconv_ref[here, :] = d_conv.astype(BF16)
                if at == 0:
                    first_ref[row] = d_conv[:3].astype(BF16)
                if at == cols - strip:
                    last_ref[row] = d_conv[strip - 3 :].astype(BF16)
                field = f_ref[row, at : at + strip, :].astype(F32)
                mixed_ref[here, :] = (field + value * scale_ref[...]).astype(BF16)
            products = [value * cot_ref[here, :].astype(F32) for value, here in zip(branches, heres)]
            return tuple(total + folded(x) for total, x in zip(sums, (products, terms, grads)))

        sums_ref[1], sums_ref[2], sums_ref[3] = strips(norm_back, (zero, zero, zero))


def expand(
    order, left, right, top, bot, kernel, gain, bias, scale, b_out, mask, cot, fields, w_in, b_in, w_out, n_lon, n_lat
):
    rows, cols, channels = fields.shape
    hidden = w_in.shape[1]
    cells = rows * cols
    block = hidden // n_lon
    split = n_lat if (block // n_lat) % LANES == 0 else 1
    turn = n_lon // 2
    grads = (split, channels, block // split)
    given = (left, right, top, bot, kernel, gain, bias, scale, b_out, mask, cot, fields)

    def sent_at(h, order):
        return (0, jnp.minimum(h, turn - 1), 0, 0, 0)

    def kept_at(h, order):
        return (0, jnp.maximum(h - turn, 0), 0, 0, 0)

    return pl.pallas_call(
        expand_kernel,
        grid_spec=pltpu.PrefetchScalarGridSpec(
            num_scalar_prefetch=1,
            grid=(n_lon,),
            in_specs=[once(x.shape) for x in given]
            + [
                pl.BlockSpec((channels, block), lambda h, order: (0, order[h])),
                pl.BlockSpec((1, block), lambda h, order: (0, order[h])),
                once(w_out.shape),
            ],
            out_specs=[
                once((cells, channels)),
                once((rows, 3, channels)),
                once((rows, 3, channels)),
                once((cells, channels)),
                once((4, SUB, channels)),
                pl.BlockSpec((1, block), lambda h, order: (0, order[h])),
                pl.BlockSpec((2, None) + grads, sent_at),
                pl.BlockSpec((2, None) + grads, kept_at),
            ],
            scratch_shapes=[
                pltpu.VMEM((rows + 6, cols + 16, LANES), F32),
                pltpu.VMEM((rows, cols, channels), F32),
                pltpu.VMEM((cells, channels), F32),
                pltpu.VMEM((cells, LANES), F32),
                pltpu.VMEM((cells, channels), BF16),
                pltpu.VMEM((channels, cells), BF16),
                pltpu.VMEM((cells, channels), BF16),
                pltpu.VMEM((channels, cells), BF16),
                pltpu.VMEM((cells, block), BF16),
                pltpu.VMEM((cells, block), BF16),
                pltpu.VMEM((cells, channels), F32),
                pltpu.VMEM((cells, channels), F32),
                pltpu.VMEM((2, cells, min(block, 256)), F32),
                pltpu.VMEM((cells, hidden), F32),
            ],
        ),
        out_shape=[
            jax.ShapeDtypeStruct((cells, channels), BF16),
            jax.ShapeDtypeStruct((rows, 3, channels), BF16),
            jax.ShapeDtypeStruct((rows, 3, channels), BF16),
            jax.ShapeDtypeStruct((cells, channels), BF16),
            jax.ShapeDtypeStruct((4, SUB, channels), F32),
            jax.ShapeDtypeStruct((1, hidden), F32),
            jax.ShapeDtypeStruct((2, turn) + grads, BF16),
            jax.ShapeDtypeStruct((2, turn) + grads, BF16),
        ],
        compiler_params=params(56),
        cost_estimate=estimate(20),
        name="expand",
    )(order, *given, w_in, b_in, w_out)


def fill_window(window, center, l_ref, r_ref, t_ref, b_ref, lanes):
    rows, cols, _ = center.shape
    window[0:3, 5 : 11 + cols, :] = t_ref[:, :, lanes].astype(F32)
    window[3 : 3 + rows, 5:8, :] = l_ref[:, :, lanes].astype(F32)
    window[3 : 3 + rows, 8 : 8 + cols, :] = center
    window[3 : 3 + rows, 8 + cols : 11 + cols, :] = r_ref[:, :, lanes].astype(F32)
    window[3 + rows : 6 + rows, 5 : 11 + cols, :] = b_ref[:, :, lanes].astype(F32)


def filter_grad_kernel(first, f_ref, m_ref, l_ref, r_ref, t_ref, b_ref, d_ref, sums_ref, gbi_ref, *rest):
    o_ref, window, grad = rest[-3:]
    rows, cols, channels = f_ref.shape
    blocks = channels // LANES

    def block(index, _):
        lanes = lane_block(first + index)
        fill_window(window, f_ref[:, :, lanes].astype(F32) * m_ref[...], l_ref, r_ref, t_ref, b_ref, lanes)
        grad[...] = d_ref[:, :, lanes].astype(F32)
        for col_off in range(7):

            def band(step, sums):
                start = pl.multiple_of(step * SUB, SUB)
                sums = list(sums)
                held = {}
                for src in range(rows + 6):
                    if src < rows:
                        held[src] = grad[src, pl.ds(start, SUB), :]
                    cells = shifted(window, src, start, 5 + col_off)
                    for row_off in range(7):
                        out = src - row_off
                        if 0 <= out < rows:
                            sums[row_off] = sums[row_off] + held[out] * cells
                return tuple(sums)

            sums = tuple(jnp.zeros((SUB, LANES), F32) for _ in range(7))
            sums = lax.fori_loop(0, cols // SUB, band, sums)
            for row_off in range(7):
                at = row_off * 8 + col_off
                o_ref[index, at : at + 1, :] = jnp.sum(sums[row_off], axis=0, keepdims=True)
        for row_off in range(7):
            o_ref[index, row_off * 8 + 7 : row_off * 8 + 8, :] = jnp.zeros((1, LANES), F32)
        for at, source in enumerate((1, 2, 3, 0)):
            o_ref[index, 56 + at : 57 + at, :] = jnp.sum(sums_ref[source, :, lanes], axis=0, keepdims=True)
        for at in range(4):
            o_ref[index, 60 + at : 61 + at, :] = gbi_ref[:, lane_block(at * blocks + first + index)]
        return 0

    lax.fori_loop(0, o_ref.shape[0], block, 0)


def filter_grad(fields, mask, left, right, top, bot, d_conv, sums, gbi, half, old=None):
    rows, cols, channels = fields.shape
    blocks = channels // LANES
    whole = (fields, mask, left, right, top, bot, d_conv, sums, gbi)
    more = [] if old is None else [old]
    return pl.pallas_call(
        functools.partial(filter_grad_kernel, half * (blocks // 2)),
        grid=(1,),
        out_shape=jax.ShapeDtypeStruct((blocks, 64, LANES), F32),
        in_specs=[once(x.shape) for x in whole] + [UNUSED] * len(more),
        out_specs=pl.BlockSpec((blocks // 2, 64, LANES), lambda i: (half, 0, 0)),
        scratch_shapes=[
            pltpu.VMEM((rows + 6, cols + 16, LANES), F32),
            pltpu.VMEM((rows, cols, LANES), F32),
        ],
        input_output_aliases={9: 0} if more else {},
        compiler_params=params(16),
        cost_estimate=estimate(4),
        name="filter_grad",
    )(*whole, *more)


def input_grad_kernel(first, d_ref, l_ref, r_ref, t_ref, b_ref, k_ref, m_ref, cot_ref, *rest):
    o_ref, window, grad = rest[-3:]
    rows, cols, channels = d_ref.shape
    tall = o_ref.shape[0]
    low, high = max(0, first - 3), min(rows, first + tall + 3)
    inside = slice(low - first + 3, high - first + 3)
    group = 32 // tall * SUB

    def block(lanes):
        if first < 3:
            window[0 : 3 - first, 5 : 11 + cols, :] = t_ref[first:3, :, lanes].astype(F32)
        if first + tall > rows - 3:
            below = first + tall + 3 - rows
            window[tall + 6 - below : tall + 6, 5 : 11 + cols, :] = b_ref[:below, :, lanes].astype(F32)
        window[inside, 5:8, :] = l_ref[low:high, :, lanes].astype(F32)
        window[inside, 8 : 8 + cols, :] = d_ref[low:high, :, lanes].astype(F32)
        window[inside, 8 + cols : 11 + cols, :] = r_ref[low:high, :, lanes].astype(F32)
        for left in range(0, cols, group):
            starts = range(left, min(left + group, cols), SUB)
            sums = band_conv(window, k_ref, lanes, starts, tall, 3, True)
            for (row, start), value in sums.items():
                grad[row, start : start + SUB, :] = value
        o_ref[:, :, lanes] = (cot_ref[:, :, lanes].astype(F32) + m_ref[...] * grad[...]).astype(BF16)

    each_lane_block(channels, block)


def input_grad(d_conv, left, right, top, bot, kernel, mask, cot, first, quarters, old=None):
    rows, cols, channels = d_conv.shape
    tall = rows // 4 * quarters

    def rows_of(width):
        return pl.BlockSpec((tall, cols, width), lambda i: (first // quarters, 0, 0))

    whole = (d_conv, left, right, top, bot, kernel)
    more = [] if old is None else [old]
    return pl.pallas_call(
        functools.partial(input_grad_kernel, rows // 4 * first),
        grid=(1,),
        out_shape=jax.ShapeDtypeStruct((rows, cols, channels), BF16),
        in_specs=[once(x.shape) for x in whole]
        + [rows_of(LANES), rows_of(channels)]
        + [UNUSED] * len(more),
        out_specs=rows_of(channels),
        scratch_shapes=[
            pltpu.VMEM((tall + 6, cols + 16, LANES), F32),
            pltpu.VMEM((tall, cols, LANES), F32),
        ],
        input_output_aliases={8: 0} if more else {},
        compiler_params=params(16),
        cost_estimate=estimate(4),
        name="input_grad",
    )(*whole, mask, cot, *more)


def finish_kernel(
    a_ref, load_a_ref, b_ref, load_ref, small_ref, wo_ref, wi_ref, gk_ref, gsc_ref, gga_ref, gsh_ref, gbo_ref, gbi_ref
):
    channels = wi_ref.shape[0]
    border = a_ref.shape[3]
    rest = channels - border
    blocks = channels // LANES
    for index, ref in ((0, wo_ref), (1, wi_ref)):
        came_a = load_a_ref[index * border : (index + 1) * border, :].astype(F32)
        came_b = load_ref[index * rest : (index + 1) * rest, :].astype(F32)
        grad = jnp.concatenate([a_ref[index, 0, 0] + came_a, b_ref[index, 1, 0] + came_b], axis=0)
        ref[...] = grad.T if index == 0 else grad
    for block in range(blocks):
        at = 2 * rest + block * 64
        total = small_ref[block] + load_ref[at : at + 64, :].astype(F32)
        lanes = slice(block * LANES, (block + 1) * LANES)
        for row in range(7):
            gk_ref[row, :, lanes] = total[row * 8 : row * 8 + 7]
        for row, ref in enumerate((gsc_ref, gga_ref, gsh_ref, gbo_ref)):
            ref[:, lanes] = total[56 + row : 57 + row]
        for row in range(4):
            to = slice(row * channels + block * LANES, row * channels + (block + 1) * LANES)
            gbi_ref[:, to] = total[60 + row : 61 + row]


def finish(first, load_first, second, load, small, hidden):
    channels = first.shape[3] + second.shape[3]
    width = first.shape[4]
    line = jax.ShapeDtypeStruct((1, channels), F32)
    return pl.pallas_call(
        finish_kernel,
        out_shape=[
            jax.ShapeDtypeStruct((width, channels), F32),
            jax.ShapeDtypeStruct((channels, width), F32),
            jax.ShapeDtypeStruct((7, 7, channels), F32),
            line,
            line,
            line,
            line,
            jax.ShapeDtypeStruct((1, hidden), F32),
        ],
        compiler_params=params(16),
        cost_estimate=estimate(2),
        name="finish",
    )(first, load_first, second, load, small)


def swap(values, axis, bit):
    count = lax.axis_size(axis)
    return lax.ppermute(values, axis, [(i, i ^ bit) for i in range(count)])


def bits_of(axis):
    return [1 << k for k in range(int(math.log2(lax.axis_size(axis))))]


def after(value, *others):
    return lax.optimization_barrier((value,) + others)[0]


def halves(values, axis, dim, bit):
    mine = (lax.axis_index(axis) // bit) % 2 == 1
    shape = values.shape
    paired = values.reshape(shape[:dim] + (shape[dim] // 2, 2) + shape[dim + 1 :])
    low = lax.index_in_dim(paired, 0, dim + 1, keepdims=False)
    high = lax.index_in_dim(paired, 1, dim + 1, keepdims=False)
    return jnp.where(mine, high, low), jnp.where(mine, low, high).astype(BF16)


def side_halo(last, first):
    count = lax.axis_size("lon")
    ahead = [(i, (i + 1) % count) for i in range(count)]
    back = [((i + 1) % count, i) for i in range(count)]
    return lax.ppermute(last, "lon", ahead), lax.ppermute(first, "lon", back)


def end_rows(head, tail, left, right):
    rows = left.shape[0]
    return (
        jnp.concatenate([left[rows - 3 :], tail, right[rows - 3 :]], axis=1),
        jnp.concatenate([left[:3], head, right[:3]], axis=1),
    )


def end_halo(tail, head):
    count = lax.axis_size("lat")
    ahead = [(i, i + 1) for i in range(count - 1)]
    back = [(i + 1, i) for i in range(count - 1)]
    return lax.ppermute(tail, "lat", ahead), lax.ppermute(head, "lat", back)


def per_device(
    fields,
    land_mask,
    cotangent,
    kernel,
    layer_norm_gain,
    layer_norm_bias,
    w_in,
    b_in,
    w_out,
    b_out,
    layer_scale,
):
    rows, cols, channels = fields.shape
    cells = rows * cols
    hidden = w_in.shape[1]
    n_lon, n_lat = lax.axis_size("lon"), lax.axis_size("lat")
    gain, bias = layer_norm_gain.reshape(1, -1), layer_norm_bias.reshape(1, -1)
    scale = layer_scale.reshape(1, -1)
    cot_rows = cotangent.reshape(cells, channels)
    mask = jnp.broadcast_to(land_mask.astype(F32)[:, :, None], (rows, cols, LANES))
    ocean = land_mask.astype(BF16)[:, :, None]
    left, right = side_halo(fields[:, cols - 3 :] * ocean[:, cols - 3 :], fields[:, :3] * ocean[:, :3])
    lon = lax.axis_index("lon")
    core, side_y = lon % 2, (lon // 2) % 2
    quads = 4 * jnp.arange(n_lon // 4, dtype=jnp.int32)
    order = jnp.concatenate(
        [quads + 2 * y + c for c in (1 - core, core) for y in (1 - side_y, side_y)]
    )
    top, bot = end_halo(
        *end_rows(
            fields[:3] * ocean[:3], fields[rows - 3 :] * ocean[rows - 3 :],
            after(left, mask, order), after(right, mask, order),
        )
    )

    d_conv, d_first, d_last, mixed, sums, g_bi, sent, kept = expand(
        order, left, right, top, bot, kernel, gain, bias, scale, b_out.reshape(1, -1), mask, cot_rows,
        fields, w_in, b_in.reshape(1, -1), w_out, n_lon, n_lat,
    )
    got = swap(sent, "lon", 1)
    d_conv = d_conv.reshape(rows, cols, channels)
    d_left, d_right = side_halo(d_last, d_first)

    far = n_lon // 4
    border = channels * 9 // 16
    lon_bits = [("lon", 1, bit) for bit in bits_of("lon")[2:]]
    lat_bits = [("lat", 2, bit) for bit in bits_of("lat")]

    def split_lat(x):
        if x.shape[2] != n_lat:
            x = x.reshape(x.shape[0], x.shape[1], x.shape[3], n_lat, -1).transpose(0, 1, 3, 2, 4)
        return x

    def pair(lons, piece, last=None):
        a, b = (kept, got) if last is None else (after(kept, last), after(got, last))
        return split_lat(a[:, lons, :, piece].astype(F32) + b[:, lons, :, piece].astype(F32))

    def fold(mine, sent, axis, bit, last):
        return after(mine, last) + after(swap(sent, axis, bit), last).astype(F32)

    first, second = slice(0, border), slice(border, channels)
    near_lons, far_lons = slice(far, 2 * far), slice(0, far)
    far_first = pair(far_lons, first).astype(BF16)
    got_first = swap(far_first, "lon", 2)
    cut_b = halves(pair(slice(0, 2 * far), second), *lat_bits[0])
    rest = (mask, left, right, top, bot, d_conv, sums, g_bi)
    small = filter_grad(after(fields, far_first, cut_b[1]), *rest, 0)
    d_tail, d_head = end_rows(
        d_conv[:3], d_conv[rows - 3 :], after(d_left, small), after(d_right, small)
    )
    d_top, d_bot = end_halo(d_tail, d_head)
    for (axis, _, bit), follow in zip(lat_bits[:-1], lat_bits[1:]):
        cut_b = halves(fold(*cut_b, axis, bit, small), *follow)

    def pack(sent, small):
        return jnp.concatenate([sent.reshape(-1, LANES), small.astype(BF16).reshape(-1, LANES)])

    def ride(came, sent, small, last):
        size = sent.size // LANES
        own = after(lax.reduce_precision(small, 8, 7), last)
        return came[:size].reshape(sent.shape).astype(F32), own + came[size:].astype(F32).reshape(small.shape)

    small = filter_grad(after(fields, d_tail, d_head, cut_b[1]), *rest, 1, small)
    alone = small
    whole = pair(near_lons, first, alone) + after(got_first, alone).astype(F32)
    whole_b = fold(*cut_b, lat_bits[-1][0], lat_bits[-1][2], alone)
    far_second = whole_b[:, far_lons].astype(BF16)
    back = (d_left, d_right, d_top, d_bot, kernel, mask, cotangent)
    grad_fields, block = None, 0
    steps = lon_bits + lat_bits
    early = halves(whole, *steps[0])[1]
    small = after(alone, early, far_second) + after(swap(alone, "lon", 1), early, far_second)
    for index, (axis, dim, bit) in enumerate(steps):
        mine, sent = halves(whole, axis, dim, bit)
        load = pack(sent, small)
        last = load
        if index >= len(steps) - 2:
            count = 2 if grad_fields is None else 1
            last = grad_fields = input_grad(
                after(d_conv, load, far_second), *back, block, count, grad_fields
            )
            block += count
        load_a, mine_a = after(swap(load, axis, bit), last), after(mine, last)
        came, small = ride(load_a, sent, small, last)
        whole = mine_a + came
    load = pack(far_second, small)
    last = grad_fields = input_grad(after(d_conv, load), *back, block, 1, grad_fields)
    if not lon_bits and whole.shape[-1] == LANES:
        load = after(swap(load, "lon", 2), last)
        grad_wo, grad_wi, grad_k, *lines, g_bi = finish(
            mine_a, load_a, after(whole_b, last), load, after(lax.reduce_precision(small, 8, 7), last), hidden
        )
        g_scale, g_gain, g_shift, g_bo = (line.reshape(channels) for line in lines)
    else:
        came, small = ride(after(swap(load, "lon", 2), last), far_second, small, last)
        whole_b = after(whole_b, last)[:, near_lons] + came
        for axis, dim, bit in lon_bits:
            whole_b = fold(*halves(whole_b, axis, dim, bit), axis, bit, last)
        grad_w = jnp.concatenate([x[:, 0, 0] for x in (whole, whole_b)], axis=1)
        grad_wo, grad_wi = grad_w[0].T, grad_w[1]
        small = small.transpose(1, 0, 2).reshape(8, 8, channels)
        grad_k, g_bi = small[:7, :7], small[7, 4:]
        g_scale, g_gain, g_shift, g_bo = (small[7, i] for i in range(4))
    return (
        mixed.reshape(rows, cols, channels),
        grad_fields,
        grad_k,
        g_gain,
        g_shift,
        grad_wi,
        g_bi.reshape(hidden),
        grad_wo,
        g_bo,
        g_scale,
    )


def solution(mesh):
    placed = (
        P(("grp", "lat"), "lon", None),
        P(("grp", "lat"), "lon"),
        P(("grp", "lat"), "lon", None),
        P(),
        P(),
        P(),
        P(),
        P(),
        P(),
        P(),
        P(),
    )
    return jax.shard_map(
        per_device,
        mesh=mesh,
        in_specs=placed,
        out_specs=(
            P(("grp", "lat"), "lon", None),
            P(("grp", "lat"), "lon", None),
            P("grp", None, None),
            P("grp"),
            P("grp"),
            P("grp", ("lon", "lat")),
            P("grp"),
            P(("lon", "lat"), "grp"),
            P("grp"),
            P("grp"),
        ),
        check_vma=False,
    )
```
